128 devices in a mesh: section: 2 (over core), tensor: 4 (over x), dp: 16 (over z, y).
Axes of the slice: x: 4, y: 4, z: 4, core: 2. Of those that a mesh axis runs over, the one named last changes fastest.
Arguments:
- layer_inputs: bfloat16 [2, 2, 2048, 768], P('section', None, 'dp'), may hold values from -6 to 6
- cotangent: bfloat16 [2, 2048, 768], P(None, 'dp'), may hold values from -6 to 6
- doc_groups: int32 [2, 16], replicated, may hold values from 0 to 16, as said below
- retrieved_at: int32 [2, 16, 256], P(None, 'dp'), may hold values from 0 to 2047, as said below
- sa_qkv: bfloat16 [2, 768, 3, 768], P('section', None, None, 'tensor'), may hold values from -0.21875 to 0.21875
- sa_out: bfloat16 [2, 768, 768], P('section', 'tensor'), may hold values from -0.4375 to 0.4375
- ffn_in: bfloat16 [2, 768, 3072], P('section', None, 'tensor'), may hold values from -0.21875 to 0.21875
- ffn_out: bfloat16 [2, 3072, 768], P('section', 'tensor'), may hold values from -0.109375 to 0.109375
- norm_gain: float32 [2, 2, 768], P('section'), may hold values from 0.5 to 1.5
- norm_bias: float32 [2, 2, 768], P('section'), may hold values from -1.25 to 1.25
- cross_q: bfloat16 [768, 768], P(None, 'tensor'), may hold values from -0.21875 to 0.21875
- cross_kv: bfloat16 [768, 2, 768], P(None, None, 'tensor'), may hold values from -0.21875 to 0.21875
- cross_out: bfloat16 [768, 768], P('tensor'), may hold values from -0.4375 to 0.4375
- cross_gain: float32 [768], replicated, may hold values from 0.5 to 1.5
- cross_bias: float32 [768], replicated, may hold values from -1.25 to 1.25
Outputs:
- block_out: bfloat16 [2, 2, 2048, 768], P('section', None, 'dp')
- input_grad: float32 [2, 2, 2048, 768], P('section', None, 'dp')
- grad_sa_qkv: float32 [2, 768, 3, 768], P('section', None, None, 'tensor')
- grad_sa_out: float32 [2, 768, 768], P('section', 'tensor')
- grad_ffn_in: float32 [2, 768, 3072], P('section', None, 'tensor')
- grad_ffn_out: float32 [2, 3072, 768], P('section', 'tensor')
- grad_norm_gain: float32 [2, 2, 768], P('section')
- grad_norm_bias: float32 [2, 2, 768], P('section')
- grad_cross_q: float32 [768, 768], P(None, 'tensor')
- grad_cross_kv: float32 [768, 2, 768], P(None, None, 'tensor')
- grad_cross_out: float32 [768, 768], P('tensor')
- grad_cross_gain: float32 [768], replicated
- grad_cross_bias: float32 [768], replicated
The draws below stay inside these ranges and needn't reach their ends.
Inputs may be any that keep to these rules, and one draw needn't show every extreme that they name: `doc_groups`: group 0 starts a document; the documents of a micro-batch tile its 16 groups in order, each covering at least 256 tokens; in one micro-batch a single document covers all groups. `retrieved_at`: each entry is below the length in tokens of the document that its group belongs to; the 256 entries of one block are distinct and rising.
All inputs are finite; a program needn't handle non-finite values.
Results may differ from the reference program's by a relative error of at most 0.033.
Values may be sent and summed in bfloat16 or wider, within the bound.
A program may use at most 128 MiB of HBM per device.

```python
import jax
import jax.numpy as jnp
from jax import lax

D = 768
HEADS = 12
HEAD = 64
FF = 3072
TOK = 128
MICRO = 2
TOPK = 256
GROUPS = 16
TOKENS = 2048


def docs_and_offsets(key):
    key_entire, key_coin, key_pick = jax.random.split(key, 3)
    fewest = (TOPK + TOK - 1) // TOK
    entire = jax.random.randint(key_entire, (), 0, MICRO)
    group_ids = jnp.arange(GROUPS, dtype=jnp.int32)
    allowed = (group_ids % fewest == 0) & (group_ids > 0) & (group_ids <= GROUPS - fewest)
    coin_flips = jax.random.randint(key_coin, (MICRO, GROUPS), 0, 2) == 1
    single_doc = (jnp.arange(MICRO) == entire)[:, None]
    begins = (group_ids == 0)[None, :] | allowed[None, :] & coin_flips & jnp.logical_not(single_doc)
    after_mask = group_ids[None, :] > group_ids[:, None]
    next_start = jnp.min(jnp.where(begins[:, None, :] & after_mask[None], group_ids[None, None, :], GROUPS), axis=2)
    group_counts = jnp.where(begins, next_start - group_ids[None, :], 0).astype(jnp.int32)
    doc_first = jnp.max(jnp.where(begins[:, None, :] & jnp.logical_not(after_mask)[None], group_ids[None, None, :], 0), axis=2)
    doc_span = jnp.take_along_axis(group_counts, doc_first, axis=1) * TOK
    slot_ids = jnp.arange(TOPK, dtype=jnp.int32)
    low_edge = slot_ids[None, None, :] * doc_span[:, :, None] // TOPK
    high_edge = (slot_ids[None, None, :] + 1) * doc_span[:, :, None] // TOPK
    interval = high_edge - low_edge
    jitter = jax.random.randint(key_pick, (MICRO, GROUPS, TOPK), 0, 1 << 20) % interval
    jitter = jnp.where(slot_ids == 0, 0, jnp.where(slot_ids == TOPK - 1, interval - 1, jitter))
    return (group_counts, (low_edge + jitter).astype(jnp.int32))


def draw_doc_groups(key, part):
    group_counts, offsets = docs_and_offsets(key)
    return group_counts


def draw_retrieved_at(key, part):
    group_counts, offsets = docs_and_offsets(key)
    return offsets


def block_levels(own_key, dims, pieces, low, top_value):
    level = 1.0
    for dim, shards_of in pieces:
        heights = jax.random.uniform(jax.random.fold_in(jax.random.fold_in(own_key, 6), dim), (shards_of,), jnp.float32, low / len(pieces), top_value / len(pieces))
        level = level * jnp.repeat(jnp.exp(heights), dims[dim] // shards_of).reshape((-1,) + (1,) * (len(dims) - 1 - dim))
    return level


def noise(stream_key, shape, deviation, most, cuts=(), kind=jnp.bfloat16):
    gain = block_levels(stream_key, shape, cuts, -0.22, 0.18) if cuts else 1.0
    result = jax.random.normal(stream_key, shape, jnp.float32) * deviation * gain
    return jnp.minimum(jnp.maximum(result, -most), most).astype(kind)


def setup_inputs(seed: int = 0) -> dict:
    seeds = jax.random.split(jax.random.key(seed), 16)
    return {
        "layer_inputs": noise(seeds[0], (2, MICRO, TOKENS, D), 1.0, 6.0, ((0, 2), (2, 16))),
        "cotangent": noise(seeds[1], (MICRO, TOKENS, D), 1.0, 6.0, ((1, 16),)),
        "doc_groups": draw_doc_groups(jax.random.fold_in(seeds[15], 71), 0),
        "retrieved_at": draw_retrieved_at(jax.random.fold_in(seeds[15], 71), 0),
        "sa_qkv": noise(seeds[4], (2, D, 3, D), D ** -0.5, 0.21875, ((0, 2), (3, 4))),
        "sa_out": noise(seeds[5], (2, D, D), (D // 4) ** -0.5, 0.4375, ((0, 2), (1, 4))),
        "ffn_in": noise(seeds[6], (2, D, FF), D ** -0.5, 0.21875, ((0, 2), (2, 4))),
        "ffn_out": noise(seeds[7], (2, FF, D), FF ** -0.5, 0.109375, ((0, 2), (1, 4))),
        "norm_gain": jnp.clip(1.0 + 0.1 * jax.random.normal(seeds[8], (2, 2, D), jnp.float32), 0.5, 1.5),
        "norm_bias": noise(seeds[9], (2, 2, D), 0.2, 1.25, ((0, 2),), jnp.float32),
        "cross_q": noise(seeds[10], (D, D), D ** -0.5, 0.21875, ((1, 4),)),
        "cross_kv": noise(seeds[11], (D, 2, D), D ** -0.5, 0.21875, ((2, 4),)),
        "cross_out": noise(seeds[12], (D, D), (D // 4) ** -0.5, 0.4375, ((0, 4),)),
        "cross_gain": jnp.clip(1.0 + 0.1 * jax.random.normal(seeds[13], (D,), jnp.float32), 0.5, 1.5),
        "cross_bias": noise(seeds[14], (D,), 0.2, 1.25, (), jnp.float32),
    }


@jax.custom_vjp
def lower_bits(v):
    return lax.optimization_barrier(v.astype(jnp.bfloat16)).astype(jnp.float32)

@jax.custom_vjp
def lower_bits_backward(v):
    return v

def low_keep(v):
    return (lower_bits(v), None)

def low_pass(kept, grad):
    return (grad,)

def back_keep(v):
    return (v, None)

def back_low(kept, grad):
    return (lower_bits(grad),)
lower_bits.defvjp(low_keep, low_pass)
lower_bits_backward.defvjp(back_keep, back_low)
epsilon = 1e-05

def matrix_product(spec, lhs_mat, rhs_mat):
    return jnp.einsum(spec, lhs_mat, rhs_mat, precision=lax.Precision.HIGHEST)

def layer_norm(residual, gain_row, bias_row):
    center = residual - lax.optimization_barrier(jnp.mean(residual, axis=-1, keepdims=True))
    spread = lax.rsqrt(lax.optimization_barrier(jnp.mean(center * center, axis=-1, keepdims=True)) + epsilon)
    return center * spread * gain_row + bias_row

def split_heads(values):
    return values.reshape(values.shape[0], values.shape[1], HEADS, HEAD)

def attention(queries, key_rows, value_rows, causal):
    scores = lower_bits_backward(matrix_product('bqhe,bkhe->bhqk', queries, key_rows) * HEAD ** (-0.5))
    if causal:
        positions_q = jnp.arange(queries.shape[1], dtype=jnp.int32)
        scores = jnp.where(positions_q[None, None, :, None] >= positions_q[None, None, None, :], scores, -1000000000.0)
    row_max = lax.optimization_barrier(jnp.max(scores, axis=-1, keepdims=True))
    exponent = jnp.exp(scores - row_max)
    attn_probs = lower_bits(exponent / lax.optimization_barrier(jnp.sum(exponent, axis=-1, keepdims=True)))
    attended = matrix_product('bhqk,bkhe->bqhe', attn_probs, value_rows)
    return lower_bits_backward(lower_bits(attended.reshape(attended.shape[0], attended.shape[1], -1)))

def self_block(inputs, w_qkv, w_out, gain_row, bias_row, causal):
    packed = lower_bits_backward(lower_bits(matrix_product('btd,dce->btce', lower_bits(inputs), w_qkv)))
    attended = attention(split_heads(packed[:, :, 0]), split_heads(packed[:, :, 1]), split_heads(packed[:, :, 2]), causal)
    branch = lower_bits_backward(matrix_product('bte,ed->btd', attended, w_out))
    return layer_norm(inputs + branch, gain_row, bias_row)

def feed_forward(inputs, w_in, w_out, gain_row, bias_row):
    hidden = lower_bits_backward(matrix_product('btd,df->btf', lower_bits(inputs), w_in))
    active = lower_bits(jax.nn.gelu(hidden, approximate=False))
    branch = lower_bits_backward(matrix_product('btf,fd->btd', active, w_out))
    return layer_norm(inputs + branch, gain_row, bias_row)

def cross_block(inputs, gathered_rows, w_query, pair_weight, w_out, gain_row, bias_row):
    queries = lower_bits_backward(lower_bits(matrix_product('btd,de->bte', lower_bits(inputs), w_query)))
    paired_row_block = lower_bits_backward(lower_bits(matrix_product('pir,rfw->pifw', gathered_rows, pair_weight)))
    attended = attention(split_heads(queries), split_heads(paired_row_block[:, :, 0]), split_heads(paired_row_block[:, :, 1]), False)
    branch = lower_bits_backward(matrix_product('bte,ed->btd', attended, w_out))
    return layer_norm(inputs + branch, gain_row, bias_row)

def reference(layer_inputs, cotangent, doc_groups, retrieved_at, sa_qkv, sa_out, ffn_in, ffn_out, norm_gain, norm_bias, cross_q, cross_kv, cross_out, cross_gain, cross_bias):
    group_ids = jnp.arange(GROUPS, dtype=jnp.int32)
    doc_first = lax.cummax(jnp.where(doc_groups > 0, group_ids[None, :], 0).astype(jnp.int32), axis=1)
    positions = (doc_first[:, :, None] * TOK + retrieved_at).astype(jnp.int32)
    flat_positions = positions.reshape(MICRO, GROUPS * TOPK, 1)

    def forward(float_inputs, w_qkv, w_sa_out, w_in, w_ff_out, gains, biases, w_query, pair_weight, w_cross_out, gain_cross, bias_cross):
        enc_in = float_inputs[0].reshape(MICRO * GROUPS, TOK, D)
        enc_mid = self_block(enc_in, w_qkv[0], w_sa_out[0], gains[0, 0], biases[0, 0], False)
        enc_out = feed_forward(enc_mid, w_in[0], w_ff_out[0], gains[0, 1], biases[0, 1])
        states = lower_bits(enc_out).reshape(MICRO, TOKENS, D)
        gathered_rows = jnp.take_along_axis(states, flat_positions, axis=1).reshape(MICRO * GROUPS, TOPK, D)
        dec_in = float_inputs[1].reshape(MICRO * GROUPS, TOK, D)
        dec_mid = self_block(dec_in, w_qkv[1], w_sa_out[1], gains[1, 0], biases[1, 0], True)
        dec_cross = cross_block(dec_mid, gathered_rows, w_query, pair_weight, w_cross_out, gain_cross, bias_cross)
        dec_out = feed_forward(dec_cross, w_in[1], w_ff_out[1], gains[1, 1], biases[1, 1])
        return (dec_out.reshape(MICRO, TOKENS, D), enc_out.reshape(MICRO, TOKENS, D))
    floats = (layer_inputs.astype(jnp.float32), sa_qkv.astype(jnp.float32), sa_out.astype(jnp.float32), ffn_in.astype(jnp.float32), ffn_out.astype(jnp.float32), norm_gain.astype(jnp.float32), norm_bias.astype(jnp.float32), cross_q.astype(jnp.float32), cross_kv.astype(jnp.float32), cross_out.astype(jnp.float32), cross_gain.astype(jnp.float32), cross_bias.astype(jnp.float32))
    dec_out, pullback, enc_out = jax.vjp(forward, *floats, has_aux=True)
    grads = pullback(cotangent.astype(jnp.float32))
    block_out = jnp.stack([enc_out, dec_out]).astype(jnp.bfloat16)
    return (block_out, grads[0], grads[1], grads[2], grads[3], grads[4], grads[5], grads[6], grads[7], grads[8], grads[9], grads[10], grads[11])
```

```python
import jax
import jax.numpy as jnp
from jax import lax
from jax.experimental import pallas as pl
from jax.experimental.pallas import tpu as pltpu
from jax.sharding import PartitionSpec as P

BF = jnp.bfloat16
F32 = jnp.float32
MESH = pl.DeviceIdType.MESH
VMEM = pltpu.VMEM
DMA = pltpu.SemaphoreType.DMA

HEAD = 64
NH = 3
EPS = 1e-05
SCALE = HEAD**-0.5
TOK = 128
D = 768
SH = 32
KEYS = 256
QW = NH * HEAD
RINGS = (2, 1, 3)

A_BO, A_IG, A_Y1, A_Y2, A_DR2, A_DRC, A_DR1 = 0, 2, 4, 6, 7, 9, 10
N_AG = 12
R_SA, R_FF, R_CR, R_DFF, R_DQ, R_DSA, R_DST = 0, 2, 4, 5, 7, 8, 10
N_RS = 11
BLOCKS = {"ffd": 768, "ffe": 768, "crx": 384, "sad": 384, "sae": 384}


def nn(a, b):
    return jnp.dot(a, b, preferred_element_type=F32)


def nt(a, b):
    return lax.dot_general(a, b, (((1,), (1,)), ((), ())), preferred_element_type=F32)


def tn(a, b):
    return lax.dot_general(a, b, (((0,), (0,)), ((), ())), preferred_element_type=F32)


def scratch_list():
    out = [
        ("xin", VMEM((2, TOK, D), BF)),
        ("nv", VMEM((2, 8, D), F32)),
        ("wsa", VMEM((2, 768, D), BF)),
        ("wff", VMEM((2, 2, 768, D), BF)),
        ("wcr", VMEM((768, D), BF)),
        ("cot", VMEM((TOK, D), BF)),
        ("pk", VMEM((2, 3 * QW, TOK), BF)),
        ("pt", VMEM((2, NH, TOK, TOK), F32)),
        ("ot", VMEM((2, QW, TOK), BF)),
        ("n1", VMEM((2, SH, D), F32)),
        ("n2", VMEM((2, SH, D), F32)),
        ("nc", VMEM((SH, D), F32)),
        ("sp", VMEM((5, SH, 128), F32)),
        ("y1f", VMEM((2, SH, D), F32)),
        ("y2f", VMEM((SH, D), F32)),
        ("dres", VMEM((2, SH, D), F32)),
        ("act", VMEM((2, TOK, D), BF)),
        ("slope", VMEM((2, TOK, D), F32)),
        ("du", VMEM((2, TOK, D), BF)),
        ("dpk", VMEM((2, 3 * QW, TOK), BF)),
        ("qct", VMEM((QW, TOK), BF)),
        ("dqct", VMEM((QW, TOK), BF)),
        ("kvct", VMEM((2 * QW, KEYS), BF)),
        ("dkvct", VMEM((2 * QW, KEYS), BF)),
        ("ptc", VMEM((NH, KEYS, TOK), F32)),
        ("oct", VMEM((QW, TOK), BF)),
        ("hot", VMEM((16 * TOK, KEYS), BF)),
        ("kvt", VMEM((16, 2 * QW, TOK), BF)),
        ("dks", VMEM((16, 2 * QW, TOK), BF)),
        ("dk1", VMEM((3, 4, 2 * QW, TOK), BF)),
        ("dk2", VMEM((3, 2 * QW, TOK), BF)),
        ("dkv", VMEM((2 * QW, TOK), BF)),
        ("vec", VMEM((16, D), F32)),
        ("vx", VMEM((4, 16, D), F32)),
        ("vc", VMEM((2, 16, D), F32)),
        ("vy", VMEM((4, 16, D), F32)),
        ("vz", VMEM((4, 16, D), F32)),
        ("ag", VMEM((N_AG, TOK, D), BF)),
        ("rs", VMEM((N_RS, TOK, D), BF)),
        ("rr", VMEM((N_RS, 3, SH, D), BF)),
        ("bor", VMEM((TOK, D), BF)),
        ("igr", VMEM((TOK, D), BF)),
        ("gof", VMEM((2, 2, 768, 384), BF)),
        ("gos", VMEM((2, 2, 384, 384), BF)),
        ("goc", VMEM((2, 384, 384), BF)),
        ("gtf", VMEM((2, 768, 384), BF)),
        ("gts", VMEM((2, 384, 384), BF)),
        ("gtc", VMEM((2, 384, 384), BF)),
        ("m_w", DMA((2, 6))),
        ("m_ws", DMA((6,))),
        ("m_l", DMA((4,))),
        ("m_ags", DMA((N_AG, 3))),
        ("m_agr", DMA((N_AG, 3))),
        ("m_rss", DMA((N_RS, 3))),
        ("m_rsr", DMA((N_RS, 3))),
        ("m_kvs", DMA((15,))),
        ("m_kvr", DMA((15,))),
        ("m_dks", DMA((6,))),
        ("m_dkr", DMA((6,))),
        ("m_vs", DMA((10,))),
        ("m_vr", DMA((10,))),
        ("m_hs", DMA((5,))),
        ("m_hr", DMA((5,))),
    ]
    for name, rows in BLOCKS.items():
        out += [
            ("g_" + name, VMEM((2, 2, rows, 384), BF)),
            ("x_" + name, VMEM((2, rows, 384), BF)),
            ("a_" + name, VMEM((3, 2, rows // 4, 384), BF)),
            ("b_" + name, VMEM((3, rows // 8, 384), BF)),
            ("s_" + name, DMA((13,))),
            ("r_" + name, DMA((13,))),
        ]
    return out


class Refs:
    pass


def ln_forward(r, gain, bias):
    center = r - jnp.mean(r, axis=-1, keepdims=True)
    spread = lax.rsqrt(jnp.mean(center * center, axis=-1, keepdims=True) + EPS)
    n = center * spread
    return n * gain + bias, n, spread


def ln_backward(n, spread, gain, dy):
    s = dy * gain
    dr = spread * (
        s - jnp.mean(s, axis=-1, keepdims=True) - n * jnp.mean(s * n, axis=-1, keepdims=True)
    )
    return dr, jnp.sum(dy * n, axis=0, keepdims=True), jnp.sum(dy, axis=0, keepdims=True)


def kernel(names, n_in, n_out, *refs):
    (x_h, cot_h, dgr, ret, nrm_h, qkv_h, out_h, win_h, wfo_h, cq_h, ckv_h, co_h) = refs[:n_in]
    bo_o, ig_o, of_o, os_o, oc_o, on_o, oe_o = refs[n_in : n_in + n_out]
    R = Refs()
    for name, ref in zip(names, refs[n_in + n_out :]):
        setattr(R, name, ref)
    c = lax.axis_index("section")
    t = lax.axis_index("tensor")
    d = lax.axis_index("dp")
    o = 1 - c
    y = lax.rem(d, 4)
    z = d // 4
    p = y + c * (z - y)
    q = z + c * (y - z)
    sp, sq = 1 + 3 * c, 4 - 3 * c
    rows_t = pl.ds(pl.multiple_of(t * SH, SH), SH)

    def dev_x(k):
        return (c, lax.rem(t + k, 4), d)

    def dev_p(k):
        return (c, t, lax.rem(p + k, 4) * sp + q * sq)

    def dev_q(k):
        return (c, t, p * sp + lax.rem(q + k, 4) * sq)

    def dev_y(k):
        return (c, t, z * 4 + lax.rem(y + k, 4))

    def dev_z(k):
        return (c, t, lax.rem(z + k, 4) * 4 + y)

    dev_c = (o, t, d)
    sends = []

    def push(src, dst, ss, rs, dev):
        cp = pltpu.make_async_remote_copy(
            src_ref=src, dst_ref=dst, send_sem=ss, recv_sem=rs, device_id=dev, device_id_type=MESH
        )
        cp.start()
        sends.append(cp)
        return cp

    def landed(dst, rs, dev):
        pltpu.make_async_remote_copy(
            src_ref=dst, dst_ref=dst, send_sem=rs, recv_sem=rs, device_id=dev, device_id_type=MESH
        ).wait_recv()

    items = [
        (x_h.at[c], R.xin.at[c]),
        (nrm_h, R.nv.at[c]),
        (qkv_h, R.wsa.at[c, pl.ds(0, 576)]),
        (out_h, R.wsa.at[c, pl.ds(576, 192)]),
        (win_h, R.wff.at[c, 0]),
        (wfo_h, R.wff.at[c, 1]),
    ]

    def own(i):
        pltpu.make_async_copy(items[i][0], items[i][1], R.m_w.at[c, i]).start()

    def other(i):
        src = x_h.at[o] if i == 0 else items[i][0]
        push(src, items[i][1], R.m_ws.at[i], R.m_w.at[c, i], dev_c)

    for i in range(4):
        own(i)
    singles = [
        pltpu.make_async_copy(cq_h, R.wcr.at[pl.ds(0, 192)], R.m_l.at[0]),
        pltpu.make_async_copy(co_h, R.wcr.at[pl.ds(192, 192)], R.m_l.at[1]),
        pltpu.make_async_copy(ckv_h, R.wcr.at[pl.ds(384, 384)], R.m_l.at[2]),
        pltpu.make_async_copy(cot_h.at[c], R.cot, R.m_l.at[3]),
    ]
    for cp in singles:
        cp.start()
    own(4)
    own(5)
    bar = pltpu.get_barrier_semaphore()
    peers = [f(k) for f in (dev_x, dev_y, dev_z) for k in (1, 2, 3)] + [dev_c]
    for dev in peers:
        pl.semaphore_signal(bar, inc=1, device_id=dev, device_id_type=MESH)
    pl.semaphore_wait(bar, len(peers))
    for i in range(6):
        other(i)

    def need(s, i):
        src = x_h.at[s] if i == 0 else items[i][0]
        dst = [
            R.xin.at[s],
            R.nv.at[s],
            R.wsa.at[s, pl.ds(0, 576)],
            R.wsa.at[s, pl.ds(576, 192)],
            R.wff.at[s, 0],
            R.wff.at[s, 1],
        ][i]
        pltpu.make_async_copy(src, dst, R.m_w.at[s, i]).wait()

    def rs_start(i, value):
        R.rs[i] = value.astype(BF)
        for k in RINGS:
            to = lax.rem(t + k, 4)
            push(
                R.rs.at[i, pl.ds(pl.multiple_of(to * SH, SH), SH)],
                R.rr.at[i, k - 1],
                R.m_rss.at[i, k - 1],
                R.m_rsr.at[i, k - 1],
                dev_x(k),
            )

    def rs_sum(i):
        for k in (1, 3, 2):
            landed(R.rr.at[i, k - 1], R.m_rsr.at[i, k - 1], dev_x(k))
        total = R.rs[i, rows_t, :].astype(F32)
        for k in range(3):
            total += R.rr[i, k].astype(F32)
        return total

    def ag_start(i, value):
        R.ag[i, rows_t, :] = value.astype(BF)
        for k in RINGS:
            push(
                R.ag.at[i, rows_t],
                R.ag.at[i, rows_t],
                R.m_ags.at[i, k - 1],
                R.m_agr.at[i, k - 1],
                dev_x(k),
            )

    def ag_wait(i):
        for k in (1, 3, 2):
            landed(R.ag.at[i, rows_t], R.m_agr.at[i, k - 1], dev_x(k))

    def norm_row(s, i):
        return R.nv[s, pl.ds(i, 1), :]

    def self_forward(s):
        need(s, 0)
        need(s, 2)
        R.pk[s] = nt(R.wsa[s, 0:576, :], R.xin[s]).astype(BF)
        for h in range(NH):
            qt = R.pk[s, h * 64 : h * 64 + 64, :]
            kt = R.pk[s, QW + h * 64 : QW + h * 64 + 64, :]
            vt = R.pk[s, 2 * QW + h * 64 : 2 * QW + h * 64 + 64, :]
            st = tn(kt, qt) * SCALE
            if s == 1:
                key = lax.broadcasted_iota(jnp.int32, (TOK, TOK), 0)
                qry = lax.broadcasted_iota(jnp.int32, (TOK, TOK), 1)
                st = jnp.where(key <= qry, st, -1000000000.0)
            e = jnp.exp(st - jnp.max(st, axis=0, keepdims=True))
            pr = e / jnp.sum(e, axis=0, keepdims=True)
            R.pt[s, h] = pr
            R.ot[s, h * 64 : h * 64 + 64, :] = nn(vt, pr.astype(BF)).astype(BF)
        need(s, 3)
        rs_start(R_SA + s, tn(R.ot[s], R.wsa[s, 576:768, :]))

    def put_norm(slot, spread):
        R.sp[slot] = jnp.broadcast_to(spread, (SH, 128))

    def get_norm(slot):
        return R.sp[slot, :, 0:1]

    def self_finish(s):
        total = rs_sum(R_SA + s)
        r = R.xin[s, rows_t, :].astype(F32) + total
        need(s, 1)
        out, n, spread = ln_forward(r, norm_row(s, 0), norm_row(s, 2))
        ag_start(A_Y1 + s, out)
        R.y1f[s] = out
        R.n1[s] = n
        put_norm(s, spread)

    def ffn_forward(s, gathered):
        u = nn(R.ag[gathered], R.wff[s, 0])
        cdf = 0.5 * (1.0 + lax.erf(u * 0.7071067811865476))
        R.act[s] = (u * cdf).astype(BF)
        R.slope[s] = cdf + u * jnp.exp(-0.5 * u * u) * 0.3989422804014327
        rs_start(R_FF + s, nn(R.act[s], R.wff[s, 1]))

    def ffn_backward(s):
        ag_wait(A_DR2 + s)
        dg = nt(R.ag[A_DR2 + s], R.wff[s, 1])
        R.du[s] = (dg * R.slope[s]).astype(BF)
        rs_start(R_DFF + s, nt(R.du[s], R.wff[s, 0]))

    def put(ref, piece, r0, value):
        rows = value.shape[0]
        ref[piece, 0, r0 : r0 + rows, :] = value[:, 0:384].astype(BF)
        ref[piece, 1, r0 : r0 + rows, :] = value[:, 384:768].astype(BF)

    def ffn_grads(s, gathered, ref):
        put(ref, 0, 0, tn(R.ag[gathered], R.du[s]))
        put(ref, 1, 0, tn(R.act[s], R.ag[A_DR2 + s]))

    def blk(name):
        return tuple(getattr(R, pre + name) for pre in ("g_", "x_", "a_", "b_", "s_", "r_"))

    goal = {
        "ffd": R.gof.at[1],
        "ffe": R.gof.at[0],
        "sad": R.gos.at[1],
        "sae": R.gos.at[0],
        "crx": R.goc,
    }

    def g0(name):
        g, x, a, b, s, r = blk(name)
        push(g.at[o], x, s.at[0], r.at[0], dev_c)

    def p_rows(name, at):
        quarter = BLOCKS[name] // 4
        return pl.ds(pl.multiple_of(at * quarter, quarter), quarter)

    def q_rows(name, at_p, at_q):
        quarter, eighth = BLOCKS[name] // 4, BLOCKS[name] // 8
        return pl.ds(pl.multiple_of(at_p * quarter + (at_q // 2) * eighth, eighth), eighth)

    def g1(name):
        g, x, a, b, s, r = blk(name)
        landed(x, r.at[0], dev_c)
        g[c] = (g[c].astype(F32) + x[...].astype(F32)).astype(BF)
        for k in RINGS:
            to = lax.rem(p + k, 4)
            push(
                g.at[c, :, p_rows(name, to)], a.at[k - 1], s.at[k], r.at[k], dev_p(k)
            )

    def g2(name):
        g, x, a, b, s, r = blk(name)
        for k in (1, 3, 2):
            landed(a.at[k - 1], r.at[k], dev_p(k))
        mine = p_rows(name, p)
        total = g[c, :, mine, :].astype(F32)
        for k in range(3):
            total += a[k].astype(F32)
        g[c, :, mine, :] = total.astype(BF)
        for k in RINGS:
            to = lax.rem(q + k, 4)
            push(
                g.at[c, lax.rem(to, 2), q_rows(name, p, to)],
                b.at[k - 1],
                s.at[3 + k],
                r.at[3 + k],
                dev_q(k),
            )

    def g3(name):
        g, x, a, b, s, r = blk(name)
        for k in (1, 3, 2):
            landed(b.at[k - 1], r.at[3 + k], dev_q(k))
        rows, half = q_rows(name, p, q), lax.rem(q, 2)
        total = g[c, half, rows, :].astype(F32)
        for k in range(3):
            total += b[k].astype(F32)
        fin = goal[name]
        fin[half, rows, :] = total.astype(BF)
        for k in RINGS:
            push(fin.at[half, rows], fin.at[half, rows], s.at[6 + k], r.at[6 + k], dev_q(k))

    def g4(name):
        g, x, a, b, s, r = blk(name)
        fin = goal[name]
        for k in (1, 3, 2):
            landed(fin.at[lax.rem(q, 2), q_rows(name, p, q)], r.at[6 + k], dev_q(k))
        mine = p_rows(name, p)
        for k in RINGS:
            push(fin.at[:, mine], fin.at[:, mine], s.at[9 + k], r.at[9 + k], dev_p(k))

    def g5(name):
        g, x, a, b, s, r = blk(name)
        fin = goal[name]
        for k in (1, 3, 2):
            landed(fin.at[:, p_rows(name, p)], r.at[9 + k], dev_p(k))

    def vec_put(row, dg, db, step=2):
        R.vec[row : row + 1, :] = dg
        R.vec[row + step : row + step + 1, :] = db

    def vec_send(buf, at, value, base, dev, count):
        buf[at] = value
        for k in range(1, count):
            push(buf.at[at], buf.at[at], R.m_vs.at[base + k - 1], R.m_vr.at[base + k - 1], dev(k))

    def vec_sum(buf, at, base, dev, count):
        for k in range(1, count):
            landed(buf.at[at], R.m_vr.at[base + k - 1], dev(k))
        total = buf[0]
        for k in range(1, count):
            total += buf[k]
        return total

    def dev_c1(k):
        return dev_c

    for j in (10, 11, 12, 13, 14, 15):
        R.vec[j : j + 1, :] = jnp.zeros((1, D), F32)
    self_forward(0)
    self_forward(1)
    self_finish(0)
    self_finish(1)
    ag_wait(A_Y1)
    need(0, 4)
    need(0, 5)
    ffn_forward(0, A_Y1)

    for cp in singles:
        cp.wait()
    ag_wait(A_Y1 + 1)
    R.qct[...] = nt(R.wcr[0:192, :], R.ag[A_Y1 + 1]).astype(BF)
    micro = lax.broadcasted_iota(jnp.int32, (2, 16), 0)
    group = lax.broadcasted_iota(jnp.int32, (2, 16), 1)
    live = (micro == c) & (group <= d) & (dgr[...] > 0)
    first = jnp.max(jnp.where(live, group, 0), axis=1, keepdims=True)
    first = jnp.max(first, axis=0, keepdims=True)
    pick = lax.broadcasted_iota(jnp.int32, (2, KEYS), 0) == c
    rows = jnp.max(jnp.where(pick, ret[...], 0), axis=0, keepdims=True) + first * TOK
    g_at = rows // TOK
    b_at = jnp.where(c == 0, g_at, lax.rem(g_at, 4) * 4 + g_at // 4)
    at = b_at * TOK + lax.rem(rows, TOK)

    def build(i, carry):
        n = lax.broadcasted_iota(jnp.int32, (TOK, KEYS), 0) + i * TOK
        R.hot[pl.ds(pl.multiple_of(i * TOK, TOK), TOK), :] = jnp.where(n == at, 1.0, 0.0).astype(BF)
        return carry

    lax.fori_loop(0, 16, build, 0)

    out, n, spread = ln_forward(R.y1f[0] + rs_sum(R_FF), norm_row(0, 1), norm_row(0, 3))
    ag_start(A_BO, out)
    R.n2[0] = n
    put_norm(2, spread)
    ag_wait(A_BO)
    mine = q * 4 + p
    R.kvt[mine] = nt(R.wcr[384:768, :], R.ag[A_BO]).astype(BF)

    def kv_send(k, dev, slot, at_block):
        push(R.kvt.at[at_block], R.kvt.at[at_block], R.m_kvs.at[slot], R.m_kvr.at[slot], dev)

    for k in RINGS:
        kv_send(k, dev_p(k), k - 1, mine)
    for k in RINGS:
        kv_send(k, dev_q(k), 2 + k, mine)
    for j in (1, 3, 2):
        landed(R.kvt.at[mine], R.m_kvr.at[j - 1], dev_p(j))
        came = q * 4 + lax.rem(p + 4 - j, 4)
        for k in RINGS:
            kv_send(k, dev_q(k), 6 + (j - 1) * 3 + k - 1, came)
    for slot in range(3, 15):
        landed(R.kvt.at[mine], R.m_kvr.at[slot], dev_q(1))

    def gather(i, total):
        pair = jnp.concatenate([R.kvt[2 * i], R.kvt[2 * i + 1]], axis=1)
        return total + nn(pair, R.hot[pl.ds(pl.multiple_of(i * 256, 256), 256), :])

    R.kvct[...] = lax.fori_loop(0, 8, gather, jnp.zeros((2 * QW, KEYS), F32)).astype(BF)
    for h in range(NH):
        lo = h * 64
        st = tn(R.kvct[lo : lo + 64, :], R.qct[lo : lo + 64, :]) * SCALE
        e = jnp.exp(st - jnp.max(st, axis=0, keepdims=True))
        pr = e / jnp.sum(e, axis=0, keepdims=True)
        R.ptc[h] = pr
        R.oct[lo : lo + 64, :] = nn(R.kvct[QW + lo : QW + lo + 64, :], pr.astype(BF)).astype(BF)
    rs_start(R_CR, tn(R.oct[...], R.wcr[192:384, :]))
    need(1, 4)
    need(1, 5)
    out, n, spread = ln_forward(R.y1f[1] + rs_sum(R_CR), norm_row(0, 4), norm_row(0, 5))
    ag_start(A_Y2, out)
    R.y2f[...] = out
    R.nc[...] = n
    put_norm(4, spread)
    ag_wait(A_Y2)
    ffn_forward(1, A_Y2)
    out, n, spread = ln_forward(R.y2f[...] + rs_sum(R_FF + 1), norm_row(1, 1), norm_row(1, 3))

    dr, dg, db = ln_backward(n, spread, norm_row(1, 1), R.cot[rows_t, :].astype(F32))
    ag_start(A_DR2 + 1, dr)
    R.dres[1] = dr
    vec_put(5, dg, db)
    ag_start(A_BO + 1, out)
    ffn_backward(1)
    ffn_grads(1, A_Y2, R.g_ffd)
    g0("ffd")
    dy = R.dres[1] + rs_sum(R_DFF + 1)
    dr, dg, db = ln_backward(R.nc[...], get_norm(4), norm_row(0, 4), dy)
    ag_start(A_DRC, dr)
    R.dres[1] = dr
    vec_put(8, dg, db, 1)
    g1("ffd")
    ag_wait(A_DRC)

    def attend_backward(qt, kt, vt, pr, dot):
        dvt = nt(dot, pr.astype(BF))
        dpt = tn(vt, dot)
        dst = (pr * (dpt - jnp.sum(dpt * pr, axis=0, keepdims=True))).astype(BF)
        return nn(kt, dst) * SCALE, nt(qt, dst) * SCALE, dvt

    doc = nt(R.wcr[192:384, :], R.ag[A_DRC]).astype(BF)
    for h in range(NH):
        lo = h * 64
        dqt, dkt, dvt = attend_backward(
            R.qct[lo : lo + 64, :],
            R.kvct[lo : lo + 64, :],
            R.kvct[QW + lo : QW + lo + 64, :],
            R.ptc[h],
            doc[lo : lo + 64, :],
        )
        R.dqct[lo : lo + 64, :] = dqt.astype(BF)
        R.dkvct[lo : lo + 64, :] = dkt.astype(BF)
        R.dkvct[QW + lo : QW + lo + 64, :] = dvt.astype(BF)

    def scatter(i, carry):
        part = nt(R.dkvct[...], R.hot[pl.ds(pl.multiple_of(i * TOK, TOK), TOK), :])
        R.dks[i] = part.astype(BF)
        return carry

    lax.fori_loop(0, 16, scatter, 0)
    for k in RINGS:
        to = lax.rem(q + k, 4)
        push(
            R.dks.at[pl.ds(to * 4, 4)],
            R.dk1.at[k - 1],
            R.m_dks.at[k - 1],
            R.m_dkr.at[k - 1],
            dev_q(k),
        )
    rs_start(R_DQ, tn(R.dqct[...], R.wcr[0:192, :]))
    put(R.g_crx, 0, 0, nn(R.dqct[...], R.ag[A_Y1 + 1]))
    put(R.g_crx, 0, 192, nn(R.oct[...], R.ag[A_DRC]))
    g2("ffd")
    for k in (1, 3, 2):
        landed(R.dk1.at[k - 1], R.m_dkr.at[k - 1], dev_q(k))
    for j in range(4):
        at_block = q * 4 + j
        total = R.dks[at_block].astype(F32)
        for k in range(3):
            total += R.dk1[k, j].astype(F32)
        R.dks[at_block] = total.astype(BF)
    for k in RINGS:
        to = lax.rem(p + k, 4)
        push(
            R.dks.at[q * 4 + to], R.dk2.at[k - 1], R.m_dks.at[2 + k], R.m_dkr.at[2 + k], dev_p(k)
        )
    dy = R.dres[1] + rs_sum(R_DQ)
    dr, dg, db = ln_backward(R.n1[1], get_norm(1), norm_row(1, 0), dy)
    ag_start(A_DR1 + 1, dr)
    R.dres[1] = dr
    vec_put(4, dg, db)
    for k in (1, 3, 2):
        landed(R.dk2.at[k - 1], R.m_dkr.at[2 + k], dev_p(k))
    total = R.dks[mine].astype(F32)
    for k in range(3):
        total += R.dk2[k].astype(F32)
    R.dkv[...] = total.astype(BF)
    rs_start(R_DST, tn(R.dkv[...], R.wcr[384:768, :]))
    put(R.g_crx, 1, 0, nn(R.dkv[...], R.ag[A_BO]))
    g0("crx")
    g3("ffd")

    def self_backward(s):
        ag_wait(A_DR1 + s)
        dot = nt(R.wsa[s, 576:768, :], R.ag[A_DR1 + s]).astype(BF)
        for h in range(NH):
            lo = h * 64
            dqt, dkt, dvt = attend_backward(
                R.pk[s, lo : lo + 64, :],
                R.pk[s, QW + lo : QW + lo + 64, :],
                R.pk[s, 2 * QW + lo : 2 * QW + lo + 64, :],
                R.pt[s, h],
                dot[lo : lo + 64, :],
            )
            R.dpk[s, lo : lo + 64, :] = dqt.astype(BF)
            R.dpk[s, QW + lo : QW + lo + 64, :] = dkt.astype(BF)
            R.dpk[s, 2 * QW + lo : 2 * QW + lo + 64, :] = dvt.astype(BF)
        rs_start(R_DSA + s, tn(R.dpk[s], R.wsa[s, 0:576, :]))

    def self_grads(s, ref):
        put(ref, 0, 0, nn(R.dpk[s, 0:384, :], R.xin[s]))
        put(ref, 1, 0, nn(R.dpk[s, 384:576, :], R.xin[s]))
        put(ref, 1, 192, nn(R.ot[s], R.ag[A_DR1 + s]))

    dy = rs_sum(R_DST)
    dr, dg, db = ln_backward(R.n2[0], get_norm(2), norm_row(0, 1), dy)
    ag_start(A_DR2, dr)
    R.dres[0] = dr
    vec_put(1, dg, db)
    g1("crx")
    ffn_backward(0)
    ffn_grads(0, A_Y1, R.g_ffe)
    g0("ffe")
    g4("ffd")
    dy = R.dres[0] + rs_sum(R_DFF)
    dr, dg, db = ln_backward(R.n1[0], get_norm(0), norm_row(0, 0), dy)
    ag_start(A_DR1, dr)
    R.dres[0] = dr
    vec_put(0, dg, db)
    g1("ffe")
    g2("crx")
    self_backward(0)
    self_grads(0, R.g_sae)
    g0("sae")
    self_backward(1)
    self_grads(1, R.g_sad)
    g0("sad")
    g1("sae")
    vec_send(R.vx, t, R.vec[...], 0, dev_x, 4)
    ag_start(A_IG, R.dres[0] + rs_sum(R_DSA))
    g1("sad")
    g2("ffe")
    g3("crx")
    ag_start(A_IG + 1, R.dres[1] + rs_sum(R_DSA + 1))
    total = vec_sum(R.vx, t, 0, dev_x, 4)
    vec_send(R.vc, c, total, 3, dev_c1, 2)
    g2("sae")
    g2("sad")
    g3("ffe")
    g4("crx")
    total = vec_sum(R.vc, c, 3, dev_c1, 2)
    vec_send(R.vy, y, total, 4, dev_y, 4)
    ag_wait(A_BO + 1)
    ag_wait(A_IG)
    ag_wait(A_IG + 1)
    push(R.ag.at[A_BO + o], R.bor, R.m_hs.at[0], R.m_hr.at[0], dev_c)
    push(R.ag.at[A_IG + o], R.igr, R.m_hs.at[1], R.m_hr.at[1], dev_c)
    g3("sae")
    g3("sad")
    g4("ffe")
    total = vec_sum(R.vy, y, 4, dev_y, 4)
    vec_send(R.vz, z, total, 7, dev_z, 4)
    g4("sae")
    g4("sad")
    bo_o[c] = R.ag[A_BO + c]
    ig_o[c] = R.ag[A_IG + c]
    g5("ffd")
    g5("crx")
    push(R.goc, R.gtc, R.m_hs.at[2], R.m_hr.at[2], dev_c)
    g5("ffe")
    push(R.gof.at[o], R.gtf, R.m_hs.at[3], R.m_hr.at[3], dev_c)
    total = vec_sum(R.vz, z, 7, dev_z, 4)
    on_o[...] = jnp.where(c == 0, total[0:4, :], total[4:8, :])
    oe_o[...] = total[8:10, :]
    landed(R.bor, R.m_hr.at[0], dev_c)
    bo_o[o] = R.bor[...]
    landed(R.igr, R.m_hr.at[1], dev_c)
    ig_o[o] = R.igr[...]

    def spread_out(dst, piece, src):
        dst[piece, :, 0:384] = src[0]
        dst[piece, :, 384:768] = src[1]

    landed(R.gtc, R.m_hr.at[2], dev_c)
    spread_out(oc_o, c, R.goc)
    spread_out(oc_o, o, R.gtc)
    landed(R.gtf, R.m_hr.at[3], dev_c)
    spread_out(of_o, c, R.gof.at[c])
    spread_out(of_o, o, R.gtf)
    g5("sae")
    g5("sad")
    push(R.gos.at[o], R.gts, R.m_hs.at[4], R.m_hr.at[4], dev_c)
    spread_out(os_o, c, R.gos.at[c])
    landed(R.gts, R.m_hr.at[4], dev_c)
    spread_out(os_o, o, R.gts)
    for cp in sends:
        cp.wait_send()


def body(
    layer_inputs,
    cotangent,
    doc_groups,
    retrieved_at,
    sa_qkv,
    sa_out,
    ffn_in,
    ffn_out,
    norm_gain,
    norm_bias,
    cross_q,
    cross_kv,
    cross_out,
    cross_gain,
    cross_bias,
):
    nrm = jnp.concatenate(
        [
            norm_gain[0],
            norm_bias[0],
            cross_gain[None],
            cross_bias[None],
            jnp.zeros((2, D), F32),
        ],
        axis=0,
    )
    ins = (
        layer_inputs[0],
        cotangent,
        doc_groups,
        retrieved_at[:, 0, :],
        nrm,
        jnp.transpose(sa_qkv[0], (1, 2, 0)).reshape(576, D),
        sa_out[0],
        ffn_in[0],
        ffn_out[0],
        jnp.transpose(cross_q, (1, 0)),
        jnp.transpose(cross_kv, (1, 2, 0)).reshape(384, D),
        cross_out,
    )
    hbm = pl.BlockSpec(memory_space=pl.ANY)
    vm = pl.BlockSpec(memory_space=VMEM)
    outs = (
        jax.ShapeDtypeStruct((2, TOK, D), BF),
        jax.ShapeDtypeStruct((2, TOK, D), BF),
        jax.ShapeDtypeStruct((2, 768, D), BF),
        jax.ShapeDtypeStruct((2, 384, D), BF),
        jax.ShapeDtypeStruct((2, 384, D), BF),
        jax.ShapeDtypeStruct((4, D), F32),
        jax.ShapeDtypeStruct((2, D), F32),
    )
    names = [n for n, _ in scratch_list()]

    def run(*refs):
        kernel(names, len(ins), len(outs), *refs)

    bo, ig, gf, gs, gc, gn, ge = pl.pallas_call(
        run,
        out_shape=outs,
        in_specs=[hbm, hbm, vm, vm] + [hbm] * 8,
        out_specs=[vm] * len(outs),
        scratch_shapes=[s for _, s in scratch_list()],
        compiler_params=pltpu.CompilerParams(
            collective_id=0, has_side_effects=True, vmem_limit_bytes=62 << 20
        ),
        name="layers",
    )(*ins)
    sa = gs.reshape(768, D)
    cr = gc.reshape(768, D)
    d_qkv = jnp.transpose(sa[0:576].astype(F32).reshape(3, 192, D), (2, 0, 1))
    d_q = jnp.transpose(cr[0:192].astype(F32), (1, 0))
    d_kv = jnp.transpose(cr[384:768].astype(F32).reshape(2, 192, D), (2, 0, 1))
    return (
        bo[None],
        ig.astype(F32)[None],
        d_qkv[None],
        sa[576:768].astype(F32)[None],
        gf[0].astype(F32)[None],
        gf[1].astype(F32)[None],
        gn[0:2][None],
        gn[2:4][None],
        d_q,
        d_kv,
        cr[192:384].astype(F32),
        ge[0],
        ge[1],
    )


def solution(mesh):
    placed = (
        P("section", None, "dp", None),
        P(None, "dp", None),
        P(),
        P(None, "dp", None),
        P("section", None, None, "tensor"),
        P("section", "tensor", None),
        P("section", None, "tensor"),
        P("section", "tensor", None),
        P("section", None, None),
        P("section", None, None),
        P(None, "tensor"),
        P(None, None, "tensor"),
        P("tensor", None),
        P(),
        P(),
    )
    return jax.shard_map(
        body,
        mesh=mesh,
        in_specs=placed,
        out_specs=(
            P("section", None, "dp", None),
            P("section", None, "dp", None),
            P("section", None, None, "tensor"),
            P("section", "tensor", None),
            P("section", None, "tensor"),
            P("section", "tensor", None),
            P("section", None, None),
            P("section", None, None),
            P(None, "tensor"),
            P(None, None, "tensor"),
            P("tensor", None),
            P(),
            P(),
        ),
        check_vma=False,
    )
```

```python
import jax
import jax.numpy as jnp
from jax import lax
from jax.experimental import pallas as pl
from jax.experimental.pallas import tpu as pltpu
from jax.sharding import PartitionSpec as P

BF = jnp.bfloat16
F32 = jnp.float32
MESH = pl.DeviceIdType.MESH
VMEM = pltpu.VMEM
DMA = pltpu.SemaphoreType.DMA

HEAD = 64
NH = 3
EPS = 1e-05
SCALE = HEAD**-0.5
TOK = 128
D = 768
SH = 32
KEYS = 256
QW = NH * HEAD
RINGS = (2, 1, 3)

A_BO, A_IG, A_Y1, A_Y2, A_DR2, A_DRC, A_DR1 = 0, 2, 4, 6, 7, 9, 10
N_AG = 12
R_SA, R_FF, R_CR, R_DFF, R_DQ, R_DSA, R_DST = 0, 2, 4, 5, 7, 8, 10
N_RS = 11
BLOCKS = {"ffd": 768, "ffe": 768, "crx": 384, "sad": 384, "sae": 384}


def nn(a, b):
    return jnp.dot(a, b, preferred_element_type=F32)


def nt(a, b):
    return lax.dot_general(a, b, (((1,), (1,)), ((), ())), preferred_element_type=F32)


def tn(a, b):
    return lax.dot_general(a, b, (((0,), (0,)), ((), ())), preferred_element_type=F32)


def scratch_list():
    out = [
        ("xin", VMEM((2, TOK, D), BF)),
        ("nv", VMEM((2, 2, 2, D), F32)),
        ("wsa", VMEM((2, 768, D), BF)),
        ("wff", VMEM((2, 2, 768, D), BF)),
        ("wcr", VMEM((768, D), BF)),
        ("cot", VMEM((TOK, D), BF)),
        ("pk", VMEM((2, 3 * QW, TOK), BF)),
        ("pt", VMEM((2, NH, TOK, TOK), F32)),
        ("ot", VMEM((2, QW, TOK), BF)),
        ("n1", VMEM((2, SH, D), F32)),
        ("n2", VMEM((2, SH, D), F32)),
        ("nc", VMEM((SH, D), F32)),
        ("sp", VMEM((5, SH, 128), F32)),
        ("y1f", VMEM((2, SH, D), F32)),
        ("y2f", VMEM((SH, D), F32)),
        ("dres", VMEM((2, SH, D), F32)),
        ("act", VMEM((2, TOK, D), BF)),
        ("slope", VMEM((2, TOK, D), F32)),
        ("du", VMEM((2, TOK, D), BF)),
        ("dpk", VMEM((2, 3 * QW, TOK), BF)),
        ("qct", VMEM((QW, TOK), BF)),
        ("dqct", VMEM((QW, TOK), BF)),
        ("kvct", VMEM((2 * QW, KEYS), BF)),
        ("dkvct", VMEM((2 * QW, KEYS), BF)),
        ("ptc", VMEM((NH, KEYS, TOK), F32)),
        ("oct", VMEM((QW, TOK), BF)),
        ("hot", VMEM((16 * TOK, KEYS), BF)),
        ("kvt", VMEM((16, 2 * QW, TOK), BF)),
        ("dks", VMEM((16, 2 * QW, TOK), BF)),
        ("dk1", VMEM((3, 4, 2 * QW, TOK), BF)),
        ("dk2", VMEM((3, 2 * QW, TOK), BF)),
        ("dkv", VMEM((2 * QW, TOK), BF)),
        ("vec", VMEM((16, D), F32)),
        ("vx", VMEM((4, 16, D), F32)),
        ("vc", VMEM((2, 16, D), F32)),
        ("vy", VMEM((4, 16, D), F32)),
        ("vz", VMEM((4, 16, D), F32)),
        ("ag", VMEM((N_AG, TOK, D), BF)),
        ("rs", VMEM((N_RS, TOK, D), BF)),
        ("rr", VMEM((N_RS, 3, SH, D), BF)),
        ("kva", VMEM((2 * QW, KEYS), F32)),
        ("gof", VMEM((2, 2, 768, 384), BF)),
        ("gos", VMEM((2, 2, 384, 384), BF)),
        ("goc", VMEM((2, 384, 384), BF)),
        ("m_w", DMA((2, 7))),
        ("m_ws", DMA((7,))),
        ("m_l", DMA((4,))),
        ("m_ags", DMA((N_AG, 3))),
        ("m_agr", DMA((N_AG, 3))),
        ("m_rss", DMA((N_RS, 3))),
        ("m_rsr", DMA((N_RS, 3))),
        ("m_kvs", DMA((15,))),
        ("m_kvr", DMA((15,))),
        ("m_dks", DMA((6,))),
        ("m_dkr", DMA((6,))),
        ("m_vs", DMA((10,))),
        ("m_vr", DMA((10,))),
        ("m_hs", DMA((3,))),
        ("m_hr", DMA((3,))),
        ("m_o", DMA((3,))),
    ]
    for name, rows in BLOCKS.items():
        out += [
            ("g_" + name, VMEM((2, 2, rows, 384), BF)),
            ("x_" + name, VMEM((2, rows, 384), BF)),
            ("a_" + name, VMEM((3, 2, rows // 4, 384), BF)),
            ("b_" + name, VMEM((3, rows // 8, 384), BF)),
            ("s_" + name, DMA((14,))),
            ("r_" + name, DMA((10,))),
            ("f_" + name, DMA((2, 4))),
        ]
    return out


class Refs:
    pass


def ln_forward(r, gain, bias):
    center = r - jnp.mean(r, axis=-1, keepdims=True)
    spread = lax.rsqrt(jnp.mean(center * center, axis=-1, keepdims=True) + EPS)
    n = center * spread
    return n * gain + bias, n, spread


def ln_backward(n, spread, gain, dy):
    s = dy * gain
    dr = spread * (
        s - jnp.mean(s, axis=-1, keepdims=True) - n * jnp.mean(s * n, axis=-1, keepdims=True)
    )
    return dr, jnp.sum(dy * n, axis=0, keepdims=True), jnp.sum(dy, axis=0, keepdims=True)


def kernel(names, n_in, n_out, *refs):
    (x_h, cot_h, dgr, ret, ng_h, nb_h, cg, cb, qkv_h, out_h, win_h, wfo_h, cq_h, ckv_h, co_h) = refs[
        :n_in
    ]
    bo_o, ig_o, of_o, os_o, oc_o, on_o, oe_o = refs[n_in : n_in + n_out]
    R = Refs()
    for name, ref in zip(names, refs[n_in + n_out :]):
        setattr(R, name, ref)
    c = lax.axis_index("section")
    t = lax.axis_index("tensor")
    d = lax.axis_index("dp")
    o = 1 - c
    y = lax.rem(d, 4)
    z = d // 4
    p = y + c * (z - y)
    q = z + c * (y - z)
    sp, sq = 1 + 3 * c, 4 - 3 * c
    rows_t = pl.ds(pl.multiple_of(t * SH, SH), SH)

    def dev_x(k):
        return (c, lax.rem(t + k, 4), d)

    def dp_p(k):
        return lax.rem(p + k, 4) * sp + q * sq

    def dev_p(k):
        return (c, t, dp_p(k))

    def dev_q(k):
        return (c, t, p * sp + lax.rem(q + k, 4) * sq)

    def dev_y(k):
        return (c, t, z * 4 + lax.rem(y + k, 4))

    def dev_z(k):
        return (c, t, lax.rem(z + k, 4) * 4 + y)

    dev_c = (o, t, d)
    sends = []

    def push(src, dst, ss, rs, dev, wait=True):
        cp = pltpu.make_async_remote_copy(
            src_ref=src, dst_ref=dst, send_sem=ss, recv_sem=rs, device_id=dev, device_id_type=MESH
        )
        cp.start()
        if wait:
            sends.append(cp)
        return cp

    def landed(dst, rs, dev):
        pltpu.make_async_remote_copy(
            src_ref=dst, dst_ref=dst, send_sem=rs, recv_sem=rs, device_id=dev, device_id_type=MESH
        ).wait_recv()

    def places(s):
        return [
            R.xin.at[s],
            R.wsa.at[s, pl.ds(0, 576)],
            R.wsa.at[s, pl.ds(576, 192)],
            R.nv.at[s, 0],
            R.nv.at[s, 1],
            R.wff.at[s, 0],
            R.wff.at[s, 1],
        ]

    items = [x_h.at[c], qkv_h, out_h, ng_h, nb_h, win_h, wfo_h]
    bar = pltpu.get_barrier_semaphore()
    peers = [dev_c]
    for k in (1, 2, 3):
        for dev in (dev_x(k), dev_y(k), dev_z(k)):
            peers.append(dev)
        peers.append((o,) + dev_y(k)[1:])
        peers.append((o,) + dev_z(k)[1:])
    for dev in peers:
        pl.semaphore_signal(bar, inc=1, device_id=dev, device_id_type=MESH)

    def own(i):
        pltpu.make_async_copy(items[i], places(c)[i], R.m_w.at[c, i]).start()

    def other(i):
        src = x_h.at[o] if i == 0 else items[i]
        push(src, places(c)[i], R.m_ws.at[i], R.m_w.at[c, i], dev_c)

    for i in range(5):
        own(i)
    singles = [
        pltpu.make_async_copy(cq_h, R.wcr.at[pl.ds(0, 192)], R.m_l.at[0]),
        pltpu.make_async_copy(co_h, R.wcr.at[pl.ds(192, 192)], R.m_l.at[1]),
        pltpu.make_async_copy(ckv_h, R.wcr.at[pl.ds(384, 384)], R.m_l.at[2]),
        pltpu.make_async_copy(cot_h.at[c], R.cot, R.m_l.at[3]),
    ]
    pl.semaphore_wait(bar, len(peers))
    for i in range(5):
        other(i)
    for i in (5, 6):
        own(i)
        other(i)
    for cp in singles:
        cp.start()

    def need(s, i):
        src = x_h.at[s] if i == 0 else items[i]
        pltpu.make_async_copy(src, places(s)[i], R.m_w.at[s, i]).wait()

    def rs_start(i, value):
        R.rs[i] = value.astype(BF)
        for k in RINGS:
            to = lax.rem(t + k, 4)
            push(
                R.rs.at[i, pl.ds(pl.multiple_of(to * SH, SH), SH)],
                R.rr.at[i, k - 1],
                R.m_rss.at[i, k - 1],
                R.m_rsr.at[i, k - 1],
                dev_x(k),
            )

    def rs_sum(i):
        for k in (1, 3, 2):
            landed(R.rr.at[i, k - 1], R.m_rsr.at[i, k - 1], dev_x(k))
        total = R.rs[i, rows_t, :].astype(F32)
        for k in range(3):
            total += R.rr[i, k].astype(F32)
        return total

    def ag_start(i, value):
        R.ag[i, rows_t, :] = value.astype(BF)
        for k in RINGS:
            push(
                R.ag.at[i, rows_t],
                R.ag.at[i, rows_t],
                R.m_ags.at[i, k - 1],
                R.m_agr.at[i, k - 1],
                dev_x(k),
            )

    def ag_wait(i):
        for k in (1, 3, 2):
            landed(R.ag.at[i, rows_t], R.m_agr.at[i, k - 1], dev_x(k))

    def gain_row(s, i):
        return R.nv[s, 0, i : i + 1, :]

    def bias_row(s, i):
        return R.nv[s, 1, i : i + 1, :]

    cross_gain = cg[...].reshape(1, D)
    cross_bias = cb[...].reshape(1, D)

    def self_forward(s):
        need(s, 0)
        need(s, 1)
        R.pk[s] = nt(R.wsa[s, 0:576, :], R.xin[s]).astype(BF)
        for h in range(NH):
            qt = R.pk[s, h * 64 : h * 64 + 64, :]
            kt = R.pk[s, QW + h * 64 : QW + h * 64 + 64, :]
            vt = R.pk[s, 2 * QW + h * 64 : 2 * QW + h * 64 + 64, :]
            st = tn(kt, qt) * SCALE
            if s == 1:
                key = lax.broadcasted_iota(jnp.int32, (TOK, TOK), 0)
                qry = lax.broadcasted_iota(jnp.int32, (TOK, TOK), 1)
                st = jnp.where(key <= qry, st, -1000000000.0)
            e = jnp.exp(st - jnp.max(st, axis=0, keepdims=True))
            pr = e / jnp.sum(e, axis=0, keepdims=True)
            R.pt[s, h] = pr
            R.ot[s, h * 64 : h * 64 + 64, :] = nn(vt, pr.astype(BF)).astype(BF)
        need(s, 2)
        rs_start(R_SA + s, tn(R.ot[s], R.wsa[s, 576:768, :]))

    def put_norm(slot, spread):
        R.sp[slot] = jnp.broadcast_to(spread, (SH, 128))

    def get_norm(slot):
        return R.sp[slot, :, 0:1]

    def self_finish(s):
        total = rs_sum(R_SA + s)
        r = R.xin[s, rows_t, :].astype(F32) + total
        need(s, 3)
        need(s, 4)
        out, n, spread = ln_forward(r, gain_row(s, 0), bias_row(s, 0))
        ag_start(A_Y1 + s, out)
        R.y1f[s] = out
        R.n1[s] = n
        put_norm(s, spread)

    def ffn_forward(s, gathered):
        u = nn(R.ag[gathered], R.wff[s, 0])
        cdf = 0.5 * (1.0 + lax.erf(u * 0.7071067811865476))
        R.act[s] = (u * cdf).astype(BF)
        R.slope[s] = cdf + u * jnp.exp(-0.5 * u * u) * 0.3989422804014327
        rs_start(R_FF + s, nn(R.act[s], R.wff[s, 1]))

    def ffn_backward(s):
        ag_wait(A_DR2 + s)
        dg = nt(R.ag[A_DR2 + s], R.wff[s, 1])
        R.du[s] = (dg * R.slope[s]).astype(BF)
        rs_start(R_DFF + s, nt(R.du[s], R.wff[s, 0]))

    def put(ref, piece, r0, value):
        rows = value.shape[0]
        ref[piece, 0, r0 : r0 + rows, :] = value[:, 0:384].astype(BF)
        ref[piece, 1, r0 : r0 + rows, :] = value[:, 384:768].astype(BF)

    def ffn_grads(s, gathered, ref):
        put(ref, 0, 0, tn(R.ag[gathered], R.du[s]))
        put(ref, 1, 0, tn(R.act[s], R.ag[A_DR2 + s]))

    def blk(name):
        return tuple(getattr(R, pre + name) for pre in ("g_", "x_", "a_", "b_", "s_", "r_"))

    goal = {
        "ffd": R.gof.at[1],
        "ffe": R.gof.at[0],
        "sad": R.gos.at[1],
        "sae": R.gos.at[0],
        "crx": R.goc,
    }

    def g0(name):
        g, x, a, b, s, r = blk(name)
        push(g.at[o], x, s.at[0], r.at[0], dev_c)

    def p_rows(name, at):
        quarter = BLOCKS[name] // 4
        return pl.ds(pl.multiple_of(at * quarter, quarter), quarter)

    def q_rows(name, at_p, at_q):
        quarter, eighth = BLOCKS[name] // 4, BLOCKS[name] // 8
        return pl.ds(pl.multiple_of(at_p * quarter + (at_q // 2) * eighth, eighth), eighth)

    def g1(name):
        g, x, a, b, s, r = blk(name)
        landed(x, r.at[0], dev_c)
        g[c] = (g[c].astype(F32) + x[...].astype(F32)).astype(BF)
        for k in RINGS:
            to = lax.rem(p + k, 4)
            push(
                g.at[c, :, p_rows(name, to)], a.at[k - 1], s.at[k], r.at[k], dev_p(k)
            )

    def g2(name):
        g, x, a, b, s, r = blk(name)
        for k in (1, 3, 2):
            landed(a.at[k - 1], r.at[k], dev_p(k))
        mine = p_rows(name, p)
        total = g[c, :, mine, :].astype(F32)
        for k in range(3):
            total += a[k].astype(F32)
        g[c, :, mine, :] = total.astype(BF)
        for k in RINGS:
            to = lax.rem(q + k, 4)
            push(
                g.at[c, lax.rem(to, 2), q_rows(name, p, to)],
                b.at[k - 1],
                s.at[3 + k],
                r.at[3 + k],
                dev_q(k),
            )

    def g3(name):
        g, x, a, b, s, r = blk(name)
        for k in (1, 3, 2):
            landed(b.at[k - 1], r.at[3 + k], dev_q(k))
        rows, half = q_rows(name, p, q), lax.rem(q, 2)
        total = g[c, half, rows, :].astype(F32)
        for k in range(3):
            total += b[k].astype(F32)
        fin = goal[name]
        fin[half, rows, :] = total.astype(BF)
        for k in RINGS:
            push(fin.at[half, rows], fin.at[half, rows], s.at[6 + k], r.at[6 + k], dev_q(k))

    final = {"ffd": (1, of_o), "ffe": (0, of_o), "sad": (1, os_o), "sae": (0, os_o)}

    def g4(name):
        g, x, a, b, s, r = blk(name)
        fin = goal[name]
        for k in (1, 3, 2):
            landed(fin.at[lax.rem(q, 2), q_rows(name, p, q)], r.at[6 + k], dev_q(k))
        mine = p_rows(name, p)
        if name not in final:
            for k in RINGS:
                push(
                    fin.at[:, mine], fin.at[:, mine], s.at[9 + k], R.f_crx.at[c, k], dev_p(k)
                )
            return
        owner, dst = final[name]
        f = getattr(R, "f_" + name)
        for k in RINGS:
            push(
                fin.at[:, mine], dst.at[c, :, mine], s.at[9 + k], f.at[c, k], (owner, t, dp_p(k))
            )

        @pl.when(c == owner)
        def _():
            pltpu.make_async_copy(fin.at[:, mine], dst.at[c, :, mine], f.at[c, 0]).start()

        @pl.when(c != owner)
        def _():
            push(fin.at[:, mine], dst.at[c, :, mine], s.at[13], f.at[c, 0], dev_c, False)

    def g5(name):
        fin = goal[name]
        mine = p_rows(name, p)
        if name not in final:
            for k in (1, 3, 2):
                landed(fin.at[:, mine], R.f_crx.at[c, k], dev_p(k))
            return
        owner, dst = final[name]
        f = getattr(R, "f_" + name)

        @pl.when(c == owner)
        def _():
            for piece in (0, 1):
                for k in range(4):
                    landed(dst.at[piece, :, mine], f.at[piece, k], dev_p(1))

        @pl.when(c != owner)
        def _():
            pltpu.make_async_remote_copy(
                src_ref=fin.at[:, mine],
                dst_ref=dst.at[c, :, mine],
                send_sem=getattr(R, "s_" + name).at[13],
                recv_sem=f.at[c, 0],
                device_id=dev_c,
                device_id_type=MESH,
            ).wait_send()

    def vec_put(row, dg, db, step=2):
        R.vec[row : row + 1, :] = dg
        R.vec[row + step : row + step + 1, :] = db

    def vec_send(buf, at, value, base, dev, count):
        buf[at] = value
        for k in range(1, count):
            push(buf.at[at], buf.at[at], R.m_vs.at[base + k - 1], R.m_vr.at[base + k - 1], dev(k))

    def vec_sum(buf, at, base, dev, count):
        for k in range(1, count):
            landed(buf.at[at], R.m_vr.at[base + k - 1], dev(k))
        total = buf[0]
        for k in range(1, count):
            total += buf[k]
        return total

    def dev_c1(k):
        return dev_c

    for j in (10, 11, 12, 13, 14, 15):
        R.vec[j : j + 1, :] = jnp.zeros((1, D), F32)
    self_forward(0)
    self_forward(1)
    self_finish(0)
    self_finish(1)
    ag_wait(A_Y1)
    need(0, 5)
    need(0, 6)
    ffn_forward(0, A_Y1)

    for cp in singles:
        cp.wait()
    ag_wait(A_Y1 + 1)
    R.qct[...] = nt(R.wcr[0:192, :], R.ag[A_Y1 + 1]).astype(BF)
    micro = lax.broadcasted_iota(jnp.int32, (2, 16), 0)
    group = lax.broadcasted_iota(jnp.int32, (2, 16), 1)
    live = (micro == c) & (group <= d) & (dgr[...] > 0)
    first = jnp.max(jnp.where(live, group, 0), axis=1, keepdims=True)
    first = jnp.max(first, axis=0, keepdims=True)
    rows = jnp.where(c == 0, ret[0], ret[1]) + first * TOK
    g_at = rows // TOK
    b_at = jnp.where(c == 0, g_at, lax.rem(g_at, 4) * 4 + g_at // 4)
    at = b_at * TOK + lax.rem(rows, TOK)

    def build(i, carry):
        n = lax.broadcasted_iota(jnp.int32, (TOK, KEYS), 0) + i * TOK
        R.hot[pl.ds(pl.multiple_of(i * TOK, TOK), TOK), :] = jnp.where(n == at, 1.0, 0.0).astype(BF)
        return carry

    lax.fori_loop(0, 16, build, 0)

    out, n, spread = ln_forward(R.y1f[0] + rs_sum(R_FF), gain_row(0, 1), bias_row(0, 1))
    ag_start(A_BO, out)
    R.n2[0] = n
    put_norm(2, spread)
    ag_wait(A_BO)
    mine = q * 4 + p
    R.kvt[mine] = nt(R.wcr[384:768, :], R.ag[A_BO]).astype(BF)

    def kv_send(k, dev, slot, at_block):
        push(R.kvt.at[at_block], R.kvt.at[at_block], R.m_kvs.at[slot], R.m_kvr.at[slot], dev)

    def gather(b):
        hot = R.hot[pl.ds(pl.multiple_of(b * TOK, TOK), TOK), :]
        R.kva[...] += nn(R.kvt[b], hot)

    for k in RINGS:
        kv_send(k, dev_p(k), k - 1, mine)
    for k in RINGS:
        kv_send(k, dev_q(k), 2 + k, mine)
    R.kva[...] = jnp.zeros((2 * QW, KEYS), F32)
    gather(mine)
    for j in (1, 3, 2):
        landed(R.kvt.at[mine], R.m_kvr.at[j - 1], dev_p(j))
        came = q * 4 + lax.rem(p + 4 - j, 4)
        for k in RINGS:
            kv_send(k, dev_q(k), 6 + (j - 1) * 3 + k - 1, came)
        gather(came)
    for j in (0, 1, 3, 2):
        for k in (1, 3, 2):
            slot = 2 + k if j == 0 else 6 + (j - 1) * 3 + k - 1
            landed(R.kvt.at[mine], R.m_kvr.at[slot], dev_q(k))
            gather(lax.rem(q + 4 - k, 4) * 4 + lax.rem(p + 4 - j, 4))

    R.kvct[...] = R.kva[...].astype(BF)
    for h in range(NH):
        lo = h * 64
        st = tn(R.kvct[lo : lo + 64, :], R.qct[lo : lo + 64, :]) * SCALE
        e = jnp.exp(st - jnp.max(st, axis=0, keepdims=True))
        pr = e / jnp.sum(e, axis=0, keepdims=True)
        R.ptc[h] = pr
        R.oct[lo : lo + 64, :] = nn(R.kvct[QW + lo : QW + lo + 64, :], pr.astype(BF)).astype(BF)
    rs_start(R_CR, tn(R.oct[...], R.wcr[192:384, :]))
    need(1, 5)
    need(1, 6)
    out, n, spread = ln_forward(R.y1f[1] + rs_sum(R_CR), cross_gain, cross_bias)
    ag_start(A_Y2, out)
    R.y2f[...] = out
    R.nc[...] = n
    put_norm(4, spread)
    ag_wait(A_Y2)
    ffn_forward(1, A_Y2)
    out, n, spread = ln_forward(R.y2f[...] + rs_sum(R_FF + 1), gain_row(1, 1), bias_row(1, 1))

    dr, dg, db = ln_backward(n, spread, gain_row(1, 1), R.cot[rows_t, :].astype(F32))
    ag_start(A_DR2 + 1, dr)
    R.dres[1] = dr
    vec_put(5, dg, db)
    ffn_backward(1)
    ag_start(A_BO + 1, out)
    ffn_grads(1, A_Y2, R.g_ffd)
    g0("ffd")
    dy = R.dres[1] + rs_sum(R_DFF + 1)
    dr, dg, db = ln_backward(R.nc[...], get_norm(4), cross_gain, dy)
    ag_start(A_DRC, dr)
    R.dres[1] = dr
    vec_put(8, dg, db, 1)
    g1("ffd")
    ag_wait(A_DRC)

    def attend_backward(qt, kt, vt, pr, dot):
        dvt = nt(dot, pr.astype(BF))
        dpt = tn(vt, dot)
        dst = (pr * (dpt - jnp.sum(dpt * pr, axis=0, keepdims=True))).astype(BF)
        return nn(kt, dst) * SCALE, nt(qt, dst) * SCALE, dvt

    doc = nt(R.wcr[192:384, :], R.ag[A_DRC]).astype(BF)
    for h in range(NH):
        lo = h * 64
        dqt, dkt, dvt = attend_backward(
            R.qct[lo : lo + 64, :],
            R.kvct[lo : lo + 64, :],
            R.kvct[QW + lo : QW + lo + 64, :],
            R.ptc[h],
            doc[lo : lo + 64, :],
        )
        R.dqct[lo : lo + 64, :] = dqt.astype(BF)
        R.dkvct[lo : lo + 64, :] = dkt.astype(BF)
        R.dkvct[QW + lo : QW + lo + 64, :] = dvt.astype(BF)

    for k in RINGS + (0,):
        to = lax.rem(q + k, 4)
        for j in range(4):
            b = to * 4 + j
            hot = R.hot[pl.ds(pl.multiple_of(b * TOK, TOK), TOK), :]
            R.dks[b] = nt(R.dkvct[...], hot).astype(BF)
        if k:
            push(
                R.dks.at[pl.ds(to * 4, 4)],
                R.dk1.at[k - 1],
                R.m_dks.at[k - 1],
                R.m_dkr.at[k - 1],
                dev_q(k),
            )
    rs_start(R_DQ, tn(R.dqct[...], R.wcr[0:192, :]))
    put(R.g_crx, 0, 0, nn(R.dqct[...], R.ag[A_Y1 + 1]))
    put(R.g_crx, 0, 192, nn(R.oct[...], R.ag[A_DRC]))
    dy = R.dres[1] + rs_sum(R_DQ)
    dr, dg, db = ln_backward(R.n1[1], get_norm(1), gain_row(1, 0), dy)
    ag_start(A_DR1 + 1, dr)
    R.dres[1] = dr
    vec_put(4, dg, db)
    g2("ffd")

    def self_backward(s):
        ag_wait(A_DR1 + s)
        dot = nt(R.wsa[s, 576:768, :], R.ag[A_DR1 + s]).astype(BF)
        for h in range(NH):
            lo = h * 64
            dqt, dkt, dvt = attend_backward(
                R.pk[s, lo : lo + 64, :],
                R.pk[s, QW + lo : QW + lo + 64, :],
                R.pk[s, 2 * QW + lo : 2 * QW + lo + 64, :],
                R.pt[s, h],
                dot[lo : lo + 64, :],
            )
            R.dpk[s, lo : lo + 64, :] = dqt.astype(BF)
            R.dpk[s, QW + lo : QW + lo + 64, :] = dkt.astype(BF)
            R.dpk[s, 2 * QW + lo : 2 * QW + lo + 64, :] = dvt.astype(BF)

    def self_grads(s, ref):
        put(ref, 0, 0, nn(R.dpk[s, 0:384, :], R.xin[s]))
        put(ref, 1, 0, nn(R.dpk[s, 384:576, :], R.xin[s]))
        put(ref, 1, 192, nn(R.ot[s], R.ag[A_DR1 + s]))

    def input_part(s):
        rs_start(R_DSA + s, tn(R.dpk[s], R.wsa[s, 0:576, :]))

    for k in (1, 3, 2):
        landed(R.dk1.at[k - 1], R.m_dkr.at[k - 1], dev_q(k))
    for k in RINGS + (0,):
        to = lax.rem(p + k, 4)
        b = q * 4 + to
        total = R.dks[b].astype(F32)
        for j in range(3):
            total += R.dk1[j, to].astype(F32)
        R.dks[b] = total.astype(BF)
        if k:
            push(R.dks.at[b], R.dk2.at[k - 1], R.m_dks.at[2 + k], R.m_dkr.at[2 + k], dev_p(k))
    self_backward(1)
    input_part(1)
    self_grads(1, R.g_sad)
    g0("sad")
    for k in (1, 3, 2):
        landed(R.dk2.at[k - 1], R.m_dkr.at[2 + k], dev_p(k))
    total = R.dks[mine].astype(F32)
    for k in range(3):
        total += R.dk2[k].astype(F32)
    R.dkv[...] = total.astype(BF)
    rs_start(R_DST, tn(R.dkv[...], R.wcr[384:768, :]))
    put(R.g_crx, 1, 0, nn(R.dkv[...], R.ag[A_BO]))
    g0("crx")
    g3("ffd")
    g1("sad")
    dy = rs_sum(R_DST)
    dr, dg, db = ln_backward(R.n2[0], get_norm(2), gain_row(0, 1), dy)
    ag_start(A_DR2, dr)
    R.dres[0] = dr
    vec_put(1, dg, db)
    g4("ffd")
    g1("crx")
    ffn_backward(0)
    ffn_grads(0, A_Y1, R.g_ffe)
    g0("ffe")
    g2("sad")
    ag_start(A_IG + 1, R.dres[1] + rs_sum(R_DSA + 1))
    dy = R.dres[0] + rs_sum(R_DFF)
    dr, dg, db = ln_backward(R.n1[0], get_norm(0), gain_row(0, 0), dy)
    ag_start(A_DR1, dr)
    R.dres[0] = dr
    vec_put(0, dg, db)
    vec_send(R.vx, t, R.vec[...], 0, dev_x, 4)
    g1("ffe")
    g2("crx")
    g3("sad")
    self_backward(0)
    self_grads(0, R.g_sae)
    g0("sae")
    input_part(0)
    total = vec_sum(R.vx, t, 0, dev_x, 4)
    vec_send(R.vc, c, total, 3, dev_c1, 2)
    g4("sad")
    g3("crx")
    g1("sae")
    g2("ffe")
    total = vec_sum(R.vc, c, 3, dev_c1, 2)
    vec_send(R.vy, y, total, 4, dev_y, 4)
    ag_start(A_IG, R.dres[0] + rs_sum(R_DSA))
    g4("crx")
    ag_wait(A_BO + 1)
    push(R.ag.at[A_BO + o], bo_o.at[c], R.m_hs.at[0], R.m_hr.at[0], dev_c)
    outs = [pltpu.make_async_copy(R.ag.at[A_BO + c], bo_o.at[c], R.m_o.at[0])]
    outs[0].start()
    g3("ffe")
    g2("sae")
    total = vec_sum(R.vy, y, 4, dev_y, 4)
    vec_send(R.vz, z, total, 7, dev_z, 4)
    g4("ffe")
    g3("sae")
    g5("crx")
    push(R.goc, oc_o.at[c], R.m_hs.at[1], R.m_hr.at[1], dev_c)
    outs.append(pltpu.make_async_copy(R.goc, oc_o.at[c], R.m_o.at[1]))
    outs[1].start()
    ag_wait(A_IG)
    ag_wait(A_IG + 1)
    push(R.ag.at[A_IG + o], ig_o.at[c], R.m_hs.at[2], R.m_hr.at[2], dev_c)
    outs.append(pltpu.make_async_copy(R.ag.at[A_IG + c], ig_o.at[c], R.m_o.at[2]))
    outs[2].start()
    total = vec_sum(R.vz, z, 7, dev_z, 4)
    on_o[...] = jnp.where(c == 0, total[0:4, :], total[4:8, :])
    oe_o[...] = total[8:10, :]
    g4("sae")
    g5("ffd")
    g5("sad")
    g5("ffe")
    landed(bo_o.at[c], R.m_hr.at[0], dev_c)
    landed(oc_o.at[c], R.m_hr.at[1], dev_c)
    landed(ig_o.at[c], R.m_hr.at[2], dev_c)
    for cp in outs:
        cp.wait()
    g5("sae")
    for cp in sends:
        cp.wait_send()


JOBS = (
    [("gf", 0, r, "win", r) for r in (0, 192, 384, 576)]
    + [("gf", 1, r, "wfo", r) for r in (0, 192, 384, 576)]
    + [("gc", 0, 0, "q", 0), ("gc", 0, 192, "co", 0), ("gc", 1, 0, "kv", 0), ("gc", 1, 192, "kv", 192)]
    + [("gs", 0, 0, "qkv", 0), ("gs", 0, 192, "qkv", 192), ("gs", 1, 0, "qkv", 384)]
    + [("gs", 1, 192, "out", 0)]
)


def widen(*refs):
    bo, ig, gf, gs, gc, gn, ge = refs[:7]
    bo_o, ig_o, qkv_o, out_o, win_o, wfo_o, ng_o, nb_o, q_o, kv_o, co_o, cg_o, cb_o = refs[7:20]
    low, wide, ig_low, ig_wide, rows, m_in, m_out, m_x = refs[20:]
    from_ = {"gf": gf, "gs": gs, "gc": gc}
    to = {"qkv": qkv_o, "out": out_o, "win": win_o, "wfo": wfo_o, "q": q_o, "kv": kv_o, "co": co_o}
    straight = pltpu.make_async_copy(bo, bo_o, m_x.at[0])
    straight.start()
    ig_in = pltpu.make_async_copy(ig, ig_low, m_x.at[1])
    ig_in.start()
    loads = []
    small = [
        pltpu.make_async_copy(gn, rows.at[pl.ds(0, 4)], m_x.at[3]),
        pltpu.make_async_copy(ge, rows.at[pl.ds(4, 2)], m_x.at[4]),
    ]
    for cp in small:
        cp.start()
    for i, (src, piece, r0, dst, d0) in enumerate(JOBS):
        cp = pltpu.make_async_copy(
            from_[src].at[piece, :, pl.ds(r0, 192)], low.at[i], m_in.at[i]
        )
        cp.start()
        loads.append(cp)
    ig_in.wait()
    ig_wide[...] = ig_low[...].astype(F32)
    stores = [pltpu.make_async_copy(ig_wide, ig_o, m_x.at[2])]
    stores[0].start()
    for cp in small:
        cp.wait()
    ng_o[...] = rows[0:2, :]
    nb_o[...] = rows[2:4, :]
    cg_o[...] = rows[4:5, :].reshape(D)
    cb_o[...] = rows[5:6, :].reshape(D)
    for i, (src, piece, r0, dst, d0) in enumerate(JOBS):
        loads[i].wait()
        wide[i, :, 0:384] = low[i, 0].astype(F32)
        wide[i, :, 384:768] = low[i, 1].astype(F32)
        cp = pltpu.make_async_copy(wide.at[i], to[dst].at[pl.ds(d0, 192)], m_out.at[i])
        cp.start()
        stores.append(cp)
    for cp in stores:
        cp.wait()
    straight.wait()


def body(
    layer_inputs,
    cotangent,
    doc_groups,
    retrieved_at,
    sa_qkv,
    sa_out,
    ffn_in,
    ffn_out,
    norm_gain,
    norm_bias,
    cross_q,
    cross_kv,
    cross_out,
    cross_gain,
    cross_bias,
):
    ins = (
        layer_inputs[0],
        cotangent,
        doc_groups,
        retrieved_at,
        norm_gain[0],
        norm_bias[0],
        cross_gain,
        cross_bias,
        jnp.transpose(sa_qkv[0], (1, 2, 0)).reshape(576, D),
        sa_out[0],
        ffn_in[0],
        ffn_out[0],
        jnp.transpose(cross_q, (1, 0)),
        jnp.transpose(cross_kv, (1, 2, 0)).reshape(384, D),
        cross_out,
    )
    hbm = pl.BlockSpec(memory_space=pl.ANY)
    vm = pl.BlockSpec(memory_space=VMEM)
    outs = (
        jax.ShapeDtypeStruct((2, TOK, D), BF),
        jax.ShapeDtypeStruct((2, TOK, D), BF),
        jax.ShapeDtypeStruct((2, 2, 768, 384), BF),
        jax.ShapeDtypeStruct((2, 2, 384, 384), BF),
        jax.ShapeDtypeStruct((2, 2, 384, 384), BF),
        jax.ShapeDtypeStruct((4, D), F32),
        jax.ShapeDtypeStruct((2, D), F32),
    )
    names = [n for n, _ in scratch_list()]

    def run(*refs):
        kernel(names, len(ins), len(outs), *refs)

    results = pl.pallas_call(
        run,
        out_shape=outs,
        in_specs=[hbm, hbm, vm, vm, hbm, hbm, vm, vm] + [hbm] * 7,
        out_specs=[hbm] * 5 + [vm] * 2,
        scratch_shapes=[s for _, s in scratch_list()],
        compiler_params=pltpu.CompilerParams(
            collective_id=0, has_side_effects=True, vmem_limit_bytes=62 << 20
        ),
        name="layers",
    )(*ins)
    wide_outs = (
        jax.ShapeDtypeStruct((2, TOK, D), BF),
        jax.ShapeDtypeStruct((2, TOK, D), F32),
        jax.ShapeDtypeStruct((576, D), F32),
        jax.ShapeDtypeStruct((192, D), F32),
        jax.ShapeDtypeStruct((768, D), F32),
        jax.ShapeDtypeStruct((768, D), F32),
        jax.ShapeDtypeStruct((2, D), F32),
        jax.ShapeDtypeStruct((2, D), F32),
        jax.ShapeDtypeStruct((192, D), F32),
        jax.ShapeDtypeStruct((384, D), F32),
        jax.ShapeDtypeStruct((192, D), F32),
        jax.ShapeDtypeStruct((D,), F32),
        jax.ShapeDtypeStruct((D,), F32),
    )
    bo, ig, d_qkv, d_out, d_in, d_fo, ng, nb, d_q, d_kv, d_co, dcg, dcb = pl.pallas_call(
        widen,
        out_shape=wide_outs,
        in_specs=[hbm] * 7,
        out_specs=[hbm] * 6 + [vm] * 2 + [hbm] * 3 + [vm] * 2,
        scratch_shapes=[
            VMEM((len(JOBS), 2, 192, 384), BF),
            VMEM((len(JOBS), 192, D), F32),
            VMEM((2, TOK, D), BF),
            VMEM((2, TOK, D), F32),
            VMEM((8, D), F32),
            DMA((len(JOBS),)),
            DMA((len(JOBS),)),
            DMA((5,)),
        ],
        compiler_params=pltpu.CompilerParams(vmem_limit_bytes=32 << 20),
        name="widen",
    )(*[pltpu.with_memory_space_constraint(r, pltpu.HBM) for r in results])
    return (
        bo[None],
        ig[None],
        jnp.transpose(d_qkv.reshape(3, 192, D), (2, 0, 1))[None],
        d_out[None],
        d_in[None],
        d_fo[None],
        ng[None],
        nb[None],
        jnp.transpose(d_q, (1, 0)),
        jnp.transpose(d_kv.reshape(2, 192, D), (2, 0, 1)),
        d_co,
        dcg,
        dcb,
    )


def solution(mesh):
    placed = (
        P("section", None, "dp", None),
        P(None, "dp", None),
        P(),
        P(None, "dp", None),
        P("section", None, None, "tensor"),
        P("section", "tensor", None),
        P("section", None, "tensor"),
        P("section", "tensor", None),
        P("section", None, None),
        P("section", None, None),
        P(None, "tensor"),
        P(None, None, "tensor"),
        P("tensor", None),
        P(),
        P(),
    )
    return jax.shard_map(
        body,
        mesh=mesh,
        in_specs=placed,
        out_specs=(
            P("section", None, "dp", None),
            P("section", None, "dp", None),
            P("section", None, None, "tensor"),
            P("section", "tensor", None),
            P("section", None, "tensor"),
            P("section", "tensor", None),
            P("section", None, None),
            P("section", None, None),
            P(None, "tensor"),
            P(None, None, "tensor"),
            P("tensor", None),
            P(),
            P(),
        ),
        check_vma=False,
    )
```

```python
import jax
import jax.numpy as jnp
from jax import lax
from jax.experimental import pallas as pl
from jax.experimental.pallas import tpu as pltpu
from jax.sharding import PartitionSpec as P

BF = jnp.bfloat16
F32 = jnp.float32
MESH = pl.DeviceIdType.MESH
VMEM = pltpu.VMEM
DMA = pltpu.SemaphoreType.DMA

HEAD = 64
NH = 3
EPS = 1e-05
SCALE = HEAD**-0.5
TOK = 128
D = 768
SH = 32
KEYS = 256
QW = NH * HEAD
RINGS = (2, 1, 3)

A_BO, A_IG, A_Y1, A_Y2, A_DR2, A_DRC, A_DR1 = 0, 2, 4, 6, 7, 9, 10
N_AG = 12
R_SA, R_FF, R_CR, R_DFF, R_DQ, R_DSA, R_DST = 0, 2, 4, 5, 7, 8, 10
N_RS = 11
BLOCKS = {"ffd": 768, "ffe": 768, "crx": 384, "sad": 384, "sae": 384}


def nn(a, b):
    return jnp.dot(a, b, preferred_element_type=F32)


def nt(a, b):
    return lax.dot_general(a, b, (((1,), (1,)), ((), ())), preferred_element_type=F32)


def tn(a, b):
    return lax.dot_general(a, b, (((0,), (0,)), ((), ())), preferred_element_type=F32)


def scratch_list():
    out = [
        ("xin", VMEM((2, TOK, D), BF)),
        ("nv", VMEM((2, 2, 2, D), F32)),
        ("wsa", VMEM((2, 768, D), BF)),
        ("wff", VMEM((2, 2, 768, D), BF)),
        ("wcr", VMEM((768, D), BF)),
        ("cot", VMEM((TOK, D), BF)),
        ("pk", VMEM((2, 3 * QW, TOK), BF)),
        ("pt", VMEM((2, NH, TOK, TOK), F32)),
        ("ot", VMEM((2, QW, TOK), BF)),
        ("n1", VMEM((2, SH, D), F32)),
        ("n2", VMEM((2, SH, D), F32)),
        ("nc", VMEM((SH, D), F32)),
        ("sp", VMEM((5, SH, 128), F32)),
        ("y1f", VMEM((2, SH, D), F32)),
        ("y2f", VMEM((SH, D), F32)),
        ("dres", VMEM((2, SH, D), F32)),
        ("act", VMEM((2, TOK, D), BF)),
        ("slope", VMEM((2, TOK, D), F32)),
        ("du", VMEM((2, TOK, D), BF)),
        ("dpk", VMEM((2, 3 * QW, TOK), BF)),
        ("qct", VMEM((QW, TOK), BF)),
        ("dqct", VMEM((QW, TOK), BF)),
        ("kvct", VMEM((2 * QW, KEYS), BF)),
        ("dkvct", VMEM((2 * QW, KEYS), BF)),
        ("ptc", VMEM((NH, KEYS, TOK), F32)),
        ("oct", VMEM((QW, TOK), BF)),
        ("pos", VMEM((4, 8, KEYS), jnp.int32)),
        ("hot", VMEM((4, 4 * TOK, KEYS), BF)),
        ("kvt", VMEM((4, 2 * QW, TOK), BF)),
        ("kvs", VMEM((4, 2 * QW, KEYS), BF)),
        ("kvr", VMEM((3, 2 * QW, KEYS), BF)),
        ("dkr", VMEM((3, 2 * QW, KEYS), BF)),
        ("dkf", VMEM((4, 2 * QW, TOK), F32)),
        ("dks", VMEM((4, 2 * QW, TOK), BF)),
        ("dk2", VMEM((3, 2 * QW, TOK), BF)),
        ("dkv", VMEM((2 * QW, TOK), BF)),
        ("vec", VMEM((16, D), F32)),
        ("vx", VMEM((4, 16, D), F32)),
        ("vc", VMEM((2, 16, D), F32)),
        ("vy", VMEM((4, 16, D), F32)),
        ("vz", VMEM((4, 16, D), F32)),
        ("ag", VMEM((N_AG, TOK, D), BF)),
        ("rs", VMEM((N_RS, TOK, D), BF)),
        ("rr", VMEM((N_RS, 3, SH, D), BF)),
        ("gof", VMEM((2, 2, 768, 384), BF)),
        ("gos", VMEM((2, 2, 384, 384), BF)),
        ("goc", VMEM((2, 384, 384), BF)),
        ("m_w", DMA((2, 7))),
        ("m_ws", DMA((7,))),
        ("m_l", DMA((4,))),
        ("m_ags", DMA((N_AG, 3))),
        ("m_agr", DMA((N_AG, 3))),
        ("m_rss", DMA((N_RS, 3))),
        ("m_rsr", DMA((N_RS, 3))),
        ("m_kvs", DMA((9,))),
        ("m_kvr", DMA((9,))),
        ("m_dks", DMA((6,))),
        ("m_dkr", DMA((6,))),
        ("m_vs", DMA((10,))),
        ("m_vr", DMA((10,))),
        ("m_hs", DMA((3,))),
        ("m_hr", DMA((3,))),
        ("m_o", DMA((3,))),
    ]
    for name, rows in BLOCKS.items():
        out += [
            ("g_" + name, VMEM((2, 2, rows, 384), BF)),
            ("x_" + name, VMEM((2, rows, 384), BF)),
            ("a_" + name, VMEM((3, 2, rows // 4, 384), BF)),
            ("b_" + name, VMEM((3, rows // 8, 384), BF)),
            ("s_" + name, DMA((14,))),
            ("r_" + name, DMA((10,))),
            ("f_" + name, DMA((2, 4))),
        ]
    return out


class Refs:
    pass


def ln_forward(r, gain, bias):
    center = r - jnp.mean(r, axis=-1, keepdims=True)
    spread = lax.rsqrt(jnp.mean(center * center, axis=-1, keepdims=True) + EPS)
    n = center * spread
    return n * gain + bias, n, spread


def ln_backward(n, spread, gain, dy):
    s = dy * gain
    dr = spread * (
        s - jnp.mean(s, axis=-1, keepdims=True) - n * jnp.mean(s * n, axis=-1, keepdims=True)
    )
    return dr, jnp.sum(dy * n, axis=0, keepdims=True), jnp.sum(dy, axis=0, keepdims=True)


def kernel(names, n_in, n_out, *refs):
    (x_h, cot_h, dgr, ret, ng_h, nb_h, cg, cb, qkv_h, out_h, win_h, wfo_h, cq_h, ckv_h, co_h) = refs[
        :n_in
    ]
    bo_o, ig_o, of_o, os_o, oc_o, on_o, oe_o = refs[n_in : n_in + n_out]
    R = Refs()
    for name, ref in zip(names, refs[n_in + n_out :]):
        setattr(R, name, ref)
    c = lax.axis_index("section")
    t = lax.axis_index("tensor")
    d = lax.axis_index("dp")
    o = 1 - c
    y = lax.rem(d, 4)
    z = d // 4
    p = y + c * (z - y)
    q = z + c * (y - z)
    sp, sq = 1 + 3 * c, 4 - 3 * c
    rows_t = pl.ds(pl.multiple_of(t * SH, SH), SH)

    def dev_x(k):
        return (c, lax.rem(t + k, 4), d)

    def dp_p(k):
        return lax.rem(p + k, 4) * sp + q * sq

    def dev_p(k):
        return (c, t, dp_p(k))

    def dev_q(k):
        return (c, t, p * sp + lax.rem(q + k, 4) * sq)

    def dev_y(k):
        return (c, t, z * 4 + lax.rem(y + k, 4))

    def dev_z(k):
        return (c, t, lax.rem(z + k, 4) * 4 + y)

    dev_c = (o, t, d)
    sends = []

    def push(src, dst, ss, rs, dev, wait=True):
        cp = pltpu.make_async_remote_copy(
            src_ref=src, dst_ref=dst, send_sem=ss, recv_sem=rs, device_id=dev, device_id_type=MESH
        )
        cp.start()
        if wait:
            sends.append(cp)
        return cp

    def landed(dst, rs, dev):
        pltpu.make_async_remote_copy(
            src_ref=dst, dst_ref=dst, send_sem=rs, recv_sem=rs, device_id=dev, device_id_type=MESH
        ).wait_recv()

    def places(s):
        return [
            R.xin.at[s],
            R.wsa.at[s, pl.ds(0, 576)],
            R.wsa.at[s, pl.ds(576, 192)],
            R.nv.at[s, 0],
            R.nv.at[s, 1],
            R.wff.at[s, 0],
            R.wff.at[s, 1],
        ]

    items = [x_h.at[c], qkv_h, out_h, ng_h, nb_h, win_h, wfo_h]
    bar = pltpu.get_barrier_semaphore()
    peers = [dev_c]
    for k in (1, 2, 3):
        for dev in (dev_x(k), dev_y(k), dev_z(k)):
            peers.append(dev)
        peers.append((o,) + dev_y(k)[1:])
        peers.append((o,) + dev_z(k)[1:])
    for dev in peers:
        pl.semaphore_signal(bar, inc=1, device_id=dev, device_id_type=MESH)

    def own(i):
        pltpu.make_async_copy(items[i], places(c)[i], R.m_w.at[c, i]).start()

    def other(i):
        src = x_h.at[o] if i == 0 else items[i]
        push(src, places(c)[i], R.m_ws.at[i], R.m_w.at[c, i], dev_c)

    for i in range(5):
        own(i)
    singles = [
        pltpu.make_async_copy(cq_h, R.wcr.at[pl.ds(0, 192)], R.m_l.at[0]),
        pltpu.make_async_copy(co_h, R.wcr.at[pl.ds(192, 192)], R.m_l.at[1]),
        pltpu.make_async_copy(ckv_h, R.wcr.at[pl.ds(384, 384)], R.m_l.at[2]),
        pltpu.make_async_copy(cot_h.at[c], R.cot, R.m_l.at[3]),
    ]
    pl.semaphore_wait(bar, len(peers))
    for i in range(5):
        other(i)
    for i in (5, 6):
        own(i)
        other(i)
    for cp in singles:
        cp.start()

    def need(s, i):
        src = x_h.at[s] if i == 0 else items[i]
        pltpu.make_async_copy(src, places(s)[i], R.m_w.at[s, i]).wait()

    def rs_start(i, value):
        R.rs[i] = value.astype(BF)
        for k in RINGS:
            to = lax.rem(t + k, 4)
            push(
                R.rs.at[i, pl.ds(pl.multiple_of(to * SH, SH), SH)],
                R.rr.at[i, k - 1],
                R.m_rss.at[i, k - 1],
                R.m_rsr.at[i, k - 1],
                dev_x(k),
            )

    def rs_sum(i):
        for k in (1, 3, 2):
            landed(R.rr.at[i, k - 1], R.m_rsr.at[i, k - 1], dev_x(k))
        total = R.rs[i, rows_t, :].astype(F32)
        for k in range(3):
            total += R.rr[i, k].astype(F32)
        return total

    def ag_start(i, value):
        R.ag[i, rows_t, :] = value.astype(BF)
        for k in RINGS:
            push(
                R.ag.at[i, rows_t],
                R.ag.at[i, rows_t],
                R.m_ags.at[i, k - 1],
                R.m_agr.at[i, k - 1],
                dev_x(k),
            )

    def ag_wait(i):
        for k in (1, 3, 2):
            landed(R.ag.at[i, rows_t], R.m_agr.at[i, k - 1], dev_x(k))

    def gain_row(s, i):
        return R.nv[s, 0, i : i + 1, :]

    def bias_row(s, i):
        return R.nv[s, 1, i : i + 1, :]

    cross_gain = cg[...].reshape(1, D)
    cross_bias = cb[...].reshape(1, D)

    def self_forward(s):
        need(s, 0)
        need(s, 1)
        R.pk[s] = nt(R.wsa[s, 0:576, :], R.xin[s]).astype(BF)
        for h in range(NH):
            qt = R.pk[s, h * 64 : h * 64 + 64, :]
            kt = R.pk[s, QW + h * 64 : QW + h * 64 + 64, :]
            vt = R.pk[s, 2 * QW + h * 64 : 2 * QW + h * 64 + 64, :]
            st = tn(kt, qt) * SCALE
            if s == 1:
                key = lax.broadcasted_iota(jnp.int32, (TOK, TOK), 0)
                qry = lax.broadcasted_iota(jnp.int32, (TOK, TOK), 1)
                st = jnp.where(key <= qry, st, -1000000000.0)
            e = jnp.exp(st - jnp.max(st, axis=0, keepdims=True))
            pr = e / jnp.sum(e, axis=0, keepdims=True)
            R.pt[s, h] = pr
            R.ot[s, h * 64 : h * 64 + 64, :] = nn(vt, pr.astype(BF)).astype(BF)
        need(s, 2)
        rs_start(R_SA + s, tn(R.ot[s], R.wsa[s, 576:768, :]))

    def put_norm(slot, spread):
        R.sp[slot] = jnp.broadcast_to(spread, (SH, 128))

    def get_norm(slot):
        return R.sp[slot, :, 0:1]

    def self_finish(s):
        total = rs_sum(R_SA + s)
        r = R.xin[s, rows_t, :].astype(F32) + total
        need(s, 3)
        need(s, 4)
        out, n, spread = ln_forward(r, gain_row(s, 0), bias_row(s, 0))
        ag_start(A_Y1 + s, out)
        R.y1f[s] = out
        R.n1[s] = n
        put_norm(s, spread)

    def ffn_forward(s, gathered):
        u = nn(R.ag[gathered], R.wff[s, 0])
        cdf = 0.5 * (1.0 + lax.erf(u * 0.7071067811865476))
        R.act[s] = (u * cdf).astype(BF)
        R.slope[s] = cdf + u * jnp.exp(-0.5 * u * u) * 0.3989422804014327
        rs_start(R_FF + s, nn(R.act[s], R.wff[s, 1]))

    def ffn_backward(s):
        ag_wait(A_DR2 + s)
        dg = nt(R.ag[A_DR2 + s], R.wff[s, 1])
        R.du[s] = (dg * R.slope[s]).astype(BF)
        rs_start(R_DFF + s, nt(R.du[s], R.wff[s, 0]))

    def put(ref, piece, r0, value):
        rows = value.shape[0]
        ref[piece, 0, r0 : r0 + rows, :] = value[:, 0:384].astype(BF)
        ref[piece, 1, r0 : r0 + rows, :] = value[:, 384:768].astype(BF)

    def ffn_grads(s, gathered, ref):
        put(ref, 0, 0, tn(R.ag[gathered], R.du[s]))
        put(ref, 1, 0, tn(R.act[s], R.ag[A_DR2 + s]))

    def blk(name):
        return tuple(getattr(R, pre + name) for pre in ("g_", "x_", "a_", "b_", "s_", "r_"))

    goal = {
        "ffd": R.gof.at[1],
        "ffe": R.gof.at[0],
        "sad": R.gos.at[1],
        "sae": R.gos.at[0],
        "crx": R.goc,
    }

    def g0(name):
        g, x, a, b, s, r = blk(name)
        push(g.at[o], x, s.at[0], r.at[0], dev_c)

    def p_rows(name, at):
        quarter = BLOCKS[name] // 4
        return pl.ds(pl.multiple_of(at * quarter, quarter), quarter)

    def q_rows(name, at_p, at_q):
        quarter, eighth = BLOCKS[name] // 4, BLOCKS[name] // 8
        return pl.ds(pl.multiple_of(at_p * quarter + (at_q // 2) * eighth, eighth), eighth)

    def g1(name):
        g, x, a, b, s, r = blk(name)
        landed(x, r.at[0], dev_c)
        g[c] = (g[c].astype(F32) + x[...].astype(F32)).astype(BF)
        for k in RINGS:
            to = lax.rem(p + k, 4)
            push(
                g.at[c, :, p_rows(name, to)], a.at[k - 1], s.at[k], r.at[k], dev_p(k)
            )

    def g2(name):
        g, x, a, b, s, r = blk(name)
        for k in (1, 3, 2):
            landed(a.at[k - 1], r.at[k], dev_p(k))
        mine = p_rows(name, p)
        total = g[c, :, mine, :].astype(F32)
        for k in range(3):
            total += a[k].astype(F32)
        g[c, :, mine, :] = total.astype(BF)
        for k in RINGS:
            to = lax.rem(q + k, 4)
            push(
                g.at[c, lax.rem(to, 2), q_rows(name, p, to)],
                b.at[k - 1],
                s.at[3 + k],
                r.at[3 + k],
                dev_q(k),
            )

    def g3(name):
        g, x, a, b, s, r = blk(name)
        for k in (1, 3, 2):
            landed(b.at[k - 1], r.at[3 + k], dev_q(k))
        rows, half = q_rows(name, p, q), lax.rem(q, 2)
        total = g[c, half, rows, :].astype(F32)
        for k in range(3):
            total += b[k].astype(F32)
        fin = goal[name]
        fin[half, rows, :] = total.astype(BF)
        for k in RINGS:
            push(fin.at[half, rows], fin.at[half, rows], s.at[6 + k], r.at[6 + k], dev_q(k))

    final = {"ffd": (1, of_o), "ffe": (0, of_o), "sad": (1, os_o), "sae": (0, os_o)}

    def g4(name):
        g, x, a, b, s, r = blk(name)
        fin = goal[name]
        for k in (1, 3, 2):
            landed(fin.at[lax.rem(q, 2), q_rows(name, p, q)], r.at[6 + k], dev_q(k))
        mine = p_rows(name, p)
        if name not in final:
            for k in RINGS:
                push(
                    fin.at[:, mine], fin.at[:, mine], s.at[9 + k], R.f_crx.at[c, k], dev_p(k)
                )
            return
        owner, dst = final[name]
        f = getattr(R, "f_" + name)
        for k in RINGS:
            push(
                fin.at[:, mine], dst.at[c, :, mine], s.at[9 + k], f.at[c, k], (owner, t, dp_p(k))
            )

        @pl.when(c == owner)
        def _():
            pltpu.make_async_copy(fin.at[:, mine], dst.at[c, :, mine], f.at[c, 0]).start()

        @pl.when(c != owner)
        def _():
            push(fin.at[:, mine], dst.at[c, :, mine], s.at[13], f.at[c, 0], dev_c, False)

    def g5(name):
        fin = goal[name]
        mine = p_rows(name, p)
        if name not in final:
            for k in (1, 3, 2):
                landed(fin.at[:, mine], R.f_crx.at[c, k], dev_p(k))
            return
        owner, dst = final[name]
        f = getattr(R, "f_" + name)

        @pl.when(c == owner)
        def _():
            for piece in (0, 1):
                for k in range(4):
                    landed(dst.at[piece, :, mine], f.at[piece, k], dev_p(1))

        @pl.when(c != owner)
        def _():
            pltpu.make_async_remote_copy(
                src_ref=fin.at[:, mine],
                dst_ref=dst.at[c, :, mine],
                send_sem=getattr(R, "s_" + name).at[13],
                recv_sem=f.at[c, 0],
                device_id=dev_c,
                device_id_type=MESH,
            ).wait_send()

    def vec_put(row, dg, db, step=2):
        R.vec[row : row + 1, :] = dg
        R.vec[row + step : row + step + 1, :] = db

    def vec_send(buf, at, value, base, dev, count):
        buf[at] = value
        for k in range(1, count):
            push(buf.at[at], buf.at[at], R.m_vs.at[base + k - 1], R.m_vr.at[base + k - 1], dev(k))

    def vec_sum(buf, at, base, dev, count):
        for k in range(1, count):
            landed(buf.at[at], R.m_vr.at[base + k - 1], dev(k))
        total = buf[0]
        for k in range(1, count):
            total += buf[k]
        return total

    def dev_c1(k):
        return dev_c

    for j in (10, 11, 12, 13, 14, 15):
        R.vec[j : j + 1, :] = jnp.zeros((1, D), F32)

    micro = lax.broadcasted_iota(jnp.int32, (2, 16), 0)
    group = lax.broadcasted_iota(jnp.int32, (2, 16), 1)
    live = (micro == c) & (group <= d) & (dgr[...] > 0)
    first = jnp.max(jnp.where(live, group, 0), axis=1, keepdims=True)
    first = jnp.max(first, axis=0, keepdims=True)
    rows = jnp.where(c == 0, ret[0], ret[1]) + first * TOK
    g_at = rows // TOK
    b_at = jnp.where(c == 0, g_at, lax.rem(g_at, 4) * 4 + g_at // 4)
    at = b_at * TOK + lax.rem(rows, TOK)
    R.pos[0] = jnp.broadcast_to(at, (8, KEYS))
    for k in RINGS:
        push(R.pos.at[0], R.pos.at[k], R.m_kvs.at[5 + k], R.m_kvr.at[5 + k], dev_q(k))
    self_forward(0)
    self_forward(1)
    self_finish(0)
    self_finish(1)
    ag_wait(A_Y1)
    need(0, 5)
    need(0, 6)
    ffn_forward(0, A_Y1)

    for cp in singles:
        cp.wait()
    ag_wait(A_Y1 + 1)
    R.qct[...] = nt(R.wcr[0:192, :], R.ag[A_Y1 + 1]).astype(BF)
    for k in (1, 3, 2):
        landed(R.pos.at[k], R.m_kvr.at[5 + k], dev_q(k))

    def build(i, carry):
        n = lax.broadcasted_iota(jnp.int32, (TOK, KEYS), 0) + (q * 4 + i) * TOK
        rows = pl.ds(pl.multiple_of(i * TOK, TOK), TOK)
        for k in range(4):
            R.hot[k, rows, :] = jnp.where(n == R.pos[k, 0:1, :], 1.0, 0.0).astype(BF)
        return carry

    lax.fori_loop(0, 4, build, 0)

    out, n, spread = ln_forward(R.y1f[0] + rs_sum(R_FF), gain_row(0, 1), bias_row(0, 1))
    ag_start(A_BO, out)
    R.n2[0] = n
    put_norm(2, spread)
    ag_wait(A_BO)
    R.kvt[p] = nt(R.wcr[384:768, :], R.ag[A_BO]).astype(BF)

    for k in RINGS:
        push(R.kvt.at[p], R.kvt.at[p], R.m_kvs.at[k - 1], R.m_kvr.at[k - 1], dev_p(k))
    for k in (1, 3, 2):
        landed(R.kvt.at[p], R.m_kvr.at[k - 1], dev_p(k))
    column = jnp.concatenate([R.kvt[j] for j in range(4)], axis=1)
    for k in RINGS + (0,):
        R.kvs[k] = nn(column, R.hot[k]).astype(BF)
        if k:
            push(
                R.kvs.at[k], R.kvr.at[3 - k], R.m_kvs.at[6 - k], R.m_kvr.at[6 - k], dev_q(4 - k)
            )
    for k in (1, 3, 2):
        landed(R.kvr.at[k - 1], R.m_kvr.at[2 + k], dev_q(k))

    total = R.kvs[0].astype(F32)
    for k in range(3):
        total += R.kvr[k].astype(F32)
    R.kvct[...] = total.astype(BF)
    for h in range(NH):
        lo = h * 64
        st = tn(R.kvct[lo : lo + 64, :], R.qct[lo : lo + 64, :]) * SCALE
        e = jnp.exp(st - jnp.max(st, axis=0, keepdims=True))
        pr = e / jnp.sum(e, axis=0, keepdims=True)
        R.ptc[h] = pr
        R.oct[lo : lo + 64, :] = nn(R.kvct[QW + lo : QW + lo + 64, :], pr.astype(BF)).astype(BF)
    rs_start(R_CR, tn(R.oct[...], R.wcr[192:384, :]))
    need(1, 5)
    need(1, 6)
    out, n, spread = ln_forward(R.y1f[1] + rs_sum(R_CR), cross_gain, cross_bias)
    ag_start(A_Y2, out)
    R.y2f[...] = out
    R.nc[...] = n
    put_norm(4, spread)
    ag_wait(A_Y2)
    ffn_forward(1, A_Y2)
    out, n, spread = ln_forward(R.y2f[...] + rs_sum(R_FF + 1), gain_row(1, 1), bias_row(1, 1))

    dr, dg, db = ln_backward(n, spread, gain_row(1, 1), R.cot[rows_t, :].astype(F32))
    ag_start(A_DR2 + 1, dr)
    R.dres[1] = dr
    vec_put(5, dg, db)
    ffn_backward(1)
    ag_start(A_BO + 1, out)
    ffn_grads(1, A_Y2, R.g_ffd)
    g0("ffd")
    dy = R.dres[1] + rs_sum(R_DFF + 1)
    dr, dg, db = ln_backward(R.nc[...], get_norm(4), cross_gain, dy)
    ag_start(A_DRC, dr)
    R.dres[1] = dr
    vec_put(8, dg, db, 1)
    g1("ffd")
    ag_wait(A_DRC)

    def attend_backward(qt, kt, vt, pr, dot):
        dvt = nt(dot, pr.astype(BF))
        dpt = tn(vt, dot)
        dst = (pr * (dpt - jnp.sum(dpt * pr, axis=0, keepdims=True))).astype(BF)
        return nn(kt, dst) * SCALE, nt(qt, dst) * SCALE, dvt

    doc = nt(R.wcr[192:384, :], R.ag[A_DRC]).astype(BF)
    for h in range(NH):
        lo = h * 64
        dqt, dkt, dvt = attend_backward(
            R.qct[lo : lo + 64, :],
            R.kvct[lo : lo + 64, :],
            R.kvct[QW + lo : QW + lo + 64, :],
            R.ptc[h],
            doc[lo : lo + 64, :],
        )
        R.dqct[lo : lo + 64, :] = dqt.astype(BF)
        R.dkvct[lo : lo + 64, :] = dkt.astype(BF)
        R.dkvct[QW + lo : QW + lo + 64, :] = dvt.astype(BF)

    for k in RINGS:
        push(R.dkvct, R.dkr.at[k - 1], R.m_dks.at[k - 1], R.m_dkr.at[k - 1], dev_q(k))
    rs_start(R_DQ, tn(R.dqct[...], R.wcr[0:192, :]))
    put(R.g_crx, 0, 0, nn(R.dqct[...], R.ag[A_Y1 + 1]))
    put(R.g_crx, 0, 192, nn(R.oct[...], R.ag[A_DRC]))
    dy = R.dres[1] + rs_sum(R_DQ)
    dr, dg, db = ln_backward(R.n1[1], get_norm(1), gain_row(1, 0), dy)
    ag_start(A_DR1 + 1, dr)
    R.dres[1] = dr
    vec_put(4, dg, db)
    g2("ffd")

    def self_backward(s):
        ag_wait(A_DR1 + s)
        dot = nt(R.wsa[s, 576:768, :], R.ag[A_DR1 + s]).astype(BF)
        for h in range(NH):
            lo = h * 64
            dqt, dkt, dvt = attend_backward(
                R.pk[s, lo : lo + 64, :],
                R.pk[s, QW + lo : QW + lo + 64, :],
                R.pk[s, 2 * QW + lo : 2 * QW + lo + 64, :],
                R.pt[s, h],
                dot[lo : lo + 64, :],
            )
            R.dpk[s, lo : lo + 64, :] = dqt.astype(BF)
            R.dpk[s, QW + lo : QW + lo + 64, :] = dkt.astype(BF)
            R.dpk[s, 2 * QW + lo : 2 * QW + lo + 64, :] = dvt.astype(BF)

    def self_grads(s, ref):
        put(ref, 0, 0, nn(R.dpk[s, 0:384, :], R.xin[s]))
        put(ref, 1, 0, nn(R.dpk[s, 384:576, :], R.xin[s]))
        put(ref, 1, 192, nn(R.ot[s], R.ag[A_DR1 + s]))

    def input_part(s):
        rs_start(R_DSA + s, tn(R.dpk[s], R.wsa[s, 0:576, :]))

    for j in range(4):
        R.dkf[j] = nt(R.dkvct[...], R.hot[0, j * TOK : (j + 1) * TOK, :])
    for k in (1, 3, 2):
        landed(R.dkr.at[k - 1], R.m_dkr.at[k - 1], dev_q(k))
    for k in RINGS + (0,):
        to = lax.rem(p + k, 4)
        part = R.dkf[to]
        for j in (1, 2, 3):
            hot = R.hot[j, pl.ds(pl.multiple_of(to * TOK, TOK), TOK), :]
            part += nt(R.dkr[j - 1], hot)
        R.dks[to] = part.astype(BF)
        if k:
            push(R.dks.at[to], R.dk2.at[k - 1], R.m_dks.at[2 + k], R.m_dkr.at[2 + k], dev_p(k))
    self_backward(1)
    input_part(1)
    self_grads(1, R.g_sad)
    g0("sad")
    g3("ffd")
    for k in (1, 3, 2):
        landed(R.dk2.at[k - 1], R.m_dkr.at[2 + k], dev_p(k))
    total = R.dks[p].astype(F32)
    for k in range(3):
        total += R.dk2[k].astype(F32)
    R.dkv[...] = total.astype(BF)
    rs_start(R_DST, tn(R.dkv[...], R.wcr[384:768, :]))
    put(R.g_crx, 1, 0, nn(R.dkv[...], R.ag[A_BO]))
    g0("crx")
    g1("sad")
    dy = rs_sum(R_DST)
    dr, dg, db = ln_backward(R.n2[0], get_norm(2), gain_row(0, 1), dy)
    ag_start(A_DR2, dr)
    R.dres[0] = dr
    vec_put(1, dg, db)
    g4("ffd")
    g1("crx")
    ffn_backward(0)
    ffn_grads(0, A_Y1, R.g_ffe)
    g0("ffe")
    g2("sad")
    ag_start(A_IG + 1, R.dres[1] + rs_sum(R_DSA + 1))
    dy = R.dres[0] + rs_sum(R_DFF)
    dr, dg, db = ln_backward(R.n1[0], get_norm(0), gain_row(0, 0), dy)
    ag_start(A_DR1, dr)
    R.dres[0] = dr
    vec_put(0, dg, db)
    vec_send(R.vx, t, R.vec[...], 0, dev_x, 4)
    g1("ffe")
    g2("crx")
    g3("sad")
    self_backward(0)
    self_grads(0, R.g_sae)
    g0("sae")
    input_part(0)
    total = vec_sum(R.vx, t, 0, dev_x, 4)
    vec_send(R.vc, c, total, 3, dev_c1, 2)
    g4("sad")
    g3("crx")
    g1("sae")
    g2("ffe")
    total = vec_sum(R.vc, c, 3, dev_c1, 2)
    vec_send(R.vy, y, total, 4, dev_y, 4)
    ag_start(A_IG, R.dres[0] + rs_sum(R_DSA))
    g4("crx")
    ag_wait(A_BO + 1)
    push(R.ag.at[A_BO + o], bo_o.at[c], R.m_hs.at[0], R.m_hr.at[0], dev_c)
    outs = [pltpu.make_async_copy(R.ag.at[A_BO + c], bo_o.at[c], R.m_o.at[0])]
    outs[0].start()
    g3("ffe")
    g2("sae")
    total = vec_sum(R.vy, y, 4, dev_y, 4)
    vec_send(R.vz, z, total, 7, dev_z, 4)
    g4("ffe")
    g3("sae")
    g5("crx")
    push(R.goc, oc_o.at[c], R.m_hs.at[1], R.m_hr.at[1], dev_c)
    outs.append(pltpu.make_async_copy(R.goc, oc_o.at[c], R.m_o.at[1]))
    outs[1].start()
    ag_wait(A_IG)
    ag_wait(A_IG + 1)
    push(R.ag.at[A_IG + o], ig_o.at[c], R.m_hs.at[2], R.m_hr.at[2], dev_c)
    outs.append(pltpu.make_async_copy(R.ag.at[A_IG + c], ig_o.at[c], R.m_o.at[2]))
    outs[2].start()
    total = vec_sum(R.vz, z, 7, dev_z, 4)
    on_o[...] = jnp.where(c == 0, total[0:4, :], total[4:8, :])
    oe_o[...] = total[8:10, :]
    g4("sae")
    g5("ffd")
    g5("sad")
    g5("ffe")
    landed(bo_o.at[c], R.m_hr.at[0], dev_c)
    landed(oc_o.at[c], R.m_hr.at[1], dev_c)
    landed(ig_o.at[c], R.m_hr.at[2], dev_c)
    for cp in outs:
        cp.wait()
    g5("sae")
    for cp in sends:
        cp.wait_send()


JOBS = (
    [("gf", 0, r, "win", r) for r in (0, 192, 384, 576)]
    + [("gf", 1, r, "wfo", r) for r in (0, 192, 384, 576)]
    + [("gc", 0, 0, "q", 0), ("gc", 0, 192, "co", 0), ("gc", 1, 0, "kv", 0), ("gc", 1, 192, "kv", 192)]
    + [("gs", 0, 0, "qkv", 0), ("gs", 0, 192, "qkv", 192), ("gs", 1, 0, "qkv", 384)]
    + [("gs", 1, 192, "out", 0)]
)


def widen(*refs):
    bo, ig, gf, gs, gc, gn, ge = refs[:7]
    bo_o, ig_o, qkv_o, out_o, win_o, wfo_o, ng_o, nb_o, q_o, kv_o, co_o, cg_o, cb_o = refs[7:20]
    wide, ig_wide, m_out, m_x = refs[20:]
    from_ = {"gf": gf, "gs": gs, "gc": gc}
    to = {"qkv": qkv_o, "out": out_o, "win": win_o, "wfo": wfo_o, "q": q_o, "kv": kv_o, "co": co_o}
    stores = [pltpu.make_async_copy(bo, bo_o, m_x.at[0])]
    stores[0].start()
    for i, (src, piece, r0, dst, d0) in enumerate(JOBS):
        wide[i, :, 0:384] = from_[src][piece, 0, r0 : r0 + 192, :].astype(F32)
        wide[i, :, 384:768] = from_[src][piece, 1, r0 : r0 + 192, :].astype(F32)
        cp = pltpu.make_async_copy(wide.at[i], to[dst].at[pl.ds(d0, 192)], m_out.at[i])
        cp.start()
        stores.append(cp)
    ig_wide[...] = ig[...].astype(F32)
    stores.append(pltpu.make_async_copy(ig_wide, ig_o, m_x.at[1]))
    stores[-1].start()
    ng_o[...] = gn[0:2, :]
    nb_o[...] = gn[2:4, :]
    cg_o[...] = ge[0:1, :].reshape(D)
    cb_o[...] = ge[1:2, :].reshape(D)
    for cp in stores:
        cp.wait()


def body(
    layer_inputs,
    cotangent,
    doc_groups,
    retrieved_at,
    sa_qkv,
    sa_out,
    ffn_in,
    ffn_out,
    norm_gain,
    norm_bias,
    cross_q,
    cross_kv,
    cross_out,
    cross_gain,
    cross_bias,
):
    ins = (
        layer_inputs[0],
        cotangent,
        doc_groups,
        retrieved_at,
        norm_gain[0],
        norm_bias[0],
        cross_gain,
        cross_bias,
        jnp.transpose(sa_qkv[0], (1, 2, 0)).reshape(576, D),
        sa_out[0],
        ffn_in[0],
        ffn_out[0],
        jnp.transpose(cross_q, (1, 0)),
        jnp.transpose(cross_kv, (1, 2, 0)).reshape(384, D),
        cross_out,
    )
    hbm = pl.BlockSpec(memory_space=pl.ANY)
    vm = pl.BlockSpec(memory_space=VMEM)
    outs = (
        VMEM((2, TOK, D), BF),
        VMEM((2, TOK, D), BF),
        VMEM((2, 2, 768, 384), BF),
        VMEM((2, 2, 384, 384), BF),
        VMEM((2, 2, 384, 384), BF),
        VMEM((4, D), F32),
        VMEM((2, D), F32),
    )
    names = [n for n, _ in scratch_list()]

    def run(*refs):
        kernel(names, len(ins), len(outs), *refs)

    results = pl.pallas_call(
        run,
        out_shape=outs,
        in_specs=[hbm, hbm, vm, vm, hbm, hbm, vm, vm] + [hbm] * 7,
        out_specs=[vm] * len(outs),
        scratch_shapes=[s for _, s in scratch_list()],
        compiler_params=pltpu.CompilerParams(
            collective_id=0, has_side_effects=True, vmem_limit_bytes=52 << 20
        ),
        name="layers",
    )(*ins)
    wide_outs = (
        jax.ShapeDtypeStruct((2, TOK, D), BF),
        jax.ShapeDtypeStruct((2, TOK, D), F32),
        jax.ShapeDtypeStruct((576, D), F32),
        jax.ShapeDtypeStruct((192, D), F32),
        jax.ShapeDtypeStruct((768, D), F32),
        jax.ShapeDtypeStruct((768, D), F32),
        jax.ShapeDtypeStruct((2, D), F32),
        jax.ShapeDtypeStruct((2, D), F32),
        jax.ShapeDtypeStruct((192, D), F32),
        jax.ShapeDtypeStruct((384, D), F32),
        jax.ShapeDtypeStruct((192, D), F32),
        jax.ShapeDtypeStruct((D,), F32),
        jax.ShapeDtypeStruct((D,), F32),
    )
    bo, ig, d_qkv, d_out, d_in, d_fo, ng, nb, d_q, d_kv, d_co, dcg, dcb = pl.pallas_call(
        widen,
        out_shape=wide_outs,
        in_specs=[vm] * 7,
        out_specs=[hbm] * 6 + [vm] * 2 + [hbm] * 3 + [vm] * 2,
        scratch_shapes=[
            VMEM((len(JOBS), 192, D), F32),
            VMEM((2, TOK, D), F32),
            DMA((len(JOBS),)),
            DMA((2,)),
        ],
        compiler_params=pltpu.CompilerParams(vmem_limit_bytes=32 << 20),
        name="widen",
    )(*[pltpu.with_memory_space_constraint(r, VMEM) for r in results])
    return (
        bo[None],
        ig[None],
        jnp.transpose(d_qkv.reshape(3, 192, D), (2, 0, 1))[None],
        d_out[None],
        d_in[None],
        d_fo[None],
        ng[None],
        nb[None],
        jnp.transpose(d_q, (1, 0)),
        jnp.transpose(d_kv.reshape(2, 192, D), (2, 0, 1)),
        d_co,
        dcg,
        dcb,
    )


def solution(mesh):
    placed = (
        P("section", None, "dp", None),
        P(None, "dp", None),
        P(),
        P(None, "dp", None),
        P("section", None, None, "tensor"),
        P("section", "tensor", None),
        P("section", None, "tensor"),
        P("section", "tensor", None),
        P("section", None, None),
        P("section", None, None),
        P(None, "tensor"),
        P(None, None, "tensor"),
        P("tensor", None),
        P(),
        P(),
    )
    return jax.shard_map(
        body,
        mesh=mesh,
        in_specs=placed,
        out_specs=(
            P("section", None, "dp", None),
            P("section", None, "dp", None),
            P("section", None, None, "tensor"),
            P("section", "tensor", None),
            P("section", None, "tensor"),
            P("section", "tensor", None),
            P("section", None, None),
            P("section", None, None),
            P(None, "tensor"),
            P(None, None, "tensor"),
            P("tensor", None),
            P(),
            P(),
        ),
        check_vma=False,
    )
```

```python
import jax
import jax.numpy as jnp
from jax import lax
from jax.experimental import pallas as pl
from jax.experimental.pallas import tpu as pltpu
from jax.sharding import PartitionSpec as P

BF = jnp.bfloat16
F32 = jnp.float32
MESH = pl.DeviceIdType.MESH
VMEM = pltpu.VMEM
DMA = pltpu.SemaphoreType.DMA

HEAD = 64
NH = 3
EPS = 1e-05
HEADS = (0, 64, 128)
SCALE = HEAD**-0.5
TOK = 128
D = 768
SH = 32
KEYS = 256
QW = NH * HEAD
RINGS = (2, 1, 3)

A_BO, A_IG, A_Y1, A_Y2, A_DR2, A_DRC, A_DR1 = 0, 2, 4, 6, 7, 9, 10
N_AG = 12
R_SA, R_FF, R_CR, R_DFF, R_DQ, R_DSA, R_DST = 0, 2, 4, 5, 7, 8, 10
N_RS = 11
BLOCKS = {"ffd": 768, "ffe": 768, "crx": 384, "sad": 384, "sae": 384}


def nn(a, b):
    return jnp.dot(a, b, preferred_element_type=F32)


def nt(a, b):
    return lax.dot_general(a, b, (((1,), (1,)), ((), ())), preferred_element_type=F32)


def tn(a, b):
    return lax.dot_general(a, b, (((0,), (0,)), ((), ())), preferred_element_type=F32)


def scratch_list():
    out = [
        ("xin", VMEM((2, TOK, D), BF)),
        ("nv", VMEM((2, 2, 2, D), F32)),
        ("wsa", VMEM((2, 768, D), BF)),
        ("wff", VMEM((2, 2, 768, D), BF)),
        ("wcr", VMEM((768, D), BF)),
        ("cot", VMEM((TOK, D), BF)),
        ("pk", VMEM((2, 3 * QW, TOK), BF)),
        ("pt", VMEM((2, NH, TOK, TOK), F32)),
        ("ot", VMEM((2, QW, TOK), BF)),
        ("n1", VMEM((2, SH, D), F32)),
        ("n2", VMEM((2, SH, D), F32)),
        ("nc", VMEM((SH, D), F32)),
        ("sp", VMEM((5, SH, 128), F32)),
        ("y1f", VMEM((2, SH, D), F32)),
        ("y2f", VMEM((SH, D), F32)),
        ("dres", VMEM((2, SH, D), F32)),
        ("act", VMEM((2, TOK, D), BF)),
        ("slope", VMEM((2, TOK, D), F32)),
        ("hid", VMEM((TOK, D), F32)),
        ("du", VMEM((2, TOK, D), BF)),
        ("dpk", VMEM((2, 3 * QW, TOK), BF)),
        ("qct", VMEM((QW, TOK), BF)),
        ("dqct", VMEM((QW, TOK), BF)),
        ("kvct", VMEM((2 * QW, KEYS), BF)),
        ("dkvct", VMEM((2 * QW, KEYS), BF)),
        ("ptc", VMEM((NH, KEYS, TOK), F32)),
        ("oct", VMEM((QW, TOK), BF)),
        ("pos", VMEM((4, 8, KEYS), jnp.int32)),
        ("hot", VMEM((4, 4 * TOK, KEYS), BF)),
        ("kvt", VMEM((4, 2 * QW, TOK), BF)),
        ("kvs", VMEM((4, 2 * QW, KEYS), BF)),
        ("kvr", VMEM((3, 2 * QW, KEYS), BF)),
        ("dkr", VMEM((3, 2 * QW, KEYS), BF)),
        ("dkf", VMEM((4, 2 * QW, TOK), F32)),
        ("dks", VMEM((4, 2 * QW, TOK), BF)),
        ("dk2", VMEM((3, 2 * QW, TOK), BF)),
        ("dkv", VMEM((2 * QW, TOK), BF)),
        ("vec", VMEM((16, D), F32)),
        ("vx", VMEM((4, 16, D), BF)),
        ("vc", VMEM((2, 16, D), BF)),
        ("vy", VMEM((4, 16, D), BF)),
        ("vz", VMEM((4, 16, D), BF)),
        ("ag", VMEM((N_AG, TOK, D), BF)),
        ("rs", VMEM((N_RS, TOK, D), BF)),
        ("rr", VMEM((N_RS, 3, SH, D), BF)),
        ("gof", VMEM((2, 2, 768, 384), BF)),
        ("gos", VMEM((2, 2, 384, 384), BF)),
        ("goc", VMEM((2, 384, 384), BF)),
        ("m_w", DMA((2, 7))),
        ("m_ws", DMA((7,))),
        ("m_l", DMA((4,))),
        ("m_ags", DMA((N_AG, 3))),
        ("m_agr", DMA((N_AG, 3))),
        ("m_rss", DMA((N_RS, 3))),
        ("m_rsr", DMA((N_RS, 3))),
        ("m_kvs", DMA((9,))),
        ("m_kvr", DMA((9,))),
        ("m_dks", DMA((6,))),
        ("m_dkr", DMA((6,))),
        ("m_vs", DMA((10,))),
        ("m_vr", DMA((10,))),
        ("m_hs", DMA((2,))),
        ("m_hr", DMA((2,))),
        ("m_o", DMA((2,))),
    ]
    for name, rows in BLOCKS.items():
        out += [
            ("g_" + name, VMEM((2, 2, rows, 384), BF)),
            ("x_" + name, VMEM((2, rows, 384), BF)),
            ("h_" + name, VMEM((2, 2, rows // 8, 384), BF)),
            ("a_" + name, VMEM((2, 2, rows // 4, 384), BF)),
            ("b_" + name, VMEM((3, rows // 8, 384), BF)),
            ("s_" + name, DMA((18,))),
            ("r_" + name, DMA((16,))),
            ("f_" + name, DMA((2, 5))),
        ]
    return out


class Refs:
    pass


def ln_forward(r, gain, bias):
    center = r - jnp.mean(r, axis=-1, keepdims=True)
    spread = lax.rsqrt(jnp.mean(center * center, axis=-1, keepdims=True) + EPS)
    n = center * spread
    return n * gain + bias, n, spread


def ln_backward(n, spread, gain, dy):
    s = dy * gain
    dr = spread * (
        s - jnp.mean(s, axis=-1, keepdims=True) - n * jnp.mean(s * n, axis=-1, keepdims=True)
    )
    return dr, jnp.sum(dy * n, axis=0, keepdims=True), jnp.sum(dy, axis=0, keepdims=True)


def kernel(names, n_in, n_out, *refs):
    (x_h, cot_h, dgr, ret, ng_h, nb_h, cg, cb, qkv_h, out_h, win_h, wfo_h, cq_h, ckv_h, co_h) = refs[
        :n_in
    ]
    bo_o, ig_o, of_o, os_o, oc_o, on_o, oe_o = refs[n_in : n_in + n_out]
    R = Refs()
    for name, ref in zip(names, refs[n_in + n_out :]):
        setattr(R, name, ref)
    c = lax.axis_index("section")
    t = lax.axis_index("tensor")
    d = lax.axis_index("dp")
    o = 1 - c
    y = lax.rem(d, 4)
    z = d // 4
    p = y + c * (z - y)
    q = z + c * (y - z)
    sp, sq = 1 + 3 * c, 4 - 3 * c
    rows_t = pl.ds(pl.multiple_of(t * SH, SH), SH)

    def dev_x(k):
        return (c, lax.rem(t + k, 4), d)

    def dp_p(k):
        return lax.rem(p + k, 4) * sp + q * sq

    def dev_p(k):
        return (c, t, dp_p(k))

    def dev_q(k):
        return (c, t, p * sp + lax.rem(q + k, 4) * sq)

    def dev_y(k):
        return (c, t, z * 4 + lax.rem(y + k, 4))

    def dev_z(k):
        return (c, t, lax.rem(z + k, 4) * 4 + y)

    dev_c = (o, t, d)
    sends = {}

    def flush(kind, keep=0):
        queue = sends.get(kind, [])
        while len(queue) > keep:
            queue.pop(0).wait_send()

    def push(src, dst, ss, rs, dev, kind="", wait=True):
        cp = pltpu.make_async_remote_copy(
            src_ref=src, dst_ref=dst, send_sem=ss, recv_sem=rs, device_id=dev, device_id_type=MESH
        )
        cp.start()
        if wait:
            sends.setdefault(kind, []).append(cp)
        return cp

    def landed(dst, rs, dev):
        pltpu.make_async_remote_copy(
            src_ref=dst, dst_ref=dst, send_sem=rs, recv_sem=rs, device_id=dev, device_id_type=MESH
        ).wait_recv()

    def places(s):
        return [
            R.xin.at[s],
            R.wsa.at[s, pl.ds(0, 576)],
            R.wsa.at[s, pl.ds(576, 192)],
            R.nv.at[s, 0],
            R.nv.at[s, 1],
            R.wff.at[s, 0],
            R.wff.at[s, 1],
        ]

    items = [x_h.at[c], qkv_h, out_h, ng_h, nb_h, win_h, wfo_h]
    bar = pltpu.get_barrier_semaphore()
    peers = [dev_c]
    for k in (1, 2, 3):
        for dev in (dev_x(k), dev_y(k), dev_z(k)):
            peers.append(dev)
        peers.append((o,) + dev_y(k)[1:])
        peers.append((o,) + dev_z(k)[1:])
    for dev in peers:
        pl.semaphore_signal(bar, inc=1, device_id=dev, device_id_type=MESH)

    def own(i):
        pltpu.make_async_copy(items[i], places(c)[i], R.m_w.at[c, i]).start()

    def other(i):
        src = x_h.at[o] if i == 0 else items[i]
        push(src, places(c)[i], R.m_ws.at[i], R.m_w.at[c, i], dev_c)

    for i in range(5):
        own(i)
    singles = [
        pltpu.make_async_copy(cq_h, R.wcr.at[pl.ds(0, 192)], R.m_l.at[0]),
        pltpu.make_async_copy(co_h, R.wcr.at[pl.ds(192, 192)], R.m_l.at[1]),
        pltpu.make_async_copy(ckv_h, R.wcr.at[pl.ds(384, 384)], R.m_l.at[2]),
        pltpu.make_async_copy(cot_h.at[c], R.cot, R.m_l.at[3]),
    ]
    pl.semaphore_wait(bar, len(peers))
    for i in range(5):
        other(i)
    for i in (5, 6):
        own(i)
        other(i)
    for cp in singles:
        cp.start()

    def need(s, i):
        src = x_h.at[s] if i == 0 else items[i]
        pltpu.make_async_copy(src, places(s)[i], R.m_w.at[s, i]).wait()

    def rs_start(i, value):
        R.rs[i] = value.astype(BF)
        for k in RINGS:
            to = lax.rem(t + k, 4)
            push(
                R.rs.at[i, pl.ds(pl.multiple_of(to * SH, SH), SH)],
                R.rr.at[i, k - 1],
                R.m_rss.at[i, k - 1],
                R.m_rsr.at[i, k - 1],
                dev_x(k),
                "x",
            )

    def rs_sum(i):
        flush("x", 9)
        for k in (1, 3, 2):
            landed(R.rr.at[i, k - 1], R.m_rsr.at[i, k - 1], dev_x(k))
        total = R.rs[i, rows_t, :].astype(F32)
        for k in range(3):
            total += R.rr[i, k].astype(F32)
        return total

    def ag_start(i, value):
        R.ag[i, rows_t, :] = value.astype(BF)
        for k in RINGS:
            push(
                R.ag.at[i, rows_t],
                R.ag.at[i, rows_t],
                R.m_ags.at[i, k - 1],
                R.m_agr.at[i, k - 1],
                dev_x(k),
                "x",
            )

    def ag_wait(i):
        flush("x", 9)
        for k in (1, 3, 2):
            landed(R.ag.at[i, rows_t], R.m_agr.at[i, k - 1], dev_x(k))

    def gain_row(s, i):
        return R.nv[s, 0, i : i + 1, :]

    def bias_row(s, i):
        return R.nv[s, 1, i : i + 1, :]

    cross_gain = cg[...].reshape(1, D)
    cross_bias = cb[...].reshape(1, D)

    def softmax(scores):
        tops = [jnp.max(st, axis=0, keepdims=True) for st in scores]
        exps = [jnp.exp(st - top) for st, top in zip(scores, tops)]
        sums = [jnp.sum(e, axis=0, keepdims=True) for e in exps]
        return [e / total for e, total in zip(exps, sums)]

    def attend_backward(qts, kts, vts, prs, dots):
        heads = range(NH)
        dpts = [tn(vts[h], dots[h]) for h in heads]
        dvts = [nt(dots[h], prs[h].astype(BF)) for h in heads]
        sums = [jnp.sum(dpts[h] * prs[h], axis=0, keepdims=True) for h in heads]
        dsts = [(prs[h] * (dpts[h] - sums[h])).astype(BF) for h in heads]
        dqts = [nn(kts[h], dsts[h]) * SCALE for h in heads]
        dkts = [nt(qts[h], dsts[h]) * SCALE for h in heads]
        return dqts, dkts, dvts

    def self_forward(s):
        need(s, 0)
        need(s, 1)
        R.pk[s] = nt(R.wsa[s, 0:576, :], R.xin[s]).astype(BF)
        scores = [
            tn(R.pk[s, QW + lo : QW + lo + 64, :], R.pk[s, lo : lo + 64, :]) * SCALE for lo in HEADS
        ]
        if s == 1:
            key = lax.broadcasted_iota(jnp.int32, (TOK, TOK), 0)
            qry = lax.broadcasted_iota(jnp.int32, (TOK, TOK), 1)
            scores = [jnp.where(key <= qry, st, -1000000000.0) for st in scores]
        probs = softmax(scores)
        for h, lo in enumerate(HEADS):
            vt = R.pk[s, 2 * QW + lo : 2 * QW + lo + 64, :]
            R.ot[s, lo : lo + 64, :] = nn(vt, probs[h].astype(BF)).astype(BF)
            R.pt[s, h] = probs[h]
        need(s, 2)
        rs_start(R_SA + s, tn(R.ot[s], R.wsa[s, 576:768, :]))

    def put_norm(slot, spread):
        R.sp[slot] = jnp.broadcast_to(spread, (SH, 128))

    def get_norm(slot):
        return R.sp[slot, :, 0:1]

    def self_finish(s):
        total = rs_sum(R_SA + s)
        r = R.xin[s, rows_t, :].astype(F32) + total
        need(s, 3)
        need(s, 4)
        out, n, spread = ln_forward(r, gain_row(s, 0), bias_row(s, 0))
        ag_start(A_Y1 + s, out)
        R.y1f[s] = out
        R.n1[s] = n
        put_norm(s, spread)

    def ffn_forward(s, gathered):
        u = nn(R.ag[gathered], R.wff[s, 0])
        cdf = 0.5 * (1.0 + lax.erf(u * 0.7071067811865476))
        R.act[s] = (u * cdf).astype(BF)
        R.hid[...] = u
        R.slope[s] = cdf
        rs_start(R_FF + s, nn(R.act[s], R.wff[s, 1]))
        u = R.hid[...]
        R.slope[s] += u * jnp.exp(-0.5 * u * u) * 0.3989422804014327

    def ffn_backward(s):
        ag_wait(A_DR2 + s)
        dg = nt(R.ag[A_DR2 + s], R.wff[s, 1])
        R.du[s] = (dg * R.slope[s]).astype(BF)
        rs_start(R_DFF + s, nt(R.du[s], R.wff[s, 0]))

    def put(ref, piece, r0, value):
        rows = value.shape[0]
        ref[piece, 0, r0 : r0 + rows, :] = value[:, 0:384].astype(BF)
        ref[piece, 1, r0 : r0 + rows, :] = value[:, 384:768].astype(BF)

    def ffn_grads(s, gathered, ref):
        put(ref, 0, 0, tn(R.ag[gathered], R.du[s]))
        put(ref, 1, 0, tn(R.act[s], R.ag[A_DR2 + s]))

    def blk(name):
        return tuple(getattr(R, pre + name) for pre in ("g_", "x_", "a_", "b_", "s_", "r_"))

    goal = {
        "ffd": R.gof.at[1],
        "ffe": R.gof.at[0],
        "sad": R.gos.at[1],
        "sae": R.gos.at[0],
        "crx": R.goc,
    }

    def g0(name):
        g, x, a, b, s, r = blk(name)
        push(g.at[o], x, s.at[0], r.at[0], dev_c, name)

    def p_rows(name, at):
        quarter = BLOCKS[name] // 4
        return pl.ds(pl.multiple_of(at * quarter, quarter), quarter)

    def q_rows(name, at_p, at_q):
        quarter, eighth = BLOCKS[name] // 4, BLOCKS[name] // 8
        return pl.ds(pl.multiple_of(at_p * quarter + (at_q // 2) * eighth, eighth), eighth)

    def half_rows(name, at, half):
        quarter, eighth = BLOCKS[name] // 4, BLOCKS[name] // 8
        return pl.ds(pl.multiple_of(at * quarter + half * eighth, eighth), eighth)

    def p_at(k):
        return lax.rem(p + k, 4)

    def g1(name):
        g, x, a, b, s, r = blk(name)
        landed(x, r.at[0], dev_c)
        g[c] = (g[c].astype(F32) + x[...].astype(F32)).astype(BF)
        h = getattr(R, "h_" + name)
        for i, k in ((0, 1), (1, 3)):
            part = g.at[c, :, half_rows(name, p_at(2), i)]
            push(part, h.at[i], s.at[1 + i], r.at[1 + i], dev_p(k), name)

    def g1b(name):
        g, x, a, b, s, r = blk(name)
        h = getattr(R, "h_" + name)
        for i, k in ((0, 1), (1, 3)):
            landed(h.at[i], r.at[1 + i], dev_p(k))
            part = half_rows(name, p_at(k), i)
            g[c, :, part, :] = (g[c, :, part, :].astype(F32) + h[i].astype(F32)).astype(BF)
            push(
                g.at[c, :, p_rows(name, p_at(k))], a.at[i], s.at[3 + i], r.at[3 + i], dev_p(k), name
            )

    def g2(name):
        g, x, a, b, s, r = blk(name)
        mine = p_rows(name, p)
        total = g[c, :, mine, :].astype(F32)
        for i in (0, 1):
            landed(a.at[i], r.at[3 + i], dev_p(1))
            total += a[i].astype(F32)
        g[c, :, mine, :] = total.astype(BF)
        for k in RINGS:
            to = lax.rem(q + k, 4)
            push(
                g.at[c, lax.rem(to, 2), q_rows(name, p, to)],
                b.at[k - 1],
                s.at[4 + k],
                r.at[4 + k],
                dev_q(k),
                name,
            )

    def g3(name):
        g, x, a, b, s, r = blk(name)
        flush(name, 3)
        for k in (1, 3, 2):
            landed(b.at[k - 1], r.at[4 + k], dev_q(k))
        rows, half = q_rows(name, p, q), lax.rem(q, 2)
        total = g[c, half, rows, :].astype(F32)
        for k in range(3):
            total += b[k].astype(F32)
        fin = goal[name]
        fin[half, rows, :] = total.astype(BF)
        for k in RINGS:
            push(fin.at[half, rows], fin.at[half, rows], s.at[7 + k], r.at[7 + k], dev_q(k), name)

    final = {"ffd": (1, of_o), "ffe": (0, of_o), "sad": (1, os_o), "sae": (0, os_o)}

    def hop(name, rows, j):
        owner, dst = final[name]
        fin, f = goal[name], getattr(R, "f_" + name)

        @pl.when(c == owner)
        def _():
            pltpu.make_async_copy(fin.at[:, rows], dst.at[c, :, rows], f.at[c, j]).start()

        @pl.when(c != owner)
        def _():
            s = getattr(R, "s_" + name)
            push(fin.at[:, rows], dst.at[c, :, rows], s.at[15 + j], f.at[c, j], dev_c, wait=False)

    def hop_gone(name, rows, j):
        owner, dst = final[name]
        fin, f = goal[name], getattr(R, "f_" + name)

        @pl.when(c != owner)
        def _():
            s = getattr(R, "s_" + name)
            pltpu.make_async_remote_copy(
                src_ref=fin.at[:, rows],
                dst_ref=dst.at[c, :, rows],
                send_sem=s.at[15 + j],
                recv_sem=f.at[c, j],
                device_id=dev_c,
                device_id_type=MESH,
            ).wait_send()

    def g4(name):
        g, x, a, b, s, r = blk(name)
        fin = goal[name]
        for k in (1, 3, 2):
            landed(fin.at[lax.rem(q, 2), q_rows(name, p, q)], r.at[7 + k], dev_q(k))
        mine = p_rows(name, p)
        for i, k in ((0, 1), (1, 3)):
            push(fin.at[:, mine], fin.at[:, mine], s.at[11 + i], r.at[11 + i], dev_p(k), name)
        if name in final:
            hop(name, mine, 0)

    def g4b(name):
        g, x, a, b, s, r = blk(name)
        fin = goal[name]
        for i, k in ((0, 1), (1, 3)):
            landed(fin.at[:, p_rows(name, p)], r.at[11 + i], dev_p(k))
            part = half_rows(name, p_at(4 - k), i)
            if name in final:
                owner, dst = final[name]
                f = getattr(R, "f_" + name)
                to = (owner, t, dp_p(k))
                push(
                    fin.at[:, part], dst.at[c, :, part], s.at[13 + i], f.at[c, 3 + i], to, name
                )
            else:
                push(
                    fin.at[:, part], fin.at[:, part], s.at[13 + i], r.at[13 + i], dev_p(k), name
                )
        if name in final:
            for i, k in ((0, 1), (1, 3)):
                hop(name, p_rows(name, p_at(4 - k)), 1 + i)

    def g5(name):
        g, x, a, b, s, r = blk(name)
        flush(name, 2)
        fin = goal[name]
        if name not in final:
            f = getattr(R, "f_" + name)
            for i, k in ((0, 1), (1, 3)):
                landed(fin.at[:, half_rows(name, p, i)], r.at[13 + i], dev_p(k))
            push(fin, oc_o.at[c], s.at[15], f.at[c, 0], dev_c, name)
            pltpu.make_async_copy(fin, oc_o.at[c], f.at[c, 1]).start()

    def g6(name):
        f = getattr(R, "f_" + name)
        if name not in final:
            landed(oc_o.at[o], f.at[o, 0], dev_c)
            landed(oc_o.at[c], f.at[c, 1], dev_c)
            return
        owner, dst = final[name]

        @pl.when(c == owner)
        def _():
            for piece in (0, 1):
                for j in range(5):
                    rows = p_rows(name, p) if j < 3 else half_rows(name, p, 0)
                    landed(dst.at[piece, :, rows], f.at[piece, j], dev_c)

        for j, k in ((0, 0), (1, 3), (2, 1)):
            hop_gone(name, p_rows(name, p_at(k)), j)

    def vec_put(row, dg, db, step=2):
        R.vec[row : row + 1, :] = dg
        R.vec[row + step : row + step + 1, :] = db

    def vec_send(buf, at, value, base, dev, count):
        buf[at] = value.astype(BF)
        for k in range(1, count):
            push(buf.at[at], buf.at[at], R.m_vs.at[base + k - 1], R.m_vr.at[base + k - 1], dev(k))

    def vec_sum(buf, at, base, dev, count):
        for k in range(1, count):
            landed(buf.at[at], R.m_vr.at[base + k - 1], dev(k))
        total = buf[0].astype(F32)
        for k in range(1, count):
            total += buf[k].astype(F32)
        return total

    def dev_c1(k):
        return dev_c

    for j in (10, 11, 12, 13, 14, 15):
        R.vec[j : j + 1, :] = jnp.zeros((1, D), F32)

    micro = lax.broadcasted_iota(jnp.int32, (2, 16), 0)
    group = lax.broadcasted_iota(jnp.int32, (2, 16), 1)
    live = (micro == c) & (group <= d) & (dgr[...] > 0)
    first = jnp.max(jnp.where(live, group, 0), axis=1, keepdims=True)
    first = jnp.max(first, axis=0, keepdims=True)
    rows = jnp.where(c == 0, ret[0], ret[1]) + first * TOK
    g_at = rows // TOK
    b_at = jnp.where(c == 0, g_at, lax.rem(g_at, 4) * 4 + g_at // 4)
    at = b_at * TOK + lax.rem(rows, TOK)
    R.pos[0] = jnp.broadcast_to(at, (8, KEYS))
    for k in RINGS:
        push(R.pos.at[0], R.pos.at[k], R.m_kvs.at[5 + k], R.m_kvr.at[5 + k], dev_q(k))
    self_forward(0)
    self_forward(1)
    self_finish(0)
    self_finish(1)
    ag_wait(A_Y1)
    need(0, 5)
    need(0, 6)
    ffn_forward(0, A_Y1)

    for cp in singles:
        cp.wait()
    ag_wait(A_Y1 + 1)
    R.qct[...] = nt(R.wcr[0:192, :], R.ag[A_Y1 + 1]).astype(BF)
    for k in (1, 3, 2):
        landed(R.pos.at[k], R.m_kvr.at[5 + k], dev_q(k))

    def build(i, carry):
        n = lax.broadcasted_iota(jnp.int32, (TOK, KEYS), 0) + (q * 4 + i) * TOK
        rows = pl.ds(pl.multiple_of(i * TOK, TOK), TOK)
        for k in range(4):
            R.hot[k, rows, :] = jnp.where(n == R.pos[k, 0:1, :], 1.0, 0.0).astype(BF)
        return carry

    lax.fori_loop(0, 4, build, 0)

    out, n, spread = ln_forward(R.y1f[0] + rs_sum(R_FF), gain_row(0, 1), bias_row(0, 1))
    ag_start(A_BO, out)
    R.n2[0] = n
    put_norm(2, spread)
    ag_wait(A_BO)
    R.kvt[p] = nt(R.wcr[384:768, :], R.ag[A_BO]).astype(BF)

    for k in RINGS:
        push(R.kvt.at[p], R.kvt.at[p], R.m_kvs.at[k - 1], R.m_kvr.at[k - 1], dev_p(k))
    for k in (1, 3, 2):
        landed(R.kvt.at[p], R.m_kvr.at[k - 1], dev_p(k))
    column = jnp.concatenate([R.kvt[j] for j in range(4)], axis=1)
    for k in RINGS + (0,):
        R.kvs[k] = nn(column, R.hot[k]).astype(BF)
        if k:
            push(
                R.kvs.at[k], R.kvr.at[3 - k], R.m_kvs.at[6 - k], R.m_kvr.at[6 - k], dev_q(4 - k)
            )
    for k in (1, 3, 2):
        landed(R.kvr.at[k - 1], R.m_kvr.at[2 + k], dev_q(k))

    total = R.kvs[0].astype(F32)
    for k in range(3):
        total += R.kvr[k].astype(F32)
    R.kvct[...] = total.astype(BF)
    probs = softmax(
        [tn(R.kvct[lo : lo + 64, :], R.qct[lo : lo + 64, :]) * SCALE for lo in HEADS]
    )
    for h, lo in enumerate(HEADS):
        vt = R.kvct[QW + lo : QW + lo + 64, :]
        R.oct[lo : lo + 64, :] = nn(vt, probs[h].astype(BF)).astype(BF)
        R.ptc[h] = probs[h]
    rs_start(R_CR, tn(R.oct[...], R.wcr[192:384, :]))
    need(1, 5)
    need(1, 6)
    out, n, spread = ln_forward(R.y1f[1] + rs_sum(R_CR), cross_gain, cross_bias)
    ag_start(A_Y2, out)
    R.y2f[...] = out
    R.nc[...] = n
    put_norm(4, spread)
    ag_wait(A_Y2)
    ffn_forward(1, A_Y2)
    out, n, spread = ln_forward(R.y2f[...] + rs_sum(R_FF + 1), gain_row(1, 1), bias_row(1, 1))

    dr, dg, db = ln_backward(n, spread, gain_row(1, 1), R.cot[rows_t, :].astype(F32))
    ag_start(A_DR2 + 1, dr)
    R.dres[1] = dr
    vec_put(5, dg, db)
    ffn_backward(1)
    ag_start(A_BO + 1, out)
    flush("")
    ffn_grads(1, A_Y2, R.g_ffd)
    g0("ffd")
    dy = R.dres[1] + rs_sum(R_DFF + 1)
    dr, dg, db = ln_backward(R.nc[...], get_norm(4), cross_gain, dy)
    ag_start(A_DRC, dr)
    R.dres[1] = dr
    vec_put(8, dg, db, 1)
    g1("ffd")
    ag_wait(A_DRC)

    doc = nt(R.wcr[192:384, :], R.ag[A_DRC]).astype(BF)
    dqts, dkts, dvts = attend_backward(
        [R.qct[lo : lo + 64, :] for lo in HEADS],
        [R.kvct[lo : lo + 64, :] for lo in HEADS],
        [R.kvct[QW + lo : QW + lo + 64, :] for lo in HEADS],
        [R.ptc[h] for h in range(NH)],
        [doc[lo : lo + 64, :] for lo in HEADS],
    )
    for h, lo in enumerate(HEADS):
        R.dkvct[lo : lo + 64, :] = dkts[h].astype(BF)
        R.dkvct[QW + lo : QW + lo + 64, :] = dvts[h].astype(BF)
        R.dqct[lo : lo + 64, :] = dqts[h].astype(BF)

    for k in RINGS:
        push(R.dkvct, R.dkr.at[k - 1], R.m_dks.at[k - 1], R.m_dkr.at[k - 1], dev_q(k))
    rs_start(R_DQ, tn(R.dqct[...], R.wcr[0:192, :]))
    put(R.g_crx, 0, 0, nn(R.dqct[...], R.ag[A_Y1 + 1]))
    put(R.g_crx, 0, 192, nn(R.oct[...], R.ag[A_DRC]))
    g1b("ffd")
    dy = R.dres[1] + rs_sum(R_DQ)
    dr, dg, db = ln_backward(R.n1[1], get_norm(1), gain_row(1, 0), dy)
    ag_start(A_DR1 + 1, dr)
    R.dres[1] = dr
    vec_put(4, dg, db)

    def self_backward(s):
        ag_wait(A_DR1 + s)
        dot = nt(R.wsa[s, 576:768, :], R.ag[A_DR1 + s]).astype(BF)
        dqts, dkts, dvts = attend_backward(
            [R.pk[s, lo : lo + 64, :] for lo in HEADS],
            [R.pk[s, QW + lo : QW + lo + 64, :] for lo in HEADS],
            [R.pk[s, 2 * QW + lo : 2 * QW + lo + 64, :] for lo in HEADS],
            [R.pt[s, h] for h in range(NH)],
            [dot[lo : lo + 64, :] for lo in HEADS],
        )
        for h, lo in enumerate(HEADS):
            R.dpk[s, lo : lo + 64, :] = dqts[h].astype(BF)
            R.dpk[s, QW + lo : QW + lo + 64, :] = dkts[h].astype(BF)
            R.dpk[s, 2 * QW + lo : 2 * QW + lo + 64, :] = dvts[h].astype(BF)

    def self_grads(s, ref):
        put(ref, 0, 0, nn(R.dpk[s, 0:384, :], R.xin[s]))
        put(ref, 1, 0, nn(R.dpk[s, 384:576, :], R.xin[s]))
        put(ref, 1, 192, nn(R.ot[s], R.ag[A_DR1 + s]))

    def input_part(s):
        rs_start(R_DSA + s, tn(R.dpk[s], R.wsa[s, 0:576, :]))

    for j in range(4):
        R.dkf[j] = nt(R.dkvct[...], R.hot[0, j * TOK : (j + 1) * TOK, :])
    for k in (1, 3, 2):
        landed(R.dkr.at[k - 1], R.m_dkr.at[k - 1], dev_q(k))
    for k in RINGS + (0,):
        to = lax.rem(p + k, 4)
        part = R.dkf[to]
        for j in (1, 2, 3):
            hot = R.hot[j, pl.ds(pl.multiple_of(to * TOK, TOK), TOK), :]
            part += nt(R.dkr[j - 1], hot)
        R.dks[to] = part.astype(BF)
        if k:
            push(R.dks.at[to], R.dk2.at[k - 1], R.m_dks.at[2 + k], R.m_dkr.at[2 + k], dev_p(k))
    g2("ffd")
    self_backward(1)
    input_part(1)
    self_grads(1, R.g_sad)
    g0("sad")
    for k in (1, 3, 2):
        landed(R.dk2.at[k - 1], R.m_dkr.at[2 + k], dev_p(k))
    total = R.dks[p].astype(F32)
    for k in range(3):
        total += R.dk2[k].astype(F32)
    R.dkv[...] = total.astype(BF)
    rs_start(R_DST, tn(R.dkv[...], R.wcr[384:768, :]))
    put(R.g_crx, 1, 0, nn(R.dkv[...], R.ag[A_BO]))
    g0("crx")
    g3("ffd")
    g1("sad")
    dy = rs_sum(R_DST)
    dr, dg, db = ln_backward(R.n2[0], get_norm(2), gain_row(0, 1), dy)
    ag_start(A_DR2, dr)
    R.dres[0] = dr
    vec_put(1, dg, db)
    g1("crx")
    g4("ffd")
    g1b("sad")
    flush("")
    ffn_backward(0)
    ffn_grads(0, A_Y1, R.g_ffe)
    g0("ffe")
    g1b("crx")
    g2("sad")
    g4b("ffd")
    dy = R.dres[0] + rs_sum(R_DFF)
    dr, dg, db = ln_backward(R.n1[0], get_norm(0), gain_row(0, 0), dy)
    ag_start(A_DR1, dr)
    R.dres[0] = dr
    vec_put(0, dg, db)
    vec_send(R.vx, t, R.vec[...], 0, dev_x, 4)
    g1("ffe")
    ag_start(A_IG + 1, R.dres[1] + rs_sum(R_DSA + 1))
    g2("crx")
    self_backward(0)
    g1b("ffe")
    self_grads(0, R.g_sae)
    g0("sae")
    input_part(0)
    g3("sad")
    g3("crx")
    total = vec_sum(R.vx, t, 0, dev_x, 4)
    vec_send(R.vc, c, total, 3, dev_c1, 2)
    g1("sae")
    total = vec_sum(R.vc, c, 3, dev_c1, 2)
    vec_send(R.vy, y, total, 4, dev_y, 4)
    ag_start(A_IG, R.dres[0] + rs_sum(R_DSA))
    g2("ffe")
    g1b("sae")
    g4("sad")
    g4("crx")
    total = vec_sum(R.vy, y, 4, dev_y, 4)
    vec_send(R.vz, z, total, 7, dev_z, 4)
    ag_wait(A_BO + 1)
    push(R.ag.at[A_BO + o], bo_o.at[c], R.m_hs.at[0], R.m_hr.at[0], dev_c)
    outs = [pltpu.make_async_copy(R.ag.at[A_BO + c], bo_o.at[c], R.m_o.at[0])]
    outs[0].start()
    g3("ffe")
    g2("sae")
    ag_wait(A_IG)
    ag_wait(A_IG + 1)
    push(R.ag.at[A_IG + o], ig_o.at[c], R.m_hs.at[1], R.m_hr.at[1], dev_c)
    outs.append(pltpu.make_async_copy(R.ag.at[A_IG + c], ig_o.at[c], R.m_o.at[1]))
    outs[1].start()
    g4b("sad")
    g4b("crx")
    total = vec_sum(R.vz, z, 7, dev_z, 4)
    on_o[...] = jnp.where(c == 0, total[0:4, :], total[4:8, :])
    oe_o[...] = total[8:10, :]
    g4("ffe")
    g3("sae")
    flush("x")
    flush("")
    g5("crx")
    g4("sae")
    g4b("ffe")
    g4b("sae")
    landed(bo_o.at[c], R.m_hr.at[0], dev_c)
    landed(ig_o.at[c], R.m_hr.at[1], dev_c)
    for cp in outs:
        cp.wait()
    g6("ffd")
    g6("sad")
    g6("crx")
    g6("ffe")
    g6("sae")
    for kind in list(sends):
        flush(kind)


JOBS = (
    [("gf", 0, r, "win", r) for r in (0, 192, 384, 576)]
    + [("gf", 1, r, "wfo", r) for r in (0, 192, 384, 576)]
    + [("gc", 0, 0, "q", 0), ("gc", 0, 192, "co", 0), ("gc", 1, 0, "kv", 0), ("gc", 1, 192, "kv", 192)]
    + [("gs", 0, 0, "qkv", 0), ("gs", 0, 192, "qkv", 192), ("gs", 1, 0, "qkv", 384)]
    + [("gs", 1, 192, "out", 0)]
)


def widen(*refs):
    bo, ig, gf, gs, gc, gn, ge = refs[:7]
    bo_o, ig_o, qkv_o, out_o, win_o, wfo_o, ng_o, nb_o, q_o, kv_o, co_o, cg_o, cb_o = refs[7:20]
    wide, ig_wide, m_out, m_x = refs[20:]
    from_ = {"gf": gf, "gs": gs, "gc": gc}
    to = {"qkv": qkv_o, "out": out_o, "win": win_o, "wfo": wfo_o, "q": q_o, "kv": kv_o, "co": co_o}
    stores = [pltpu.make_async_copy(bo, bo_o, m_x.at[0])]
    stores[0].start()
    for i, (src, piece, r0, dst, d0) in enumerate(JOBS):
        wide[i, :, 0:384] = from_[src][piece, 0, r0 : r0 + 192, :].astype(F32)
        wide[i, :, 384:768] = from_[src][piece, 1, r0 : r0 + 192, :].astype(F32)
        cp = pltpu.make_async_copy(wide.at[i], to[dst].at[pl.ds(d0, 192)], m_out.at[i])
        cp.start()
        stores.append(cp)
    ig_wide[...] = ig[...].astype(F32)
    stores.append(pltpu.make_async_copy(ig_wide, ig_o, m_x.at[1]))
    stores[-1].start()
    ng_o[...] = gn[0:2, :]
    nb_o[...] = gn[2:4, :]
    cg_o[...] = ge[0:1, :].reshape(D)
    cb_o[...] = ge[1:2, :].reshape(D)
    for cp in stores:
        cp.wait()


def body(
    layer_inputs,
    cotangent,
    doc_groups,
    retrieved_at,
    sa_qkv,
    sa_out,
    ffn_in,
    ffn_out,
    norm_gain,
    norm_bias,
    cross_q,
    cross_kv,
    cross_out,
    cross_gain,
    cross_bias,
):
    ins = (
        layer_inputs[0],
        cotangent,
        doc_groups,
        retrieved_at,
        norm_gain[0],
        norm_bias[0],
        cross_gain,
        cross_bias,
        jnp.transpose(sa_qkv[0], (1, 2, 0)).reshape(576, D),
        sa_out[0],
        ffn_in[0],
        ffn_out[0],
        jnp.transpose(cross_q, (1, 0)),
        jnp.transpose(cross_kv, (1, 2, 0)).reshape(384, D),
        cross_out,
    )
    hbm = pl.BlockSpec(memory_space=pl.ANY)
    vm = pl.BlockSpec(memory_space=VMEM)
    outs = (
        VMEM((2, TOK, D), BF),
        VMEM((2, TOK, D), BF),
        VMEM((2, 2, 768, 384), BF),
        VMEM((2, 2, 384, 384), BF),
        VMEM((2, 2, 384, 384), BF),
        VMEM((4, D), F32),
        VMEM((2, D), F32),
    )
    names = [n for n, _ in scratch_list()]

    def run(*refs):
        kernel(names, len(ins), len(outs), *refs)

    results = pl.pallas_call(
        run,
        out_shape=outs,
        in_specs=[hbm, hbm, vm, vm, hbm, hbm, vm, vm] + [hbm] * 7,
        out_specs=[vm] * len(outs),
        scratch_shapes=[s for _, s in scratch_list()],
        compiler_params=pltpu.CompilerParams(
            collective_id=0, has_side_effects=True, vmem_limit_bytes=52 << 20
        ),
        name="layers",
    )(*ins)
    wide_outs = (
        jax.ShapeDtypeStruct((2, TOK, D), BF),
        jax.ShapeDtypeStruct((2, TOK, D), F32),
        jax.ShapeDtypeStruct((576, D), F32),
        jax.ShapeDtypeStruct((192, D), F32),
        jax.ShapeDtypeStruct((768, D), F32),
        jax.ShapeDtypeStruct((768, D), F32),
        jax.ShapeDtypeStruct((2, D), F32),
        jax.ShapeDtypeStruct((2, D), F32),
        jax.ShapeDtypeStruct((192, D), F32),
        jax.ShapeDtypeStruct((384, D), F32),
        jax.ShapeDtypeStruct((192, D), F32),
        jax.ShapeDtypeStruct((D,), F32),
        jax.ShapeDtypeStruct((D,), F32),
    )
    bo, ig, d_qkv, d_out, d_in, d_fo, ng, nb, d_q, d_kv, d_co, dcg, dcb = pl.pallas_call(
        widen,
        out_shape=wide_outs,
        in_specs=[vm] * 7,
        out_specs=[hbm] * 6 + [vm] * 2 + [hbm] * 3 + [vm] * 2,
        scratch_shapes=[
            VMEM((len(JOBS), 192, D), F32),
            VMEM((2, TOK, D), F32),
            DMA((len(JOBS),)),
            DMA((2,)),
        ],
        compiler_params=pltpu.CompilerParams(vmem_limit_bytes=32 << 20),
        name="widen",
    )(*[pltpu.with_memory_space_constraint(r, VMEM) for r in results])
    return (
        bo[None],
        ig[None],
        jnp.transpose(d_qkv.reshape(3, 192, D), (2, 0, 1))[None],
        d_out[None],
        d_in[None],
        d_fo[None],
        ng[None],
        nb[None],
        jnp.transpose(d_q, (1, 0)),
        jnp.transpose(d_kv.reshape(2, 192, D), (2, 0, 1)),
        d_co,
        dcg,
        dcb,
    )


def solution(mesh):
    placed = (
        P("section", None, "dp", None),
        P(None, "dp", None),
        P(),
        P(None, "dp", None),
        P("section", None, None, "tensor"),
        P("section", "tensor", None),
        P("section", None, "tensor"),
        P("section", "tensor", None),
        P("section", None, None),
        P("section", None, None),
        P(None, "tensor"),
        P(None, None, "tensor"),
        P("tensor", None),
        P(),
        P(),
    )
    return jax.shard_map(
        body,
        mesh=mesh,
        in_specs=placed,
        out_specs=(
            P("section", None, "dp", None),
            P("section", None, "dp", None),
            P("section", None, None, "tensor"),
            P("section", "tensor", None),
            P("section", None, "tensor"),
            P("section", "tensor", None),
            P("section", None, None),
            P("section", None, None),
            P(None, "tensor"),
            P(None, None, "tensor"),
            P("tensor", None),
            P(),
            P(),
        ),
        check_vma=False,
    )
```

```python
import jax
import jax.numpy as jnp
from jax import lax
from jax.experimental import pallas as pl
from jax.experimental.pallas import tpu as pltpu
from jax.sharding import PartitionSpec as P

BF = jnp.bfloat16
F32 = jnp.float32
MESH = pl.DeviceIdType.MESH
VMEM = pltpu.VMEM
DMA = pltpu.SemaphoreType.DMA

HEAD = 64
NH = 3
EPS = 1e-05
HEADS = (0, 64, 128)
SCALE = HEAD**-0.5
TOK = 128
D = 768
SH = 32
KEYS = 256
QW = NH * HEAD
RINGS = (2, 1, 3)

A_BO, A_IG, A_Y1, A_Y2, A_DR2, A_DRC, A_DR1 = 0, 2, 4, 6, 7, 9, 10
N_AG = 12
R_SA, R_FF, R_CR, R_DFF, R_DQ, R_DSA, R_DST = 0, 2, 4, 5, 7, 8, 10
N_RS = 11
BLOCKS = {"ffd": 768, "ffo": 384, "ffi": 384, "crx": 384, "sad": 384, "sae": 384}
WORKER = {"ffd": 1, "crx": 1, "sad": 1, "ffo": 0, "ffi": 0, "sae": 1}
OWNER = {"ffd": 1, "sad": 1, "ffo": 0, "ffi": 0, "sae": 0}
GROUP = {"ffd": "a", "crx": "b", "ffo": "b", "sad": "c", "ffi": "c", "sae": "d"}
SECOND_RS = (R_SA + 1, R_DSA + 1)
SECOND_AG = (A_BO + 1, A_IG + 1, A_Y1 + 1)


def nn(a, b):
    return jnp.dot(a, b, preferred_element_type=F32)


def nt(a, b):
    return lax.dot_general(a, b, (((1,), (1,)), ((), ())), preferred_element_type=F32)


def tn(a, b):
    return lax.dot_general(a, b, (((0,), (0,)), ((), ())), preferred_element_type=F32)


def scratch_list():
    out = [
        ("xin", VMEM((2, TOK, D), BF)),
        ("nv", VMEM((2, 2, 2, D), F32)),
        ("wsa", VMEM((2, 768, D), BF)),
        ("wff", VMEM((2, 2, 768, D), BF)),
        ("wcr", VMEM((768, D), BF)),
        ("cot", VMEM((TOK, D), BF)),
        ("pk", VMEM((2, 3 * QW, TOK), BF)),
        ("pt", VMEM((2, NH, TOK, TOK), F32)),
        ("ot", VMEM((2, QW, TOK), BF)),
        ("n1", VMEM((2, SH, D), F32)),
        ("n2", VMEM((2, SH, D), F32)),
        ("nc", VMEM((SH, D), F32)),
        ("sp", VMEM((5, SH, 128), F32)),
        ("y1f", VMEM((2, SH, D), F32)),
        ("y2f", VMEM((SH, D), F32)),
        ("dres", VMEM((2, SH, D), F32)),
        ("act", VMEM((2, TOK, D), BF)),
        ("slope", VMEM((2, TOK, D), F32)),
        ("hid", VMEM((TOK, D), F32)),
        ("du", VMEM((2, TOK, D), BF)),
        ("dpk", VMEM((2, 3 * QW, TOK), BF)),
        ("qct", VMEM((QW, TOK), BF)),
        ("dqct", VMEM((QW, TOK), BF)),
        ("kvct", VMEM((2 * QW, KEYS), BF)),
        ("dkvct", VMEM((2 * QW, KEYS), BF)),
        ("ptc", VMEM((NH, KEYS, TOK), F32)),
        ("oct", VMEM((QW, TOK), BF)),
        ("pos", VMEM((4, 8, KEYS), jnp.int32)),
        ("hot", VMEM((4, 4 * TOK, KEYS), BF)),
        ("kvt", VMEM((4, 2 * QW, TOK), BF)),
        ("kvs", VMEM((4, 2 * QW, KEYS), BF)),
        ("kvr", VMEM((3, 2 * QW, KEYS), BF)),
        ("dkr", VMEM((3, 2 * QW, KEYS), BF)),
        ("dkf", VMEM((4, 2 * QW, TOK), F32)),
        ("dks", VMEM((4, 2 * QW, TOK), BF)),
        ("dk2", VMEM((3, 2 * QW, TOK), BF)),
        ("dkv", VMEM((2 * QW, TOK), BF)),
        ("vec", VMEM((16, D), F32)),
        ("vx", VMEM((4, 16, D), BF)),
        ("vc", VMEM((2, 16, D), BF)),
        ("vy", VMEM((4, 16, D), BF)),
        ("vz", VMEM((4, 16, D), BF)),
        ("ag", VMEM((N_AG, TOK, D), BF)),
        ("rs", VMEM((N_RS, TOK, D), BF)),
        ("rr", VMEM((N_RS, 3, SH, D), BF)),
        ("m_w", DMA((2, 7))),
        ("m_ws", DMA((7,))),
        ("m_l", DMA((4,))),
        ("m_ags", DMA((2, 3))),
        ("m_agr", DMA((2, 3))),
        ("m_rss", DMA((2, 3))),
        ("m_rsr", DMA((2, 3))),
        ("m_dps", DMA((10,))),
        ("m_kvr", DMA((9,))),
        ("m_dkr", DMA((6,))),
        ("m_vr", DMA((10,))),
        ("m_hs", DMA((2,))),
        ("m_hr", DMA((3,))),
        ("m_g0", DMA((len(BLOCKS), 2))),
        ("f_sae", DMA((2, 5))),
        ("m_o", DMA((2,))),
    ]
    for name, rows in BLOCKS.items():
        out += [
            ("g_" + name, VMEM((2, 2, rows, 384), BF)),
            ("x_" + name, VMEM((2, 2, rows, 384), BF)),
            ("h_" + name, VMEM((2, 2, 2, rows // 8, 384), BF)),
            ("a_" + name, VMEM((2, 2, 2, rows // 4, 384), BF)),
            ("b_" + name, VMEM((2, 3, rows // 8, 384), BF)),
        ]
    for group in sorted(set(GROUP.values())):
        out.append(("s_" + group, DMA((2, 6 if group == GROUP["sae"] else 3))))
        out.append(("r_" + group, DMA((2, 9 if group == GROUP["sae"] else 11))))
    return out


class Refs:
    pass


def ln_forward(r, gain, bias):
    center = r - jnp.mean(r, axis=-1, keepdims=True)
    spread = lax.rsqrt(jnp.mean(center * center, axis=-1, keepdims=True) + EPS)
    n = center * spread
    return n * gain + bias, n, spread


def ln_backward(n, spread, gain, dy):
    s = dy * gain
    dr = spread * (
        s - jnp.mean(s, axis=-1, keepdims=True) - n * jnp.mean(s * n, axis=-1, keepdims=True)
    )
    return dr, jnp.sum(dy * n, axis=0, keepdims=True), jnp.sum(dy, axis=0, keepdims=True)


def kernel(names, n_in, n_out, *refs):
    (x_h, cot_h, dgr, ret, ng_h, nb_h, cg, cb, qkv_h, out_h, win_h, wfo_h, cq_h, ckv_h, co_h) = refs[
        :n_in
    ]
    bo_o, ig_o, of_o, os_o, oc_o, on_o, oe_o = refs[n_in : n_in + n_out]
    R = Refs()
    for name, ref in zip(names, refs[n_in + n_out :]):
        setattr(R, name, ref)
    c = lax.axis_index("section")
    t = lax.axis_index("tensor")
    d = lax.axis_index("dp")
    o = 1 - c
    y = lax.rem(d, 4)
    z = d // 4
    p = y + c * (z - y)
    q = z + c * (y - z)
    sp, sq = 1 + 3 * c, 4 - 3 * c
    rows_t = pl.ds(pl.multiple_of(t * SH, SH), SH)

    def dev_x(k):
        return (c, lax.rem(t + k, 4), d)

    def dp_p(k):
        return lax.rem(p + k, 4) * sp + q * sq

    def dev_p(k):
        return (c, t, dp_p(k))

    def dev_q(k):
        return (c, t, p * sp + lax.rem(q + k, 4) * sq)

    def dev_y(k):
        return (c, t, z * 4 + lax.rem(y + k, 4))

    def dev_z(k):
        return (c, t, lax.rem(z + k, 4) * 4 + y)

    dev_c = (o, t, d)
    sends = {}

    def flush(kind, keep=0):
        queue = sends.get(kind, [])
        while len(queue) > keep:
            queue.pop(0).wait_send()

    def push(src, dst, ss, rs, dev, kind="", wait=True):
        cp = pltpu.make_async_remote_copy(
            src_ref=src, dst_ref=dst, send_sem=ss, recv_sem=rs, device_id=dev, device_id_type=MESH
        )
        cp.start()
        if wait:
            sends.setdefault(kind, []).append(cp)
        return cp

    def landed(dst, rs, dev):
        pltpu.make_async_remote_copy(
            src_ref=dst, dst_ref=dst, send_sem=rs, recv_sem=rs, device_id=dev, device_id_type=MESH
        ).wait_recv()

    def places(s):
        return [
            R.xin.at[s],
            R.wsa.at[s, pl.ds(0, 576)],
            R.wsa.at[s, pl.ds(576, 192)],
            R.nv.at[s, 0],
            R.nv.at[s, 1],
            R.wff.at[s, 0],
            R.wff.at[s, 1],
        ]

    items = [x_h.at[c], qkv_h, out_h, ng_h, nb_h, win_h, wfo_h]
    bar = pltpu.get_barrier_semaphore()
    peers = [dev_c]
    for k in (1, 2, 3):
        for dev in (dev_x(k), dev_y(k), dev_z(k)):
            peers.append(dev)
    for k in (1, 3):
        peers.append((o,) + dev_y(k)[1:])
        peers.append((o,) + dev_z(k)[1:])
    for dev in peers:
        pl.semaphore_signal(bar, inc=1, device_id=dev, device_id_type=MESH)

    def own(i):
        pltpu.make_async_copy(items[i], places(c)[i], R.m_w.at[c, i]).start()

    def other(i):
        src = x_h.at[o] if i == 0 else items[i]
        push(src, places(c)[i], R.m_ws.at[i], R.m_w.at[c, i], dev_c)

    for i in range(5):
        own(i)
    singles = [
        pltpu.make_async_copy(cq_h, R.wcr.at[pl.ds(0, 192)], R.m_l.at[0]),
        pltpu.make_async_copy(co_h, R.wcr.at[pl.ds(192, 192)], R.m_l.at[1]),
        pltpu.make_async_copy(ckv_h, R.wcr.at[pl.ds(384, 384)], R.m_l.at[2]),
        pltpu.make_async_copy(cot_h.at[c], R.cot, R.m_l.at[3]),
    ]
    pl.semaphore_wait(bar, len(peers))
    for i in range(5):
        other(i)
    for i in (5, 6):
        own(i)
        other(i)
    for cp in singles:
        cp.start()

    def need(s, i):
        src = x_h.at[s] if i == 0 else items[i]
        pltpu.make_async_copy(src, places(s)[i], R.m_w.at[s, i]).wait()

    def rs_start(i, value):
        m = int(i in SECOND_RS)
        flush(("rs", m))
        R.rs[i] = value.astype(BF)
        for k in RINGS:
            to = lax.rem(t + k, 4)
            push(
                R.rs.at[i, pl.ds(pl.multiple_of(to * SH, SH), SH)],
                R.rr.at[i, k - 1],
                R.m_rss.at[m, k - 1],
                R.m_rsr.at[m, k - 1],
                dev_x(k),
                ("rs", m),
            )

    def rs_sum(i):
        for k in (1, 3, 2):
            landed(R.rr.at[i, k - 1], R.m_rsr.at[int(i in SECOND_RS), k - 1], dev_x(k))
        total = R.rs[i, rows_t, :].astype(F32)
        for k in range(3):
            total += R.rr[i, k].astype(F32)
        return total

    def ag_start(i, value):
        m = int(i in SECOND_AG)
        flush(("ag", m))
        R.ag[i, rows_t, :] = value.astype(BF)
        for k in RINGS:
            push(
                R.ag.at[i, rows_t],
                R.ag.at[i, rows_t],
                R.m_ags.at[m, k - 1],
                R.m_agr.at[m, k - 1],
                dev_x(k),
                ("ag", m),
            )

    def ag_wait(i):
        for k in (1, 3, 2):
            landed(R.ag.at[i, rows_t], R.m_agr.at[int(i in SECOND_AG), k - 1], dev_x(k))

    def gain_row(s, i):
        return R.nv[s, 0, i : i + 1, :]

    def bias_row(s, i):
        return R.nv[s, 1, i : i + 1, :]

    cross_gain = cg[...].reshape(1, D)
    cross_bias = cb[...].reshape(1, D)

    def softmax(scores):
        tops = [jnp.max(st, axis=0, keepdims=True) for st in scores]
        exps = [jnp.exp(st - top) for st, top in zip(scores, tops)]
        sums = [jnp.sum(e, axis=0, keepdims=True) for e in exps]
        return [e / total for e, total in zip(exps, sums)]

    def attend_backward(qts, kts, vts, prs, dots):
        heads = range(NH)
        dpts = [tn(vts[h], dots[h]) for h in heads]
        dvts = [nt(dots[h], prs[h].astype(BF)) for h in heads]
        sums = [jnp.sum(dpts[h] * prs[h], axis=0, keepdims=True) for h in heads]
        dsts = [(prs[h] * (dpts[h] - sums[h])).astype(BF) for h in heads]
        dqts = [nn(kts[h], dsts[h]) * SCALE for h in heads]
        dkts = [nt(qts[h], dsts[h]) * SCALE for h in heads]
        return dqts, dkts, dvts

    def self_forward(s):
        need(s, 0)
        need(s, 1)
        R.pk[s] = nt(R.wsa[s, 0:576, :], R.xin[s]).astype(BF)
        scores = [
            tn(R.pk[s, QW + lo : QW + lo + 64, :], R.pk[s, lo : lo + 64, :]) * SCALE for lo in HEADS
        ]
        if s == 1:
            key = lax.broadcasted_iota(jnp.int32, (TOK, TOK), 0)
            qry = lax.broadcasted_iota(jnp.int32, (TOK, TOK), 1)
            scores = [jnp.where(key <= qry, st, -1000000000.0) for st in scores]
        probs = softmax(scores)
        for h, lo in enumerate(HEADS):
            vt = R.pk[s, 2 * QW + lo : 2 * QW + lo + 64, :]
            R.ot[s, lo : lo + 64, :] = nn(vt, probs[h].astype(BF)).astype(BF)
            R.pt[s, h] = probs[h]
        need(s, 2)
        rs_start(R_SA + s, tn(R.ot[s], R.wsa[s, 576:768, :]))

    def put_norm(slot, spread):
        R.sp[slot] = jnp.broadcast_to(spread, (SH, 128))

    def get_norm(slot):
        return R.sp[slot, :, 0:1]

    def self_finish(s):
        total = rs_sum(R_SA + s)
        r = R.xin[s, rows_t, :].astype(F32) + total
        need(s, 3)
        need(s, 4)
        out, n, spread = ln_forward(r, gain_row(s, 0), bias_row(s, 0))
        ag_start(A_Y1 + s, out)
        R.y1f[s] = out
        R.n1[s] = n
        put_norm(s, spread)

    def ffn_forward(s, gathered):
        u = nn(R.ag[gathered], R.wff[s, 0])
        cdf = 0.5 * (1.0 + lax.erf(u * 0.7071067811865476))
        R.act[s] = (u * cdf).astype(BF)
        R.hid[...] = u
        R.slope[s] = cdf
        rs_start(R_FF + s, nn(R.act[s], R.wff[s, 1]))
        u = R.hid[...]
        R.slope[s] += u * jnp.exp(-0.5 * u * u) * 0.3989422804014327

    def ffn_backward(s):
        ag_wait(A_DR2 + s)
        dg = nt(R.ag[A_DR2 + s], R.wff[s, 1])
        R.du[s] = (dg * R.slope[s]).astype(BF)
        rs_start(R_DFF + s, nt(R.du[s], R.wff[s, 0]))

    def put(ref, piece, r0, value):
        rows = value.shape[0]
        ref[piece, 0, r0 : r0 + rows, :] = value[:, 0:384].astype(BF)
        ref[piece, 1, r0 : r0 + rows, :] = value[:, 384:768].astype(BF)

    def out_grad(s):
        return tn(R.act[s], R.ag[A_DR2 + s])

    def in_grad(s, gathered):
        return tn(R.ag[gathered], R.du[s])

    def put_halves(ref, value):
        put(ref, 0, 0, value[0:384])
        put(ref, 1, 0, value[384:768])

    def blk(name):
        bufs = tuple(getattr(R, pre + name) for pre in ("g_", "x_", "h_", "a_", "b_"))
        return bufs + (getattr(R, "s_" + GROUP[name]), getattr(R, "r_" + GROUP[name]))

    place = ((y, z), (z, y))
    devs = ((dev_y, dev_z), (dev_z, dev_y))

    def quarter(name, where):
        rows = BLOCKS[name] // 4
        return pl.ds(pl.multiple_of(where * rows, rows), rows)

    def eighth(name, where, half):
        rows = BLOCKS[name] // 8
        return pl.ds(pl.multiple_of(where * 2 * rows + half * rows, rows), rows)

    def step(where, k):
        return lax.rem(where + k, 4)

    def work(name):
        return pl.when(c == WORKER[name])

    def gone(src, sem):
        pltpu.make_async_remote_copy(
            src_ref=src, dst_ref=src, send_sem=sem, recv_sem=sem, device_id=dev_c, device_id_type=MESH
        ).wait_send()

    def ship(src, dst, ss, rs, dev):
        push(src, dst, ss, rs, dev, wait=False)

    def result(name, i, rows, half=slice(None)):
        if name == "crx":
            return oc_o.at[i, half, rows]
        if name == "ffd":
            return of_o.at[i, half, rows]
        if name in ("ffi", "ffo"):
            rows = pl.ds(pl.multiple_of(i * 384 + rows.start, 48), rows.size)
            return of_o.at[int(name == "ffo"), half, rows]
        return os_o.at[i, half, rows]

    def spot(name, i, rows, half=slice(None)):
        return R.x_sae.at[i, half, rows] if name == "sae" else result(name, i, rows, half)

    def g0(name, pieces=(0, 1)):
        g, x = blk(name)[:2]

        @pl.when(c != WORKER[name])
        def _():
            for i in pieces:
                sem = R.m_g0.at[tuple(BLOCKS).index(name), i]
                ship(g.at[i], x.at[i], sem, blk(name)[6].at[i, 0], dev_c)

    def g1(name, pieces=(0, 1)):
        g, x, h, a, b, s, r = blk(name)

        @work(name)
        def _():
            for i in pieces:
                landed(x.at[i], r.at[i, 0], dev_c)
                g[i] = g[i] + x[i]
                far = step(place[i][0], 2)
                for j, k in ((0, 1), (1, 3)):
                    part = g.at[i, :, eighth(name, far, j)]
                    ship(part, h.at[i, j], s.at[i, j], r.at[i, 1 + j], devs[i][0](k))

    def g1b(name, pieces=(0, 1)):
        g, x, h, a, b, s, r = blk(name)

        @work(name)
        def _():
            for j, k in ((0, 1), (1, 3)):
                for i in pieces:
                    near = step(place[i][0], k)
                    landed(h.at[i, j], r.at[i, 1 + j], dev_c)
                    part = eighth(name, near, j)
                    g[i, :, part, :] = g[i, :, part, :] + h[i, j]
                    part = g.at[i, :, quarter(name, near)]
                    gone(h.at[i, j], s.at[i, j])
                    ship(part, a.at[i, j], s.at[i, j], r.at[i, 3 + j], devs[i][0](k))

    def sub(name, i, where):
        return eighth(name, place[i][0], where // 2), lax.rem(where, 2)

    def g2(name, pieces=(0, 1)):
        g, x, h, a, b, s, r = blk(name)

        @work(name)
        def _():
            for i in pieces:
                mine = quarter(name, place[i][0])
                total = g[i, :, mine, :].astype(F32)
                for j in (0, 1):
                    landed(a.at[i, j], r.at[i, 3 + j], dev_c)
                    total += a[i, j].astype(F32)
                    gone(a.at[i, j], s.at[i, j])
                g[i, :, mine, :] = total.astype(BF)
                for k in RINGS:
                    rows, half = sub(name, i, step(place[i][1], k))
                    part = g.at[i, half, rows]
                    ship(part, b.at[i, k - 1], s.at[i, k - 1], r.at[i, 4 + k], devs[i][1](k))

    def g3(name, pieces=(0, 1)):
        g, x, h, a, b, s, r = blk(name)

        @work(name)
        def _():
            for i in pieces:
                for k in (1, 3, 2):
                    landed(b.at[i, k - 1], r.at[i, 4 + k], dev_c)
                rows, half = sub(name, i, place[i][1])
                total = g[i, half, rows, :].astype(F32)
                for k in range(3):
                    total += b[i, k].astype(F32)
                part = spot(name, i, rows, half)
                part[...] = total.astype(BF)
                for k in RINGS:
                    gone(b.at[i, k - 1], s.at[i, k - 1])
                    ship(part, part, s.at[i, k - 1], r.at[i, (3, 4, 8)[k - 1]], devs[i][1](k))

    def g4(name, pieces=(0, 1)):
        g, x, h, a, b, s, r = blk(name)

        @work(name)
        def _():
            for i in pieces:
                mine = quarter(name, place[i][0])
                part = spot(name, i, mine)
                for k in (1, 3, 2):
                    landed(b.at[i, k - 1], r.at[i, (3, 4, 8)[k - 1]], dev_c)
                    gone(b.at[i, k - 1], s.at[i, k - 1])
                for j, k in ((0, 1), (1, 3)):
                    ship(part, part, s.at[i, j], r.at[i, 2 - j], devs[i][0](k))
                if name == "sae":
                    ship(part, result(name, i, mine), s.at[i, 3], R.f_sae.at[i, 0], dev_c)

    def g4b(name, pieces=(0, 1)):
        g, x, h, a, b, s, r = blk(name)

        @work(name)
        def _():
            for j, k in ((0, 1), (1, 3)):
                for i in pieces:
                    behind = step(place[i][0], 4 - k)
                    landed(a.at[i, j], r.at[i, 2 - j], dev_c)
                    gone(a.at[i, j], s.at[i, j])
                    rows = eighth(name, behind, j)
                    part, to = spot(name, i, rows), devs[i][0](k)
                    if name == "sae":
                        to = (OWNER[name],) + to[1:]
                        ship(part, result(name, i, rows), s.at[i, j], R.f_sae.at[i, 3 + j], to)
                    else:
                        ship(part, part, s.at[i, j], r.at[i, 9 + j], to)
            if name == "sae":
                for j, k in ((0, 1), (1, 3)):
                    for i in pieces:
                        rows = quarter(name, step(place[i][0], 4 - k))
                        part = x.at[i, :, rows]
                        ship(part, result(name, i, rows), s.at[i, 4 + j], R.f_sae.at[i, 1 + j], dev_c)

    def g5(name):
        g, x, h, a, b, s, r = blk(name)

        @work(name)
        def _():
            for i in (0, 1):
                for j in (0, 1):
                    landed(h.at[i, j], r.at[i, 9 + j], dev_c)
            if name == "crx":
                ship(oc_o, oc_o, s.at[0, 2], R.m_hr.at[2], dev_c)

    def g6(name):
        g, x, h, a, b, s, r = blk(name)

        @pl.when(c != WORKER[name])
        def _():
            for i in (0, 1):
                gone(g.at[i], R.m_g0.at[tuple(BLOCKS).index(name), i])
            if name == "crx":
                landed(oc_o, R.m_hr.at[2], dev_c)
            if name == "sae":
                for i in (0, 1):
                    for j in range(5):
                        landed(a.at[i, 0] if j < 3 else h.at[i, 0], R.f_sae.at[i, j], dev_c)

        @work(name)
        def _():
            for i in (0, 1):
                for j in (0, 1):
                    gone(h.at[i, j], s.at[i, j])
                if name == "sae":
                    for j in (0, 1, 2):
                        gone(a.at[i, 0], s.at[i, 3 + j])
            if name == "crx":
                gone(oc_o, s.at[0, 2])

    def vec_put(row, dg, db, step=2):
        R.vec[row : row + 1, :] = dg
        R.vec[row + step : row + step + 1, :] = db

    def vec_send(buf, at, value, base, dev, count):
        buf[at] = value.astype(BF)
        for k in range(1, count):
            push(buf.at[at], buf.at[at], R.m_dps.at[base + k - 1], R.m_vr.at[base + k - 1], dev(k))

    def vec_sum(buf, at, base, dev, count):
        for k in range(1, count):
            landed(buf.at[at], R.m_vr.at[base + k - 1], dev(k))
        total = buf[0].astype(F32)
        for k in range(1, count):
            total += buf[k].astype(F32)
        return total

    def dev_c1(k):
        return dev_c

    for j in (10, 11, 12, 13, 14, 15):
        R.vec[j : j + 1, :] = jnp.zeros((1, D), F32)

    micro = lax.broadcasted_iota(jnp.int32, (2, 16), 0)
    group = lax.broadcasted_iota(jnp.int32, (2, 16), 1)
    live = (micro == c) & (group <= d) & (dgr[...] > 0)
    first = jnp.max(jnp.where(live, group, 0), axis=1, keepdims=True)
    first = jnp.max(first, axis=0, keepdims=True)
    rows = jnp.where(c == 0, ret[0], ret[1]) + first * TOK
    g_at = rows // TOK
    b_at = jnp.where(c == 0, g_at, lax.rem(g_at, 4) * 4 + g_at // 4)
    at = b_at * TOK + lax.rem(rows, TOK)
    R.pos[0] = jnp.broadcast_to(at, (8, KEYS))
    for k in RINGS:
        push(R.pos.at[0], R.pos.at[k], R.m_dps.at[5 + k], R.m_kvr.at[5 + k], dev_q(k))
    self_forward(0)
    self_forward(1)
    self_finish(0)
    self_finish(1)
    ag_wait(A_Y1)
    need(0, 5)
    need(0, 6)
    ffn_forward(0, A_Y1)

    for cp in singles:
        cp.wait()
    ag_wait(A_Y1 + 1)
    R.qct[...] = nt(R.wcr[0:192, :], R.ag[A_Y1 + 1]).astype(BF)
    for k in (1, 3, 2):
        landed(R.pos.at[k], R.m_kvr.at[5 + k], dev_q(k))

    def build(i, carry):
        n = lax.broadcasted_iota(jnp.int32, (TOK, KEYS), 0) + (q * 4 + i) * TOK
        rows = pl.ds(pl.multiple_of(i * TOK, TOK), TOK)
        for k in range(4):
            R.hot[k, rows, :] = jnp.where(n == R.pos[k, 0:1, :], 1.0, 0.0).astype(BF)
        return carry

    lax.fori_loop(0, 4, build, 0)

    out, n, spread = ln_forward(R.y1f[0] + rs_sum(R_FF), gain_row(0, 1), bias_row(0, 1))
    ag_start(A_BO, out)
    R.n2[0] = n
    put_norm(2, spread)
    ag_wait(A_BO)
    R.kvt[p] = nt(R.wcr[384:768, :], R.ag[A_BO]).astype(BF)

    for k in RINGS:
        push(R.kvt.at[p], R.kvt.at[p], R.m_dps.at[k - 1], R.m_kvr.at[k - 1], dev_p(k))
    for k in (1, 3, 2):
        landed(R.kvt.at[p], R.m_kvr.at[k - 1], dev_p(k))
    column = jnp.concatenate([R.kvt[j] for j in range(4)], axis=1)
    for k in RINGS + (0,):
        R.kvs[k] = nn(column, R.hot[k]).astype(BF)
        if k:
            push(
                R.kvs.at[k], R.kvr.at[3 - k], R.m_dps.at[6 - k], R.m_kvr.at[6 - k], dev_q(4 - k)
            )
    for k in (1, 3, 2):
        landed(R.kvr.at[k - 1], R.m_kvr.at[2 + k], dev_q(k))

    total = R.kvs[0].astype(F32)
    for k in range(3):
        total += R.kvr[k].astype(F32)
    R.kvct[...] = total.astype(BF)
    probs = softmax(
        [tn(R.kvct[lo : lo + 64, :], R.qct[lo : lo + 64, :]) * SCALE for lo in HEADS]
    )
    for h, lo in enumerate(HEADS):
        vt = R.kvct[QW + lo : QW + lo + 64, :]
        R.oct[lo : lo + 64, :] = nn(vt, probs[h].astype(BF)).astype(BF)
        R.ptc[h] = probs[h]
    rs_start(R_CR, tn(R.oct[...], R.wcr[192:384, :]))
    need(1, 5)
    need(1, 6)
    out, n, spread = ln_forward(R.y1f[1] + rs_sum(R_CR), cross_gain, cross_bias)
    ag_start(A_Y2, out)
    R.y2f[...] = out
    R.nc[...] = n
    put_norm(4, spread)
    ag_wait(A_Y2)
    ffn_forward(1, A_Y2)
    out, n, spread = ln_forward(R.y2f[...] + rs_sum(R_FF + 1), gain_row(1, 1), bias_row(1, 1))

    dr, dg, db = ln_backward(n, spread, gain_row(1, 1), R.cot[rows_t, :].astype(F32))
    ag_start(A_DR2 + 1, dr)
    R.dres[1] = dr
    vec_put(5, dg, db)
    ffn_backward(1)
    ag_start(A_BO + 1, out)
    flush("")
    put(R.g_ffd, 0, 0, in_grad(1, A_Y2))
    put(R.g_ffd, 1, 0, out_grad(1))
    g0("ffd")
    dy = R.dres[1] + rs_sum(R_DFF + 1)
    dr, dg, db = ln_backward(R.nc[...], get_norm(4), cross_gain, dy)
    ag_start(A_DRC, dr)
    R.dres[1] = dr
    vec_put(8, dg, db, 1)
    g1("ffd")
    ag_wait(A_DRC)

    doc = nt(R.wcr[192:384, :], R.ag[A_DRC]).astype(BF)
    dqts, dkts, dvts = attend_backward(
        [R.qct[lo : lo + 64, :] for lo in HEADS],
        [R.kvct[lo : lo + 64, :] for lo in HEADS],
        [R.kvct[QW + lo : QW + lo + 64, :] for lo in HEADS],
        [R.ptc[h] for h in range(NH)],
        [doc[lo : lo + 64, :] for lo in HEADS],
    )
    for h, lo in enumerate(HEADS):
        R.dkvct[lo : lo + 64, :] = dkts[h].astype(BF)
        R.dkvct[QW + lo : QW + lo + 64, :] = dvts[h].astype(BF)
        R.dqct[lo : lo + 64, :] = dqts[h].astype(BF)

    for k in RINGS:
        push(R.dkvct, R.dkr.at[k - 1], R.m_dps.at[k - 1], R.m_dkr.at[k - 1], dev_q(k))
    rs_start(R_DQ, tn(R.dqct[...], R.wcr[0:192, :]))
    put(R.g_crx, 0, 0, nn(R.dqct[...], R.ag[A_Y1 + 1]))
    put(R.g_crx, 0, 192, nn(R.oct[...], R.ag[A_DRC]))
    g1b("ffd")
    dy = R.dres[1] + rs_sum(R_DQ)
    dr, dg, db = ln_backward(R.n1[1], get_norm(1), gain_row(1, 0), dy)
    ag_start(A_DR1 + 1, dr)
    R.dres[1] = dr
    vec_put(4, dg, db)

    def self_backward(s):
        ag_wait(A_DR1 + s)
        dot = nt(R.wsa[s, 576:768, :], R.ag[A_DR1 + s]).astype(BF)
        dqts, dkts, dvts = attend_backward(
            [R.pk[s, lo : lo + 64, :] for lo in HEADS],
            [R.pk[s, QW + lo : QW + lo + 64, :] for lo in HEADS],
            [R.pk[s, 2 * QW + lo : 2 * QW + lo + 64, :] for lo in HEADS],
            [R.pt[s, h] for h in range(NH)],
            [dot[lo : lo + 64, :] for lo in HEADS],
        )
        for h, lo in enumerate(HEADS):
            R.dpk[s, lo : lo + 64, :] = dqts[h].astype(BF)
            R.dpk[s, QW + lo : QW + lo + 64, :] = dkts[h].astype(BF)
            R.dpk[s, 2 * QW + lo : 2 * QW + lo + 64, :] = dvts[h].astype(BF)

    def self_grads(s, ref):
        put(ref, 0, 0, nn(R.dpk[s, 0:384, :], R.xin[s]))
        put(ref, 1, 0, nn(R.dpk[s, 384:576, :], R.xin[s]))
        put(ref, 1, 192, nn(R.ot[s], R.ag[A_DR1 + s]))

    def input_part(s):
        rs_start(R_DSA + s, tn(R.dpk[s], R.wsa[s, 0:576, :]))

    for j in range(4):
        R.dkf[j] = nt(R.dkvct[...], R.hot[0, j * TOK : (j + 1) * TOK, :])
    for k in (1, 3, 2):
        landed(R.dkr.at[k - 1], R.m_dkr.at[k - 1], dev_q(k))
    for k in RINGS + (0,):
        to = lax.rem(p + k, 4)
        part = R.dkf[to]
        for j in (1, 2, 3):
            hot = R.hot[j, pl.ds(pl.multiple_of(to * TOK, TOK), TOK), :]
            part += nt(R.dkr[j - 1], hot)
        R.dks[to] = part.astype(BF)
        if k:
            push(R.dks.at[to], R.dk2.at[k - 1], R.m_dps.at[2 + k], R.m_dkr.at[2 + k], dev_p(k))
    g2("ffd")
    self_backward(1)
    input_part(1)
    self_grads(1, R.g_sad)
    g0("sad")
    for k in (1, 3, 2):
        landed(R.dk2.at[k - 1], R.m_dkr.at[2 + k], dev_p(k))
    total = R.dks[p].astype(F32)
    for k in range(3):
        total += R.dk2[k].astype(F32)
    R.dkv[...] = total.astype(BF)
    rs_start(R_DST, tn(R.dkv[...], R.wcr[384:768, :]))
    put(R.g_crx, 1, 0, nn(R.dkv[...], R.ag[A_BO]))
    g0("crx")
    g1("sad")
    g3("ffd")
    g1("crx")
    g1b("sad")
    dy = rs_sum(R_DST)
    dr, dg, db = ln_backward(R.n2[0], get_norm(2), gain_row(0, 1), dy)
    ag_start(A_DR2, dr)
    R.dres[0] = dr
    vec_put(1, dg, db)
    flush("")
    ag_wait(A_BO + 1)
    push(R.ag.at[A_BO + o], bo_o.at[c], R.m_hs.at[0], R.m_hr.at[0], dev_c)
    outs = [pltpu.make_async_copy(R.ag.at[A_BO + c], bo_o.at[c], R.m_o.at[0])]
    outs[0].start()
    g4("ffd")
    g1b("crx")
    g2("sad")
    ffn_backward(0)
    put_halves(R.g_ffo, out_grad(0))
    g0("ffo")
    put_halves(R.g_ffi, in_grad(0, A_Y1))
    g0("ffi")
    g4b("ffd")
    g2("crx")
    g1("ffo")
    dy = R.dres[0] + rs_sum(R_DFF)
    dr, dg, db = ln_backward(R.n1[0], get_norm(0), gain_row(0, 0), dy)
    ag_start(A_DR1, dr)
    R.dres[0] = dr
    vec_put(0, dg, db)
    g1("ffi")
    vec_send(R.vx, t, R.vec[...], 0, dev_x, 4)
    g3("sad")
    ag_start(A_IG + 1, R.dres[1] + rs_sum(R_DSA + 1))
    g1b("ffo")
    g3("crx")
    self_backward(0)
    g1b("ffi")
    self_grads(0, R.g_sae)
    g0("sae")
    input_part(0)
    g4("sad")
    g2("ffo")
    g4("crx")
    total = vec_sum(R.vx, t, 0, dev_x, 4)
    vec_send(R.vc, c, total, 3, dev_c1, 2)
    g1("sae")
    g2("ffi")
    total = vec_sum(R.vc, c, 3, dev_c1, 2)
    vec_send(R.vy, y, total, 4, dev_y, 4)
    g4b("sad")
    g1b("sae")
    ag_start(A_IG, R.dres[0] + rs_sum(R_DSA))
    g3("ffo")
    g4b("crx")
    g3("ffi")
    g2("sae")
    total = vec_sum(R.vy, y, 4, dev_y, 4)
    vec_send(R.vz, z, total, 7, dev_z, 4)
    g4("ffo")
    g4("ffi")
    ag_wait(A_IG)
    ag_wait(A_IG + 1)
    push(R.ag.at[A_IG + o], ig_o.at[c], R.m_hs.at[1], R.m_hr.at[1], dev_c)
    outs.append(pltpu.make_async_copy(R.ag.at[A_IG + c], ig_o.at[c], R.m_o.at[1]))
    outs[1].start()
    g3("sae")
    g5("crx")
    total = vec_sum(R.vz, z, 7, dev_z, 4)
    on_o[...] = jnp.where(c == 0, total[0:4, :], total[4:8, :])
    oe_o[...] = total[8:10, :]
    flush("")
    g4b("ffo")
    g4("sae")
    g4b("ffi")
    g4b("sae")
    landed(bo_o.at[c], R.m_hr.at[0], dev_c)
    landed(ig_o.at[c], R.m_hr.at[1], dev_c)
    for cp in outs:
        cp.wait()
    g5("ffd")
    g5("sad")
    g5("ffo")
    g5("ffi")
    for name in ("ffd", "sad", "crx", "ffo", "ffi", "sae"):
        g6(name)
    for kind in list(sends):
        flush(kind)


JOBS = (
    [("gf", 0, r, "win", r) for r in (0, 192, 384, 576)]
    + [("gf", 1, r, "wfo", r) for r in (0, 192, 384, 576)]
    + [("gc", 0, 0, "q", 0), ("gc", 0, 192, "co", 0), ("gc", 1, 0, "kv", 0), ("gc", 1, 192, "kv", 192)]
    + [("gs", 0, 0, "qkv", 0), ("gs", 0, 192, "qkv", 192), ("gs", 1, 0, "qkv", 384)]
    + [("gs", 1, 192, "out", 0)]
)


def widen(*refs):
    bo, ig, gf, gs, gc, gn, ge = refs[:7]
    bo_o, ig_o, qkv_o, out_o, win_o, wfo_o, ng_o, nb_o, q_o, kv_o, co_o, cg_o, cb_o = refs[7:20]
    wide, ig_wide, m_out, m_x = refs[20:]
    from_ = {"gf": gf, "gs": gs, "gc": gc}
    to = {"qkv": qkv_o, "out": out_o, "win": win_o, "wfo": wfo_o, "q": q_o, "kv": kv_o, "co": co_o}
    stores = [pltpu.make_async_copy(bo, bo_o, m_x.at[0])]
    stores[0].start()
    for i, (src, piece, r0, dst, d0) in enumerate(JOBS):
        wide[i, :, 0:384] = from_[src][piece, 0, r0 : r0 + 192, :].astype(F32)
        wide[i, :, 384:768] = from_[src][piece, 1, r0 : r0 + 192, :].astype(F32)
        cp = pltpu.make_async_copy(wide.at[i], to[dst].at[pl.ds(d0, 192)], m_out.at[i])
        cp.start()
        stores.append(cp)
    ig_wide[...] = ig[...].astype(F32)
    stores.append(pltpu.make_async_copy(ig_wide, ig_o, m_x.at[1]))
    stores[-1].start()
    ng_o[...] = gn[0:2, :]
    nb_o[...] = gn[2:4, :]
    cg_o[...] = ge[0:1, :].reshape(D)
    cb_o[...] = ge[1:2, :].reshape(D)
    for cp in stores:
        cp.wait()


def body(
    layer_inputs,
    cotangent,
    doc_groups,
    retrieved_at,
    sa_qkv,
    sa_out,
    ffn_in,
    ffn_out,
    norm_gain,
    norm_bias,
    cross_q,
    cross_kv,
    cross_out,
    cross_gain,
    cross_bias,
):
    ins = (
        layer_inputs[0],
        cotangent,
        doc_groups,
        retrieved_at,
        norm_gain[0],
        norm_bias[0],
        cross_gain,
        cross_bias,
        jnp.transpose(sa_qkv[0], (1, 2, 0)).reshape(576, D),
        sa_out[0],
        ffn_in[0],
        ffn_out[0],
        jnp.transpose(cross_q, (1, 0)),
        jnp.transpose(cross_kv, (1, 2, 0)).reshape(384, D),
        cross_out,
    )
    hbm = pl.BlockSpec(memory_space=pl.ANY)
    vm = pl.BlockSpec(memory_space=VMEM)
    outs = (
        VMEM((2, TOK, D), BF),
        VMEM((2, TOK, D), BF),
        VMEM((2, 2, 768, 384), BF),
        VMEM((2, 2, 384, 384), BF),
        VMEM((2, 2, 384, 384), BF),
        VMEM((4, D), F32),
        VMEM((2, D), F32),
    )
    names = [n for n, _ in scratch_list()]

    def run(*refs):
        kernel(names, len(ins), len(outs), *refs)

    results = pl.pallas_call(
        run,
        out_shape=outs,
        in_specs=[hbm, hbm, vm, vm, hbm, hbm, vm, vm] + [hbm] * 7,
        out_specs=[vm] * len(outs),
        scratch_shapes=[s for _, s in scratch_list()],
        compiler_params=pltpu.CompilerParams(
            collective_id=0, has_side_effects=True, vmem_limit_bytes=52 << 20
        ),
        name="layers",
    )(*ins)
    wide_outs = (
        jax.ShapeDtypeStruct((2, TOK, D), BF),
        jax.ShapeDtypeStruct((2, TOK, D), F32),
        jax.ShapeDtypeStruct((576, D), F32),
        jax.ShapeDtypeStruct((192, D), F32),
        jax.ShapeDtypeStruct((768, D), F32),
        jax.ShapeDtypeStruct((768, D), F32),
        jax.ShapeDtypeStruct((2, D), F32),
        jax.ShapeDtypeStruct((2, D), F32),
        jax.ShapeDtypeStruct((192, D), F32),
        jax.ShapeDtypeStruct((384, D), F32),
        jax.ShapeDtypeStruct((192, D), F32),
        jax.ShapeDtypeStruct((D,), F32),
        jax.ShapeDtypeStruct((D,), F32),
    )
    bo, ig, d_qkv, d_out, d_in, d_fo, ng, nb, d_q, d_kv, d_co, dcg, dcb = pl.pallas_call(
        widen,
        out_shape=wide_outs,
        in_specs=[vm] * 7,
        out_specs=[hbm] * 6 + [vm] * 2 + [hbm] * 3 + [vm] * 2,
        scratch_shapes=[
            VMEM((len(JOBS), 192, D), F32),
            VMEM((2, TOK, D), F32),
            DMA((len(JOBS),)),
            DMA((2,)),
        ],
        compiler_params=pltpu.CompilerParams(vmem_limit_bytes=32 << 20),
        name="widen",
    )(*[pltpu.with_memory_space_constraint(r, VMEM) for r in results])
    return (
        bo[None],
        ig[None],
        jnp.transpose(d_qkv.reshape(3, 192, D), (2, 0, 1))[None],
        d_out[None],
        d_in[None],
        d_fo[None],
        ng[None],
        nb[None],
        jnp.transpose(d_q, (1, 0)),
        jnp.transpose(d_kv.reshape(2, 192, D), (2, 0, 1)),
        d_co,
        dcg,
        dcb,
    )


def solution(mesh):
    placed = (
        P("section", None, "dp", None),
        P(None, "dp", None),
        P(),
        P(None, "dp", None),
        P("section", None, None, "tensor"),
        P("section", "tensor", None),
        P("section", None, "tensor"),
        P("section", "tensor", None),
        P("section", None, None),
        P("section", None, None),
        P(None, "tensor"),
        P(None, None, "tensor"),
        P("tensor", None),
        P(),
        P(),
    )
    return jax.shard_map(
        body,
        mesh=mesh,
        in_specs=placed,
        out_specs=(
            P("section", None, "dp", None),
            P("section", None, "dp", None),
            P("section", None, None, "tensor"),
            P("section", "tensor", None),
            P("section", None, "tensor"),
            P("section", "tensor", None),
            P("section", None, None),
            P("section", None, None),
            P(None, "tensor"),
            P(None, None, "tensor"),
            P("tensor", None),
            P(),
            P(),
        ),
        check_vma=False,
    )
```

```python
import jax
import jax.numpy as jnp
from jax import lax
from jax.experimental import pallas as pl
from jax.experimental.pallas import tpu as pltpu
from jax.sharding import PartitionSpec as P

BF = jnp.bfloat16
F32 = jnp.float32
MESH = pl.DeviceIdType.MESH
VMEM = pltpu.VMEM
DMA = pltpu.SemaphoreType.DMA

HEAD = 64
NH = 3
EPS = 1e-05
HEADS = (0, 64, 128)
SCALE = HEAD**-0.5
TOK = 128
D = 768
SH = 32
KEYS = 256
QW = NH * HEAD
RINGS = (2, 1, 3)

A_BO, A_IG, A_Y1, A_Y2, A_DR2, A_DRC, A_DR1 = 0, 2, 4, 6, 7, 9, 10
N_AG = 12
R_SA, R_FF, R_CR, R_DFF, R_DQ, R_DSA, R_DST = 0, 2, 4, 5, 7, 8, 10
N_RS = 11
BLOCKS = {"ffd": 768, "ffo": 384, "ffi": 384, "crx": 384, "sad": 384, "sae": 384}
WORKER = {"ffd": 1, "crx": 1, "sad": 1, "ffo": 0, "ffi": 0, "sae": 1}
OWNER = {"ffd": 1, "sad": 1, "ffo": 0, "ffi": 0, "sae": 0}
WHOLE = ("sae",)
GROUP = {"ffd": "a", "crx": "b", "ffo": "b", "sad": "c", "ffi": "c", "sae": "d"}
SECOND_RS = (R_SA + 1, R_DSA + 1)
SECOND_AG = (A_BO + 1, A_IG + 1, A_Y1 + 1)


def nn(a, b):
    return jnp.dot(a, b, preferred_element_type=F32)


def nt(a, b):
    return lax.dot_general(a, b, (((1,), (1,)), ((), ())), preferred_element_type=F32)


def tn(a, b):
    return lax.dot_general(a, b, (((0,), (0,)), ((), ())), preferred_element_type=F32)


def scratch_list():
    out = [
        ("xin", VMEM((2, TOK, D), BF)),
        ("nv", VMEM((2, 2, 2, D), F32)),
        ("wsa", VMEM((2, 768, D), BF)),
        ("wff", VMEM((2, 2, 768, D), BF)),
        ("wcr", VMEM((768, D), BF)),
        ("cot", VMEM((TOK, D), BF)),
        ("pk", VMEM((2, 3 * QW, TOK), BF)),
        ("pt", VMEM((2, NH, TOK, TOK), F32)),
        ("ot", VMEM((2, QW, TOK), BF)),
        ("n1", VMEM((2, SH, D), F32)),
        ("n2", VMEM((2, SH, D), F32)),
        ("nc", VMEM((SH, D), F32)),
        ("sp", VMEM((5, SH, 128), F32)),
        ("y1f", VMEM((2, SH, D), F32)),
        ("y2f", VMEM((SH, D), F32)),
        ("dres", VMEM((2, SH, D), F32)),
        ("act", VMEM((2, TOK, D), BF)),
        ("slope", VMEM((2, TOK, D), F32)),
        ("hid", VMEM((TOK, D), F32)),
        ("du", VMEM((2, TOK, D), BF)),
        ("dpk", VMEM((2, 3 * QW, TOK), BF)),
        ("qct", VMEM((QW, TOK), BF)),
        ("dqct", VMEM((QW, TOK), BF)),
        ("kvct", VMEM((2 * QW, KEYS), BF)),
        ("dkvct", VMEM((2 * QW, KEYS), BF)),
        ("ptc", VMEM((NH, KEYS, TOK), F32)),
        ("oct", VMEM((QW, TOK), BF)),
        ("pos", VMEM((4, 8, KEYS), jnp.int32)),
        ("hot", VMEM((4, 4 * TOK, KEYS), BF)),
        ("kvt", VMEM((4, 2 * QW, TOK), BF)),
        ("kvf", VMEM((4, 2 * QW, KEYS), F32)),
        ("kvs", VMEM((4, 2 * QW, KEYS), BF)),
        ("kvr", VMEM((3, 2 * QW, KEYS), BF)),
        ("dkr", VMEM((3, 2 * QW, KEYS), BF)),
        ("dkf", VMEM((4, 2 * QW, TOK), F32)),
        ("dks", VMEM((4, 2 * QW, TOK), BF)),
        ("dk2", VMEM((3, 2 * QW, TOK), BF)),
        ("dkv", VMEM((2 * QW, TOK), BF)),
        ("vec", VMEM((16, D), F32)),
        ("vx", VMEM((4, 16, D), BF)),
        ("vc", VMEM((2, 16, D), BF)),
        ("vy", VMEM((4, 16, D), BF)),
        ("vz", VMEM((4, 16, D), BF)),
        ("ag", VMEM((N_AG, TOK, D), BF)),
        ("rs", VMEM((N_RS, TOK, D), BF)),
        ("rr", VMEM((N_RS, 3, SH, D), BF)),
        ("m_w", DMA((2, 7))),
        ("m_ws", DMA((7,))),
        ("m_l", DMA((4,))),
        ("m_ags", DMA((2, 3))),
        ("m_agr", DMA((2, 3))),
        ("m_rss", DMA((2, 3))),
        ("m_rsr", DMA((2, 3))),
        ("m_dps", DMA((10,))),
        ("m_kvr", DMA((9,))),
        ("m_dkr", DMA((6,))),
        ("m_vr", DMA((10,))),
        ("m_hs", DMA((2,))),
        ("m_hr", DMA((3,))),
        ("m_g0", DMA((len(BLOCKS), 2))),
        ("f_sae", DMA((2, 4))),
        ("m_o", DMA((2,))),
    ]
    for name, rows in BLOCKS.items():
        out += [
            ("g_" + name, VMEM((2, 2, rows, 384), BF)),
            ("x_" + name, VMEM((2, 2, rows, 384), BF)),
            ("h_" + name, VMEM((2, 2, 2, rows // 8, 384), BF)),
            ("a_" + name, VMEM((2, 3 if name == "sae" else 2, 2, rows // 4, 384), BF)),
            (
                "b_" + name,
                VMEM((2, 4, 2, rows // 4, 384) if name in WHOLE else (2, 3, rows // 8, 384), BF),
            ),
        ]
    for group in sorted(set(GROUP.values())):
        out.append(("s_" + group, DMA((2, 4 if group == GROUP["sae"] else 3))))
        out.append(("r_" + group, DMA((2, 9 if group == GROUP["sae"] else 11))))
    return out


class Refs:
    pass


def ln_forward(r, gain, bias):
    center = r - jnp.mean(r, axis=-1, keepdims=True)
    spread = lax.rsqrt(jnp.mean(center * center, axis=-1, keepdims=True) + EPS)
    n = center * spread
    return n * gain + bias, n, spread


def ln_backward(n, spread, gain, dy):
    s = dy * gain
    dr = spread * (
        s - jnp.mean(s, axis=-1, keepdims=True) - n * jnp.mean(s * n, axis=-1, keepdims=True)
    )
    return dr, jnp.sum(dy * n, axis=0, keepdims=True), jnp.sum(dy, axis=0, keepdims=True)


def kernel(names, n_in, n_out, *refs):
    (x_h, cot_h, dgr, ret, ng_h, nb_h, cg, cb, qkv_h, out_h, win_h, wfo_h, cq_h, ckv_h, co_h) = refs[
        :n_in
    ]
    bo_o, ig_o, of_o, os_o, oc_o, on_o, oe_o = refs[n_in : n_in + n_out]
    R = Refs()
    for name, ref in zip(names, refs[n_in + n_out :]):
        setattr(R, name, ref)
    c = lax.axis_index("section")
    t = lax.axis_index("tensor")
    d = lax.axis_index("dp")
    o = 1 - c
    y = lax.rem(d, 4)
    z = d // 4
    p = y + c * (z - y)
    q = z + c * (y - z)
    sp, sq = 1 + 3 * c, 4 - 3 * c
    rows_t = pl.ds(pl.multiple_of(t * SH, SH), SH)

    def dev_x(k):
        return (c, lax.rem(t + k, 4), d)

    def dp_p(k):
        return lax.rem(p + k, 4) * sp + q * sq

    def dev_p(k):
        return (c, t, dp_p(k))

    def dev_q(k):
        return (c, t, p * sp + lax.rem(q + k, 4) * sq)

    def dev_y(k):
        return (c, t, z * 4 + lax.rem(y + k, 4))

    def dev_z(k):
        return (c, t, lax.rem(z + k, 4) * 4 + y)

    dev_c = (o, t, d)
    sends = {}

    def flush(kind, keep=0):
        queue = sends.get(kind, [])
        while len(queue) > keep:
            queue.pop(0).wait_send()

    def push(src, dst, ss, rs, dev, kind="", wait=True):
        cp = pltpu.make_async_remote_copy(
            src_ref=src, dst_ref=dst, send_sem=ss, recv_sem=rs, device_id=dev, device_id_type=MESH
        )
        cp.start()
        if wait:
            sends.setdefault(kind, []).append(cp)
        return cp

    def landed(dst, rs, dev):
        pltpu.make_async_remote_copy(
            src_ref=dst, dst_ref=dst, send_sem=rs, recv_sem=rs, device_id=dev, device_id_type=MESH
        ).wait_recv()

    def places(s):
        return [
            R.xin.at[s],
            R.wsa.at[s, pl.ds(0, 576)],
            R.wsa.at[s, pl.ds(576, 192)],
            R.nv.at[s, 0],
            R.nv.at[s, 1],
            R.wff.at[s, 0],
            R.wff.at[s, 1],
        ]

    items = [x_h.at[c], qkv_h, out_h, ng_h, nb_h, win_h, wfo_h]
    bar = pltpu.get_barrier_semaphore()
    peers = [dev_c]
    for k in (1, 2, 3):
        for dev in (dev_x(k), dev_y(k), dev_z(k)):
            peers.append(dev)
    for k in (1, 2, 3):
        peers.append((o,) + dev_y(k)[1:])
        peers.append((o,) + dev_z(k)[1:])
    for dev in peers:
        pl.semaphore_signal(bar, inc=1, device_id=dev, device_id_type=MESH)

    def own(i):
        pltpu.make_async_copy(items[i], places(c)[i], R.m_w.at[c, i]).start()

    def other(i):
        src = x_h.at[o] if i == 0 else items[i]
        push(src, places(c)[i], R.m_ws.at[i], R.m_w.at[c, i], dev_c)

    for i in range(5):
        own(i)
    singles = [
        pltpu.make_async_copy(cq_h, R.wcr.at[pl.ds(0, 192)], R.m_l.at[0]),
        pltpu.make_async_copy(co_h, R.wcr.at[pl.ds(192, 192)], R.m_l.at[1]),
        pltpu.make_async_copy(ckv_h, R.wcr.at[pl.ds(384, 384)], R.m_l.at[2]),
        pltpu.make_async_copy(cot_h.at[c], R.cot, R.m_l.at[3]),
    ]
    pl.semaphore_wait(bar, len(peers))
    for i in range(5):
        other(i)
    for i in (5, 6):
        own(i)
        other(i)
    for cp in singles:
        cp.start()

    def need(s, i):
        src = x_h.at[s] if i == 0 else items[i]
        pltpu.make_async_copy(src, places(s)[i], R.m_w.at[s, i]).wait()

    def rs_start(i, value):
        m = int(i in SECOND_RS)
        flush(("rs", m))
        R.rs[i] = value.astype(BF)
        for k in RINGS:
            to = lax.rem(t + k, 4)
            push(
                R.rs.at[i, pl.ds(pl.multiple_of(to * SH, SH), SH)],
                R.rr.at[i, k - 1],
                R.m_rss.at[m, k - 1],
                R.m_rsr.at[m, k - 1],
                dev_x(k),
                ("rs", m),
            )

    def rs_sum(i):
        for k in (1, 3, 2):
            landed(R.rr.at[i, k - 1], R.m_rsr.at[int(i in SECOND_RS), k - 1], dev_x(k))
        total = R.rs[i, rows_t, :].astype(F32)
        for k in range(3):
            total += R.rr[i, k].astype(F32)
        return total

    def ag_start(i, value):
        m = int(i in SECOND_AG)
        flush(("ag", m))
        R.ag[i, rows_t, :] = value.astype(BF)
        for k in RINGS:
            push(
                R.ag.at[i, rows_t],
                R.ag.at[i, rows_t],
                R.m_ags.at[m, k - 1],
                R.m_agr.at[m, k - 1],
                dev_x(k),
                ("ag", m),
            )

    def ag_wait(i):
        for k in (1, 3, 2):
            landed(R.ag.at[i, rows_t], R.m_agr.at[int(i in SECOND_AG), k - 1], dev_x(k))

    def gain_row(s, i):
        return R.nv[s, 0, i : i + 1, :]

    def bias_row(s, i):
        return R.nv[s, 1, i : i + 1, :]

    cross_gain = cg[...].reshape(1, D)
    cross_bias = cb[...].reshape(1, D)

    def softmax(scores):
        tops = [jnp.max(st, axis=0, keepdims=True) for st in scores]
        exps = [jnp.exp(st - top) for st, top in zip(scores, tops)]
        sums = [jnp.sum(e, axis=0, keepdims=True) for e in exps]
        return [e / total for e, total in zip(exps, sums)]

    def attend_backward(qts, kts, vts, prs, dots):
        heads = range(NH)
        dpts = [tn(vts[h], dots[h]) for h in heads]
        dvts = [nt(dots[h], prs[h].astype(BF)) for h in heads]
        sums = [jnp.sum(dpts[h] * prs[h], axis=0, keepdims=True) for h in heads]
        dsts = [(prs[h] * (dpts[h] - sums[h])).astype(BF) for h in heads]
        dqts = [nn(kts[h], dsts[h]) * SCALE for h in heads]
        dkts = [nt(qts[h], dsts[h]) * SCALE for h in heads]
        return dqts, dkts, dvts

    def self_forward(s):
        need(s, 0)
        need(s, 1)
        R.pk[s] = nt(R.wsa[s, 0:576, :], R.xin[s]).astype(BF)
        scores = [
            tn(R.pk[s, QW + lo : QW + lo + 64, :], R.pk[s, lo : lo + 64, :]) * SCALE for lo in HEADS
        ]
        if s == 1:
            key = lax.broadcasted_iota(jnp.int32, (TOK, TOK), 0)
            qry = lax.broadcasted_iota(jnp.int32, (TOK, TOK), 1)
            scores = [jnp.where(key <= qry, st, -1000000000.0) for st in scores]
        probs = softmax(scores)
        for h, lo in enumerate(HEADS):
            vt = R.pk[s, 2 * QW + lo : 2 * QW + lo + 64, :]
            R.ot[s, lo : lo + 64, :] = nn(vt, probs[h].astype(BF)).astype(BF)
            R.pt[s, h] = probs[h]
        need(s, 2)
        rs_start(R_SA + s, tn(R.ot[s], R.wsa[s, 576:768, :]))

    def put_norm(slot, spread):
        R.sp[slot] = jnp.broadcast_to(spread, (SH, 128))

    def get_norm(slot):
        return R.sp[slot, :, 0:1]

    def self_finish(s):
        total = rs_sum(R_SA + s)
        r = R.xin[s, rows_t, :].astype(F32) + total
        need(s, 3)
        need(s, 4)
        out, n, spread = ln_forward(r, gain_row(s, 0), bias_row(s, 0))
        ag_start(A_Y1 + s, out)
        R.y1f[s] = out
        R.n1[s] = n
        put_norm(s, spread)

    def ffn_forward(s, gathered):
        u = nn(R.ag[gathered], R.wff[s, 0])
        cdf = 0.5 * (1.0 + lax.erf(u * 0.7071067811865476))
        R.act[s] = (u * cdf).astype(BF)
        R.hid[...] = u
        R.slope[s] = cdf
        rs_start(R_FF + s, nn(R.act[s], R.wff[s, 1]))
        u = R.hid[...]
        R.slope[s] += u * jnp.exp(-0.5 * u * u) * 0.3989422804014327

    def ffn_backward(s):
        ag_wait(A_DR2 + s)
        dg = nt(R.ag[A_DR2 + s], R.wff[s, 1])
        R.du[s] = (dg * R.slope[s]).astype(BF)
        rs_start(R_DFF + s, nt(R.du[s], R.wff[s, 0]))

    def put(ref, piece, r0, value):
        rows = value.shape[0]
        ref[piece, 0, r0 : r0 + rows, :] = value[:, 0:384].astype(BF)
        ref[piece, 1, r0 : r0 + rows, :] = value[:, 384:768].astype(BF)

    def out_grad(s):
        return tn(R.act[s], R.ag[A_DR2 + s])

    def in_grad(s, gathered):
        return tn(R.ag[gathered], R.du[s])

    def put_halves(ref, value):
        put(ref, 0, 0, value[0:384])
        put(ref, 1, 0, value[384:768])

    def blk(name):
        bufs = tuple(getattr(R, pre + name) for pre in ("g_", "x_", "h_", "a_", "b_"))
        return bufs + (getattr(R, "s_" + GROUP[name]), getattr(R, "r_" + GROUP[name]))

    place = ((y, z), (z, y))
    devs = ((dev_y, dev_z), (dev_z, dev_y))

    def quarter(name, where):
        rows = BLOCKS[name] // 4
        return pl.ds(pl.multiple_of(where * rows, rows), rows)

    def eighth(name, where, half):
        rows = BLOCKS[name] // 8
        return pl.ds(pl.multiple_of(where * 2 * rows + half * rows, rows), rows)

    def step(where, k):
        return lax.rem(where + k, 4)

    def work(name):
        return pl.when(c == WORKER[name])

    def gone(src, sem):
        pltpu.make_async_remote_copy(
            src_ref=src, dst_ref=src, send_sem=sem, recv_sem=sem, device_id=dev_c, device_id_type=MESH
        ).wait_send()

    def ship(src, dst, ss, rs, dev):
        push(src, dst, ss, rs, dev, wait=False)

    def result(name, i, rows, half=slice(None)):
        if name == "crx":
            return oc_o.at[i, half, rows]
        if name == "ffd":
            return of_o.at[i, half, rows]
        if name in ("ffi", "ffo"):
            rows = pl.ds(pl.multiple_of(i * 384 + rows.start, 48), rows.size)
            return of_o.at[int(name == "ffo"), half, rows]
        return os_o.at[i, half, rows]

    def spot(name, i, rows, half=slice(None)):
        return R.x_sae.at[i, half, rows] if name == "sae" else result(name, i, rows, half)

    def g0(name, pieces=(0, 1)):
        g, x = blk(name)[:2]

        @pl.when(c != WORKER[name])
        def _():
            for i in pieces:
                sem = R.m_g0.at[tuple(BLOCKS).index(name), i]
                ship(g.at[i], x.at[i], sem, blk(name)[6].at[i, 0], dev_c)

    def g1(name, pieces=(0, 1)):
        g, x, h, a, b, s, r = blk(name)

        @work(name)
        def _():
            for i in pieces:
                landed(x.at[i], r.at[i, 0], dev_c)
                g[i] = g[i] + x[i]
                if name == "sae":
                    for k in RINGS:
                        part = g.at[i, :, quarter(name, step(place[i][0], k))]
                        ship(part, a.at[i, k - 1], s.at[i, k - 1], r.at[i, k], devs[i][0](k))
                    continue
                far = step(place[i][0], 2)
                for j, k in ((0, 1), (1, 3)):
                    part = g.at[i, :, eighth(name, far, j)]
                    ship(part, h.at[i, j], s.at[i, j], r.at[i, 1 + j], devs[i][0](k))

    def g1b(name, pieces=(0, 1)):
        g, x, h, a, b, s, r = blk(name)

        @work(name)
        def _():
            for j, k in ((0, 1), (1, 3)):
                for i in pieces:
                    near = step(place[i][0], k)
                    landed(h.at[i, j], r.at[i, 1 + j], dev_c)
                    part = eighth(name, near, j)
                    g[i, :, part, :] = g[i, :, part, :] + h[i, j]
                    part = g.at[i, :, quarter(name, near)]
                    gone(h.at[i, j], s.at[i, j])
                    ship(part, a.at[i, j], s.at[i, j], r.at[i, 3 + j], devs[i][0](k))

    def sub(name, i, where):
        return eighth(name, place[i][0], where // 2), lax.rem(where, 2)

    def g2(name, pieces=(0, 1)):
        g, x, h, a, b, s, r = blk(name)

        @work(name)
        def _():
            for i in pieces:
                mine = quarter(name, place[i][0])
                total = g[i, :, mine, :].astype(F32)
                for j in range(a.shape[1]):
                    landed(a.at[i, j], r.at[i, j + (1 if name == "sae" else 3)], dev_c)
                    total += a[i, j].astype(F32)
                    gone(a.at[i, j], s.at[i, j])
                g[i, :, mine, :] = total.astype(BF)
                if name in WHOLE:
                    part = g.at[i, :, mine]
                    for k in RINGS:
                        dst = b.at[i, place[i][1]]
                        ship(part, dst, s.at[i, k - 1], r.at[i, 4 + k], devs[i][1](k))
                    continue
                for k in RINGS:
                    rows, half = sub(name, i, step(place[i][1], k))
                    part = g.at[i, half, rows]
                    ship(part, b.at[i, k - 1], s.at[i, k - 1], r.at[i, 4 + k], devs[i][1](k))

    def g3(name, pieces=(0, 1)):
        g, x, h, a, b, s, r = blk(name)

        @work(name)
        def _():
            for i in pieces:
                if name in WHOLE:
                    mine = quarter(name, place[i][0])
                    b[i, place[i][1]] = g[i, :, mine, :]
                    for k in (1, 3, 2):
                        landed(a.at[i, 0], r.at[i, 4 + k], dev_c)
                        gone(a.at[i, 0], s.at[i, k - 1])
                    total = b[i, 0].astype(F32)
                    for j in (1, 2, 3):
                        total += b[i, j].astype(F32)
                    spot(name, i, mine)[...] = total.astype(BF)
                    continue
                for k in (1, 3, 2):
                    landed(b.at[i, k - 1], r.at[i, 4 + k], dev_c)
                rows, half = sub(name, i, place[i][1])
                total = g[i, half, rows, :].astype(F32)
                for k in range(3):
                    total += b[i, k].astype(F32)
                part = spot(name, i, rows, half)
                part[...] = total.astype(BF)
                for k in RINGS:
                    gone(b.at[i, k - 1], s.at[i, k - 1])
                    ship(part, part, s.at[i, k - 1], r.at[i, (3, 4, 8)[k - 1]], devs[i][1](k))

    def g4(name, pieces=(0, 1)):
        g, x, h, a, b, s, r = blk(name)

        @work(name)
        def _():
            for i in pieces:
                mine = quarter(name, place[i][0])
                part = spot(name, i, mine)
                for k in () if name in WHOLE else (1, 3, 2):
                    landed(b.at[i, k - 1], r.at[i, (3, 4, 8)[k - 1]], dev_c)
                    gone(b.at[i, k - 1], s.at[i, k - 1])
                if name == "sae":
                    dst = result(name, i, mine)
                    for k in RINGS:
                        to = (OWNER[name],) + devs[i][0](k)[1:]
                        ship(part, dst, s.at[i, k - 1], R.f_sae.at[i, k], to)
                    ship(part, dst, s.at[i, 3], R.f_sae.at[i, 0], dev_c)
                    continue
                for j, k in ((0, 1), (1, 3)):
                    ship(part, part, s.at[i, j], r.at[i, 2 - j], devs[i][0](k))

    def g4b(name, pieces=(0, 1)):
        g, x, h, a, b, s, r = blk(name)

        @work(name)
        def _():
            for j, k in ((0, 1), (1, 3)):
                for i in pieces:
                    behind = step(place[i][0], 4 - k)
                    landed(a.at[i, j], r.at[i, 2 - j], dev_c)
                    gone(a.at[i, j], s.at[i, j])
                    rows = eighth(name, behind, j)
                    part = spot(name, i, rows)
                    ship(part, part, s.at[i, j], r.at[i, 9 + j], devs[i][0](k))

    def g5(name):
        g, x, h, a, b, s, r = blk(name)

        @work(name)
        def _():
            for i in (0, 1):
                for j in (0, 1):
                    landed(h.at[i, j], r.at[i, 9 + j], dev_c)
            if name == "crx":
                ship(oc_o, oc_o, s.at[0, 2], R.m_hr.at[2], dev_c)

    def g6(name):
        g, x, h, a, b, s, r = blk(name)

        @pl.when(c != WORKER[name])
        def _():
            for i in (0, 1):
                gone(g.at[i], R.m_g0.at[tuple(BLOCKS).index(name), i])
            if name == "crx":
                landed(oc_o, R.m_hr.at[2], dev_c)
            if name == "sae":
                for i in (0, 1):
                    for j in range(4):
                        landed(a.at[i, 0], R.f_sae.at[i, j], dev_c)

        @work(name)
        def _():
            for i in (0, 1):
                if name == "sae":
                    for j in range(4):
                        gone(a.at[i, 0], s.at[i, j])
                    continue
                for j in (0, 1):
                    gone(h.at[i, j], s.at[i, j])
            if name == "crx":
                gone(oc_o, s.at[0, 2])

    def vec_put(row, dg, db, step=2):
        R.vec[row : row + 1, :] = dg
        R.vec[row + step : row + step + 1, :] = db

    def vec_send(buf, at, value, base, dev, count):
        buf[at] = value.astype(BF)
        for k in range(1, count):
            push(buf.at[at], buf.at[at], R.m_dps.at[base + k - 1], R.m_vr.at[base + k - 1], dev(k))

    def vec_sum(buf, at, base, dev, count):
        for k in range(1, count):
            landed(buf.at[at], R.m_vr.at[base + k - 1], dev(k))
        total = buf[0].astype(F32)
        for k in range(1, count):
            total += buf[k].astype(F32)
        return total

    def dev_c1(k):
        return dev_c

    for j in (10, 11, 12, 13, 14, 15):
        R.vec[j : j + 1, :] = jnp.zeros((1, D), F32)

    micro = lax.broadcasted_iota(jnp.int32, (2, 16), 0)
    group = lax.broadcasted_iota(jnp.int32, (2, 16), 1)
    live = (micro == c) & (group <= d) & (dgr[...] > 0)
    first = jnp.max(jnp.where(live, group, 0), axis=1, keepdims=True)
    first = jnp.max(first, axis=0, keepdims=True)
    rows = jnp.where(c == 0, ret[0], ret[1]) + first * TOK
    g_at = rows // TOK
    b_at = jnp.where(c == 0, g_at, lax.rem(g_at, 4) * 4 + g_at // 4)
    at = b_at * TOK + lax.rem(rows, TOK)
    R.pos[0] = jnp.broadcast_to(at, (8, KEYS))
    for k in RINGS:
        push(R.pos.at[0], R.pos.at[k], R.m_dps.at[5 + k], R.m_kvr.at[5 + k], dev_q(k))
    self_forward(0)
    self_finish(0)
    ag_wait(A_Y1)
    need(0, 5)
    need(0, 6)
    ffn_forward(0, A_Y1)

    for cp in singles:
        cp.wait()
    for k in (1, 3, 2):
        landed(R.pos.at[k], R.m_kvr.at[5 + k], dev_q(k))

    def build(i, carry):
        n = lax.broadcasted_iota(jnp.int32, (TOK, KEYS), 0) + (q * 4 + i) * TOK
        rows = pl.ds(pl.multiple_of(i * TOK, TOK), TOK)
        for k in range(4):
            R.hot[k, rows, :] = jnp.where(n == R.pos[k, 0:1, :], 1.0, 0.0).astype(BF)
        return carry

    lax.fori_loop(0, 4, build, 0)

    out, n, spread = ln_forward(R.y1f[0] + rs_sum(R_FF), gain_row(0, 1), bias_row(0, 1))
    ag_start(A_BO, out)
    R.n2[0] = n
    put_norm(2, spread)
    ag_wait(A_BO)
    R.kvt[p] = nt(R.wcr[384:768, :], R.ag[A_BO]).astype(BF)

    for k in RINGS:
        push(R.kvt.at[p], R.kvt.at[p], R.m_dps.at[k - 1], R.m_kvr.at[k - 1], dev_p(k))

    def picked(k, j):
        return nn(R.kvt[j], R.hot[k, pl.ds(pl.multiple_of(j * TOK, TOK), TOK), :])

    self_forward(1)
    for k in range(4):
        R.kvf[k] = picked(k, p)
    for j in (1, 3):
        landed(R.kvt.at[p], R.m_kvr.at[j - 1], dev_p(j))
        for k in range(4):
            R.kvf[k] += picked(k, lax.rem(p + 4 - j, 4))
    landed(R.kvt.at[p], R.m_kvr.at[1], dev_p(2))
    for k in RINGS + (0,):
        R.kvs[k] = (R.kvf[k] + picked(k, lax.rem(p + 2, 4))).astype(BF)
        if k:
            push(
                R.kvs.at[k], R.kvr.at[3 - k], R.m_dps.at[6 - k], R.m_kvr.at[6 - k], dev_q(4 - k)
            )
    self_finish(1)
    ag_wait(A_Y1 + 1)
    R.qct[...] = nt(R.wcr[0:192, :], R.ag[A_Y1 + 1]).astype(BF)
    for k in (1, 3, 2):
        landed(R.kvr.at[k - 1], R.m_kvr.at[2 + k], dev_q(k))

    total = R.kvs[0].astype(F32)
    for k in range(3):
        total += R.kvr[k].astype(F32)
    R.kvct[...] = total.astype(BF)
    probs = softmax(
        [tn(R.kvct[lo : lo + 64, :], R.qct[lo : lo + 64, :]) * SCALE for lo in HEADS]
    )
    for h, lo in enumerate(HEADS):
        vt = R.kvct[QW + lo : QW + lo + 64, :]
        R.oct[lo : lo + 64, :] = nn(vt, probs[h].astype(BF)).astype(BF)
        R.ptc[h] = probs[h]
    rs_start(R_CR, tn(R.oct[...], R.wcr[192:384, :]))
    need(1, 5)
    need(1, 6)
    out, n, spread = ln_forward(R.y1f[1] + rs_sum(R_CR), cross_gain, cross_bias)
    ag_start(A_Y2, out)
    R.y2f[...] = out
    R.nc[...] = n
    put_norm(4, spread)
    ag_wait(A_Y2)
    ffn_forward(1, A_Y2)
    out, n, spread = ln_forward(R.y2f[...] + rs_sum(R_FF + 1), gain_row(1, 1), bias_row(1, 1))

    dr, dg, db = ln_backward(n, spread, gain_row(1, 1), R.cot[rows_t, :].astype(F32))
    ag_start(A_DR2 + 1, dr)
    R.dres[1] = dr
    vec_put(5, dg, db)
    ffn_backward(1)
    ag_start(A_BO + 1, out)
    flush("")
    put(R.g_ffd, 0, 0, in_grad(1, A_Y2))
    put(R.g_ffd, 1, 0, out_grad(1))
    g0("ffd")
    dy = R.dres[1] + rs_sum(R_DFF + 1)
    dr, dg, db = ln_backward(R.nc[...], get_norm(4), cross_gain, dy)
    ag_start(A_DRC, dr)
    R.dres[1] = dr
    vec_put(8, dg, db, 1)
    g1("ffd")
    ag_wait(A_DRC)

    doc = nt(R.wcr[192:384, :], R.ag[A_DRC]).astype(BF)
    dqts, dkts, dvts = attend_backward(
        [R.qct[lo : lo + 64, :] for lo in HEADS],
        [R.kvct[lo : lo + 64, :] for lo in HEADS],
        [R.kvct[QW + lo : QW + lo + 64, :] for lo in HEADS],
        [R.ptc[h] for h in range(NH)],
        [doc[lo : lo + 64, :] for lo in HEADS],
    )
    for h, lo in enumerate(HEADS):
        R.dkvct[lo : lo + 64, :] = dkts[h].astype(BF)
        R.dkvct[QW + lo : QW + lo + 64, :] = dvts[h].astype(BF)
        R.dqct[lo : lo + 64, :] = dqts[h].astype(BF)

    for k in RINGS:
        push(R.dkvct, R.dkr.at[k - 1], R.m_dps.at[k - 1], R.m_dkr.at[k - 1], dev_q(k))
    rs_start(R_DQ, tn(R.dqct[...], R.wcr[0:192, :]))
    put(R.g_crx, 0, 0, nn(R.dqct[...], R.ag[A_Y1 + 1]))
    put(R.g_crx, 0, 192, nn(R.oct[...], R.ag[A_DRC]))
    g0("crx", (0,))
    dy = R.dres[1] + rs_sum(R_DQ)
    dr, dg, db = ln_backward(R.n1[1], get_norm(1), gain_row(1, 0), dy)
    ag_start(A_DR1 + 1, dr)
    R.dres[1] = dr
    vec_put(4, dg, db)

    def self_backward(s):
        ag_wait(A_DR1 + s)
        dot = nt(R.wsa[s, 576:768, :], R.ag[A_DR1 + s]).astype(BF)
        dqts, dkts, dvts = attend_backward(
            [R.pk[s, lo : lo + 64, :] for lo in HEADS],
            [R.pk[s, QW + lo : QW + lo + 64, :] for lo in HEADS],
            [R.pk[s, 2 * QW + lo : 2 * QW + lo + 64, :] for lo in HEADS],
            [R.pt[s, h] for h in range(NH)],
            [dot[lo : lo + 64, :] for lo in HEADS],
        )
        for h, lo in enumerate(HEADS):
            R.dpk[s, lo : lo + 64, :] = dqts[h].astype(BF)
            R.dpk[s, QW + lo : QW + lo + 64, :] = dkts[h].astype(BF)
            R.dpk[s, 2 * QW + lo : 2 * QW + lo + 64, :] = dvts[h].astype(BF)

    def self_grads(s, name):
        ref = getattr(R, "g_" + name)
        put(ref, 0, 0, nn(R.dpk[s, 0:384, :], R.xin[s]))
        g0(name, (0,))
        put(ref, 1, 0, nn(R.dpk[s, 384:576, :], R.xin[s]))
        put(ref, 1, 192, nn(R.ot[s], R.ag[A_DR1 + s]))
        g0(name, (1,))

    def input_part(s):
        rs_start(R_DSA + s, tn(R.dpk[s], R.wsa[s, 0:576, :]))

    for j in range(4):
        R.dkf[j] = nt(R.dkvct[...], R.hot[0, j * TOK : (j + 1) * TOK, :])
    for k in (1, 3):
        landed(R.dkr.at[k - 1], R.m_dkr.at[k - 1], dev_q(k))
        for j in range(4):
            R.dkf[j] += nt(R.dkr[k - 1], R.hot[k, j * TOK : (j + 1) * TOK, :])
    landed(R.dkr.at[1], R.m_dkr.at[1], dev_q(2))
    for k in RINGS + (0,):
        to = lax.rem(p + k, 4)
        hot = R.hot[2, pl.ds(pl.multiple_of(to * TOK, TOK), TOK), :]
        R.dks[to] = (R.dkf[to] + nt(R.dkr[1], hot)).astype(BF)
        if k:
            push(R.dks.at[to], R.dk2.at[k - 1], R.m_dps.at[2 + k], R.m_dkr.at[2 + k], dev_p(k))
    g1b("ffd")
    self_backward(1)
    input_part(1)
    self_grads(1, "sad")
    g1("crx", (0,))
    for k in (1, 3, 2):
        landed(R.dk2.at[k - 1], R.m_dkr.at[2 + k], dev_p(k))
    total = R.dks[p].astype(F32)
    for k in range(3):
        total += R.dk2[k].astype(F32)
    R.dkv[...] = total.astype(BF)
    rs_start(R_DST, tn(R.dkv[...], R.wcr[384:768, :]))
    put(R.g_crx, 1, 0, nn(R.dkv[...], R.ag[A_BO]))
    g0("crx", (1,))
    g2("ffd")
    g1("sad")
    g1b("crx", (0,))
    dy = rs_sum(R_DST)
    dr, dg, db = ln_backward(R.n2[0], get_norm(2), gain_row(0, 1), dy)
    ag_start(A_DR2, dr)
    R.dres[0] = dr
    vec_put(1, dg, db)
    flush("")
    ag_wait(A_BO + 1)
    push(R.ag.at[A_BO + o], bo_o.at[c], R.m_hs.at[0], R.m_hr.at[0], dev_c)
    outs = [pltpu.make_async_copy(R.ag.at[A_BO + c], bo_o.at[c], R.m_o.at[0])]
    outs[0].start()
    g3("ffd")
    g1("crx", (1,))
    g1b("sad")
    g2("crx", (0,))
    ffn_backward(0)
    put_halves(R.g_ffo, out_grad(0))
    g0("ffo")
    put_halves(R.g_ffi, in_grad(0, A_Y1))
    g0("ffi")
    g4("ffd")
    g1b("crx", (1,))
    g3("crx", (0,))
    g2("sad")
    g1("ffo")
    dy = R.dres[0] + rs_sum(R_DFF)
    dr, dg, db = ln_backward(R.n1[0], get_norm(0), gain_row(0, 0), dy)
    ag_start(A_DR1, dr)
    R.dres[0] = dr
    vec_put(0, dg, db)
    g1("ffi")
    g2("crx", (1,))
    g4b("ffd")
    g4("crx", (0,))
    g3("sad")
    g1b("ffo")
    self_backward(0)
    g1b("ffi")
    self_grads(0, "sae")
    vec_send(R.vx, t, R.vec[...], 0, dev_x, 4)
    input_part(0)
    ag_start(A_IG + 1, R.dres[1] + rs_sum(R_DSA + 1))
    g1("sae")
    g2("ffo")
    total = vec_sum(R.vx, t, 0, dev_x, 4)
    vec_send(R.vc, c, total, 3, dev_c1, 2)
    g3("crx", (1,))
    g4b("crx", (0,))
    g4("sad")
    g2("ffi")
    total = vec_sum(R.vc, c, 3, dev_c1, 2)
    vec_send(R.vy, y, total, 4, dev_y, 4)
    ag_start(A_IG, R.dres[0] + rs_sum(R_DSA))
    g3("ffo")
    g2("sae")
    g4("crx", (1,))
    g4b("sad")
    g3("ffi")
    total = vec_sum(R.vy, y, 4, dev_y, 4)
    vec_send(R.vz, z, total, 7, dev_z, 4)
    g4("ffo")
    g4b("crx", (1,))
    g3("sae")
    g4("sae")
    g5("crx")
    g4("ffi")
    ag_wait(A_IG)
    ag_wait(A_IG + 1)
    push(R.ag.at[A_IG + o], ig_o.at[c], R.m_hs.at[1], R.m_hr.at[1], dev_c)
    outs.append(pltpu.make_async_copy(R.ag.at[A_IG + c], ig_o.at[c], R.m_o.at[1]))
    outs[1].start()
    g4b("ffo")
    total = vec_sum(R.vz, z, 7, dev_z, 4)
    on_o[...] = jnp.where(c == 0, total[0:4, :], total[4:8, :])
    oe_o[...] = total[8:10, :]
    flush("")
    g4b("ffi")
    landed(bo_o.at[c], R.m_hr.at[0], dev_c)
    landed(ig_o.at[c], R.m_hr.at[1], dev_c)
    for cp in outs:
        cp.wait()
    g5("ffd")
    g5("sad")
    g5("ffo")
    g5("ffi")
    for name in ("ffd", "sad", "crx", "ffo", "ffi", "sae"):
        g6(name)
    for kind in list(sends):
        flush(kind)


JOBS = (
    [("gf", 0, r, "win", r) for r in (0, 192, 384, 576)]
    + [("gf", 1, r, "wfo", r) for r in (0, 192, 384, 576)]
    + [("gc", 0, 0, "q", 0), ("gc", 0, 192, "co", 0), ("gc", 1, 0, "kv", 0), ("gc", 1, 192, "kv", 192)]
    + [("gs", 0, 0, "qkv", 0), ("gs", 0, 192, "qkv", 192), ("gs", 1, 0, "qkv", 384)]
    + [("gs", 1, 192, "out", 0)]
)


def widen(*refs):
    bo, ig, gf, gs, gc, gn, ge = refs[:7]
    bo_o, ig_o, qkv_o, out_o, win_o, wfo_o, ng_o, nb_o, q_o, kv_o, co_o, cg_o, cb_o = refs[7:20]
    wide, ig_wide, m_out, m_x = refs[20:]
    from_ = {"gf": gf, "gs": gs, "gc": gc}
    to = {"qkv": qkv_o, "out": out_o, "win": win_o, "wfo": wfo_o, "q": q_o, "kv": kv_o, "co": co_o}
    stores = [pltpu.make_async_copy(bo, bo_o, m_x.at[0])]
    stores[0].start()
    for i, (src, piece, r0, dst, d0) in enumerate(JOBS):
        wide[i, :, 0:384] = from_[src][piece, 0, r0 : r0 + 192, :].astype(F32)
        wide[i, :, 384:768] = from_[src][piece, 1, r0 : r0 + 192, :].astype(F32)
        cp = pltpu.make_async_copy(wide.at[i], to[dst].at[pl.ds(d0, 192)], m_out.at[i])
        cp.start()
        stores.append(cp)
    ig_wide[...] = ig[...].astype(F32)
    stores.append(pltpu.make_async_copy(ig_wide, ig_o, m_x.at[1]))
    stores[-1].start()
    ng_o[...] = gn[0:2, :]
    nb_o[...] = gn[2:4, :]
    cg_o[...] = ge[0:1, :].reshape(D)
    cb_o[...] = ge[1:2, :].reshape(D)
    for cp in stores:
        cp.wait()


def body(
    layer_inputs,
    cotangent,
    doc_groups,
    retrieved_at,
    sa_qkv,
    sa_out,
    ffn_in,
    ffn_out,
    norm_gain,
    norm_bias,
    cross_q,
    cross_kv,
    cross_out,
    cross_gain,
    cross_bias,
):
    ins = (
        layer_inputs[0],
        cotangent,
        doc_groups,
        retrieved_at,
        norm_gain[0],
        norm_bias[0],
        cross_gain,
        cross_bias,
        jnp.transpose(sa_qkv[0], (1, 2, 0)).reshape(576, D),
        sa_out[0],
        ffn_in[0],
        ffn_out[0],
        jnp.transpose(cross_q, (1, 0)),
        jnp.transpose(cross_kv, (1, 2, 0)).reshape(384, D),
        cross_out,
    )
    hbm = pl.BlockSpec(memory_space=pl.ANY)
    vm = pl.BlockSpec(memory_space=VMEM)
    outs = (
        VMEM((2, TOK, D), BF),
        VMEM((2, TOK, D), BF),
        VMEM((2, 2, 768, 384), BF),
        VMEM((2, 2, 384, 384), BF),
        VMEM((2, 2, 384, 384), BF),
        VMEM((4, D), F32),
        VMEM((2, D), F32),
    )
    names = [n for n, _ in scratch_list()]

    def run(*refs):
        kernel(names, len(ins), len(outs), *refs)

    results = pl.pallas_call(
        run,
        out_shape=outs,
        in_specs=[hbm, hbm, vm, vm, hbm, hbm, vm, vm] + [hbm] * 7,
        out_specs=[vm] * len(outs),
        scratch_shapes=[s for _, s in scratch_list()],
        compiler_params=pltpu.CompilerParams(
            collective_id=0, has_side_effects=True, vmem_limit_bytes=52 << 20
        ),
        name="layers",
    )(*ins)
    wide_outs = (
        jax.ShapeDtypeStruct((2, TOK, D), BF),
        jax.ShapeDtypeStruct((2, TOK, D), F32),
        jax.ShapeDtypeStruct((576, D), F32),
        jax.ShapeDtypeStruct((192, D), F32),
        jax.ShapeDtypeStruct((768, D), F32),
        jax.ShapeDtypeStruct((768, D), F32),
        jax.ShapeDtypeStruct((2, D), F32),
        jax.ShapeDtypeStruct((2, D), F32),
        jax.ShapeDtypeStruct((192, D), F32),
        jax.ShapeDtypeStruct((384, D), F32),
        jax.ShapeDtypeStruct((192, D), F32),
        jax.ShapeDtypeStruct((D,), F32),
        jax.ShapeDtypeStruct((D,), F32),
    )
    bo, ig, d_qkv, d_out, d_in, d_fo, ng, nb, d_q, d_kv, d_co, dcg, dcb = pl.pallas_call(
        widen,
        out_shape=wide_outs,
        in_specs=[vm] * 7,
        out_specs=[hbm] * 6 + [vm] * 2 + [hbm] * 3 + [vm] * 2,
        scratch_shapes=[
            VMEM((len(JOBS), 192, D), F32),
            VMEM((2, TOK, D), F32),
            DMA((len(JOBS),)),
            DMA((2,)),
        ],
        compiler_params=pltpu.CompilerParams(vmem_limit_bytes=32 << 20),
        name="widen",
    )(*[pltpu.with_memory_space_constraint(r, VMEM) for r in results])
    return (
        bo[None],
        ig[None],
        jnp.transpose(d_qkv.reshape(3, 192, D), (2, 0, 1))[None],
        d_out[None],
        d_in[None],
        d_fo[None],
        ng[None],
        nb[None],
        jnp.transpose(d_q, (1, 0)),
        jnp.transpose(d_kv.reshape(2, 192, D), (2, 0, 1)),
        d_co,
        dcg,
        dcb,
    )


def solution(mesh):
    placed = (
        P("section", None, "dp", None),
        P(None, "dp", None),
        P(),
        P(None, "dp", None),
        P("section", None, None, "tensor"),
        P("section", "tensor", None),
        P("section", None, "tensor"),
        P("section", "tensor", None),
        P("section", None, None),
        P("section", None, None),
        P(None, "tensor"),
        P(None, None, "tensor"),
        P("tensor", None),
        P(),
        P(),
    )
    return jax.shard_map(
        body,
        mesh=mesh,
        in_specs=placed,
        out_specs=(
            P("section", None, "dp", None),
            P("section", None, "dp", None),
            P("section", None, None, "tensor"),
            P("section", "tensor", None),
            P("section", None, "tensor"),
            P("section", "tensor", None),
            P("section", None, None),
            P("section", None, None),
            P(None, "tensor"),
            P(None, None, "tensor"),
            P("tensor", None),
            P(),
            P(),
        ),
        check_vma=False,
    )
```

```python
import jax
import jax.numpy as jnp
from jax import lax
from jax.experimental import pallas as pl
from jax.experimental.pallas import tpu as pltpu
from jax.sharding import PartitionSpec as P

BF = jnp.bfloat16
F32 = jnp.float32
MESH = pl.DeviceIdType.MESH
VMEM = pltpu.VMEM
DMA = pltpu.SemaphoreType.DMA

HEAD = 64
NH = 3
EPS = 1e-05
HEADS = (0, 64, 128)
SCALE = HEAD**-0.5
TOK = 128
D = 768
SH = 32
KEYS = 256
QW = NH * HEAD
RINGS = (2, 1, 3)

A_BO, A_IG, A_Y1, A_Y2, A_DR2, A_DRC, A_DR1 = 0, 2, 4, 6, 7, 9, 10
N_AG = 12
R_SA, R_FF, R_CR, R_DFF, R_DQ, R_DSA, R_DST = 0, 2, 4, 5, 7, 8, 10
N_RS = 11
BLOCKS = {"ffd": 768, "ffo": 384, "ffi": 384, "crx": 384, "sad": 384, "sae": 384}
WORKER = {"ffd": 1, "crx": 1, "sad": 1, "ffo": 0, "ffi": 0, "sae": 1}
OWNER = {"ffd": 1, "sad": 1, "ffo": 0, "ffi": 0, "sae": 0}
WHOLE = ()
GROUP = {"ffd": "a", "crx": "b", "ffo": "b", "sad": "c", "ffi": "c", "sae": "d"}
SECOND_RS = (R_SA + 1, R_DSA + 1)
SECOND_AG = (A_BO + 1, A_IG + 1, A_Y1 + 1)


def nn(a, b):
    return jnp.dot(a, b, preferred_element_type=F32)


def nt(a, b):
    return lax.dot_general(a, b, (((1,), (1,)), ((), ())), preferred_element_type=F32)


def tn(a, b):
    return lax.dot_general(a, b, (((0,), (0,)), ((), ())), preferred_element_type=F32)


def scratch_list():
    out = [
        ("xin", VMEM((2, TOK, D), BF)),
        ("nv", VMEM((2, 2, 2, D), F32)),
        ("wsa", VMEM((2, 768, D), BF)),
        ("wff", VMEM((2, 2, 768, D), BF)),
        ("wcr", VMEM((768, D), BF)),
        ("cot", VMEM((TOK, D), BF)),
        ("pk", VMEM((2, 3 * QW, TOK), BF)),
        ("pt", VMEM((2, NH, TOK, TOK), F32)),
        ("ot", VMEM((2, QW, TOK), BF)),
        ("n1", VMEM((2, SH, D), F32)),
        ("n2", VMEM((2, SH, D), F32)),
        ("nc", VMEM((SH, D), F32)),
        ("sp", VMEM((5, SH, 128), F32)),
        ("y1f", VMEM((2, SH, D), F32)),
        ("y2f", VMEM((SH, D), F32)),
        ("dres", VMEM((2, SH, D), F32)),
        ("act", VMEM((2, TOK, D), BF)),
        ("slope", VMEM((2, TOK, D), F32)),
        ("hid", VMEM((TOK, D), F32)),
        ("du", VMEM((2, TOK, D), BF)),
        ("dpk", VMEM((2, 3 * QW, TOK), BF)),
        ("qct", VMEM((QW, TOK), BF)),
        ("dqct", VMEM((QW, TOK), BF)),
        ("kvct", VMEM((2 * QW, KEYS), BF)),
        ("dkvct", VMEM((2 * QW, KEYS), BF)),
        ("ptc", VMEM((NH, KEYS, TOK), F32)),
        ("oct", VMEM((QW, TOK), BF)),
        ("pos", VMEM((4, 8, KEYS), jnp.int32)),
        ("hot", VMEM((4, 4 * TOK, KEYS), BF)),
        ("kvt", VMEM((4, 2 * QW, TOK), BF)),
        ("kvf", VMEM((4, 2 * QW, KEYS), F32)),
        ("kvs", VMEM((4, 2 * QW, KEYS), BF)),
        ("kvr", VMEM((3, 2 * QW, KEYS), BF)),
        ("dkr", VMEM((3, 2 * QW, KEYS), BF)),
        ("dkf", VMEM((4, 2 * QW, TOK), F32)),
        ("dks", VMEM((4, 2 * QW, TOK), BF)),
        ("dk2", VMEM((3, 2 * QW, TOK), BF)),
        ("dkv", VMEM((2 * QW, TOK), BF)),
        ("vec", VMEM((16, D), F32)),
        ("vx", VMEM((4, 16, D), BF)),
        ("vc", VMEM((2, 16, D), BF)),
        ("vy", VMEM((4, 16, D), BF)),
        ("vz", VMEM((4, 16, D), BF)),
        ("ag", VMEM((N_AG, TOK, D), BF)),
        ("rs", VMEM((N_RS, TOK, D), BF)),
        ("rr", VMEM((N_RS, 3, SH, D), BF)),
        ("m_w", DMA((2, 7))),
        ("m_ws", DMA((7,))),
        ("m_l", DMA((4,))),
        ("m_ags", DMA((2, 3))),
        ("m_agr", DMA((2, 3))),
        ("m_rss", DMA((2, 3))),
        ("m_rsr", DMA((2, 3))),
        ("m_dps", DMA((10,))),
        ("m_kvr", DMA((9,))),
        ("m_dkr", DMA((6,))),
        ("m_vr", DMA((10,))),
        ("m_hs", DMA((2,))),
        ("m_hr", DMA((3,))),
        ("m_g0", DMA((len(BLOCKS), 2))),
        ("f_sae", DMA((2, 4))),
        ("m_o", DMA((2,))),
    ]
    for name, rows in BLOCKS.items():
        out += [
            ("g_" + name, VMEM((2, 2, rows, 384), BF)),
            ("x_" + name, VMEM((2, 2, rows, 384), BF)),
            ("h_" + name, VMEM((2, 2, 2, rows // 8, 384), BF)),
            ("a_" + name, VMEM((2, 3 if name == "sae" else 2, 2, rows // 4, 384), BF)),
            (
                "b_" + name,
                VMEM((2, 4, 2, rows // 4, 384) if name in WHOLE else (2, 3, rows // 8, 384), BF),
            ),
        ]
    for group in sorted(set(GROUP.values())):
        out.append(("s_" + group, DMA((2, 4 if group == GROUP["sae"] else 3))))
        out.append(("r_" + group, DMA((2, 9 if group == GROUP["sae"] else 11))))
    return out


class Refs:
    pass


def ln_forward(r, gain, bias):
    center = r - jnp.mean(r, axis=-1, keepdims=True)
    spread = lax.rsqrt(jnp.mean(center * center, axis=-1, keepdims=True) + EPS)
    n = center * spread
    return n * gain + bias, n, spread


def ln_backward(n, spread, gain, dy):
    s = dy * gain
    dr = spread * (
        s - jnp.mean(s, axis=-1, keepdims=True) - n * jnp.mean(s * n, axis=-1, keepdims=True)
    )
    return dr, jnp.sum(dy * n, axis=0, keepdims=True), jnp.sum(dy, axis=0, keepdims=True)


def kernel(names, n_in, n_out, *refs):
    (x_h, cot_h, dgr, ret, ng_h, nb_h, cg, cb, qkv_h, out_h, win_h, wfo_h, cq_h, ckv_h, co_h) = refs[
        :n_in
    ]
    bo_o, ig_o, of_o, os_o, oc_o, on_o, oe_o = refs[n_in : n_in + n_out]
    R = Refs()
    for name, ref in zip(names, refs[n_in + n_out :]):
        setattr(R, name, ref)
    c = lax.axis_index("section")
    t = lax.axis_index("tensor")
    d = lax.axis_index("dp")
    o = 1 - c
    y = lax.rem(d, 4)
    z = d // 4
    p = y + c * (z - y)
    q = z + c * (y - z)
    sp, sq = 1 + 3 * c, 4 - 3 * c
    rows_t = pl.ds(pl.multiple_of(t * SH, SH), SH)

    def dev_x(k):
        return (c, lax.rem(t + k, 4), d)

    def dp_p(k):
        return lax.rem(p + k, 4) * sp + q * sq

    def dev_p(k):
        return (c, t, dp_p(k))

    def dev_q(k):
        return (c, t, p * sp + lax.rem(q + k, 4) * sq)

    def dev_y(k):
        return (c, t, z * 4 + lax.rem(y + k, 4))

    def dev_z(k):
        return (c, t, lax.rem(z + k, 4) * 4 + y)

    dev_c = (o, t, d)
    sends = {}

    def flush(kind, keep=0):
        queue = sends.get(kind, [])
        while len(queue) > keep:
            queue.pop(0).wait_send()

    def push(src, dst, ss, rs, dev, kind="", wait=True):
        cp = pltpu.make_async_remote_copy(
            src_ref=src, dst_ref=dst, send_sem=ss, recv_sem=rs, device_id=dev, device_id_type=MESH
        )
        cp.start()
        if wait:
            sends.setdefault(kind, []).append(cp)
        return cp

    def landed(dst, rs, dev):
        pltpu.make_async_remote_copy(
            src_ref=dst, dst_ref=dst, send_sem=rs, recv_sem=rs, device_id=dev, device_id_type=MESH
        ).wait_recv()

    def places(s):
        return [
            R.xin.at[s],
            R.wsa.at[s, pl.ds(0, 576)],
            R.wsa.at[s, pl.ds(576, 192)],
            R.nv.at[s, 0],
            R.nv.at[s, 1],
            R.wff.at[s, 0],
            R.wff.at[s, 1],
        ]

    items = [x_h.at[c], qkv_h, out_h, ng_h, nb_h, win_h, wfo_h]
    bar = pltpu.get_barrier_semaphore()
    peers = [dev_c]
    for k in (1, 2, 3):
        for dev in (dev_x(k), dev_y(k), dev_z(k)):
            peers.append(dev)
    for k in (1, 2, 3):
        peers.append((o,) + dev_y(k)[1:])
        peers.append((o,) + dev_z(k)[1:])
    for dev in peers:
        pl.semaphore_signal(bar, inc=1, device_id=dev, device_id_type=MESH)

    def own(i):
        pltpu.make_async_copy(items[i], places(c)[i], R.m_w.at[c, i]).start()

    def other(i):
        src = x_h.at[o] if i == 0 else items[i]
        push(src, places(c)[i], R.m_ws.at[i], R.m_w.at[c, i], dev_c)

    for i in range(5):
        own(i)
    singles = [
        pltpu.make_async_copy(cq_h, R.wcr.at[pl.ds(0, 192)], R.m_l.at[0]),
        pltpu.make_async_copy(co_h, R.wcr.at[pl.ds(192, 192)], R.m_l.at[1]),
        pltpu.make_async_copy(ckv_h, R.wcr.at[pl.ds(384, 384)], R.m_l.at[2]),
        pltpu.make_async_copy(cot_h.at[c], R.cot, R.m_l.at[3]),
    ]
    def enter():
        pl.semaphore_wait(bar, len(peers))
        for i in range(3):
            other(i)

    def rest():
        for i in (3, 4):
            other(i)
        for i in (5, 6):
            own(i)
            other(i)
        for cp in singles:
            cp.start()

    def need(s, i):
        src = x_h.at[s] if i == 0 else items[i]
        pltpu.make_async_copy(src, places(s)[i], R.m_w.at[s, i]).wait()

    def rs_start(i, value):
        m = int(i in SECOND_RS)
        flush(("rs", m))
        R.rs[i] = value.astype(BF)
        for k in RINGS:
            to = lax.rem(t + k, 4)
            push(
                R.rs.at[i, pl.ds(pl.multiple_of(to * SH, SH), SH)],
                R.rr.at[i, k - 1],
                R.m_rss.at[m, k - 1],
                R.m_rsr.at[m, k - 1],
                dev_x(k),
                ("rs", m),
            )

    def rs_sum(i):
        for k in (1, 3, 2):
            landed(R.rr.at[i, k - 1], R.m_rsr.at[int(i in SECOND_RS), k - 1], dev_x(k))
        total = R.rs[i, rows_t, :].astype(F32)
        for k in range(3):
            total += R.rr[i, k].astype(F32)
        return total

    def ag_start(i, value):
        m = int(i in SECOND_AG)
        flush(("ag", m))
        R.ag[i, rows_t, :] = value.astype(BF)
        for k in RINGS:
            push(
                R.ag.at[i, rows_t],
                R.ag.at[i, rows_t],
                R.m_ags.at[m, k - 1],
                R.m_agr.at[m, k - 1],
                dev_x(k),
                ("ag", m),
            )

    def ag_wait(i):
        for k in (1, 3, 2):
            landed(R.ag.at[i, rows_t], R.m_agr.at[int(i in SECOND_AG), k - 1], dev_x(k))

    def gain_row(s, i):
        return R.nv[s, 0, i : i + 1, :]

    def bias_row(s, i):
        return R.nv[s, 1, i : i + 1, :]

    cross_gain = cg[...].reshape(1, D)
    cross_bias = cb[...].reshape(1, D)

    def softmax(scores):
        tops = [jnp.max(st, axis=0, keepdims=True) for st in scores]
        exps = [jnp.exp(st - top) for st, top in zip(scores, tops)]
        sums = [jnp.sum(e, axis=0, keepdims=True) for e in exps]
        return [e / total for e, total in zip(exps, sums)]

    def attend_backward(qts, kts, vts, prs, dots):
        heads = range(NH)
        dpts = [tn(vts[h], dots[h]) for h in heads]
        dvts = [nt(dots[h], prs[h].astype(BF)) for h in heads]
        sums = [jnp.sum(dpts[h] * prs[h], axis=0, keepdims=True) for h in heads]
        dsts = [(prs[h] * (dpts[h] - sums[h])).astype(BF) for h in heads]
        dqts = [nn(kts[h], dsts[h]) * SCALE for h in heads]
        dkts = [nt(qts[h], dsts[h]) * SCALE for h in heads]
        return dqts, dkts, dvts

    def self_forward(s):
        need(s, 0)
        need(s, 1)
        R.pk[s] = nt(R.wsa[s, 0:576, :], R.xin[s]).astype(BF)
        scores = [
            tn(R.pk[s, QW + lo : QW + lo + 64, :], R.pk[s, lo : lo + 64, :]) * SCALE for lo in HEADS
        ]
        if s == 1:
            key = lax.broadcasted_iota(jnp.int32, (TOK, TOK), 0)
            qry = lax.broadcasted_iota(jnp.int32, (TOK, TOK), 1)
            scores = [jnp.where(key <= qry, st, -1000000000.0) for st in scores]
        probs = softmax(scores)
        for h, lo in enumerate(HEADS):
            vt = R.pk[s, 2 * QW + lo : 2 * QW + lo + 64, :]
            R.ot[s, lo : lo + 64, :] = nn(vt, probs[h].astype(BF)).astype(BF)
            R.pt[s, h] = probs[h]
        need(s, 2)
        value = tn(R.ot[s], R.wsa[s, 576:768, :])
        if s == 0:
            enter()
        rs_start(R_SA + s, value)

    def put_norm(slot, spread):
        R.sp[slot] = jnp.broadcast_to(spread, (SH, 128))

    def get_norm(slot):
        return R.sp[slot, :, 0:1]

    def self_finish(s):
        total = rs_sum(R_SA + s)
        r = R.xin[s, rows_t, :].astype(F32) + total
        need(s, 3)
        need(s, 4)
        out, n, spread = ln_forward(r, gain_row(s, 0), bias_row(s, 0))
        ag_start(A_Y1 + s, out)
        R.y1f[s] = out
        R.n1[s] = n
        put_norm(s, spread)

    def ffn_forward(s, gathered):
        u = nn(R.ag[gathered], R.wff[s, 0])
        cdf = 0.5 * (1.0 + lax.erf(u * 0.7071067811865476))
        R.act[s] = (u * cdf).astype(BF)
        R.hid[...] = u
        R.slope[s] = cdf
        rs_start(R_FF + s, nn(R.act[s], R.wff[s, 1]))
        u = R.hid[...]
        R.slope[s] += u * jnp.exp(-0.5 * u * u) * 0.3989422804014327

    def ffn_backward(s):
        ag_wait(A_DR2 + s)
        dg = nt(R.ag[A_DR2 + s], R.wff[s, 1])
        R.du[s] = (dg * R.slope[s]).astype(BF)
        rs_start(R_DFF + s, nt(R.du[s], R.wff[s, 0]))

    def put(ref, piece, r0, value):
        rows = value.shape[0]
        ref[piece, 0, r0 : r0 + rows, :] = value[:, 0:384].astype(BF)
        ref[piece, 1, r0 : r0 + rows, :] = value[:, 384:768].astype(BF)

    def out_grad(s):
        return tn(R.act[s], R.ag[A_DR2 + s])

    def in_grad(s, gathered):
        return tn(R.ag[gathered], R.du[s])

    def put_halves(ref, value):
        put(ref, 0, 0, value[0:384])
        put(ref, 1, 0, value[384:768])

    def blk(name):
        bufs = tuple(getattr(R, pre + name) for pre in ("g_", "x_", "h_", "a_", "b_"))
        return bufs + (getattr(R, "s_" + GROUP[name]), getattr(R, "r_" + GROUP[name]))

    place = ((y, z), (z, y))
    devs = ((dev_y, dev_z), (dev_z, dev_y))

    def quarter(name, where):
        rows = BLOCKS[name] // 4
        return pl.ds(pl.multiple_of(where * rows, rows), rows)

    def eighth(name, where, half):
        rows = BLOCKS[name] // 8
        return pl.ds(pl.multiple_of(where * 2 * rows + half * rows, rows), rows)

    def step(where, k):
        return lax.rem(where + k, 4)

    def work(name):
        return pl.when(c == WORKER[name])

    def gone(src, sem):
        pltpu.make_async_remote_copy(
            src_ref=src, dst_ref=src, send_sem=sem, recv_sem=sem, device_id=dev_c, device_id_type=MESH
        ).wait_send()

    def ship(src, dst, ss, rs, dev):
        push(src, dst, ss, rs, dev, wait=False)

    def result(name, i, rows, half=slice(None)):
        if name == "crx":
            return oc_o.at[i, half, rows]
        if name == "ffd":
            return of_o.at[i, half, rows]
        if name in ("ffi", "ffo"):
            rows = pl.ds(pl.multiple_of(i * 384 + rows.start, 48), rows.size)
            return of_o.at[int(name == "ffo"), half, rows]
        return os_o.at[i, half, rows]

    def spot(name, i, rows, half=slice(None)):
        return R.x_sae.at[i, half, rows] if name == "sae" else result(name, i, rows, half)

    def g0(name, pieces=(0, 1)):
        g, x = blk(name)[:2]

        @pl.when(c != WORKER[name])
        def _():
            for i in pieces:
                sem = R.m_g0.at[tuple(BLOCKS).index(name), i]
                ship(g.at[i], x.at[i], sem, blk(name)[6].at[i, 0], dev_c)

    def g1(name, pieces=(0, 1)):
        g, x, h, a, b, s, r = blk(name)

        @work(name)
        def _():
            for i in pieces:
                landed(x.at[i], r.at[i, 0], dev_c)
                g[i] = g[i] + x[i]
                if name == "sae":
                    for k in RINGS:
                        part = g.at[i, :, quarter(name, step(place[i][0], k))]
                        ship(part, a.at[i, k - 1], s.at[i, k - 1], r.at[i, k], devs[i][0](k))
                    continue
                far = step(place[i][0], 2)
                for j, k in ((0, 1), (1, 3)):
                    part = g.at[i, :, eighth(name, far, j)]
                    ship(part, h.at[i, j], s.at[i, j], r.at[i, 1 + j], devs[i][0](k))

    def g1b(name, pieces=(0, 1)):
        g, x, h, a, b, s, r = blk(name)

        @work(name)
        def _():
            for j, k in ((0, 1), (1, 3)):
                for i in pieces:
                    near = step(place[i][0], k)
                    landed(h.at[i, j], r.at[i, 1 + j], dev_c)
                    part = eighth(name, near, j)
                    g[i, :, part, :] = g[i, :, part, :] + h[i, j]
                    part = g.at[i, :, quarter(name, near)]
                    gone(h.at[i, j], s.at[i, j])
                    ship(part, a.at[i, j], s.at[i, j], r.at[i, 3 + j], devs[i][0](k))

    def sub(name, i, where):
        return eighth(name, place[i][0], where // 2), lax.rem(where, 2)

    def g2(name, pieces=(0, 1)):
        g, x, h, a, b, s, r = blk(name)

        @work(name)
        def _():
            for i in pieces:
                mine = quarter(name, place[i][0])
                total = g[i, :, mine, :].astype(F32)
                for j in range(a.shape[1]):
                    landed(a.at[i, j], r.at[i, j + (1 if name == "sae" else 3)], dev_c)
                    total += a[i, j].astype(F32)
                    gone(a.at[i, j], s.at[i, j])
                g[i, :, mine, :] = total.astype(BF)
                if name in WHOLE:
                    part = g.at[i, :, mine]
                    for k in RINGS:
                        dst = b.at[i, place[i][1]]
                        ship(part, dst, s.at[i, k - 1], r.at[i, 4 + k], devs[i][1](k))
                    continue
                for k in RINGS:
                    rows, half = sub(name, i, step(place[i][1], k))
                    part = g.at[i, half, rows]
                    ship(part, b.at[i, k - 1], s.at[i, k - 1], r.at[i, 4 + k], devs[i][1](k))

    def g3(name, pieces=(0, 1)):
        g, x, h, a, b, s, r = blk(name)

        @work(name)
        def _():
            for i in pieces:
                if name in WHOLE:
                    mine = quarter(name, place[i][0])
                    b[i, place[i][1]] = g[i, :, mine, :]
                    for k in (1, 3, 2):
                        landed(a.at[i, 0], r.at[i, 4 + k], dev_c)
                        gone(a.at[i, 0], s.at[i, k - 1])
                    total = b[i, 0].astype(F32)
                    for j in (1, 2, 3):
                        total += b[i, j].astype(F32)
                    spot(name, i, mine)[...] = total.astype(BF)
                    continue
                for k in (1, 3, 2):
                    landed(b.at[i, k - 1], r.at[i, 4 + k], dev_c)
                rows, half = sub(name, i, place[i][1])
                total = g[i, half, rows, :].astype(F32)
                for k in range(3):
                    total += b[i, k].astype(F32)
                part = spot(name, i, rows, half)
                part[...] = total.astype(BF)
                for k in RINGS:
                    gone(b.at[i, k - 1], s.at[i, k - 1])
                    ship(part, part, s.at[i, k - 1], r.at[i, (3, 4, 8)[k - 1]], devs[i][1](k))

    def g4(name, pieces=(0, 1)):
        g, x, h, a, b, s, r = blk(name)

        @work(name)
        def _():
            for i in pieces:
                mine = quarter(name, place[i][0])
                part = spot(name, i, mine)
                for k in () if name in WHOLE else (1, 3, 2):
                    landed(b.at[i, k - 1], r.at[i, (3, 4, 8)[k - 1]], dev_c)
                    gone(b.at[i, k - 1], s.at[i, k - 1])
                if name == "sae":
                    dst = result(name, i, mine)
                    for k in RINGS:
                        to = (OWNER[name],) + devs[i][0](k)[1:]
                        ship(part, dst, s.at[i, k - 1], R.f_sae.at[i, k], to)
                    ship(part, dst, s.at[i, 3], R.f_sae.at[i, 0], dev_c)
                    continue
                for j, k in ((0, 1), (1, 3)):
                    ship(part, part, s.at[i, j], r.at[i, 2 - j], devs[i][0](k))

    def g4b(name, pieces=(0, 1)):
        g, x, h, a, b, s, r = blk(name)

        @work(name)
        def _():
            for j, k in ((0, 1), (1, 3)):
                for i in pieces:
                    behind = step(place[i][0], 4 - k)
                    landed(a.at[i, j], r.at[i, 2 - j], dev_c)
                    gone(a.at[i, j], s.at[i, j])
                    rows = eighth(name, behind, j)
                    part = spot(name, i, rows)
                    ship(part, part, s.at[i, j], r.at[i, 9 + j], devs[i][0](k))

    def g5(name):
        g, x, h, a, b, s, r = blk(name)

        @work(name)
        def _():
            for i in (0, 1):
                for j in (0, 1):
                    landed(h.at[i, j], r.at[i, 9 + j], dev_c)
            if name == "crx":
                ship(oc_o, oc_o, s.at[0, 2], R.m_hr.at[2], dev_c)

    def g6(name):
        g, x, h, a, b, s, r = blk(name)

        @pl.when(c != WORKER[name])
        def _():
            for i in (0, 1):
                gone(g.at[i], R.m_g0.at[tuple(BLOCKS).index(name), i])
            if name == "crx":
                landed(oc_o, R.m_hr.at[2], dev_c)
            if name == "sae":
                for i in (0, 1):
                    for j in range(4):
                        landed(a.at[i, 0], R.f_sae.at[i, j], dev_c)

        @work(name)
        def _():
            for i in (0, 1):
                if name == "sae":
                    for j in range(4):
                        gone(a.at[i, 0], s.at[i, j])
                    continue
                for j in (0, 1):
                    gone(h.at[i, j], s.at[i, j])
            if name == "crx":
                gone(oc_o, s.at[0, 2])

    def vec_put(row, dg, db, step=2):
        R.vec[row : row + 1, :] = dg
        R.vec[row + step : row + step + 1, :] = db

    def vec_send(buf, at, value, base, dev, count):
        buf[at] = value.astype(BF)
        for k in range(1, count):
            push(buf.at[at], buf.at[at], R.m_dps.at[base + k - 1], R.m_vr.at[base + k - 1], dev(k))

    def vec_sum(buf, at, base, dev, count):
        for k in range(1, count):
            landed(buf.at[at], R.m_vr.at[base + k - 1], dev(k))
        total = buf[0].astype(F32)
        for k in range(1, count):
            total += buf[k].astype(F32)
        return total

    def dev_c1(k):
        return dev_c

    self_forward(0)
    rest()
    for j in (10, 11, 12, 13, 14, 15):
        R.vec[j : j + 1, :] = jnp.zeros((1, D), F32)

    micro = lax.broadcasted_iota(jnp.int32, (2, 16), 0)
    group = lax.broadcasted_iota(jnp.int32, (2, 16), 1)
    live = (micro == c) & (group <= d) & (dgr[...] > 0)
    first = jnp.max(jnp.where(live, group, 0), axis=1, keepdims=True)
    first = jnp.max(first, axis=0, keepdims=True)
    rows = jnp.where(c == 0, ret[0], ret[1]) + first * TOK
    g_at = rows // TOK
    b_at = jnp.where(c == 0, g_at, lax.rem(g_at, 4) * 4 + g_at // 4)
    at = b_at * TOK + lax.rem(rows, TOK)
    R.pos[0] = jnp.broadcast_to(at, (8, KEYS))
    for k in RINGS:
        push(R.pos.at[0], R.pos.at[k], R.m_dps.at[5 + k], R.m_kvr.at[5 + k], dev_q(k))
    self_finish(0)
    ag_wait(A_Y1)
    need(0, 5)
    need(0, 6)
    ffn_forward(0, A_Y1)

    for cp in singles:
        cp.wait()
    for k in (1, 3, 2):
        landed(R.pos.at[k], R.m_kvr.at[5 + k], dev_q(k))

    def build(i, carry):
        n = lax.broadcasted_iota(jnp.int32, (TOK, KEYS), 0) + (q * 4 + i) * TOK
        rows = pl.ds(pl.multiple_of(i * TOK, TOK), TOK)
        for k in range(4):
            R.hot[k, rows, :] = jnp.where(n == R.pos[k, 0:1, :], 1.0, 0.0).astype(BF)
        return carry

    lax.fori_loop(0, 4, build, 0)

    out, n, spread = ln_forward(R.y1f[0] + rs_sum(R_FF), gain_row(0, 1), bias_row(0, 1))
    ag_start(A_BO, out)
    R.n2[0] = n
    put_norm(2, spread)
    ag_wait(A_BO)
    R.kvt[p] = nt(R.wcr[384:768, :], R.ag[A_BO]).astype(BF)

    for k in RINGS:
        push(R.kvt.at[p], R.kvt.at[p], R.m_dps.at[k - 1], R.m_kvr.at[k - 1], dev_p(k))

    def picked(k, j):
        return nn(R.kvt[j], R.hot[k, pl.ds(pl.multiple_of(j * TOK, TOK), TOK), :])

    self_forward(1)
    for k in range(4):
        R.kvf[k] = picked(k, p)
    for j in (1, 3):
        landed(R.kvt.at[p], R.m_kvr.at[j - 1], dev_p(j))
        for k in range(4):
            R.kvf[k] += picked(k, lax.rem(p + 4 - j, 4))
    landed(R.kvt.at[p], R.m_kvr.at[1], dev_p(2))
    for k in RINGS + (0,):
        R.kvs[k] = (R.kvf[k] + picked(k, lax.rem(p + 2, 4))).astype(BF)
        if k:
            push(
                R.kvs.at[k], R.kvr.at[3 - k], R.m_dps.at[6 - k], R.m_kvr.at[6 - k], dev_q(4 - k)
            )
    self_finish(1)
    ag_wait(A_Y1 + 1)
    R.qct[...] = nt(R.wcr[0:192, :], R.ag[A_Y1 + 1]).astype(BF)
    for k in (1, 3, 2):
        landed(R.kvr.at[k - 1], R.m_kvr.at[2 + k], dev_q(k))

    total = R.kvs[0].astype(F32)
    for k in range(3):
        total += R.kvr[k].astype(F32)
    R.kvct[...] = total.astype(BF)
    probs = softmax(
        [tn(R.kvct[lo : lo + 64, :], R.qct[lo : lo + 64, :]) * SCALE for lo in HEADS]
    )
    for h, lo in enumerate(HEADS):
        vt = R.kvct[QW + lo : QW + lo + 64, :]
        R.oct[lo : lo + 64, :] = nn(vt, probs[h].astype(BF)).astype(BF)
        R.ptc[h] = probs[h]
    rs_start(R_CR, tn(R.oct[...], R.wcr[192:384, :]))
    need(1, 5)
    need(1, 6)
    out, n, spread = ln_forward(R.y1f[1] + rs_sum(R_CR), cross_gain, cross_bias)
    ag_start(A_Y2, out)
    R.y2f[...] = out
    R.nc[...] = n
    put_norm(4, spread)
    ag_wait(A_Y2)
    ffn_forward(1, A_Y2)
    out, n, spread = ln_forward(R.y2f[...] + rs_sum(R_FF + 1), gain_row(1, 1), bias_row(1, 1))

    dr, dg, db = ln_backward(n, spread, gain_row(1, 1), R.cot[rows_t, :].astype(F32))
    ag_start(A_DR2 + 1, dr)
    R.dres[1] = dr
    vec_put(5, dg, db)
    ffn_backward(1)
    ag_start(A_BO + 1, out)
    flush("")
    put(R.g_ffd, 0, 0, in_grad(1, A_Y2))
    put(R.g_ffd, 1, 0, out_grad(1))
    g0("ffd")
    dy = R.dres[1] + rs_sum(R_DFF + 1)
    dr, dg, db = ln_backward(R.nc[...], get_norm(4), cross_gain, dy)
    ag_start(A_DRC, dr)
    R.dres[1] = dr
    vec_put(8, dg, db, 1)
    g1("ffd")
    ag_wait(A_DRC)

    doc = nt(R.wcr[192:384, :], R.ag[A_DRC]).astype(BF)
    dqts, dkts, dvts = attend_backward(
        [R.qct[lo : lo + 64, :] for lo in HEADS],
        [R.kvct[lo : lo + 64, :] for lo in HEADS],
        [R.kvct[QW + lo : QW + lo + 64, :] for lo in HEADS],
        [R.ptc[h] for h in range(NH)],
        [doc[lo : lo + 64, :] for lo in HEADS],
    )
    for h, lo in enumerate(HEADS):
        R.dkvct[lo : lo + 64, :] = dkts[h].astype(BF)
        R.dkvct[QW + lo : QW + lo + 64, :] = dvts[h].astype(BF)
        R.dqct[lo : lo + 64, :] = dqts[h].astype(BF)

    for k in RINGS:
        push(R.dkvct, R.dkr.at[k - 1], R.m_dps.at[k - 1], R.m_dkr.at[k - 1], dev_q(k))
    rs_start(R_DQ, tn(R.dqct[...], R.wcr[0:192, :]))
    put(R.g_crx, 0, 0, nn(R.dqct[...], R.ag[A_Y1 + 1]))
    put(R.g_crx, 0, 192, nn(R.oct[...], R.ag[A_DRC]))
    g0("crx", (0,))
    dy = R.dres[1] + rs_sum(R_DQ)
    dr, dg, db = ln_backward(R.n1[1], get_norm(1), gain_row(1, 0), dy)
    ag_start(A_DR1 + 1, dr)
    R.dres[1] = dr
    vec_put(4, dg, db)
    g1b("ffd", (0,))

    def self_backward(s):
        ag_wait(A_DR1 + s)
        dot = nt(R.wsa[s, 576:768, :], R.ag[A_DR1 + s]).astype(BF)
        dqts, dkts, dvts = attend_backward(
            [R.pk[s, lo : lo + 64, :] for lo in HEADS],
            [R.pk[s, QW + lo : QW + lo + 64, :] for lo in HEADS],
            [R.pk[s, 2 * QW + lo : 2 * QW + lo + 64, :] for lo in HEADS],
            [R.pt[s, h] for h in range(NH)],
            [dot[lo : lo + 64, :] for lo in HEADS],
        )
        for h, lo in enumerate(HEADS):
            R.dpk[s, lo : lo + 64, :] = dqts[h].astype(BF)
            R.dpk[s, QW + lo : QW + lo + 64, :] = dkts[h].astype(BF)
            R.dpk[s, 2 * QW + lo : 2 * QW + lo + 64, :] = dvts[h].astype(BF)

    def self_grads(s, name):
        ref = getattr(R, "g_" + name)
        put(ref, 0, 0, nn(R.dpk[s, 0:384, :], R.xin[s]))
        g0(name, (0,))
        put(ref, 1, 0, nn(R.dpk[s, 384:576, :], R.xin[s]))
        put(ref, 1, 192, nn(R.ot[s], R.ag[A_DR1 + s]))
        g0(name, (1,))

    def input_part(s):
        rs_start(R_DSA + s, tn(R.dpk[s], R.wsa[s, 0:576, :]))

    for j in range(4):
        R.dkf[j] = nt(R.dkvct[...], R.hot[0, j * TOK : (j + 1) * TOK, :])
    for k in (1, 3):
        landed(R.dkr.at[k - 1], R.m_dkr.at[k - 1], dev_q(k))
        for j in range(4):
            R.dkf[j] += nt(R.dkr[k - 1], R.hot[k, j * TOK : (j + 1) * TOK, :])
    landed(R.dkr.at[1], R.m_dkr.at[1], dev_q(2))
    for k in RINGS + (0,):
        to = lax.rem(p + k, 4)
        hot = R.hot[2, pl.ds(pl.multiple_of(to * TOK, TOK), TOK), :]
        R.dks[to] = (R.dkf[to] + nt(R.dkr[1], hot)).astype(BF)
        if k:
            push(R.dks.at[to], R.dk2.at[k - 1], R.m_dps.at[2 + k], R.m_dkr.at[2 + k], dev_p(k))
    g1b("ffd", (1,))
    self_backward(1)
    input_part(1)
    self_grads(1, "sad")
    g1("crx", (0,))
    for k in (1, 3, 2):
        landed(R.dk2.at[k - 1], R.m_dkr.at[2 + k], dev_p(k))
    total = R.dks[p].astype(F32)
    for k in range(3):
        total += R.dk2[k].astype(F32)
    R.dkv[...] = total.astype(BF)
    rs_start(R_DST, tn(R.dkv[...], R.wcr[384:768, :]))
    put(R.g_crx, 1, 0, nn(R.dkv[...], R.ag[A_BO]))
    g0("crx", (1,))
    g2("ffd")
    g1("sad")
    g1b("crx", (0,))
    dy = rs_sum(R_DST)
    dr, dg, db = ln_backward(R.n2[0], get_norm(2), gain_row(0, 1), dy)
    ag_start(A_DR2, dr)
    R.dres[0] = dr
    vec_put(1, dg, db)
    flush("")
    ag_wait(A_BO + 1)
    push(R.ag.at[A_BO + o], bo_o.at[c], R.m_hs.at[0], R.m_hr.at[0], dev_c)
    outs = [pltpu.make_async_copy(R.ag.at[A_BO + c], bo_o.at[c], R.m_o.at[0])]
    outs[0].start()
    g3("ffd")
    g1("crx", (1,))
    g1b("sad")
    g2("crx", (0,))
    ffn_backward(0)
    put_halves(R.g_ffo, out_grad(0))
    g0("ffo")
    put_halves(R.g_ffi, in_grad(0, A_Y1))
    g0("ffi")
    g4("ffd")
    g1b("crx", (1,))
    g3("crx", (0,))
    g2("sad")
    g1("ffo")
    dy = R.dres[0] + rs_sum(R_DFF)
    dr, dg, db = ln_backward(R.n1[0], get_norm(0), gain_row(0, 0), dy)
    ag_start(A_DR1, dr)
    R.dres[0] = dr
    vec_put(0, dg, db)
    g1("ffi")
    g4b("ffd")
    g4("crx", (0,))
    g2("crx", (1,))
    g3("sad")
    g1b("ffo")
    self_backward(0)
    g1b("ffi")
    self_grads(0, "sae")
    vec_send(R.vx, t, R.vec[...], 0, dev_x, 4)
    input_part(0)
    ag_start(A_IG + 1, R.dres[1] + rs_sum(R_DSA + 1))
    g1("sae")
    g2("ffo")
    total = vec_sum(R.vx, t, 0, dev_x, 4)
    vec_send(R.vc, c, total, 3, dev_c1, 2)
    g3("crx", (1,))
    g4b("crx", (0,))
    g4("sad")
    g2("ffi")
    total = vec_sum(R.vc, c, 3, dev_c1, 2)
    vec_send(R.vy, y, total, 4, dev_y, 4)
    ag_start(A_IG, R.dres[0] + rs_sum(R_DSA))
    g3("ffo")
    g2("sae")
    g4("crx", (1,))
    g4b("sad")
    g3("ffi")
    total = vec_sum(R.vy, y, 4, dev_y, 4)
    vec_send(R.vz, z, total, 7, dev_z, 4)
    g4("ffo")
    g3("sae")
    g4b("crx", (1,))
    g4("ffi")
    g4("sae")
    g5("crx")
    ag_wait(A_IG)
    ag_wait(A_IG + 1)
    push(R.ag.at[A_IG + o], ig_o.at[c], R.m_hs.at[1], R.m_hr.at[1], dev_c)
    outs.append(pltpu.make_async_copy(R.ag.at[A_IG + c], ig_o.at[c], R.m_o.at[1]))
    outs[1].start()
    g4b("ffo")
    total = vec_sum(R.vz, z, 7, dev_z, 4)
    on_o[...] = jnp.where(c == 0, total[0:4, :], total[4:8, :])
    oe_o[...] = total[8:10, :]
    flush("")
    g4b("ffi")
    landed(bo_o.at[c], R.m_hr.at[0], dev_c)
    landed(ig_o.at[c], R.m_hr.at[1], dev_c)
    for cp in outs:
        cp.wait()
    g5("ffd")
    g5("sad")
    g5("ffo")
    g5("ffi")
    for name in ("ffd", "sad", "crx", "ffo", "ffi", "sae"):
        g6(name)
    for kind in list(sends):
        flush(kind)


JOBS = (
    [("gf", 0, r, "win", r) for r in (0, 192, 384, 576)]
    + [("gf", 1, r, "wfo", r) for r in (0, 192, 384, 576)]
    + [("gc", 0, 0, "q", 0), ("gc", 0, 192, "co", 0), ("gc", 1, 0, "kv", 0), ("gc", 1, 192, "kv", 192)]
    + [("gs", 0, 0, "qkv", 0), ("gs", 0, 192, "qkv", 192), ("gs", 1, 0, "qkv", 384)]
    + [("gs", 1, 192, "out", 0)]
)


def widen(*refs):
    bo, ig, gf, gs, gc, gn, ge = refs[:7]
    bo_o, ig_o, qkv_o, out_o, win_o, wfo_o, ng_o, nb_o, q_o, kv_o, co_o, cg_o, cb_o = refs[7:20]
    wide, ig_wide, m_out, m_x = refs[20:]
    from_ = {"gf": gf, "gs": gs, "gc": gc}
    to = {"qkv": qkv_o, "out": out_o, "win": win_o, "wfo": wfo_o, "q": q_o, "kv": kv_o, "co": co_o}
    stores = [pltpu.make_async_copy(bo, bo_o, m_x.at[0])]
    stores[0].start()
    for i, (src, piece, r0, dst, d0) in enumerate(JOBS):
        wide[i, :, 0:384] = from_[src][piece, 0, r0 : r0 + 192, :].astype(F32)
        wide[i, :, 384:768] = from_[src][piece, 1, r0 : r0 + 192, :].astype(F32)
        cp = pltpu.make_async_copy(wide.at[i], to[dst].at[pl.ds(d0, 192)], m_out.at[i])
        cp.start()
        stores.append(cp)
    ig_wide[...] = ig[...].astype(F32)
    stores.append(pltpu.make_async_copy(ig_wide, ig_o, m_x.at[1]))
    stores[-1].start()
    ng_o[...] = gn[0:2, :]
    nb_o[...] = gn[2:4, :]
    cg_o[...] = ge[0:1, :].reshape(D)
    cb_o[...] = ge[1:2, :].reshape(D)
    for cp in stores:
        cp.wait()


def body(
    layer_inputs,
    cotangent,
    doc_groups,
    retrieved_at,
    sa_qkv,
    sa_out,
    ffn_in,
    ffn_out,
    norm_gain,
    norm_bias,
    cross_q,
    cross_kv,
    cross_out,
    cross_gain,
    cross_bias,
):
    ins = (
        layer_inputs[0],
        cotangent,
        doc_groups,
        retrieved_at,
        norm_gain[0],
        norm_bias[0],
        cross_gain,
        cross_bias,
        jnp.transpose(sa_qkv[0], (1, 2, 0)).reshape(576, D),
        sa_out[0],
        ffn_in[0],
        ffn_out[0],
        jnp.transpose(cross_q, (1, 0)),
        jnp.transpose(cross_kv, (1, 2, 0)).reshape(384, D),
        cross_out,
    )
    hbm = pl.BlockSpec(memory_space=pl.ANY)
    vm = pl.BlockSpec(memory_space=VMEM)
    outs = (
        VMEM((2, TOK, D), BF),
        VMEM((2, TOK, D), BF),
        VMEM((2, 2, 768, 384), BF),
        VMEM((2, 2, 384, 384), BF),
        VMEM((2, 2, 384, 384), BF),
        VMEM((4, D), F32),
        VMEM((2, D), F32),
    )
    names = [n for n, _ in scratch_list()]

    def run(*refs):
        kernel(names, len(ins), len(outs), *refs)

    results = pl.pallas_call(
        run,
        out_shape=outs,
        in_specs=[hbm, hbm, vm, vm, hbm, hbm, vm, vm] + [hbm] * 7,
        out_specs=[vm] * len(outs),
        scratch_shapes=[s for _, s in scratch_list()],
        compiler_params=pltpu.CompilerParams(
            collective_id=0, has_side_effects=True, vmem_limit_bytes=52 << 20
        ),
        name="layers",
    )(*ins)
    wide_outs = (
        jax.ShapeDtypeStruct((2, TOK, D), BF),
        jax.ShapeDtypeStruct((2, TOK, D), F32),
        jax.ShapeDtypeStruct((576, D), F32),
        jax.ShapeDtypeStruct((192, D), F32),
        jax.ShapeDtypeStruct((768, D), F32),
        jax.ShapeDtypeStruct((768, D), F32),
        jax.ShapeDtypeStruct((2, D), F32),
        jax.ShapeDtypeStruct((2, D), F32),
        jax.ShapeDtypeStruct((192, D), F32),
        jax.ShapeDtypeStruct((384, D), F32),
        jax.ShapeDtypeStruct((192, D), F32),
        jax.ShapeDtypeStruct((D,), F32),
        jax.ShapeDtypeStruct((D,), F32),
    )
    bo, ig, d_qkv, d_out, d_in, d_fo, ng, nb, d_q, d_kv, d_co, dcg, dcb = pl.pallas_call(
        widen,
        out_shape=wide_outs,
        in_specs=[vm] * 7,
        out_specs=[hbm] * 6 + [vm] * 2 + [hbm] * 3 + [vm] * 2,
        scratch_shapes=[
            VMEM((len(JOBS), 192, D), F32),
            VMEM((2, TOK, D), F32),
            DMA((len(JOBS),)),
            DMA((2,)),
        ],
        compiler_params=pltpu.CompilerParams(vmem_limit_bytes=32 << 20),
        name="widen",
    )(*[pltpu.with_memory_space_constraint(r, VMEM) for r in results])
    return (
        bo[None],
        ig[None],
        jnp.transpose(d_qkv.reshape(3, 192, D), (2, 0, 1))[None],
        d_out[None],
        d_in[None],
        d_fo[None],
        ng[None],
        nb[None],
        jnp.transpose(d_q, (1, 0)),
        jnp.transpose(d_kv.reshape(2, 192, D), (2, 0, 1)),
        d_co,
        dcg,
        dcb,
    )


def solution(mesh):
    placed = (
        P("section", None, "dp", None),
        P(None, "dp", None),
        P(),
        P(None, "dp", None),
        P("section", None, None, "tensor"),
        P("section", "tensor", None),
        P("section", None, "tensor"),
        P("section", "tensor", None),
        P("section", None, None),
        P("section", None, None),
        P(None, "tensor"),
        P(None, None, "tensor"),
        P("tensor", None),
        P(),
        P(),
    )
    return jax.shard_map(
        body,
        mesh=mesh,
        in_specs=placed,
        out_specs=(
            P("section", None, "dp", None),
            P("section", None, "dp", None),
            P("section", None, None, "tensor"),
            P("section", "tensor", None),
            P("section", None, "tensor"),
            P("section", "tensor", None),
            P("section", None, None),
            P("section", None, None),
            P(None, "tensor"),
            P(None, None, "tensor"),
            P("tensor", None),
            P(),
            P(),
        ),
        check_vma=False,
    )
```

```python
import jax
import jax.numpy as jnp
from jax import lax
from jax.experimental import pallas as pl
from jax.experimental.pallas import tpu as pltpu
from jax.sharding import PartitionSpec as P

BF = jnp.bfloat16
F32 = jnp.float32
MESH = pl.DeviceIdType.MESH
VMEM = pltpu.VMEM
DMA = pltpu.SemaphoreType.DMA

HEAD = 64
NH = 3
EPS = 1e-05
HEADS = (0, 64, 128)
SCALE = HEAD**-0.5
TOK = 128
D = 768
SH = 32
KEYS = 256
QW = NH * HEAD
RINGS = (2, 1, 3)

A_BO, A_IG, A_Y1, A_Y2, A_DR2, A_DRC, A_DR1 = 0, 2, 4, 6, 7, 9, 10
N_AG = 12
R_SA, R_FF, R_CR, R_DFF, R_DQ, R_DSA, R_DST = 0, 2, 4, 5, 7, 8, 10
N_RS = 11
BLOCKS = {"ffd": 768, "ffo": 384, "ffi": 384, "crx": 384, "sad": 384, "sae": 384}
WORKER = {"ffd": 1, "crx": 1, "sad": 1, "ffo": 0, "ffi": 0, "sae": 1}
OWNER = {"ffd": 1, "sad": 1, "ffo": 0, "ffi": 0, "sae": 0}
WHOLE = ()
GROUP = {"ffd": "a", "crx": "b", "ffo": "b", "sad": "c", "ffi": "c", "sae": "d"}
SECOND_RS = (R_SA + 1, R_DSA + 1)
SECOND_AG = (A_BO + 1, A_IG + 1, A_Y1 + 1)


def nn(a, b):
    return jnp.dot(a, b, preferred_element_type=F32)


def nt(a, b):
    return lax.dot_general(a, b, (((1,), (1,)), ((), ())), preferred_element_type=F32)


def tn(a, b):
    return lax.dot_general(a, b, (((0,), (0,)), ((), ())), preferred_element_type=F32)


def scratch_list():
    out = [
        ("xin", VMEM((2, TOK, D), BF)),
        ("nv", VMEM((2, 2, 2, D), F32)),
        ("wsa", VMEM((2, 768, D), BF)),
        ("wff", VMEM((2, 2, 768, D), BF)),
        ("wcr", VMEM((768, D), BF)),
        ("cot", VMEM((TOK, D), BF)),
        ("pk", VMEM((2, 3 * QW, TOK), BF)),
        ("pt", VMEM((2, NH, TOK, TOK), F32)),
        ("ot", VMEM((2, QW, TOK), BF)),
        ("n1", VMEM((2, SH, D), F32)),
        ("n2", VMEM((2, SH, D), F32)),
        ("nc", VMEM((SH, D), F32)),
        ("sp", VMEM((5, SH, 128), F32)),
        ("y1f", VMEM((2, SH, D), F32)),
        ("y2f", VMEM((SH, D), F32)),
        ("dres", VMEM((2, SH, D), F32)),
        ("act", VMEM((2, TOK, D), BF)),
        ("slope", VMEM((2, TOK, D), F32)),
        ("hid", VMEM((TOK, D), F32)),
        ("du", VMEM((2, TOK, D), BF)),
        ("dpk", VMEM((2, 3 * QW, TOK), BF)),
        ("qct", VMEM((QW, TOK), BF)),
        ("dqct", VMEM((QW, TOK), BF)),
        ("kvct", VMEM((2 * QW, KEYS), BF)),
        ("dkvct", VMEM((2 * QW, KEYS), BF)),
        ("ptc", VMEM((NH, KEYS, TOK), F32)),
        ("oct", VMEM((QW, TOK), BF)),
        ("pos", VMEM((2, 4, 8, KEYS), jnp.int32)),
        ("hot", VMEM((2, 4, 4 * TOK, KEYS), BF)),
        ("kvt", VMEM((2, 4, QW, TOK), BF)),
        ("kvf", VMEM((2, 4, QW, KEYS), F32)),
        ("kvs", VMEM((2, 4, QW, KEYS), BF)),
        ("kvr", VMEM((2, 3, QW, KEYS), BF)),
        ("dkr", VMEM((2, 3, QW, KEYS), BF)),
        ("dkf", VMEM((2, 4, QW, TOK), F32)),
        ("dks", VMEM((2, 4, QW, TOK), BF)),
        ("dk2", VMEM((2, 3, QW, TOK), BF)),
        ("dkv", VMEM((2 * QW, TOK), BF)),
        ("vec", VMEM((16, D), F32)),
        ("vx", VMEM((4, 16, D), BF)),
        ("vc", VMEM((2, 16, D), BF)),
        ("vy", VMEM((4, 16, D), BF)),
        ("vz", VMEM((4, 16, D), BF)),
        ("ag", VMEM((N_AG, TOK, D), BF)),
        ("rs", VMEM((N_RS, TOK, D), BF)),
        ("rr", VMEM((N_RS, 3, SH, D), BF)),
        ("m_w", DMA((2, 7))),
        ("m_ws", DMA((7,))),
        ("m_l", DMA((4,))),
        ("m_ags", DMA((2, 3))),
        ("m_agr", DMA((2, 3))),
        ("m_rss", DMA((2, 3))),
        ("m_rsr", DMA((2, 3))),
        ("m_dps", DMA((18,))),
        ("m_kvr", DMA((18,))),
        ("m_dkr", DMA((12,))),
        ("m_vr", DMA((10,))),
        ("m_hs", DMA((2,))),
        ("m_hr", DMA((3,))),
        ("m_g0", DMA((len(BLOCKS), 2))),
        ("f_sae", DMA((2, 4))),
        ("m_o", DMA((2,))),
    ]
    for name, rows in BLOCKS.items():
        out += [
            ("g_" + name, VMEM((2, 2, rows, 384), BF)),
            ("x_" + name, VMEM((2, 2, rows, 384), BF)),
            ("h_" + name, VMEM((2, 2, 2, rows // 8, 384), BF)),
            ("a_" + name, VMEM((2, 3 if name == "sae" else 2, 2, rows // 4, 384), BF)),
            (
                "b_" + name,
                VMEM((2, 4, 2, rows // 4, 384) if name in WHOLE else (2, 3, rows // 8, 384), BF),
            ),
        ]
    for group in sorted(set(GROUP.values())):
        out.append(("s_" + group, DMA((2, 4 if group == GROUP["sae"] else 3))))
        out.append(("r_" + group, DMA((2, 9 if group == GROUP["sae"] else 11))))
    return out


class Refs:
    pass


def ln_forward(r, gain, bias):
    center = r - jnp.mean(r, axis=-1, keepdims=True)
    spread = lax.rsqrt(jnp.mean(center * center, axis=-1, keepdims=True) + EPS)
    n = center * spread
    return n * gain + bias, n, spread


def ln_backward(n, spread, gain, dy):
    s = dy * gain
    dr = spread * (
        s - jnp.mean(s, axis=-1, keepdims=True) - n * jnp.mean(s * n, axis=-1, keepdims=True)
    )
    return dr, jnp.sum(dy * n, axis=0, keepdims=True), jnp.sum(dy, axis=0, keepdims=True)


def kernel(names, n_in, n_out, *refs):
    (x_h, cot_h, dgr, ret, ng_h, nb_h, cg, cb, qkv_h, out_h, win_h, wfo_h, cq_h, ckv_h, co_h) = refs[
        :n_in
    ]
    bo_o, ig_o, of_o, os_o, oc_o, on_o, oe_o = refs[n_in : n_in + n_out]
    R = Refs()
    for name, ref in zip(names, refs[n_in + n_out :]):
        setattr(R, name, ref)
    c = lax.axis_index("section")
    t = lax.axis_index("tensor")
    d = lax.axis_index("dp")
    o = 1 - c
    y = lax.rem(d, 4)
    z = d // 4
    p = y + c * (z - y)
    q = z + c * (y - z)
    sp, sq = 1 + 3 * c, 4 - 3 * c
    rows_t = pl.ds(pl.multiple_of(t * SH, SH), SH)

    def dev_x(k):
        return (c, lax.rem(t + k, 4), d)

    def dp_p(k):
        return lax.rem(p + k, 4) * sp + q * sq

    def dev_p(k):
        return (c, t, dp_p(k))

    def dev_q(k):
        return (c, t, p * sp + lax.rem(q + k, 4) * sq)

    def dev_y(k):
        return (c, t, z * 4 + lax.rem(y + k, 4))

    def dev_z(k):
        return (c, t, lax.rem(z + k, 4) * 4 + y)

    dev_c = (o, t, d)
    sends = {}

    def flush(kind, keep=0):
        queue = sends.get(kind, [])
        while len(queue) > keep:
            queue.pop(0).wait_send()

    def push(src, dst, ss, rs, dev, kind="", wait=True):
        cp = pltpu.make_async_remote_copy(
            src_ref=src, dst_ref=dst, send_sem=ss, recv_sem=rs, device_id=dev, device_id_type=MESH
        )
        cp.start()
        if wait:
            sends.setdefault(kind, []).append(cp)
        return cp

    def landed(dst, rs, dev):
        pltpu.make_async_remote_copy(
            src_ref=dst, dst_ref=dst, send_sem=rs, recv_sem=rs, device_id=dev, device_id_type=MESH
        ).wait_recv()

    def places(s):
        return [
            R.xin.at[s],
            R.wsa.at[s, pl.ds(0, 576)],
            R.wsa.at[s, pl.ds(576, 192)],
            R.nv.at[s, 0],
            R.nv.at[s, 1],
            R.wff.at[s, 0],
            R.wff.at[s, 1],
        ]

    items = [x_h.at[c], qkv_h, out_h, ng_h, nb_h, win_h, wfo_h]
    bar = pltpu.get_barrier_semaphore()
    peers = [dev_c]
    for k in (1, 2, 3):
        for dev in (dev_x(k), dev_y(k), dev_z(k)):
            peers.append(dev)
    for k in (1, 2, 3):
        peers.append((o,) + dev_y(k)[1:])
        peers.append((o,) + dev_z(k)[1:])
    for dev in peers:
        pl.semaphore_signal(bar, inc=1, device_id=dev, device_id_type=MESH)

    def own(i):
        pltpu.make_async_copy(items[i], places(c)[i], R.m_w.at[c, i]).start()

    def other(i):
        src = x_h.at[o] if i == 0 else items[i]
        push(src, places(c)[i], R.m_ws.at[i], R.m_w.at[c, i], dev_c)

    for i in range(5):
        own(i)
    singles = [
        pltpu.make_async_copy(cq_h, R.wcr.at[pl.ds(0, 192)], R.m_l.at[0]),
        pltpu.make_async_copy(co_h, R.wcr.at[pl.ds(192, 192)], R.m_l.at[1]),
        pltpu.make_async_copy(ckv_h, R.wcr.at[pl.ds(384, 384)], R.m_l.at[2]),
        pltpu.make_async_copy(cot_h.at[c], R.cot, R.m_l.at[3]),
    ]
    def enter():
        pl.semaphore_wait(bar, len(peers))
        for i in range(3):
            other(i)

    def rest():
        for i in (3, 4):
            other(i)
        for i in (5, 6):
            own(i)
            other(i)
        for cp in singles:
            cp.start()

    def need(s, i):
        src = x_h.at[s] if i == 0 else items[i]
        pltpu.make_async_copy(src, places(s)[i], R.m_w.at[s, i]).wait()

    def rs_start(i, value):
        m = int(i in SECOND_RS)
        flush(("rs", m))
        R.rs[i] = value.astype(BF)
        for k in RINGS:
            to = lax.rem(t + k, 4)
            push(
                R.rs.at[i, pl.ds(pl.multiple_of(to * SH, SH), SH)],
                R.rr.at[i, k - 1],
                R.m_rss.at[m, k - 1],
                R.m_rsr.at[m, k - 1],
                dev_x(k),
                ("rs", m),
            )

    def rs_sum(i):
        for k in (1, 3, 2):
            landed(R.rr.at[i, k - 1], R.m_rsr.at[int(i in SECOND_RS), k - 1], dev_x(k))
        total = R.rs[i, rows_t, :].astype(F32)
        for k in range(3):
            total += R.rr[i, k].astype(F32)
        return total

    def ag_start(i, value):
        m = int(i in SECOND_AG)
        flush(("ag", m))
        R.ag[i, rows_t, :] = value.astype(BF)
        for k in RINGS:
            push(
                R.ag.at[i, rows_t],
                R.ag.at[i, rows_t],
                R.m_ags.at[m, k - 1],
                R.m_agr.at[m, k - 1],
                dev_x(k),
                ("ag", m),
            )

    def ag_wait(i):
        for k in (1, 3, 2):
            landed(R.ag.at[i, rows_t], R.m_agr.at[int(i in SECOND_AG), k - 1], dev_x(k))

    def gain_row(s, i):
        return R.nv[s, 0, i : i + 1, :]

    def bias_row(s, i):
        return R.nv[s, 1, i : i + 1, :]

    cross_gain = cg[...].reshape(1, D)
    cross_bias = cb[...].reshape(1, D)

    def softmax(scores):
        tops = [jnp.max(st, axis=0, keepdims=True) for st in scores]
        exps = [jnp.exp(st - top) for st, top in zip(scores, tops)]
        sums = [jnp.sum(e, axis=0, keepdims=True) for e in exps]
        return [e / total for e, total in zip(exps, sums)]

    def attend_backward(qts, kts, vts, prs, dots):
        heads = range(NH)
        dpts = [tn(vts[h], dots[h]) for h in heads]
        dvts = [nt(dots[h], prs[h].astype(BF)) for h in heads]
        sums = [jnp.sum(dpts[h] * prs[h], axis=0, keepdims=True) for h in heads]
        dsts = [(prs[h] * (dpts[h] - sums[h])).astype(BF) for h in heads]
        dqts = [nn(kts[h], dsts[h]) * SCALE for h in heads]
        dkts = [nt(qts[h], dsts[h]) * SCALE for h in heads]
        return dqts, dkts, dvts

    def self_forward(s):
        need(s, 0)
        need(s, 1)
        R.pk[s] = nt(R.wsa[s, 0:576, :], R.xin[s]).astype(BF)
        scores = [
            tn(R.pk[s, QW + lo : QW + lo + 64, :], R.pk[s, lo : lo + 64, :]) * SCALE for lo in HEADS
        ]
        if s == 1:
            key = lax.broadcasted_iota(jnp.int32, (TOK, TOK), 0)
            qry = lax.broadcasted_iota(jnp.int32, (TOK, TOK), 1)
            scores = [jnp.where(key <= qry, st, -1000000000.0) for st in scores]
        probs = softmax(scores)
        for h, lo in enumerate(HEADS):
            vt = R.pk[s, 2 * QW + lo : 2 * QW + lo + 64, :]
            R.ot[s, lo : lo + 64, :] = nn(vt, probs[h].astype(BF)).astype(BF)
            R.pt[s, h] = probs[h]
        need(s, 2)
        value = tn(R.ot[s], R.wsa[s, 576:768, :])
        if s == 0:
            enter()
        rs_start(R_SA + s, value)

    def put_norm(slot, spread):
        R.sp[slot] = jnp.broadcast_to(spread, (SH, 128))

    def get_norm(slot):
        return R.sp[slot, :, 0:1]

    def self_finish(s):
        total = rs_sum(R_SA + s)
        r = R.xin[s, rows_t, :].astype(F32) + total
        need(s, 3)
        need(s, 4)
        out, n, spread = ln_forward(r, gain_row(s, 0), bias_row(s, 0))
        ag_start(A_Y1 + s, out)
        R.y1f[s] = out
        R.n1[s] = n
        put_norm(s, spread)

    def ffn_forward(s, gathered):
        u = nn(R.ag[gathered], R.wff[s, 0])
        cdf = 0.5 * (1.0 + lax.erf(u * 0.7071067811865476))
        R.act[s] = (u * cdf).astype(BF)
        R.hid[...] = u
        R.slope[s] = cdf
        rs_start(R_FF + s, nn(R.act[s], R.wff[s, 1]))
        u = R.hid[...]
        R.slope[s] += u * jnp.exp(-0.5 * u * u) * 0.3989422804014327

    def ffn_backward(s):
        ag_wait(A_DR2 + s)
        dg = nt(R.ag[A_DR2 + s], R.wff[s, 1])
        R.du[s] = (dg * R.slope[s]).astype(BF)
        rs_start(R_DFF + s, nt(R.du[s], R.wff[s, 0]))

    def put(ref, piece, r0, value):
        rows = value.shape[0]
        ref[piece, 0, r0 : r0 + rows, :] = value[:, 0:384].astype(BF)
        ref[piece, 1, r0 : r0 + rows, :] = value[:, 384:768].astype(BF)

    def out_grad(s):
        return tn(R.act[s], R.ag[A_DR2 + s])

    def in_grad(s, gathered):
        return tn(R.ag[gathered], R.du[s])

    def put_halves(ref, value):
        put(ref, 0, 0, value[0:384])
        put(ref, 1, 0, value[384:768])

    def blk(name):
        bufs = tuple(getattr(R, pre + name) for pre in ("g_", "x_", "h_", "a_", "b_"))
        return bufs + (getattr(R, "s_" + GROUP[name]), getattr(R, "r_" + GROUP[name]))

    place = ((y, z), (z, y))
    devs = ((dev_y, dev_z), (dev_z, dev_y))

    def quarter(name, where):
        rows = BLOCKS[name] // 4
        return pl.ds(pl.multiple_of(where * rows, rows), rows)

    def eighth(name, where, half):
        rows = BLOCKS[name] // 8
        return pl.ds(pl.multiple_of(where * 2 * rows + half * rows, rows), rows)

    def step(where, k):
        return lax.rem(where + k, 4)

    def work(name):
        return pl.when(c == WORKER[name])

    def gone(src, sem):
        pltpu.make_async_remote_copy(
            src_ref=src, dst_ref=src, send_sem=sem, recv_sem=sem, device_id=dev_c, device_id_type=MESH
        ).wait_send()

    def ship(src, dst, ss, rs, dev):
        push(src, dst, ss, rs, dev, wait=False)

    def result(name, i, rows, half=slice(None)):
        if name == "crx":
            return oc_o.at[i, half, rows]
        if name == "ffd":
            return of_o.at[i, half, rows]
        if name in ("ffi", "ffo"):
            rows = pl.ds(pl.multiple_of(i * 384 + rows.start, 48), rows.size)
            return of_o.at[int(name == "ffo"), half, rows]
        return os_o.at[i, half, rows]

    def spot(name, i, rows, half=slice(None)):
        return R.x_sae.at[i, half, rows] if name == "sae" else result(name, i, rows, half)

    def g0(name, pieces=(0, 1)):
        g, x = blk(name)[:2]

        @pl.when(c != WORKER[name])
        def _():
            for i in pieces:
                sem = R.m_g0.at[tuple(BLOCKS).index(name), i]
                ship(g.at[i], x.at[i], sem, blk(name)[6].at[i, 0], dev_c)

    def g1(name, pieces=(0, 1)):
        g, x, h, a, b, s, r = blk(name)

        @work(name)
        def _():
            for i in pieces:
                landed(x.at[i], r.at[i, 0], dev_c)
                g[i] = g[i] + x[i]
                if name == "sae":
                    for k in RINGS:
                        part = g.at[i, :, quarter(name, step(place[i][0], k))]
                        ship(part, a.at[i, k - 1], s.at[i, k - 1], r.at[i, k], devs[i][0](k))
                    continue
                far = step(place[i][0], 2)
                for j, k in ((0, 1), (1, 3)):
                    part = g.at[i, :, eighth(name, far, j)]
                    ship(part, h.at[i, j], s.at[i, j], r.at[i, 1 + j], devs[i][0](k))

    def g1b(name, pieces=(0, 1)):
        g, x, h, a, b, s, r = blk(name)

        @work(name)
        def _():
            for j, k in ((0, 1), (1, 3)):
                for i in pieces:
                    near = step(place[i][0], k)
                    landed(h.at[i, j], r.at[i, 1 + j], dev_c)
                    part = eighth(name, near, j)
                    g[i, :, part, :] = g[i, :, part, :] + h[i, j]
                    part = g.at[i, :, quarter(name, near)]
                    gone(h.at[i, j], s.at[i, j])
                    ship(part, a.at[i, j], s.at[i, j], r.at[i, 3 + j], devs[i][0](k))

    def sub(name, i, where):
        return eighth(name, place[i][0], where // 2), lax.rem(where, 2)

    def g2(name, pieces=(0, 1)):
        g, x, h, a, b, s, r = blk(name)

        @work(name)
        def _():
            for i in pieces:
                mine = quarter(name, place[i][0])
                total = g[i, :, mine, :].astype(F32)
                for j in range(a.shape[1]):
                    landed(a.at[i, j], r.at[i, j + (1 if name == "sae" else 3)], dev_c)
                    total += a[i, j].astype(F32)
                    gone(a.at[i, j], s.at[i, j])
                g[i, :, mine, :] = total.astype(BF)
                if name in WHOLE:
                    part = g.at[i, :, mine]
                    for k in RINGS:
                        dst = b.at[i, place[i][1]]
                        ship(part, dst, s.at[i, k - 1], r.at[i, 4 + k], devs[i][1](k))
                    continue
                for k in RINGS:
                    rows, half = sub(name, i, step(place[i][1], k))
                    part = g.at[i, half, rows]
                    ship(part, b.at[i, k - 1], s.at[i, k - 1], r.at[i, 4 + k], devs[i][1](k))

    def g3(name, pieces=(0, 1)):
        g, x, h, a, b, s, r = blk(name)

        @work(name)
        def _():
            for i in pieces:
                if name in WHOLE:
                    mine = quarter(name, place[i][0])
                    b[i, place[i][1]] = g[i, :, mine, :]
                    for k in (1, 3, 2):
                        landed(a.at[i, 0], r.at[i, 4 + k], dev_c)
                        gone(a.at[i, 0], s.at[i, k - 1])
                    total = b[i, 0].astype(F32)
                    for j in (1, 2, 3):
                        total += b[i, j].astype(F32)
                    spot(name, i, mine)[...] = total.astype(BF)
                    continue
                for k in (1, 3, 2):
                    landed(b.at[i, k - 1], r.at[i, 4 + k], dev_c)
                rows, half = sub(name, i, place[i][1])
                total = g[i, half, rows, :].astype(F32)
                for k in range(3):
                    total += b[i, k].astype(F32)
                part = spot(name, i, rows, half)
                part[...] = total.astype(BF)
                for k in RINGS:
                    gone(b.at[i, k - 1], s.at[i, k - 1])
                    ship(part, part, s.at[i, k - 1], r.at[i, (3, 4, 8)[k - 1]], devs[i][1](k))

    def g4(name, pieces=(0, 1)):
        g, x, h, a, b, s, r = blk(name)

        @work(name)
        def _():
            for i in pieces:
                mine = quarter(name, place[i][0])
                part = spot(name, i, mine)
                for k in () if name in WHOLE else (1, 3, 2):
                    landed(b.at[i, k - 1], r.at[i, (3, 4, 8)[k - 1]], dev_c)
                    gone(b.at[i, k - 1], s.at[i, k - 1])
                if name == "sae":
                    dst = result(name, i, mine)
                    for k in RINGS:
                        to = (OWNER[name],) + devs[i][0](k)[1:]
                        ship(part, dst, s.at[i, k - 1], R.f_sae.at[i, k], to)
                    ship(part, dst, s.at[i, 3], R.f_sae.at[i, 0], dev_c)
                    continue
                for j, k in ((0, 1), (1, 3)):
                    ship(part, part, s.at[i, j], r.at[i, 2 - j], devs[i][0](k))

    def g4b(name, pieces=(0, 1)):
        g, x, h, a, b, s, r = blk(name)

        @work(name)
        def _():
            for j, k in ((0, 1), (1, 3)):
                for i in pieces:
                    behind = step(place[i][0], 4 - k)
                    landed(a.at[i, j], r.at[i, 2 - j], dev_c)
                    gone(a.at[i, j], s.at[i, j])
                    rows = eighth(name, behind, j)
                    part = spot(name, i, rows)
                    ship(part, part, s.at[i, j], r.at[i, 9 + j], devs[i][0](k))

    def g5(name):
        g, x, h, a, b, s, r = blk(name)

        @work(name)
        def _():
            for i in (0, 1):
                for j in (0, 1):
                    landed(h.at[i, j], r.at[i, 9 + j], dev_c)
            if name == "crx":
                ship(oc_o, oc_o, s.at[0, 2], R.m_hr.at[2], dev_c)

    def g6(name):
        g, x, h, a, b, s, r = blk(name)

        @pl.when(c != WORKER[name])
        def _():
            for i in (0, 1):
                gone(g.at[i], R.m_g0.at[tuple(BLOCKS).index(name), i])
            if name == "crx":
                landed(oc_o, R.m_hr.at[2], dev_c)
            if name == "sae":
                for i in (0, 1):
                    for j in range(4):
                        landed(a.at[i, 0], R.f_sae.at[i, j], dev_c)

        @work(name)
        def _():
            for i in (0, 1):
                if name == "sae":
                    for j in range(4):
                        gone(a.at[i, 0], s.at[i, j])
                    continue
                for j in (0, 1):
                    gone(h.at[i, j], s.at[i, j])
            if name == "crx":
                gone(oc_o, s.at[0, 2])

    def vec_put(row, dg, db, step=2):
        R.vec[row : row + 1, :] = dg
        R.vec[row + step : row + step + 1, :] = db

    def vec_send(buf, at, value, base, dev, count):
        buf[at] = value.astype(BF)
        for k in range(1, count):
            push(buf.at[at], buf.at[at], R.m_dps.at[base + k - 1], R.m_vr.at[base + k - 1], dev(k))

    def vec_sum(buf, at, base, dev, count):
        for k in range(1, count):
            landed(buf.at[at], R.m_vr.at[base + k - 1], dev(k))
        total = buf[0].astype(F32)
        for k in range(1, count):
            total += buf[k].astype(F32)
        return total

    def dev_c1(k):
        return dev_c

    self_forward(0)
    rest()
    for j in (10, 11, 12, 13, 14, 15):
        R.vec[j : j + 1, :] = jnp.zeros((1, D), F32)

    micro = lax.broadcasted_iota(jnp.int32, (2, 16), 0)
    group = lax.broadcasted_iota(jnp.int32, (2, 16), 1)
    live = (micro == c) & (group <= d) & (dgr[...] > 0)
    start = jnp.max(jnp.where(live, group, 0), axis=1, keepdims=True)
    start = jnp.max(start, axis=0, keepdims=True)
    rows = jnp.where(c == 0, ret[0], ret[1]) + start * TOK
    g_at = rows // TOK
    b_at = jnp.where(c == 0, g_at, lax.rem(g_at, 4) * 4 + g_at // 4)
    at = b_at * TOK + lax.rem(rows, TOK)
    first = (p, q)
    dev_first, dev_second = (dev_p, dev_q), (dev_q, dev_p)
    for u in (0, 1):
        R.pos[u, 0] = jnp.broadcast_to(at, (8, KEYS))
        for k in RINGS:
            m = 3 * u + k - 1
            push(R.pos.at[u, 0], R.pos.at[u, k], R.m_dps.at[m], R.m_kvr.at[m], dev_second[u](k))
    self_finish(0)
    ag_wait(A_Y1)
    need(0, 5)
    need(0, 6)
    ffn_forward(0, A_Y1)

    for cp in singles:
        cp.wait()
    for u in (0, 1):
        for k in (1, 3, 2):
            landed(R.pos.at[u, k], R.m_kvr.at[3 * u + k - 1], dev_c)

    def build(i, carry):
        rows = pl.ds(pl.multiple_of(i * TOK, TOK), TOK)
        for u in (0, 1):
            block = q * 4 + i if u == 0 else i * 4 + p
            n = lax.broadcasted_iota(jnp.int32, (TOK, KEYS), 0) + block * TOK
            for k in range(4):
                R.hot[u, k, rows, :] = jnp.where(n == R.pos[u, k, 0:1, :], 1.0, 0.0).astype(BF)
        return carry

    lax.fori_loop(0, 4, build, 0)

    out, n, spread = ln_forward(R.y1f[0] + rs_sum(R_FF), gain_row(0, 1), bias_row(0, 1))
    ag_start(A_BO, out)
    R.n2[0] = n
    put_norm(2, spread)
    ag_wait(A_BO)

    def hot(u, k, j):
        return R.hot[u, k, pl.ds(pl.multiple_of(j * TOK, TOK), TOK), :]

    def picked(u, k, j):
        return nn(R.kvt[u, j], hot(u, k, j))

    for u in (0, 1):
        R.kvt[u, first[u]] = nt(R.wcr[384 + u * QW : 384 + u * QW + QW, :], R.ag[A_BO]).astype(BF)
        for k in RINGS:
            part, m = R.kvt.at[u, first[u]], 6 + 3 * u + k - 1
            push(part, part, R.m_dps.at[m], R.m_kvr.at[m], dev_first[u](k))
    self_forward(1)
    for u in (0, 1):
        for k in range(4):
            R.kvf[u, k] = picked(u, k, first[u])
    for u in (0, 1):
        for j in (1, 3):
            landed(R.kvt.at[u, 0], R.m_kvr.at[6 + 3 * u + j - 1], dev_c)
            for k in range(4):
                R.kvf[u, k] += picked(u, k, lax.rem(first[u] + 4 - j, 4))
        landed(R.kvt.at[u, 0], R.m_kvr.at[6 + 3 * u + 1], dev_c)
        for k in RINGS + (0,):
            R.kvs[u, k] = (R.kvf[u, k] + picked(u, k, lax.rem(first[u] + 2, 4))).astype(BF)
            if k:
                m = 12 + 3 * u + 3 - k
                dst = R.kvr.at[u, 3 - k]
                push(R.kvs.at[u, k], dst, R.m_dps.at[m], R.m_kvr.at[m], dev_second[u](4 - k))
    self_finish(1)
    ag_wait(A_Y1 + 1)
    R.qct[...] = nt(R.wcr[0:192, :], R.ag[A_Y1 + 1]).astype(BF)

    def chosen(u):
        for k in (1, 3, 2):
            landed(R.kvr.at[u, k - 1], R.m_kvr.at[12 + 3 * u + k - 1], dev_c)
        total = R.kvs[u, 0].astype(F32)
        for k in range(3):
            total += R.kvr[u, k].astype(F32)
        R.kvct[u * QW : u * QW + QW, :] = total.astype(BF)

    chosen(0)
    probs = softmax(
        [tn(R.kvct[lo : lo + 64, :], R.qct[lo : lo + 64, :]) * SCALE for lo in HEADS]
    )
    chosen(1)
    for h, lo in enumerate(HEADS):
        vt = R.kvct[QW + lo : QW + lo + 64, :]
        R.oct[lo : lo + 64, :] = nn(vt, probs[h].astype(BF)).astype(BF)
        R.ptc[h] = probs[h]
    rs_start(R_CR, tn(R.oct[...], R.wcr[192:384, :]))
    need(1, 5)
    need(1, 6)
    out, n, spread = ln_forward(R.y1f[1] + rs_sum(R_CR), cross_gain, cross_bias)
    ag_start(A_Y2, out)
    R.y2f[...] = out
    R.nc[...] = n
    put_norm(4, spread)
    ag_wait(A_Y2)
    ffn_forward(1, A_Y2)
    out, n, spread = ln_forward(R.y2f[...] + rs_sum(R_FF + 1), gain_row(1, 1), bias_row(1, 1))

    dr, dg, db = ln_backward(n, spread, gain_row(1, 1), R.cot[rows_t, :].astype(F32))
    ag_start(A_DR2 + 1, dr)
    R.dres[1] = dr
    vec_put(5, dg, db)
    ffn_backward(1)
    ag_start(A_BO + 1, out)
    flush("")
    put(R.g_ffd, 0, 0, in_grad(1, A_Y2))
    put(R.g_ffd, 1, 0, out_grad(1))
    g0("ffd")
    dy = R.dres[1] + rs_sum(R_DFF + 1)
    dr, dg, db = ln_backward(R.nc[...], get_norm(4), cross_gain, dy)
    ag_start(A_DRC, dr)
    R.dres[1] = dr
    vec_put(8, dg, db, 1)
    g1("ffd")
    ag_wait(A_DRC)

    def compact(u):
        for k in RINGS:
            m = 3 * u + k - 1
            part = R.dkvct.at[pl.ds(u * QW, QW)]
            push(part, R.dkr.at[u, k - 1], R.m_dps.at[m], R.m_dkr.at[m], dev_second[u](k))

    doc = nt(R.wcr[192:384, :], R.ag[A_DRC]).astype(BF)
    heads = list(enumerate(HEADS))
    for h, lo in heads:
        dvt = nt(doc[lo : lo + 64, :], R.ptc[h].astype(BF))
        R.dkvct[QW + lo : QW + lo + 64, :] = dvt.astype(BF)
    compact(1)
    dpts = [tn(R.kvct[QW + lo : QW + lo + 64, :], doc[lo : lo + 64, :]) for h, lo in heads]
    sums = [jnp.sum(dpts[h] * R.ptc[h], axis=0, keepdims=True) for h, lo in heads]
    dsts = [(R.ptc[h] * (dpts[h] - sums[h])).astype(BF) for h, lo in heads]
    for h, lo in heads:
        dkt = nt(R.qct[lo : lo + 64, :], dsts[h]) * SCALE
        R.dkvct[lo : lo + 64, :] = dkt.astype(BF)
    compact(0)
    for h, lo in heads:
        dqt = nn(R.kvct[lo : lo + 64, :], dsts[h]) * SCALE
        R.dqct[lo : lo + 64, :] = dqt.astype(BF)
    rs_start(R_DQ, tn(R.dqct[...], R.wcr[0:192, :]))
    put(R.g_crx, 0, 0, nn(R.dqct[...], R.ag[A_Y1 + 1]))
    put(R.g_crx, 0, 192, nn(R.oct[...], R.ag[A_DRC]))
    g0("crx", (0,))
    dy = R.dres[1] + rs_sum(R_DQ)
    dr, dg, db = ln_backward(R.n1[1], get_norm(1), gain_row(1, 0), dy)
    ag_start(A_DR1 + 1, dr)
    R.dres[1] = dr
    vec_put(4, dg, db)
    g1b("ffd", (0,))

    def self_backward(s):
        ag_wait(A_DR1 + s)
        dot = nt(R.wsa[s, 576:768, :], R.ag[A_DR1 + s]).astype(BF)
        dqts, dkts, dvts = attend_backward(
            [R.pk[s, lo : lo + 64, :] for lo in HEADS],
            [R.pk[s, QW + lo : QW + lo + 64, :] for lo in HEADS],
            [R.pk[s, 2 * QW + lo : 2 * QW + lo + 64, :] for lo in HEADS],
            [R.pt[s, h] for h in range(NH)],
            [dot[lo : lo + 64, :] for lo in HEADS],
        )
        for h, lo in enumerate(HEADS):
            R.dpk[s, lo : lo + 64, :] = dqts[h].astype(BF)
            R.dpk[s, QW + lo : QW + lo + 64, :] = dkts[h].astype(BF)
            R.dpk[s, 2 * QW + lo : 2 * QW + lo + 64, :] = dvts[h].astype(BF)

    def self_grads(s, name):
        ref = getattr(R, "g_" + name)
        put(ref, 0, 0, nn(R.dpk[s, 0:384, :], R.xin[s]))
        g0(name, (0,))
        put(ref, 1, 0, nn(R.dpk[s, 384:576, :], R.xin[s]))
        put(ref, 1, 192, nn(R.ot[s], R.ag[A_DR1 + s]))
        g0(name, (1,))

    def input_part(s):
        rs_start(R_DSA + s, tn(R.dpk[s], R.wsa[s, 0:576, :]))

    for u in (1, 0):
        for j in range(4):
            R.dkf[u, j] = nt(R.dkvct[u * QW : u * QW + QW, :], hot(u, 0, j))
    for u in (1, 0):
        for k in (1, 3):
            landed(R.dkr.at[u, k - 1], R.m_dkr.at[3 * u + k - 1], dev_c)
            for j in range(4):
                R.dkf[u, j] += nt(R.dkr[u, k - 1], hot(u, k, j))
        landed(R.dkr.at[u, 1], R.m_dkr.at[3 * u + 1], dev_c)
        for k in RINGS + (0,):
            to = lax.rem(first[u] + k, 4)
            R.dks[u, to] = (R.dkf[u, to] + nt(R.dkr[u, 1], hot(u, 2, to))).astype(BF)
            if k:
                m = 6 + 3 * u + k - 1
                dst = R.dk2.at[u, k - 1]
                push(R.dks.at[u, to], dst, R.m_dps.at[m], R.m_dkr.at[m], dev_first[u](k))
    g1b("ffd", (1,))
    self_backward(1)
    input_part(1)
    self_grads(1, "sad")
    g1("crx", (0,))
    for u in (1, 0):
        for k in (1, 3, 2):
            landed(R.dk2.at[u, k - 1], R.m_dkr.at[6 + 3 * u + k - 1], dev_c)
        total = R.dks[u, first[u]].astype(F32)
        for k in range(3):
            total += R.dk2[u, k].astype(F32)
        R.dkv[u * QW : u * QW + QW, :] = total.astype(BF)
    rs_start(R_DST, tn(R.dkv[...], R.wcr[384:768, :]))
    put(R.g_crx, 1, 0, nn(R.dkv[...], R.ag[A_BO]))
    g0("crx", (1,))
    g2("ffd")
    g1("sad")
    g1b("crx", (0,))
    dy = rs_sum(R_DST)
    dr, dg, db = ln_backward(R.n2[0], get_norm(2), gain_row(0, 1), dy)
    ag_start(A_DR2, dr)
    R.dres[0] = dr
    vec_put(1, dg, db)
    flush("")
    ag_wait(A_BO + 1)
    push(R.ag.at[A_BO + o], bo_o.at[c], R.m_hs.at[0], R.m_hr.at[0], dev_c)
    outs = [pltpu.make_async_copy(R.ag.at[A_BO + c], bo_o.at[c], R.m_o.at[0])]
    outs[0].start()
    g3("ffd")
    g1("crx", (1,))
    g1b("sad")
    g2("crx", (0,))
    ffn_backward(0)
    put_halves(R.g_ffo, out_grad(0))
    g0("ffo")
    put_halves(R.g_ffi, in_grad(0, A_Y1))
    g0("ffi")
    g4("ffd")
    g1b("crx", (1,))
    g3("crx", (0,))
    g2("sad")
    g1("ffo")
    dy = R.dres[0] + rs_sum(R_DFF)
    dr, dg, db = ln_backward(R.n1[0], get_norm(0), gain_row(0, 0), dy)
    ag_start(A_DR1, dr)
    R.dres[0] = dr
    vec_put(0, dg, db)
    g1("ffi")
    g4b("ffd")
    g4("crx", (0,))
    g2("crx", (1,))
    g3("sad")
    g1b("ffo")
    self_backward(0)
    g1b("ffi")
    self_grads(0, "sae")
    vec_send(R.vx, t, R.vec[...], 0, dev_x, 4)
    input_part(0)
    ag_start(A_IG + 1, R.dres[1] + rs_sum(R_DSA + 1))
    g1("sae")
    g2("ffo")
    total = vec_sum(R.vx, t, 0, dev_x, 4)
    vec_send(R.vc, c, total, 3, dev_c1, 2)
    g3("crx", (1,))
    g4b("crx", (0,))
    g4("sad")
    g2("ffi")
    total = vec_sum(R.vc, c, 3, dev_c1, 2)
    vec_send(R.vy, y, total, 4, dev_y, 4)
    ag_start(A_IG, R.dres[0] + rs_sum(R_DSA))
    g3("ffo")
    g2("sae")
    g4("crx", (1,))
    g3("ffi")
    total = vec_sum(R.vy, y, 4, dev_y, 4)
    vec_send(R.vz, z, total, 7, dev_z, 4)
    g4("ffo")
    g3("sae")
    g4b("sad")
    g4b("crx", (1,))
    g4("ffi")
    g4("sae")
    g5("crx")
    ag_wait(A_IG)
    ag_wait(A_IG + 1)
    push(R.ag.at[A_IG + o], ig_o.at[c], R.m_hs.at[1], R.m_hr.at[1], dev_c)
    outs.append(pltpu.make_async_copy(R.ag.at[A_IG + c], ig_o.at[c], R.m_o.at[1]))
    outs[1].start()
    g4b("ffo")
    total = vec_sum(R.vz, z, 7, dev_z, 4)
    on_o[...] = jnp.where(c == 0, total[0:4, :], total[4:8, :])
    oe_o[...] = total[8:10, :]
    flush("")
    g4b("ffi")
    landed(bo_o.at[c], R.m_hr.at[0], dev_c)
    landed(ig_o.at[c], R.m_hr.at[1], dev_c)
    for cp in outs:
        cp.wait()
    g5("ffd")
    g5("sad")
    g5("ffo")
    g5("ffi")
    for name in ("ffd", "sad", "crx", "ffo", "ffi", "sae"):
        g6(name)
    for kind in list(sends):
        flush(kind)


JOBS = (
    [("gf", 0, r, "win", r) for r in (0, 192, 384, 576)]
    + [("gf", 1, r, "wfo", r) for r in (0, 192, 384, 576)]
    + [("gc", 0, 0, "q", 0), ("gc", 0, 192, "co", 0), ("gc", 1, 0, "kv", 0), ("gc", 1, 192, "kv", 192)]
    + [("gs", 0, 0, "qkv", 0), ("gs", 0, 192, "qkv", 192), ("gs", 1, 0, "qkv", 384)]
    + [("gs", 1, 192, "out", 0)]
)


def widen(*refs):
    bo, ig, gf, gs, gc, gn, ge = refs[:7]
    bo_o, ig_o, qkv_o, out_o, win_o, wfo_o, ng_o, nb_o, q_o, kv_o, co_o, cg_o, cb_o = refs[7:20]
    wide, ig_wide, m_out, m_x = refs[20:]
    from_ = {"gf": gf, "gs": gs, "gc": gc}
    to = {"qkv": qkv_o, "out": out_o, "win": win_o, "wfo": wfo_o, "q": q_o, "kv": kv_o, "co": co_o}
    stores = [pltpu.make_async_copy(bo, bo_o, m_x.at[0])]
    stores[0].start()
    for i, (src, piece, r0, dst, d0) in enumerate(JOBS):
        wide[i, :, 0:384] = from_[src][piece, 0, r0 : r0 + 192, :].astype(F32)
        wide[i, :, 384:768] = from_[src][piece, 1, r0 : r0 + 192, :].astype(F32)
        cp = pltpu.make_async_copy(wide.at[i], to[dst].at[pl.ds(d0, 192)], m_out.at[i])
        cp.start()
        stores.append(cp)
    ig_wide[...] = ig[...].astype(F32)
    stores.append(pltpu.make_async_copy(ig_wide, ig_o, m_x.at[1]))
    stores[-1].start()
    ng_o[...] = gn[0:2, :]
    nb_o[...] = gn[2:4, :]
    cg_o[...] = ge[0:1, :].reshape(D)
    cb_o[...] = ge[1:2, :].reshape(D)
    for cp in stores:
        cp.wait()


def body(
    layer_inputs,
    cotangent,
    doc_groups,
    retrieved_at,
    sa_qkv,
    sa_out,
    ffn_in,
    ffn_out,
    norm_gain,
    norm_bias,
    cross_q,
    cross_kv,
    cross_out,
    cross_gain,
    cross_bias,
):
    ins = (
        layer_inputs[0],
        cotangent,
        doc_groups,
        retrieved_at,
        norm_gain[0],
        norm_bias[0],
        cross_gain,
        cross_bias,
        jnp.transpose(sa_qkv[0], (1, 2, 0)).reshape(576, D),
        sa_out[0],
        ffn_in[0],
        ffn_out[0],
        jnp.transpose(cross_q, (1, 0)),
        jnp.transpose(cross_kv, (1, 2, 0)).reshape(384, D),
        cross_out,
    )
    hbm = pl.BlockSpec(memory_space=pl.ANY)
    vm = pl.BlockSpec(memory_space=VMEM)
    outs = (
        VMEM((2, TOK, D), BF),
        VMEM((2, TOK, D), BF),
        VMEM((2, 2, 768, 384), BF),
        VMEM((2, 2, 384, 384), BF),
        VMEM((2, 2, 384, 384), BF),
        VMEM((4, D), F32),
        VMEM((2, D), F32),
    )
    names = [n for n, _ in scratch_list()]

    def run(*refs):
        kernel(names, len(ins), len(outs), *refs)

    results = pl.pallas_call(
        run,
        out_shape=outs,
        in_specs=[hbm, hbm, vm, vm, hbm, hbm, vm, vm] + [hbm] * 7,
        out_specs=[vm] * len(outs),
        scratch_shapes=[s for _, s in scratch_list()],
        compiler_params=pltpu.CompilerParams(
            collective_id=0, has_side_effects=True, vmem_limit_bytes=52 << 20
        ),
        name="layers",
    )(*ins)
    wide_outs = (
        jax.ShapeDtypeStruct((2, TOK, D), BF),
        jax.ShapeDtypeStruct((2, TOK, D), F32),
        jax.ShapeDtypeStruct((576, D), F32),
        jax.ShapeDtypeStruct((192, D), F32),
        jax.ShapeDtypeStruct((768, D), F32),
        jax.ShapeDtypeStruct((768, D), F32),
        jax.ShapeDtypeStruct((2, D), F32),
        jax.ShapeDtypeStruct((2, D), F32),
        jax.ShapeDtypeStruct((192, D), F32),
        jax.ShapeDtypeStruct((384, D), F32),
        jax.ShapeDtypeStruct((192, D), F32),
        jax.ShapeDtypeStruct((D,), F32),
        jax.ShapeDtypeStruct((D,), F32),
    )
    bo, ig, d_qkv, d_out, d_in, d_fo, ng, nb, d_q, d_kv, d_co, dcg, dcb = pl.pallas_call(
        widen,
        out_shape=wide_outs,
        in_specs=[vm] * 7,
        out_specs=[hbm] * 6 + [vm] * 2 + [hbm] * 3 + [vm] * 2,
        scratch_shapes=[
            VMEM((len(JOBS), 192, D), F32),
            VMEM((2, TOK, D), F32),
            DMA((len(JOBS),)),
            DMA((2,)),
        ],
        compiler_params=pltpu.CompilerParams(vmem_limit_bytes=32 << 20),
        name="widen",
    )(*[pltpu.with_memory_space_constraint(r, VMEM) for r in results])
    return (
        bo[None],
        ig[None],
        jnp.transpose(d_qkv.reshape(3, 192, D), (2, 0, 1))[None],
        d_out[None],
        d_in[None],
        d_fo[None],
        ng[None],
        nb[None],
        jnp.transpose(d_q, (1, 0)),
        jnp.transpose(d_kv.reshape(2, 192, D), (2, 0, 1)),
        d_co,
        dcg,
        dcb,
    )


def solution(mesh):
    placed = (
        P("section", None, "dp", None),
        P(None, "dp", None),
        P(),
        P(None, "dp", None),
        P("section", None, None, "tensor"),
        P("section", "tensor", None),
        P("section", None, "tensor"),
        P("section", "tensor", None),
        P("section", None, None),
        P("section", None, None),
        P(None, "tensor"),
        P(None, None, "tensor"),
        P("tensor", None),
        P(),
        P(),
    )
    return jax.shard_map(
        body,
        mesh=mesh,
        in_specs=placed,
        out_specs=(
            P("section", None, "dp", None),
            P("section", None, "dp", None),
            P("section", None, None, "tensor"),
            P("section", "tensor", None),
            P("section", None, "tensor"),
            P("section", "tensor", None),
            P("section", None, None),
            P("section", None, None),
            P(None, "tensor"),
            P(None, None, "tensor"),
            P("tensor", None),
            P(),
            P(),
        ),
        check_vma=False,
    )
```

```python
import jax
import jax.numpy as jnp
from jax import lax
from jax.experimental import pallas as pl
from jax.experimental.pallas import tpu as pltpu
from jax.sharding import PartitionSpec as P

BF = jnp.bfloat16
F32 = jnp.float32
MESH = pl.DeviceIdType.MESH
VMEM = pltpu.VMEM
DMA = pltpu.SemaphoreType.DMA

HEAD = 64
NH = 3
EPS = 1e-05
HEADS = (0, 64, 128)
SCALE = HEAD**-0.5
TOK = 128
D = 768
SH = 32
KEYS = 256
QW = NH * HEAD
RINGS = (2, 1, 3)

A_BO, A_IG, A_Y1, A_Y2, A_DR2, A_DRC, A_DR1 = 0, 2, 4, 6, 7, 9, 10
N_AG = 12
R_SA, R_FF, R_CR, R_DFF, R_DQ, R_DSA, R_DST = 0, 2, 4, 5, 7, 8, 10
N_RS = 11
BLOCKS = {"ffd": 768, "ffo": 384, "ffi": 384, "crx": 384, "sad": 384, "sae": 384}
WORKER = {"ffd": 1, "crx": 1, "sad": 1, "ffo": 0, "ffi": 0, "sae": 1}
OWNER = {"ffd": 1, "sad": 1, "ffo": 0, "ffi": 0, "sae": 0}
WHOLE = ()
GROUP = {"ffd": "a", "crx": "b", "ffo": "b", "sad": "c", "ffi": "c", "sae": "d"}
SECOND_RS = (R_SA + 1, R_DSA + 1)
SECOND_AG = (A_BO + 1, A_IG + 1, A_Y1 + 1)


def nn(a, b):
    return jnp.dot(a, b, preferred_element_type=F32)


def nt(a, b):
    return lax.dot_general(a, b, (((1,), (1,)), ((), ())), preferred_element_type=F32)


def tn(a, b):
    return lax.dot_general(a, b, (((0,), (0,)), ((), ())), preferred_element_type=F32)


def scratch_list():
    out = [
        ("xin", VMEM((2, TOK, D), BF)),
        ("nv", VMEM((2, 2, 2, D), F32)),
        ("wsa", VMEM((2, 768, D), BF)),
        ("wff", VMEM((2, 2, 768, D), BF)),
        ("wcr", VMEM((768, D), BF)),
        ("cot", VMEM((TOK, D), BF)),
        ("pk", VMEM((2, 3 * QW, TOK), BF)),
        ("pt", VMEM((2, NH, TOK, TOK), F32)),
        ("ot", VMEM((2, QW, TOK), BF)),
        ("n1", VMEM((2, SH, D), F32)),
        ("n2", VMEM((2, SH, D), F32)),
        ("nc", VMEM((SH, D), F32)),
        ("sp", VMEM((5, SH, 128), F32)),
        ("y1f", VMEM((2, SH, D), F32)),
        ("y2f", VMEM((SH, D), F32)),
        ("dres", VMEM((2, SH, D), F32)),
        ("act", VMEM((2, TOK, D), BF)),
        ("slope", VMEM((2, TOK, D), F32)),
        ("hid", VMEM((TOK, D), F32)),
        ("du", VMEM((2, TOK, D), BF)),
        ("dpk", VMEM((2, 3 * QW, TOK), BF)),
        ("qct", VMEM((QW, TOK), BF)),
        ("dqct", VMEM((QW, TOK), BF)),
        ("kvct", VMEM((2 * QW, KEYS), BF)),
        ("dkvct", VMEM((2 * QW, KEYS), BF)),
        ("ptc", VMEM((NH, KEYS, TOK), F32)),
        ("oct", VMEM((QW, TOK), BF)),
        ("pos", VMEM((2, 4, 8, KEYS), jnp.int32)),
        ("hot", VMEM((2, 4, 4 * TOK, KEYS), BF)),
        ("kvt", VMEM((2, 4, QW, TOK), BF)),
        ("kvf", VMEM((2, 4, QW, KEYS), F32)),
        ("kvs", VMEM((2, 4, QW, KEYS), BF)),
        ("kvr", VMEM((2, 3, QW, KEYS), BF)),
        ("dkr", VMEM((2, 3, QW, KEYS), BF)),
        ("dkf", VMEM((2, 4, QW, TOK), F32)),
        ("dks", VMEM((2, 4, QW, TOK), BF)),
        ("dk2", VMEM((2, 3, QW, TOK), BF)),
        ("dkv", VMEM((2 * QW, TOK), BF)),
        ("vec", VMEM((16, D), F32)),
        ("vx", VMEM((4, 16, D), BF)),
        ("vc", VMEM((2, 16, D), BF)),
        ("vy", VMEM((4, 16, D), BF)),
        ("vz", VMEM((4, 16, D), BF)),
        ("ag", VMEM((N_AG, TOK, D), BF)),
        ("rs", VMEM((N_RS, TOK, D), BF)),
        ("rr", VMEM((N_RS, 3, SH, D), BF)),
        ("m_w", DMA((2, 7))),
        ("m_ws", DMA((7,))),
        ("m_l", DMA((4,))),
        ("m_ags", DMA((2, 3))),
        ("m_agr", DMA((2, 3))),
        ("m_rss", DMA((2, 3))),
        ("m_rsr", DMA((2, 3))),
        ("m_dps", DMA((18,))),
        ("m_kvr", DMA((18,))),
        ("m_dkr", DMA((12,))),
        ("m_vr", DMA((10,))),
        ("m_hs", DMA((2,))),
        ("m_hr", DMA((3,))),
        ("m_g0", DMA((len(BLOCKS), 2))),
        ("f_sae", DMA((2, 4))),
        ("m_o", DMA((2,))),
    ]
    for name, rows in BLOCKS.items():
        out += [
            ("g_" + name, VMEM((2, 2, rows, 384), BF)),
            ("x_" + name, VMEM((2, 2, rows, 384), BF)),
            ("h_" + name, VMEM((2, 2, 2, rows // 8, 384), BF)),
            ("a_" + name, VMEM((2, 3 if name == "sae" else 2, 2, rows // 4, 384), BF)),
            (
                "b_" + name,
                VMEM((2, 4, 2, rows // 4, 384) if name in WHOLE else (2, 3, rows // 8, 384), BF),
            ),
        ]
    for group in sorted(set(GROUP.values())):
        out.append(("s_" + group, DMA((2, 4 if group == GROUP["sae"] else 3))))
        out.append(("r_" + group, DMA((2, 9 if group == GROUP["sae"] else 11))))
    return out


class Refs:
    pass


def ln_forward(r, gain, bias):
    center = r - jnp.mean(r, axis=-1, keepdims=True)
    spread = lax.rsqrt(jnp.mean(center * center, axis=-1, keepdims=True) + EPS)
    n = center * spread
    return n * gain + bias, n, spread


def ln_backward(n, spread, gain, dy):
    s = dy * gain
    dr = spread * (
        s - jnp.mean(s, axis=-1, keepdims=True) - n * jnp.mean(s * n, axis=-1, keepdims=True)
    )
    return dr, jnp.sum(dy * n, axis=0, keepdims=True), jnp.sum(dy, axis=0, keepdims=True)


def kernel(names, n_in, n_out, *refs):
    (x_h, cot_h, dgr, ret, ng_h, nb_h, cg, cb, qkv_h, out_h, win_h, wfo_h, cq_h, ckv_h, co_h) = refs[
        :n_in
    ]
    bo_o, ig_o, of_o, os_o, oc_o, on_o, oe_o = refs[n_in : n_in + n_out]
    R = Refs()
    for name, ref in zip(names, refs[n_in + n_out :]):
        setattr(R, name, ref)
    c = lax.axis_index("section")
    t = lax.axis_index("tensor")
    d = lax.axis_index("dp")
    o = 1 - c
    y = lax.rem(d, 4)
    z = d // 4
    p = y + c * (z - y)
    q = z + c * (y - z)
    sp, sq = 1 + 3 * c, 4 - 3 * c
    rows_t = pl.ds(pl.multiple_of(t * SH, SH), SH)

    def dev_x(k):
        return (c, lax.rem(t + k, 4), d)

    def dp_p(k):
        return lax.rem(p + k, 4) * sp + q * sq

    def dev_p(k):
        return (c, t, dp_p(k))

    def dev_q(k):
        return (c, t, p * sp + lax.rem(q + k, 4) * sq)

    def dev_y(k):
        return (c, t, z * 4 + lax.rem(y + k, 4))

    def dev_z(k):
        return (c, t, lax.rem(z + k, 4) * 4 + y)

    dev_c = (o, t, d)
    sends = {}

    def flush(kind, keep=0):
        queue = sends.get(kind, [])
        while len(queue) > keep:
            queue.pop(0).wait_send()

    def push(src, dst, ss, rs, dev, kind="", wait=True):
        cp = pltpu.make_async_remote_copy(
            src_ref=src, dst_ref=dst, send_sem=ss, recv_sem=rs, device_id=dev, device_id_type=MESH
        )
        cp.start()
        if wait:
            sends.setdefault(kind, []).append(cp)
        return cp

    def landed(dst, rs, dev):
        pltpu.make_async_remote_copy(
            src_ref=dst, dst_ref=dst, send_sem=rs, recv_sem=rs, device_id=dev, device_id_type=MESH
        ).wait_recv()

    def places(s):
        return [
            R.xin.at[s],
            R.wsa.at[s, pl.ds(0, 576)],
            R.wsa.at[s, pl.ds(576, 192)],
            R.nv.at[s, 0],
            R.nv.at[s, 1],
            R.wff.at[s, 0],
            R.wff.at[s, 1],
        ]

    items = [x_h.at[c], qkv_h, out_h, ng_h, nb_h, win_h, wfo_h]

    def own(i):
        pltpu.make_async_copy(items[i], places(c)[i], R.m_w.at[c, i]).start()

    def other(i):
        src = x_h.at[o] if i == 0 else items[i]
        push(src, places(c)[i], R.m_ws.at[i], R.m_w.at[c, i], dev_c)

    for i in range(3):
        own(i)
    bar = pltpu.get_barrier_semaphore()
    peers = [dev_c] + [dev(k) for k in (1, 2, 3) for dev in (dev_x, dev_y, dev_z)]
    across = [(o,) + dev(k)[1:] for k in (1, 2, 3) for dev in (dev_y, dev_z)]

    def greet(devices):
        for dev in devices:
            pl.semaphore_signal(bar, inc=1, device_id=dev, device_id_type=MESH)

    greet(peers)

    @pl.when(c == 0)
    def _():
        greet(across)

    for i in (3, 4):
        own(i)
    singles = [
        pltpu.make_async_copy(cq_h, R.wcr.at[pl.ds(0, 192)], R.m_l.at[0]),
        pltpu.make_async_copy(co_h, R.wcr.at[pl.ds(192, 192)], R.m_l.at[1]),
        pltpu.make_async_copy(ckv_h, R.wcr.at[pl.ds(384, 384)], R.m_l.at[2]),
        pltpu.make_async_copy(cot_h.at[c], R.cot, R.m_l.at[3]),
    ]

    def enter():
        pl.semaphore_wait(bar, len(peers) + c * len(across))
        for i in range(3):
            other(i)

    def rest():
        for i in (3, 4):
            other(i)
        for i in (5, 6):
            own(i)
            other(i)
        for cp in singles:
            cp.start()

    def need(s, i):
        src = x_h.at[s] if i == 0 else items[i]
        pltpu.make_async_copy(src, places(s)[i], R.m_w.at[s, i]).wait()

    def rs_start(i, value):
        m = int(i in SECOND_RS)
        flush(("rs", m))
        R.rs[i] = value.astype(BF)
        for k in RINGS:
            to = lax.rem(t + k, 4)
            push(
                R.rs.at[i, pl.ds(pl.multiple_of(to * SH, SH), SH)],
                R.rr.at[i, k - 1],
                R.m_rss.at[m, k - 1],
                R.m_rsr.at[m, k - 1],
                dev_x(k),
                ("rs", m),
            )

    def rs_sum(i):
        for k in (1, 3, 2):
            landed(R.rr.at[i, k - 1], R.m_rsr.at[int(i in SECOND_RS), k - 1], dev_x(k))
        total = R.rs[i, rows_t, :].astype(F32)
        for k in range(3):
            total += R.rr[i, k].astype(F32)
        return total

    def ag_start(i, value):
        m = int(i in SECOND_AG)
        flush(("ag", m))
        R.ag[i, rows_t, :] = value.astype(BF)
        for k in RINGS:
            push(
                R.ag.at[i, rows_t],
                R.ag.at[i, rows_t],
                R.m_ags.at[m, k - 1],
                R.m_agr.at[m, k - 1],
                dev_x(k),
                ("ag", m),
            )

    def ag_wait(i):
        for k in (1, 3, 2):
            landed(R.ag.at[i, rows_t], R.m_agr.at[int(i in SECOND_AG), k - 1], dev_x(k))

    def gain_row(s, i):
        return R.nv[s, 0, i : i + 1, :]

    def bias_row(s, i):
        return R.nv[s, 1, i : i + 1, :]

    cross_gain = cg[...].reshape(1, D)
    cross_bias = cb[...].reshape(1, D)

    def softmax(scores):
        tops = [jnp.max(st, axis=0, keepdims=True) for st in scores]
        exps = [jnp.exp(st - top) for st, top in zip(scores, tops)]
        sums = [jnp.sum(e, axis=0, keepdims=True) for e in exps]
        return [e / total for e, total in zip(exps, sums)]

    def attend_backward(qts, kts, vts, prs, dots):
        heads = range(NH)
        dpts = [tn(vts[h], dots[h]) for h in heads]
        dvts = [nt(dots[h], prs[h].astype(BF)) for h in heads]
        sums = [jnp.sum(dpts[h] * prs[h], axis=0, keepdims=True) for h in heads]
        dsts = [(prs[h] * (dpts[h] - sums[h])).astype(BF) for h in heads]
        dqts = [nn(kts[h], dsts[h]) * SCALE for h in heads]
        dkts = [nt(qts[h], dsts[h]) * SCALE for h in heads]
        return dqts, dkts, dvts

    def self_forward(s):
        need(s, 0)
        need(s, 1)
        R.pk[s] = nt(R.wsa[s, 0:576, :], R.xin[s]).astype(BF)
        scores = [
            tn(R.pk[s, QW + lo : QW + lo + 64, :], R.pk[s, lo : lo + 64, :]) * SCALE for lo in HEADS
        ]
        if s == 1:
            key = lax.broadcasted_iota(jnp.int32, (TOK, TOK), 0)
            qry = lax.broadcasted_iota(jnp.int32, (TOK, TOK), 1)
            scores = [jnp.where(key <= qry, st, -1000000000.0) for st in scores]
        probs = softmax(scores)
        for h, lo in enumerate(HEADS):
            vt = R.pk[s, 2 * QW + lo : 2 * QW + lo + 64, :]
            R.ot[s, lo : lo + 64, :] = nn(vt, probs[h].astype(BF)).astype(BF)
            R.pt[s, h] = probs[h]
        need(s, 2)
        value = tn(R.ot[s], R.wsa[s, 576:768, :])
        if s == 0:
            enter()
        rs_start(R_SA + s, value)

    def put_norm(slot, spread):
        R.sp[slot] = jnp.broadcast_to(spread, (SH, 128))

    def get_norm(slot):
        return R.sp[slot, :, 0:1]

    def self_finish(s):
        total = rs_sum(R_SA + s)
        r = R.xin[s, rows_t, :].astype(F32) + total
        need(s, 3)
        need(s, 4)
        out, n, spread = ln_forward(r, gain_row(s, 0), bias_row(s, 0))
        ag_start(A_Y1 + s, out)
        R.y1f[s] = out
        R.n1[s] = n
        put_norm(s, spread)

    def ffn_forward(s, gathered):
        u = nn(R.ag[gathered], R.wff[s, 0])
        cdf = 0.5 * (1.0 + lax.erf(u * 0.7071067811865476))
        R.act[s] = (u * cdf).astype(BF)
        R.hid[...] = u
        R.slope[s] = cdf
        rs_start(R_FF + s, nn(R.act[s], R.wff[s, 1]))
        u = R.hid[...]
        R.slope[s] += u * jnp.exp(-0.5 * u * u) * 0.3989422804014327

    def ffn_backward(s):
        ag_wait(A_DR2 + s)
        dg = nt(R.ag[A_DR2 + s], R.wff[s, 1])
        R.du[s] = (dg * R.slope[s]).astype(BF)
        rs_start(R_DFF + s, nt(R.du[s], R.wff[s, 0]))

    def put(ref, piece, r0, value):
        rows = value.shape[0]
        ref[piece, 0, r0 : r0 + rows, :] = value[:, 0:384].astype(BF)
        ref[piece, 1, r0 : r0 + rows, :] = value[:, 384:768].astype(BF)

    def out_grad(s):
        return tn(R.act[s], R.ag[A_DR2 + s])

    def in_grad(s, gathered):
        return tn(R.ag[gathered], R.du[s])

    def put_halves(ref, value):
        put(ref, 0, 0, value[0:384])
        put(ref, 1, 0, value[384:768])

    def blk(name):
        bufs = tuple(getattr(R, pre + name) for pre in ("g_", "x_", "h_", "a_", "b_"))
        return bufs + (getattr(R, "s_" + GROUP[name]), getattr(R, "r_" + GROUP[name]))

    place = ((y, z), (z, y))
    devs = ((dev_y, dev_z), (dev_z, dev_y))

    def quarter(name, where):
        rows = BLOCKS[name] // 4
        return pl.ds(pl.multiple_of(where * rows, rows), rows)

    def eighth(name, where, half):
        rows = BLOCKS[name] // 8
        return pl.ds(pl.multiple_of(where * 2 * rows + half * rows, rows), rows)

    def step(where, k):
        return lax.rem(where + k, 4)

    def work(name):
        return pl.when(c == WORKER[name])

    def gone(src, sem):
        pltpu.make_async_remote_copy(
            src_ref=src, dst_ref=src, send_sem=sem, recv_sem=sem, device_id=dev_c, device_id_type=MESH
        ).wait_send()

    def ship(src, dst, ss, rs, dev):
        push(src, dst, ss, rs, dev, wait=False)

    def result(name, i, rows, half=slice(None)):
        if name == "crx":
            return oc_o.at[i, half, rows]
        if name == "ffd":
            return of_o.at[i, half, rows]
        if name in ("ffi", "ffo"):
            rows = pl.ds(pl.multiple_of(i * 384 + rows.start, 48), rows.size)
            return of_o.at[int(name == "ffo"), half, rows]
        return os_o.at[i, half, rows]

    def spot(name, i, rows, half=slice(None)):
        return R.x_sae.at[i, half, rows] if name == "sae" else result(name, i, rows, half)

    def g0(name, pieces=(0, 1)):
        g, x = blk(name)[:2]

        @pl.when(c != WORKER[name])
        def _():
            for i in pieces:
                sem = R.m_g0.at[tuple(BLOCKS).index(name), i]
                ship(g.at[i], x.at[i], sem, blk(name)[6].at[i, 0], dev_c)

    def g1(name, pieces=(0, 1)):
        g, x, h, a, b, s, r = blk(name)

        @work(name)
        def _():
            for i in pieces:
                landed(x.at[i], r.at[i, 0], dev_c)
                g[i] = g[i] + x[i]
                if name == "sae":
                    for k in RINGS:
                        part = g.at[i, :, quarter(name, step(place[i][0], k))]
                        ship(part, a.at[i, k - 1], s.at[i, k - 1], r.at[i, k], devs[i][0](k))
                    continue
                far = step(place[i][0], 2)
                for j, k in ((0, 1), (1, 3)):
                    part = g.at[i, :, eighth(name, far, j)]
                    ship(part, h.at[i, j], s.at[i, j], r.at[i, 1 + j], devs[i][0](k))

    def g1b(name, pieces=(0, 1)):
        g, x, h, a, b, s, r = blk(name)

        @work(name)
        def _():
            for j, k in ((0, 1), (1, 3)):
                for i in pieces:
                    near = step(place[i][0], k)
                    landed(h.at[i, j], r.at[i, 1 + j], dev_c)
                    part = eighth(name, near, j)
                    g[i, :, part, :] = g[i, :, part, :] + h[i, j]
                    part = g.at[i, :, quarter(name, near)]
                    gone(h.at[i, j], s.at[i, j])
                    ship(part, a.at[i, j], s.at[i, j], r.at[i, 3 + j], devs[i][0](k))

    def sub(name, i, where):
        return eighth(name, place[i][0], where // 2), lax.rem(where, 2)

    def g2(name, pieces=(0, 1)):
        g, x, h, a, b, s, r = blk(name)

        @work(name)
        def _():
            for i in pieces:
                mine = quarter(name, place[i][0])
                total = g[i, :, mine, :].astype(F32)
                for j in range(a.shape[1]):
                    landed(a.at[i, j], r.at[i, j + (1 if name == "sae" else 3)], dev_c)
                    total += a[i, j].astype(F32)
                    gone(a.at[i, j], s.at[i, j])
                g[i, :, mine, :] = total.astype(BF)
                if name in WHOLE:
                    part = g.at[i, :, mine]
                    for k in RINGS:
                        dst = b.at[i, place[i][1]]
                        ship(part, dst, s.at[i, k - 1], r.at[i, 4 + k], devs[i][1](k))
                    continue
                for k in RINGS:
                    rows, half = sub(name, i, step(place[i][1], k))
                    part = g.at[i, half, rows]
                    ship(part, b.at[i, k - 1], s.at[i, k - 1], r.at[i, 4 + k], devs[i][1](k))

    def g3(name, pieces=(0, 1)):
        g, x, h, a, b, s, r = blk(name)

        @work(name)
        def _():
            for i in pieces:
                if name in WHOLE:
                    mine = quarter(name, place[i][0])
                    b[i, place[i][1]] = g[i, :, mine, :]
                    for k in (1, 3, 2):
                        landed(a.at[i, 0], r.at[i, 4 + k], dev_c)
                        gone(a.at[i, 0], s.at[i, k - 1])
                    total = b[i, 0].astype(F32)
                    for j in (1, 2, 3):
                        total += b[i, j].astype(F32)
                    spot(name, i, mine)[...] = total.astype(BF)
                    continue
                for k in (1, 3, 2):
                    landed(b.at[i, k - 1], r.at[i, 4 + k], dev_c)
                rows, half = sub(name, i, place[i][1])
                total = g[i, half, rows, :].astype(F32)
                for k in range(3):
                    total += b[i, k].astype(F32)
                part = spot(name, i, rows, half)
                part[...] = total.astype(BF)
                for k in RINGS:
                    gone(b.at[i, k - 1], s.at[i, k - 1])
                    ship(part, part, s.at[i, k - 1], r.at[i, (3, 4, 8)[k - 1]], devs[i][1](k))

    def g4(name, pieces=(0, 1)):
        g, x, h, a, b, s, r = blk(name)

        @work(name)
        def _():
            for i in pieces:
                mine = quarter(name, place[i][0])
                part = spot(name, i, mine)
                for k in () if name in WHOLE else (1, 3, 2):
                    landed(b.at[i, k - 1], r.at[i, (3, 4, 8)[k - 1]], dev_c)
                    gone(b.at[i, k - 1], s.at[i, k - 1])
                if name == "sae":
                    dst = result(name, i, mine)
                    for k in RINGS:
                        to = (OWNER[name],) + devs[i][0](k)[1:]
                        ship(part, dst, s.at[i, k - 1], R.f_sae.at[i, k], to)
                    ship(part, dst, s.at[i, 3], R.f_sae.at[i, 0], dev_c)
                    continue
                for j, k in ((0, 1), (1, 3)):
                    ship(part, part, s.at[i, j], r.at[i, 2 - j], devs[i][0](k))

    def g4b(name, pieces=(0, 1)):
        g, x, h, a, b, s, r = blk(name)

        @work(name)
        def _():
            for j, k in ((0, 1), (1, 3)):
                for i in pieces:
                    behind = step(place[i][0], 4 - k)
                    landed(a.at[i, j], r.at[i, 2 - j], dev_c)
                    gone(a.at[i, j], s.at[i, j])
                    rows = eighth(name, behind, j)
                    part = spot(name, i, rows)
                    ship(part, part, s.at[i, j], r.at[i, 9 + j], devs[i][0](k))

    def g5(name):
        g, x, h, a, b, s, r = blk(name)

        @work(name)
        def _():
            for i in (0, 1):
                for j in (0, 1):
                    landed(h.at[i, j], r.at[i, 9 + j], dev_c)
            if name == "crx":
                ship(oc_o, oc_o, s.at[0, 2], R.m_hr.at[2], dev_c)

    def g6(name):
        g, x, h, a, b, s, r = blk(name)

        @pl.when(c != WORKER[name])
        def _():
            for i in (0, 1):
                gone(g.at[i], R.m_g0.at[tuple(BLOCKS).index(name), i])
            if name == "crx":
                landed(oc_o, R.m_hr.at[2], dev_c)
            if name == "sae":
                for i in (0, 1):
                    for j in range(4):
                        landed(a.at[i, 0], R.f_sae.at[i, j], dev_c)

        @work(name)
        def _():
            for i in (0, 1):
                if name == "sae":
                    for j in range(4):
                        gone(a.at[i, 0], s.at[i, j])
                    continue
                for j in (0, 1):
                    gone(h.at[i, j], s.at[i, j])
            if name == "crx":
                gone(oc_o, s.at[0, 2])

    def vec_put(row, dg, db, step=2):
        R.vec[row : row + 1, :] = dg
        R.vec[row + step : row + step + 1, :] = db

    def vec_send(buf, at, value, base, dev, count):
        buf[at] = value.astype(BF)
        for k in range(1, count):
            push(buf.at[at], buf.at[at], R.m_dps.at[base + k - 1], R.m_vr.at[base + k - 1], dev(k))

    def vec_sum(buf, at, base, dev, count):
        for k in range(1, count):
            landed(buf.at[at], R.m_vr.at[base + k - 1], dev(k))
        total = buf[0].astype(F32)
        for k in range(1, count):
            total += buf[k].astype(F32)
        return total

    def dev_c1(k):
        return dev_c

    self_forward(0)
    rest()
    for j in (10, 11, 12, 13, 14, 15):
        R.vec[j : j + 1, :] = jnp.zeros((1, D), F32)

    micro = lax.broadcasted_iota(jnp.int32, (2, 16), 0)
    group = lax.broadcasted_iota(jnp.int32, (2, 16), 1)
    live = (micro == c) & (group <= d) & (dgr[...] > 0)
    start = jnp.max(jnp.where(live, group, 0), axis=1, keepdims=True)
    start = jnp.max(start, axis=0, keepdims=True)
    rows = jnp.where(c == 0, ret[0], ret[1]) + start * TOK
    g_at = rows // TOK
    b_at = jnp.where(c == 0, g_at, lax.rem(g_at, 4) * 4 + g_at // 4)
    at = b_at * TOK + lax.rem(rows, TOK)
    first = (p, q)
    dev_first, dev_second = (dev_p, dev_q), (dev_q, dev_p)
    for u in (0, 1):
        R.pos[u, 0] = jnp.broadcast_to(at, (8, KEYS))
        for k in RINGS:
            m = 3 * u + k - 1
            push(R.pos.at[u, 0], R.pos.at[u, k], R.m_dps.at[m], R.m_kvr.at[m], dev_second[u](k))
    self_finish(0)
    ag_wait(A_Y1)
    need(0, 5)
    need(0, 6)
    ffn_forward(0, A_Y1)

    for cp in singles:
        cp.wait()
    for u in (0, 1):
        for k in (1, 3, 2):
            landed(R.pos.at[u, k], R.m_kvr.at[3 * u + k - 1], dev_c)

    def build(i, carry):
        rows = pl.ds(pl.multiple_of(i * TOK, TOK), TOK)
        for u in (0, 1):
            block = q * 4 + i if u == 0 else i * 4 + p
            n = lax.broadcasted_iota(jnp.int32, (TOK, KEYS), 0) + block * TOK
            for k in range(4):
                R.hot[u, k, rows, :] = jnp.where(n == R.pos[u, k, 0:1, :], 1.0, 0.0).astype(BF)
        return carry

    lax.fori_loop(0, 4, build, 0)

    out, n, spread = ln_forward(R.y1f[0] + rs_sum(R_FF), gain_row(0, 1), bias_row(0, 1))
    ag_start(A_BO, out)
    R.n2[0] = n
    put_norm(2, spread)
    self_forward(1)
    ag_wait(A_BO)

    def hot(u, k, j):
        return R.hot[u, k, pl.ds(pl.multiple_of(j * TOK, TOK), TOK), :]

    def picked(u, k, j):
        return nn(R.kvt[u, j], hot(u, k, j))

    for u in (0, 1):
        R.kvt[u, first[u]] = nt(R.wcr[384 + u * QW : 384 + u * QW + QW, :], R.ag[A_BO]).astype(BF)
        for k in RINGS:
            part, m = R.kvt.at[u, first[u]], 6 + 3 * u + k - 1
            push(part, part, R.m_dps.at[m], R.m_kvr.at[m], dev_first[u](k))
    self_finish(1)
    for u in (0, 1):
        for k in range(4):
            R.kvf[u, k] = picked(u, k, first[u])
    for u in (0, 1):
        for j in (1, 3):
            landed(R.kvt.at[u, 0], R.m_kvr.at[6 + 3 * u + j - 1], dev_c)
            for k in range(4):
                R.kvf[u, k] += picked(u, k, lax.rem(first[u] + 4 - j, 4))
        landed(R.kvt.at[u, 0], R.m_kvr.at[6 + 3 * u + 1], dev_c)
        for k in RINGS + (0,):
            R.kvs[u, k] = (R.kvf[u, k] + picked(u, k, lax.rem(first[u] + 2, 4))).astype(BF)
            if k:
                m = 12 + 3 * u + 3 - k
                dst = R.kvr.at[u, 3 - k]
                push(R.kvs.at[u, k], dst, R.m_dps.at[m], R.m_kvr.at[m], dev_second[u](4 - k))
    ag_wait(A_Y1 + 1)
    R.qct[...] = nt(R.wcr[0:192, :], R.ag[A_Y1 + 1]).astype(BF)

    def chosen(u):
        for k in (1, 3, 2):
            landed(R.kvr.at[u, k - 1], R.m_kvr.at[12 + 3 * u + k - 1], dev_c)
        total = R.kvs[u, 0].astype(F32)
        for k in range(3):
            total += R.kvr[u, k].astype(F32)
        R.kvct[u * QW : u * QW + QW, :] = total.astype(BF)

    chosen(0)
    probs = softmax(
        [tn(R.kvct[lo : lo + 64, :], R.qct[lo : lo + 64, :]) * SCALE for lo in HEADS]
    )
    chosen(1)
    for h, lo in enumerate(HEADS):
        vt = R.kvct[QW + lo : QW + lo + 64, :]
        R.oct[lo : lo + 64, :] = nn(vt, probs[h].astype(BF)).astype(BF)
        R.ptc[h] = probs[h]
    rs_start(R_CR, tn(R.oct[...], R.wcr[192:384, :]))
    need(1, 5)
    need(1, 6)
    out, n, spread = ln_forward(R.y1f[1] + rs_sum(R_CR), cross_gain, cross_bias)
    ag_start(A_Y2, out)
    R.y2f[...] = out
    R.nc[...] = n
    put_norm(4, spread)
    ag_wait(A_Y2)
    ffn_forward(1, A_Y2)
    out, n, spread = ln_forward(R.y2f[...] + rs_sum(R_FF + 1), gain_row(1, 1), bias_row(1, 1))

    dr, dg, db = ln_backward(n, spread, gain_row(1, 1), R.cot[rows_t, :].astype(F32))
    ag_start(A_DR2 + 1, dr)
    R.dres[1] = dr
    vec_put(5, dg, db)
    ffn_backward(1)
    ag_start(A_BO + 1, out)
    flush("")
    put(R.g_ffd, 0, 0, in_grad(1, A_Y2))
    g0("ffd", (0,))
    put(R.g_ffd, 1, 0, out_grad(1))
    g0("ffd", (1,))
    dy = R.dres[1] + rs_sum(R_DFF + 1)
    dr, dg, db = ln_backward(R.nc[...], get_norm(4), cross_gain, dy)
    ag_start(A_DRC, dr)
    R.dres[1] = dr
    vec_put(8, dg, db, 1)
    g1("ffd")
    ag_wait(A_DRC)

    def compact(u):
        for k in RINGS:
            m = 3 * u + k - 1
            part = R.dkvct.at[pl.ds(u * QW, QW)]
            push(part, R.dkr.at[u, k - 1], R.m_dps.at[m], R.m_dkr.at[m], dev_second[u](k))

    doc = nt(R.wcr[192:384, :], R.ag[A_DRC]).astype(BF)
    heads = list(enumerate(HEADS))
    for h, lo in heads:
        dvt = nt(doc[lo : lo + 64, :], R.ptc[h].astype(BF))
        R.dkvct[QW + lo : QW + lo + 64, :] = dvt.astype(BF)
    compact(1)
    dpts = [tn(R.kvct[QW + lo : QW + lo + 64, :], doc[lo : lo + 64, :]) for h, lo in heads]
    sums = [jnp.sum(dpts[h] * R.ptc[h], axis=0, keepdims=True) for h, lo in heads]
    dsts = [(R.ptc[h] * (dpts[h] - sums[h])).astype(BF) for h, lo in heads]
    for h, lo in heads:
        dkt = nt(R.qct[lo : lo + 64, :], dsts[h]) * SCALE
        R.dkvct[lo : lo + 64, :] = dkt.astype(BF)
    compact(0)
    for h, lo in heads:
        dqt = nn(R.kvct[lo : lo + 64, :], dsts[h]) * SCALE
        R.dqct[lo : lo + 64, :] = dqt.astype(BF)
    rs_start(R_DQ, tn(R.dqct[...], R.wcr[0:192, :]))
    put(R.g_crx, 0, 0, nn(R.dqct[...], R.ag[A_Y1 + 1]))
    put(R.g_crx, 0, 192, nn(R.oct[...], R.ag[A_DRC]))
    g0("crx", (0,))
    dy = R.dres[1] + rs_sum(R_DQ)
    dr, dg, db = ln_backward(R.n1[1], get_norm(1), gain_row(1, 0), dy)
    ag_start(A_DR1 + 1, dr)
    R.dres[1] = dr
    vec_put(4, dg, db)
    g1b("ffd", (0,))

    def self_backward(s):
        ag_wait(A_DR1 + s)
        dot = nt(R.wsa[s, 576:768, :], R.ag[A_DR1 + s]).astype(BF)
        dqts, dkts, dvts = attend_backward(
            [R.pk[s, lo : lo + 64, :] for lo in HEADS],
            [R.pk[s, QW + lo : QW + lo + 64, :] for lo in HEADS],
            [R.pk[s, 2 * QW + lo : 2 * QW + lo + 64, :] for lo in HEADS],
            [R.pt[s, h] for h in range(NH)],
            [dot[lo : lo + 64, :] for lo in HEADS],
        )
        for h, lo in enumerate(HEADS):
            R.dpk[s, lo : lo + 64, :] = dqts[h].astype(BF)
            R.dpk[s, QW + lo : QW + lo + 64, :] = dkts[h].astype(BF)
            R.dpk[s, 2 * QW + lo : 2 * QW + lo + 64, :] = dvts[h].astype(BF)

    def self_grads(s, name):
        ref = getattr(R, "g_" + name)
        put(ref, 0, 0, nn(R.dpk[s, 0:384, :], R.xin[s]))
        g0(name, (0,))
        put(ref, 1, 0, nn(R.dpk[s, 384:576, :], R.xin[s]))
        put(ref, 1, 192, nn(R.ot[s], R.ag[A_DR1 + s]))
        g0(name, (1,))

    def input_part(s):
        rs_start(R_DSA + s, tn(R.dpk[s], R.wsa[s, 0:576, :]))

    for u in (1, 0):
        for j in range(4):
            R.dkf[u, j] = nt(R.dkvct[u * QW : u * QW + QW, :], hot(u, 0, j))
    for u in (1, 0):
        for k in (1, 3):
            landed(R.dkr.at[u, k - 1], R.m_dkr.at[3 * u + k - 1], dev_c)
            for j in range(4):
                R.dkf[u, j] += nt(R.dkr[u, k - 1], hot(u, k, j))
        landed(R.dkr.at[u, 1], R.m_dkr.at[3 * u + 1], dev_c)
        for k in RINGS + (0,):
            to = lax.rem(first[u] + k, 4)
            R.dks[u, to] = (R.dkf[u, to] + nt(R.dkr[u, 1], hot(u, 2, to))).astype(BF)
            if k:
                m = 6 + 3 * u + k - 1
                dst = R.dk2.at[u, k - 1]
                push(R.dks.at[u, to], dst, R.m_dps.at[m], R.m_dkr.at[m], dev_first[u](k))
    g1b("ffd", (1,))
    self_backward(1)
    input_part(1)
    self_grads(1, "sad")
    g1("crx", (0,))
    for u in (1, 0):
        for k in (1, 3, 2):
            landed(R.dk2.at[u, k - 1], R.m_dkr.at[6 + 3 * u + k - 1], dev_c)
        total = R.dks[u, first[u]].astype(F32)
        for k in range(3):
            total += R.dk2[u, k].astype(F32)
        R.dkv[u * QW : u * QW + QW, :] = total.astype(BF)
    rs_start(R_DST, tn(R.dkv[...], R.wcr[384:768, :]))
    put(R.g_crx, 1, 0, nn(R.dkv[...], R.ag[A_BO]))
    g0("crx", (1,))
    g2("ffd")
    g1("sad")
    g1b("crx", (0,))
    dy = rs_sum(R_DST)
    dr, dg, db = ln_backward(R.n2[0], get_norm(2), gain_row(0, 1), dy)
    ag_start(A_DR2, dr)
    R.dres[0] = dr
    vec_put(1, dg, db)
    flush("")
    ag_wait(A_BO + 1)
    push(R.ag.at[A_BO + o], bo_o.at[c], R.m_hs.at[0], R.m_hr.at[0], dev_c)
    outs = [pltpu.make_async_copy(R.ag.at[A_BO + c], bo_o.at[c], R.m_o.at[0])]
    outs[0].start()
    g3("ffd")
    g1("crx", (1,))
    g1b("sad")
    g2("crx", (0,))
    ffn_backward(0)
    put_halves(R.g_ffo, out_grad(0))
    g0("ffo")
    put_halves(R.g_ffi, in_grad(0, A_Y1))
    g0("ffi")
    g4("ffd")
    g1b("crx", (1,))
    g3("crx", (0,))
    g2("sad")
    g1("ffo")
    dy = R.dres[0] + rs_sum(R_DFF)
    dr, dg, db = ln_backward(R.n1[0], get_norm(0), gain_row(0, 0), dy)
    ag_start(A_DR1, dr)
    R.dres[0] = dr
    vec_put(0, dg, db)
    g1("ffi")
    g4b("ffd")
    g4("crx", (0,))
    g2("crx", (1,))
    g3("sad")
    g1b("ffo")
    self_backward(0)
    g1b("ffi")
    self_grads(0, "sae")
    vec_send(R.vx, t, R.vec[...], 0, dev_x, 4)
    input_part(0)
    ag_start(A_IG + 1, R.dres[1] + rs_sum(R_DSA + 1))
    g1("sae")
    g2("ffo")
    total = vec_sum(R.vx, t, 0, dev_x, 4)
    vec_send(R.vc, c, total, 3, dev_c1, 2)
    g3("crx", (1,))
    g4b("crx", (0,))
    g4("sad")
    g2("ffi")
    total = vec_sum(R.vc, c, 3, dev_c1, 2)
    vec_send(R.vy, y, total, 4, dev_y, 4)
    ag_start(A_IG, R.dres[0] + rs_sum(R_DSA))
    g3("ffo")
    g2("sae")
    g4("crx", (1,))
    g3("ffi")
    total = vec_sum(R.vy, y, 4, dev_y, 4)
    vec_send(R.vz, z, total, 7, dev_z, 4)
    g4("ffo")
    g3("sae")
    g4b("sad")
    g4b("crx", (1,))
    g4("ffi")
    g4("sae")
    g5("crx")
    ag_wait(A_IG)
    ag_wait(A_IG + 1)
    push(R.ag.at[A_IG + o], ig_o.at[c], R.m_hs.at[1], R.m_hr.at[1], dev_c)
    outs.append(pltpu.make_async_copy(R.ag.at[A_IG + c], ig_o.at[c], R.m_o.at[1]))
    outs[1].start()
    g4b("ffo")
    total = vec_sum(R.vz, z, 7, dev_z, 4)
    on_o[...] = jnp.where(c == 0, total[0:4, :], total[4:8, :])
    oe_o[...] = total[8:10, :]
    flush("")
    g4b("ffi")
    landed(bo_o.at[c], R.m_hr.at[0], dev_c)
    landed(ig_o.at[c], R.m_hr.at[1], dev_c)
    for cp in outs:
        cp.wait()
    g5("ffd")
    g5("sad")
    g5("ffo")
    g5("ffi")
    for name in ("ffd", "sad", "crx", "ffo", "ffi", "sae"):
        g6(name)
    for kind in list(sends):
        flush(kind)


JOBS = (
    [("gf", 0, r, "win", r) for r in (0, 192, 384, 576)]
    + [("gf", 1, r, "wfo", r) for r in (0, 192, 384, 576)]
    + [("gc", 0, 0, "q", 0), ("gc", 0, 192, "co", 0), ("gc", 1, 0, "kv", 0), ("gc", 1, 192, "kv", 192)]
    + [("gs", 0, 0, "qkv", 0), ("gs", 0, 192, "qkv", 192), ("gs", 1, 0, "qkv", 384)]
    + [("gs", 1, 192, "out", 0)]
)


def widen(*refs):
    bo, ig, gf, gs, gc, gn, ge = refs[:7]
    bo_o, ig_o, qkv_o, out_o, win_o, wfo_o, ng_o, nb_o, q_o, kv_o, co_o, cg_o, cb_o = refs[7:20]
    wide, ig_wide, m_out, m_x = refs[20:]
    from_ = {"gf": gf, "gs": gs, "gc": gc}
    to = {"qkv": qkv_o, "out": out_o, "win": win_o, "wfo": wfo_o, "q": q_o, "kv": kv_o, "co": co_o}
    stores = [pltpu.make_async_copy(bo, bo_o, m_x.at[0])]
    stores[0].start()
    for i, (src, piece, r0, dst, d0) in enumerate(JOBS):
        wide[i, :, 0:384] = from_[src][piece, 0, r0 : r0 + 192, :].astype(F32)
        wide[i, :, 384:768] = from_[src][piece, 1, r0 : r0 + 192, :].astype(F32)
        cp = pltpu.make_async_copy(wide.at[i], to[dst].at[pl.ds(d0, 192)], m_out.at[i])
        cp.start()
        stores.append(cp)
    ig_wide[...] = ig[...].astype(F32)
    stores.append(pltpu.make_async_copy(ig_wide, ig_o, m_x.at[1]))
    stores[-1].start()
    ng_o[...] = gn[0:2, :]
    nb_o[...] = gn[2:4, :]
    cg_o[...] = ge[0:1, :].reshape(D)
    cb_o[...] = ge[1:2, :].reshape(D)
    for cp in stores:
        cp.wait()


def body(
    layer_inputs,
    cotangent,
    doc_groups,
    retrieved_at,
    sa_qkv,
    sa_out,
    ffn_in,
    ffn_out,
    norm_gain,
    norm_bias,
    cross_q,
    cross_kv,
    cross_out,
    cross_gain,
    cross_bias,
):
    ins = (
        layer_inputs[0],
        cotangent,
        doc_groups,
        retrieved_at,
        norm_gain[0],
        norm_bias[0],
        cross_gain,
        cross_bias,
        jnp.transpose(sa_qkv[0], (1, 2, 0)).reshape(576, D),
        sa_out[0],
        ffn_in[0],
        ffn_out[0],
        jnp.transpose(cross_q, (1, 0)),
        jnp.transpose(cross_kv, (1, 2, 0)).reshape(384, D),
        cross_out,
    )
    hbm = pl.BlockSpec(memory_space=pl.ANY)
    vm = pl.BlockSpec(memory_space=VMEM)
    outs = (
        VMEM((2, TOK, D), BF),
        VMEM((2, TOK, D), BF),
        VMEM((2, 2, 768, 384), BF),
        VMEM((2, 2, 384, 384), BF),
        VMEM((2, 2, 384, 384), BF),
        VMEM((4, D), F32),
        VMEM((2, D), F32),
    )
    names = [n for n, _ in scratch_list()]

    def run(*refs):
        kernel(names, len(ins), len(outs), *refs)

    results = pl.pallas_call(
        run,
        out_shape=outs,
        in_specs=[hbm, hbm, vm, vm, hbm, hbm, vm, vm] + [hbm] * 7,
        out_specs=[vm] * len(outs),
        scratch_shapes=[s for _, s in scratch_list()],
        compiler_params=pltpu.CompilerParams(
            collective_id=0, has_side_effects=True, vmem_limit_bytes=52 << 20
        ),
        name="layers",
    )(*ins)
    wide_outs = (
        jax.ShapeDtypeStruct((2, TOK, D), BF),
        jax.ShapeDtypeStruct((2, TOK, D), F32),
        jax.ShapeDtypeStruct((576, D), F32),
        jax.ShapeDtypeStruct((192, D), F32),
        jax.ShapeDtypeStruct((768, D), F32),
        jax.ShapeDtypeStruct((768, D), F32),
        jax.ShapeDtypeStruct((2, D), F32),
        jax.ShapeDtypeStruct((2, D), F32),
        jax.ShapeDtypeStruct((192, D), F32),
        jax.ShapeDtypeStruct((384, D), F32),
        jax.ShapeDtypeStruct((192, D), F32),
        jax.ShapeDtypeStruct((D,), F32),
        jax.ShapeDtypeStruct((D,), F32),
    )
    bo, ig, d_qkv, d_out, d_in, d_fo, ng, nb, d_q, d_kv, d_co, dcg, dcb = pl.pallas_call(
        widen,
        out_shape=wide_outs,
        in_specs=[vm] * 7,
        out_specs=[hbm] * 6 + [vm] * 2 + [hbm] * 3 + [vm] * 2,
        scratch_shapes=[
            VMEM((len(JOBS), 192, D), F32),
            VMEM((2, TOK, D), F32),
            DMA((len(JOBS),)),
            DMA((2,)),
        ],
        compiler_params=pltpu.CompilerParams(vmem_limit_bytes=32 << 20),
        name="widen",
    )(*[pltpu.with_memory_space_constraint(r, VMEM) for r in results])
    return (
        bo[None],
        ig[None],
        jnp.transpose(d_qkv.reshape(3, 192, D), (2, 0, 1))[None],
        d_out[None],
        d_in[None],
        d_fo[None],
        ng[None],
        nb[None],
        jnp.transpose(d_q, (1, 0)),
        jnp.transpose(d_kv.reshape(2, 192, D), (2, 0, 1)),
        d_co,
        dcg,
        dcb,
    )


def solution(mesh):
    placed = (
        P("section", None, "dp", None),
        P(None, "dp", None),
        P(),
        P(None, "dp", None),
        P("section", None, None, "tensor"),
        P("section", "tensor", None),
        P("section", None, "tensor"),
        P("section", "tensor", None),
        P("section", None, None),
        P("section", None, None),
        P(None, "tensor"),
        P(None, None, "tensor"),
        P("tensor", None),
        P(),
        P(),
    )
    return jax.shard_map(
        body,
        mesh=mesh,
        in_specs=placed,
        out_specs=(
            P("section", None, "dp", None),
            P("section", None, "dp", None),
            P("section", None, None, "tensor"),
            P("section", "tensor", None),
            P("section", None, "tensor"),
            P("section", "tensor", None),
            P("section", None, None),
            P("section", None, None),
            P(None, "tensor"),
            P(None, None, "tensor"),
            P("tensor", None),
            P(),
            P(),
        ),
        check_vma=False,
    )
```

```python
import jax
import jax.numpy as jnp
from jax import lax
from jax.experimental import pallas as pl
from jax.experimental.pallas import tpu as pltpu
from jax.sharding import PartitionSpec as P

BF = jnp.bfloat16
F32 = jnp.float32
MESH = pl.DeviceIdType.MESH
VMEM = pltpu.VMEM
DMA = pltpu.SemaphoreType.DMA

HEAD = 64
NH = 3
EPS = 1e-05
HEADS = (0, 64, 128)
SCALE = HEAD**-0.5
TOK = 128
D = 768
SH = 32
KEYS = 256
QW = NH * HEAD
RINGS = (2, 1, 3)

A_BO, A_IG, A_Y1, A_Y2, A_DR2, A_DRC, A_DR1 = 0, 2, 4, 6, 7, 9, 10
N_AG = 12
R_SA, R_FF, R_CR, R_DFF, R_DQ, R_DSA, R_DST = 0, 2, 4, 5, 7, 8, 10
N_RS = 11
BLOCKS = {"ffd": 768, "ffo": 384, "ffi": 384, "crx": 384, "sad": 384, "sae": 384}
WORKER = {"ffd": 1, "crx": 1, "sad": 1, "ffo": 0, "ffi": 0, "sae": 1}
OWNER = {"ffd": 1, "sad": 1, "ffo": 0, "ffi": 0, "sae": 0}
WHOLE = ()
GROUP = {"ffd": "a", "crx": "b", "ffo": "b", "sad": "c", "ffi": "c", "sae": "d"}
SECOND_RS = (R_SA + 1, R_DSA + 1)
SECOND_AG = (A_BO + 1, A_IG + 1, A_Y1 + 1)


def nn(a, b):
    return jnp.dot(a, b, preferred_element_type=F32)


def nt(a, b):
    return lax.dot_general(a, b, (((1,), (1,)), ((), ())), preferred_element_type=F32)


def tn(a, b):
    return lax.dot_general(a, b, (((0,), (0,)), ((), ())), preferred_element_type=F32)


def scratch_list():
    out = [
        ("xin", VMEM((2, TOK, D), BF)),
        ("nv", VMEM((2, 2, 2, D), F32)),
        ("wsa", VMEM((2, 768, D), BF)),
        ("wff", VMEM((2, 2, 768, D), BF)),
        ("wcr", VMEM((768, D), BF)),
        ("cot", VMEM((TOK, D), BF)),
        ("pk", VMEM((2, 3 * QW, TOK), BF)),
        ("pt", VMEM((2, NH, TOK, TOK), F32)),
        ("ot", VMEM((2, QW, TOK), BF)),
        ("n1", VMEM((2, SH, D), F32)),
        ("n2", VMEM((2, SH, D), F32)),
        ("nc", VMEM((SH, D), F32)),
        ("sp", VMEM((5, SH, 128), F32)),
        ("y1f", VMEM((2, SH, D), F32)),
        ("y2f", VMEM((SH, D), F32)),
        ("dres", VMEM((2, SH, D), F32)),
        ("act", VMEM((2, TOK, D), BF)),
        ("slope", VMEM((2, TOK, D), F32)),
        ("hid", VMEM((TOK, D), F32)),
        ("du", VMEM((2, TOK, D), BF)),
        ("dpk", VMEM((2, 3 * QW, TOK), BF)),
        ("qct", VMEM((QW, TOK), BF)),
        ("dqct", VMEM((QW, TOK), BF)),
        ("kvct", VMEM((2 * QW, KEYS), BF)),
        ("dkvct", VMEM((2 * QW, KEYS), BF)),
        ("ptc", VMEM((NH, KEYS, TOK), F32)),
        ("oct", VMEM((QW, TOK), BF)),
        ("pos", VMEM((2, 4, 8, KEYS), jnp.int32)),
        ("hot", VMEM((2, 4, 4 * TOK, KEYS), BF)),
        ("kvt", VMEM((2, 4, QW, TOK), BF)),
        ("kvf", VMEM((2, 4, QW, KEYS), F32)),
        ("kvs", VMEM((2, 4, QW, KEYS), BF)),
        ("kvr", VMEM((2, 3, QW, KEYS), BF)),
        ("dkr", VMEM((2, 3, QW, KEYS), BF)),
        ("dkf", VMEM((2, 4, QW, TOK), F32)),
        ("dks", VMEM((2, 4, QW, TOK), BF)),
        ("dk2", VMEM((2, 3, QW, TOK), BF)),
        ("dkv", VMEM((2 * QW, TOK), BF)),
        ("vec", VMEM((16, D), F32)),
        ("vx", VMEM((4, 16, D), BF)),
        ("vc", VMEM((2, 16, D), BF)),
        ("vy", VMEM((4, 16, D), BF)),
        ("vz", VMEM((4, 16, D), BF)),
        ("ag", VMEM((N_AG, TOK, D), BF)),
        ("rs", VMEM((N_RS, TOK, D), BF)),
        ("rr", VMEM((N_RS, 3, SH, D), BF)),
        ("m_w", DMA((2, 7))),
        ("m_ws", DMA((7,))),
        ("m_l", DMA((4,))),
        ("m_ags", DMA((2, 3))),
        ("m_agr", DMA((2, 3))),
        ("m_rss", DMA((2, 3))),
        ("m_rsr", DMA((2, 3))),
        ("m_dps", DMA((18,))),
        ("m_kvr", DMA((18,))),
        ("m_hs", DMA((2,))),
        ("m_hr", DMA((3,))),
        ("m_g0", DMA((len(BLOCKS), 2))),
        ("f_sae", DMA((2, 4))),
        ("m_o", DMA((2,))),
    ]
    for name, rows in BLOCKS.items():
        out += [
            ("g_" + name, VMEM((2, 2, rows, 384), BF)),
            ("x_" + name, VMEM((2, 2, rows, 384), BF)),
            ("h_" + name, VMEM((2, 2, 2, rows // 8, 384), BF)),
            ("a_" + name, VMEM((2, 3 if name == "sae" else 2, 2, rows // 4, 384), BF)),
            (
                "b_" + name,
                VMEM((2, 4, 2, rows // 4, 384) if name in WHOLE else (2, 3, rows // 8, 384), BF),
            ),
        ]
    for group in sorted(set(GROUP.values())):
        out.append(("s_" + group, DMA((2, 4 if group == GROUP["sae"] else 3))))
        out.append(("r_" + group, DMA((2, 8 if group == GROUP["sae"] else 10))))
    return out


class Refs:
    pass


def ln_forward(r, gain, bias):
    center = r - jnp.mean(r, axis=-1, keepdims=True)
    spread = lax.rsqrt(jnp.mean(center * center, axis=-1, keepdims=True) + EPS)
    n = center * spread
    return n * gain + bias, n, spread


def ln_backward(n, spread, gain, dy):
    s = dy * gain
    dr = spread * (
        s - jnp.mean(s, axis=-1, keepdims=True) - n * jnp.mean(s * n, axis=-1, keepdims=True)
    )
    return dr, jnp.sum(dy * n, axis=0, keepdims=True), jnp.sum(dy, axis=0, keepdims=True)


def kernel(names, n_in, n_out, *refs):
    (x_h, cot_h, dgr, ret, ng_h, nb_h, cg, cb, qkv_h, out_h, win_h, wfo_h, cq_h, ckv_h, co_h) = refs[
        :n_in
    ]
    bo_o, ig_o, of_o, os_o, oc_o, on_o, oe_o = refs[n_in : n_in + n_out]
    R = Refs()
    for name, ref in zip(names, refs[n_in + n_out :]):
        setattr(R, name, ref)
    c = lax.axis_index("section")
    t = lax.axis_index("tensor")
    d = lax.axis_index("dp")
    o = 1 - c
    y = lax.rem(d, 4)
    z = d // 4
    p = y + c * (z - y)
    q = z + c * (y - z)
    sp, sq = 1 + 3 * c, 4 - 3 * c
    rows_t = pl.ds(pl.multiple_of(t * SH, SH), SH)

    def dev_x(k):
        return (c, lax.rem(t + k, 4), d)

    def dp_p(k):
        return lax.rem(p + k, 4) * sp + q * sq

    def dev_p(k):
        return (c, t, dp_p(k))

    def dev_q(k):
        return (c, t, p * sp + lax.rem(q + k, 4) * sq)

    def dev_y(k):
        return (c, t, z * 4 + lax.rem(y + k, 4))

    def dev_z(k):
        return (c, t, lax.rem(z + k, 4) * 4 + y)

    dev_c = (o, t, d)
    sends = {}

    def flush(kind, keep=0):
        queue = sends.get(kind, [])
        while len(queue) > keep:
            queue.pop(0).wait_send()

    def push(src, dst, ss, rs, dev, kind="", wait=True):
        cp = pltpu.make_async_remote_copy(
            src_ref=src, dst_ref=dst, send_sem=ss, recv_sem=rs, device_id=dev, device_id_type=MESH
        )
        cp.start()
        if wait:
            sends.setdefault(kind, []).append(cp)
        return cp

    def landed(dst, rs, dev):
        pltpu.make_async_remote_copy(
            src_ref=dst, dst_ref=dst, send_sem=rs, recv_sem=rs, device_id=dev, device_id_type=MESH
        ).wait_recv()

    def places(s):
        return [
            R.xin.at[s],
            R.wsa.at[s, pl.ds(0, 576)],
            R.wsa.at[s, pl.ds(576, 192)],
            R.nv.at[s, 0],
            R.nv.at[s, 1],
            R.wff.at[s, 0],
            R.wff.at[s, 1],
        ]

    items = [x_h.at[c], qkv_h, out_h, ng_h, nb_h, win_h, wfo_h]

    def own(i):
        pltpu.make_async_copy(items[i], places(c)[i], R.m_w.at[c, i]).start()

    def other(i):
        src = x_h.at[o] if i == 0 else items[i]
        push(src, places(c)[i], R.m_ws.at[i], R.m_w.at[c, i], dev_c)

    for i in range(3):
        own(i)
    bar = pltpu.get_barrier_semaphore()
    peers = [dev_c] + [dev(k) for k in (1, 2, 3) for dev in (dev_x, dev_y, dev_z)]
    across = [(o,) + dev(k)[1:] for k in (1, 2, 3) for dev in (dev_y, dev_z)]

    def greet(devices):
        for dev in devices:
            pl.semaphore_signal(bar, inc=1, device_id=dev, device_id_type=MESH)

    greet(peers)

    @pl.when(c == 0)
    def _():
        greet(across)

    for i in (3, 4):
        own(i)
    singles = [
        pltpu.make_async_copy(cq_h, R.wcr.at[pl.ds(0, 192)], R.m_l.at[0]),
        pltpu.make_async_copy(co_h, R.wcr.at[pl.ds(192, 192)], R.m_l.at[1]),
        pltpu.make_async_copy(ckv_h, R.wcr.at[pl.ds(384, 384)], R.m_l.at[2]),
        pltpu.make_async_copy(cot_h.at[c], R.cot, R.m_l.at[3]),
    ]

    def enter():
        pl.semaphore_wait(bar, len(peers) + c * len(across))
        for i in range(3):
            other(i)

    def rest():
        for i in (3, 4):
            other(i)
        for i in (5, 6):
            own(i)
            other(i)
        for cp in singles:
            cp.start()

    def need(s, i):
        src = x_h.at[s] if i == 0 else items[i]
        pltpu.make_async_copy(src, places(s)[i], R.m_w.at[s, i]).wait()

    def rs_start(i, value):
        m = int(i in SECOND_RS)
        flush(("rs", m))
        R.rs[i] = value.astype(BF)
        for k in RINGS:
            to = lax.rem(t + k, 4)
            push(
                R.rs.at[i, pl.ds(pl.multiple_of(to * SH, SH), SH)],
                R.rr.at[i, k - 1],
                R.m_rss.at[m, k - 1],
                R.m_rsr.at[m, k - 1],
                dev_x(k),
                ("rs", m),
            )

    def rs_sum(i):
        for k in (1, 3, 2):
            landed(R.rr.at[i, k - 1], R.m_rsr.at[int(i in SECOND_RS), k - 1], dev_x(k))
        total = R.rs[i, rows_t, :].astype(F32)
        for k in range(3):
            total += R.rr[i, k].astype(F32)
        return total

    def ag_start(i, value):
        m = int(i in SECOND_AG)
        flush(("ag", m))
        R.ag[i, rows_t, :] = value.astype(BF)
        for k in RINGS:
            push(
                R.ag.at[i, rows_t],
                R.ag.at[i, rows_t],
                R.m_ags.at[m, k - 1],
                R.m_agr.at[m, k - 1],
                dev_x(k),
                ("ag", m),
            )

    def ag_wait(i):
        for k in (1, 3, 2):
            landed(R.ag.at[i, rows_t], R.m_agr.at[int(i in SECOND_AG), k - 1], dev_x(k))

    def gain_row(s, i):
        return R.nv[s, 0, i : i + 1, :]

    def bias_row(s, i):
        return R.nv[s, 1, i : i + 1, :]

    cross_gain = cg[...].reshape(1, D)
    cross_bias = cb[...].reshape(1, D)

    def softmax(scores):
        tops = [jnp.max(st, axis=0, keepdims=True) for st in scores]
        exps = [jnp.exp(st - top) for st, top in zip(scores, tops)]
        sums = [jnp.sum(e, axis=0, keepdims=True) for e in exps]
        return [e / total for e, total in zip(exps, sums)]

    def attend_backward(qts, kts, vts, prs, dots):
        heads = range(NH)
        dpts = [tn(vts[h], dots[h]) for h in heads]
        dvts = [nt(dots[h], prs[h].astype(BF)) for h in heads]
        sums = [jnp.sum(dpts[h] * prs[h], axis=0, keepdims=True) for h in heads]
        dsts = [(prs[h] * (dpts[h] - sums[h])).astype(BF) for h in heads]
        dqts = [nn(kts[h], dsts[h]) * SCALE for h in heads]
        dkts = [nt(qts[h], dsts[h]) * SCALE for h in heads]
        return dqts, dkts, dvts

    def self_forward(s):
        need(s, 0)
        need(s, 1)
        R.pk[s] = nt(R.wsa[s, 0:576, :], R.xin[s]).astype(BF)
        scores = [
            tn(R.pk[s, QW + lo : QW + lo + 64, :], R.pk[s, lo : lo + 64, :]) * SCALE for lo in HEADS
        ]
        if s == 1:
            key = lax.broadcasted_iota(jnp.int32, (TOK, TOK), 0)
            qry = lax.broadcasted_iota(jnp.int32, (TOK, TOK), 1)
            scores = [jnp.where(key <= qry, st, -1000000000.0) for st in scores]
        probs = softmax(scores)
        for h, lo in enumerate(HEADS):
            vt = R.pk[s, 2 * QW + lo : 2 * QW + lo + 64, :]
            R.ot[s, lo : lo + 64, :] = nn(vt, probs[h].astype(BF)).astype(BF)
            R.pt[s, h] = probs[h]
        need(s, 2)
        value = tn(R.ot[s], R.wsa[s, 576:768, :])
        if s == 0:
            enter()
        rs_start(R_SA + s, value)

    def put_norm(slot, spread):
        R.sp[slot] = jnp.broadcast_to(spread, (SH, 128))

    def get_norm(slot):
        return R.sp[slot, :, 0:1]

    def self_finish(s):
        total = rs_sum(R_SA + s)
        r = R.xin[s, rows_t, :].astype(F32) + total
        need(s, 3)
        need(s, 4)
        out, n, spread = ln_forward(r, gain_row(s, 0), bias_row(s, 0))
        ag_start(A_Y1 + s, out)
        R.y1f[s] = out
        R.n1[s] = n
        put_norm(s, spread)

    def ffn_forward(s, gathered):
        u = nn(R.ag[gathered], R.wff[s, 0])
        cdf = 0.5 * (1.0 + lax.erf(u * 0.7071067811865476))
        R.act[s] = (u * cdf).astype(BF)
        R.hid[...] = u
        R.slope[s] = cdf
        rs_start(R_FF + s, nn(R.act[s], R.wff[s, 1]))
        u = R.hid[...]
        R.slope[s] += u * jnp.exp(-0.5 * u * u) * 0.3989422804014327

    def ffn_backward(s):
        ag_wait(A_DR2 + s)
        dg = nt(R.ag[A_DR2 + s], R.wff[s, 1])
        R.du[s] = (dg * R.slope[s]).astype(BF)
        rs_start(R_DFF + s, nt(R.du[s], R.wff[s, 0]))

    def put(ref, piece, r0, value):
        rows = value.shape[0]
        ref[piece, 0, r0 : r0 + rows, :] = value[:, 0:384].astype(BF)
        ref[piece, 1, r0 : r0 + rows, :] = value[:, 384:768].astype(BF)

    def out_grad(s):
        return tn(R.act[s], R.ag[A_DR2 + s])

    def in_grad(s, gathered):
        return tn(R.ag[gathered], R.du[s])

    def put_halves(ref, value):
        put(ref, 0, 0, value[0:384])
        put(ref, 1, 0, value[384:768])

    def blk(name):
        bufs = tuple(getattr(R, pre + name) for pre in ("g_", "x_", "h_", "a_", "b_"))
        return bufs + (getattr(R, "s_" + GROUP[name]), getattr(R, "r_" + GROUP[name]))

    place = ((y, z), (z, y))
    devs = ((dev_y, dev_z), (dev_z, dev_y))

    def quarter(name, where):
        rows = BLOCKS[name] // 4
        return pl.ds(pl.multiple_of(where * rows, rows), rows)

    def eighth(name, where, half):
        rows = BLOCKS[name] // 8
        return pl.ds(pl.multiple_of(where * 2 * rows + half * rows, rows), rows)

    def step(where, k):
        return lax.rem(where + k, 4)

    def work(name):
        return pl.when(c == WORKER[name])

    def gone(src, sem):
        pltpu.make_async_remote_copy(
            src_ref=src, dst_ref=src, send_sem=sem, recv_sem=sem, device_id=dev_c, device_id_type=MESH
        ).wait_send()

    def ship(src, dst, ss, rs, dev):
        push(src, dst, ss, rs, dev, wait=False)

    def result(name, i, rows, half=slice(None)):
        if name == "crx":
            return oc_o.at[i, half, rows]
        if name == "ffd":
            return of_o.at[i, half, rows]
        if name in ("ffi", "ffo"):
            rows = pl.ds(pl.multiple_of(i * 384 + rows.start, 48), rows.size)
            return of_o.at[int(name == "ffo"), half, rows]
        return os_o.at[i, half, rows]

    def spot(name, i, rows, half=slice(None)):
        return R.x_sae.at[i, half, rows] if name == "sae" else result(name, i, rows, half)

    def g0(name, pieces=(0, 1)):
        g, x = blk(name)[:2]

        @pl.when(c != WORKER[name])
        def _():
            for i in pieces:
                sem = R.m_g0.at[tuple(BLOCKS).index(name), i]
                ship(g.at[i], x.at[i], sem, blk(name)[6].at[i, 0], dev_c)

    def g1(name, pieces=(0, 1)):
        g, x, h, a, b, s, r = blk(name)

        @work(name)
        def _():
            for i in pieces:
                landed(x.at[i], r.at[i, 0], dev_c)
                g[i] = g[i] + x[i]
                if name == "sae":
                    for k in RINGS:
                        part = g.at[i, :, quarter(name, step(place[i][0], k))]
                        ship(part, a.at[i, k - 1], s.at[i, k - 1], r.at[i, k], devs[i][0](k))
                    continue
                far = step(place[i][0], 2)
                for j, k in ((0, 1), (1, 3)):
                    part = g.at[i, :, eighth(name, far, j)]
                    ship(part, h.at[i, j], s.at[i, j], r.at[i, 1 + j], devs[i][0](k))

    def g1b(name, pieces=(0, 1)):
        g, x, h, a, b, s, r = blk(name)

        @work(name)
        def _():
            for j, k in ((0, 1), (1, 3)):
                for i in pieces:
                    near = step(place[i][0], k)
                    landed(h.at[i, j], r.at[i, 1 + j], dev_c)
                    part = eighth(name, near, j)
                    g[i, :, part, :] = g[i, :, part, :] + h[i, j]
                    part = g.at[i, :, quarter(name, near)]
                    gone(h.at[i, j], s.at[i, j])
                    ship(part, a.at[i, j], s.at[i, j], r.at[i, 3 + j], devs[i][0](k))

    def sub(name, i, where):
        return eighth(name, place[i][0], where // 2), lax.rem(where, 2)

    def g2(name, pieces=(0, 1)):
        g, x, h, a, b, s, r = blk(name)

        @work(name)
        def _():
            for i in pieces:
                mine = quarter(name, place[i][0])
                total = g[i, :, mine, :].astype(F32)
                for j in range(a.shape[1]):
                    landed(a.at[i, j], r.at[i, j + (1 if name == "sae" else 3)], dev_c)
                    total += a[i, j].astype(F32)
                    gone(a.at[i, j], s.at[i, j])
                g[i, :, mine, :] = total.astype(BF)
                if name in WHOLE:
                    part = g.at[i, :, mine]
                    for k in RINGS:
                        dst = b.at[i, place[i][1]]
                        ship(part, dst, s.at[i, k - 1], r.at[i, 4 + k], devs[i][1](k))
                    continue
                for k in RINGS:
                    rows, half = sub(name, i, step(place[i][1], k))
                    part = g.at[i, half, rows]
                    ship(part, b.at[i, k - 1], s.at[i, k - 1], r.at[i, 4 + k], devs[i][1](k))

    def g3(name, pieces=(0, 1)):
        g, x, h, a, b, s, r = blk(name)

        @work(name)
        def _():
            for i in pieces:
                if name in WHOLE:
                    mine = quarter(name, place[i][0])
                    b[i, place[i][1]] = g[i, :, mine, :]
                    for k in (1, 3, 2):
                        landed(a.at[i, 0], r.at[i, 4 + k], dev_c)
                        gone(a.at[i, 0], s.at[i, k - 1])
                    total = b[i, 0].astype(F32)
                    for j in (1, 2, 3):
                        total += b[i, j].astype(F32)
                    spot(name, i, mine)[...] = total.astype(BF)
                    continue
                for k in (1, 3, 2):
                    landed(b.at[i, k - 1], r.at[i, 4 + k], dev_c)
                rows, half = sub(name, i, place[i][1])
                total = g[i, half, rows, :].astype(F32)
                for k in range(3):
                    total += b[i, k].astype(F32)
                part = spot(name, i, rows, half)
                part[...] = total.astype(BF)
                for k in RINGS:
                    gone(b.at[i, k - 1], s.at[i, k - 1])
                    ship(part, part, s.at[i, k - 1], r.at[i, (3, 4, 0)[k - 1]], devs[i][1](k))

    def g4(name, pieces=(0, 1)):
        g, x, h, a, b, s, r = blk(name)

        @work(name)
        def _():
            for i in pieces:
                mine = quarter(name, place[i][0])
                part = spot(name, i, mine)
                for k in () if name in WHOLE else (1, 3, 2):
                    landed(b.at[i, k - 1], r.at[i, (3, 4, 0)[k - 1]], dev_c)
                    gone(b.at[i, k - 1], s.at[i, k - 1])
                if name == "sae":
                    dst = result(name, i, mine)
                    for k in RINGS:
                        to = (OWNER[name],) + devs[i][0](k)[1:]
                        ship(part, dst, s.at[i, k - 1], R.f_sae.at[i, k], to)
                    ship(part, dst, s.at[i, 3], R.f_sae.at[i, 0], dev_c)
                    continue
                for j, k in ((0, 1), (1, 3)):
                    ship(part, part, s.at[i, j], r.at[i, 2 - j], devs[i][0](k))

    def g4b(name, pieces=(0, 1)):
        g, x, h, a, b, s, r = blk(name)

        @work(name)
        def _():
            for j, k in ((0, 1), (1, 3)):
                for i in pieces:
                    behind = step(place[i][0], 4 - k)
                    landed(a.at[i, j], r.at[i, 2 - j], dev_c)
                    gone(a.at[i, j], s.at[i, j])
                    rows = eighth(name, behind, j)
                    part = spot(name, i, rows)
                    ship(part, part, s.at[i, j], r.at[i, 8 + j], devs[i][0](k))

    def g5(name):
        g, x, h, a, b, s, r = blk(name)

        @work(name)
        def _():
            for i in (0, 1):
                for j in (0, 1):
                    landed(h.at[i, j], r.at[i, 8 + j], dev_c)
            if name == "crx":
                ship(oc_o, oc_o, s.at[0, 2], R.m_hr.at[2], dev_c)

    def g6(name):
        g, x, h, a, b, s, r = blk(name)

        @pl.when(c != WORKER[name])
        def _():
            for i in (0, 1):
                gone(g.at[i], R.m_g0.at[tuple(BLOCKS).index(name), i])
            if name == "crx":
                landed(oc_o, R.m_hr.at[2], dev_c)
            if name == "sae":
                for i in (0, 1):
                    for j in range(4):
                        landed(a.at[i, 0], R.f_sae.at[i, j], dev_c)

        @work(name)
        def _():
            for i in (0, 1):
                if name == "sae":
                    for j in range(4):
                        gone(a.at[i, 0], s.at[i, j])
                    continue
                for j in (0, 1):
                    gone(h.at[i, j], s.at[i, j])
            if name == "crx":
                gone(oc_o, s.at[0, 2])

    def vec_put(row, dg, db, step=2):
        R.vec[row : row + 1, :] = dg
        R.vec[row + step : row + step + 1, :] = db

    def vec_send(buf, at, value, base, dev, count):
        buf[at] = value.astype(BF)
        for k in range(1, count):
            push(buf.at[at], buf.at[at], R.m_dps.at[base + k - 1], R.m_kvr.at[base + k - 1], dev(k))

    def vec_sum(buf, at, base, dev, count):
        for k in range(1, count):
            landed(buf.at[at], R.m_kvr.at[base + k - 1], dev(k))
        total = buf[0].astype(F32)
        for k in range(1, count):
            total += buf[k].astype(F32)
        return total

    def dev_c1(k):
        return dev_c

    self_forward(0)
    rest()
    for j in (10, 11, 12, 13, 14, 15):
        R.vec[j : j + 1, :] = jnp.zeros((1, D), F32)

    micro = lax.broadcasted_iota(jnp.int32, (2, 16), 0)
    group = lax.broadcasted_iota(jnp.int32, (2, 16), 1)
    live = (micro == c) & (group <= d) & (dgr[...] > 0)
    start = jnp.max(jnp.where(live, group, 0), axis=1, keepdims=True)
    start = jnp.max(start, axis=0, keepdims=True)
    rows = jnp.where(c == 0, ret[0], ret[1]) + start * TOK
    g_at = rows // TOK
    b_at = jnp.where(c == 0, g_at, lax.rem(g_at, 4) * 4 + g_at // 4)
    at = b_at * TOK + lax.rem(rows, TOK)
    first = (p, q)
    dev_first, dev_second = (dev_p, dev_q), (dev_q, dev_p)
    for u in (0, 1):
        R.pos[u, 0] = jnp.broadcast_to(at, (8, KEYS))
        for k in RINGS:
            m = 3 * u + k - 1
            push(R.pos.at[u, 0], R.pos.at[u, k], R.m_dps.at[m], R.m_kvr.at[m], dev_second[u](k))
    self_finish(0)
    ag_wait(A_Y1)
    need(0, 5)
    need(0, 6)
    ffn_forward(0, A_Y1)

    for cp in singles:
        cp.wait()
    for u in (0, 1):
        for k in (1, 3, 2):
            landed(R.pos.at[u, k], R.m_kvr.at[3 * u + k - 1], dev_c)

    def build(i, carry):
        rows = pl.ds(pl.multiple_of(i * TOK, TOK), TOK)
        for u in (0, 1):
            block = q * 4 + i if u == 0 else i * 4 + p
            n = lax.broadcasted_iota(jnp.int32, (TOK, KEYS), 0) + block * TOK
            for k in range(4):
                R.hot[u, k, rows, :] = jnp.where(n == R.pos[u, k, 0:1, :], 1.0, 0.0).astype(BF)
        return carry

    lax.fori_loop(0, 4, build, 0)

    out, n, spread = ln_forward(R.y1f[0] + rs_sum(R_FF), gain_row(0, 1), bias_row(0, 1))
    ag_start(A_BO, out)
    R.n2[0] = n
    put_norm(2, spread)
    self_forward(1)
    ag_wait(A_BO)

    def hot(u, k, j):
        return R.hot[u, k, pl.ds(pl.multiple_of(j * TOK, TOK), TOK), :]

    def picked(u, k, j):
        return nn(R.kvt[u, j], hot(u, k, j))

    for u in (0, 1):
        R.kvt[u, first[u]] = nt(R.wcr[384 + u * QW : 384 + u * QW + QW, :], R.ag[A_BO]).astype(BF)
        for k in RINGS:
            part, m = R.kvt.at[u, first[u]], 6 + 3 * u + k - 1
            push(part, part, R.m_dps.at[m], R.m_kvr.at[m], dev_first[u](k))
    self_finish(1)
    for u in (0, 1):
        for k in range(4):
            R.kvf[u, k] = picked(u, k, first[u])
    for u in (0, 1):
        for j in (1, 3):
            landed(R.kvt.at[u, 0], R.m_kvr.at[6 + 3 * u + j - 1], dev_c)
            for k in range(4):
                R.kvf[u, k] += picked(u, k, lax.rem(first[u] + 4 - j, 4))
        landed(R.kvt.at[u, 0], R.m_kvr.at[6 + 3 * u + 1], dev_c)
        for k in RINGS + (0,):
            R.kvs[u, k] = (R.kvf[u, k] + picked(u, k, lax.rem(first[u] + 2, 4))).astype(BF)
            if k:
                m = 12 + 3 * u + 3 - k
                dst = R.kvr.at[u, 3 - k]
                push(R.kvs.at[u, k], dst, R.m_dps.at[m], R.m_kvr.at[m], dev_second[u](4 - k))
    ag_wait(A_Y1 + 1)
    R.qct[...] = nt(R.wcr[0:192, :], R.ag[A_Y1 + 1]).astype(BF)

    def chosen(u):
        for k in (1, 3, 2):
            landed(R.kvr.at[u, k - 1], R.m_kvr.at[12 + 3 * u + k - 1], dev_c)
        total = R.kvs[u, 0].astype(F32)
        for k in range(3):
            total += R.kvr[u, k].astype(F32)
        R.kvct[u * QW : u * QW + QW, :] = total.astype(BF)

    chosen(0)
    probs = softmax(
        [tn(R.kvct[lo : lo + 64, :], R.qct[lo : lo + 64, :]) * SCALE for lo in HEADS]
    )
    chosen(1)
    for h, lo in enumerate(HEADS):
        vt = R.kvct[QW + lo : QW + lo + 64, :]
        R.oct[lo : lo + 64, :] = nn(vt, probs[h].astype(BF)).astype(BF)
        R.ptc[h] = probs[h]
    rs_start(R_CR, tn(R.oct[...], R.wcr[192:384, :]))
    need(1, 5)
    need(1, 6)
    out, n, spread = ln_forward(R.y1f[1] + rs_sum(R_CR), cross_gain, cross_bias)
    ag_start(A_Y2, out)
    R.y2f[...] = out
    R.nc[...] = n
    put_norm(4, spread)
    ag_wait(A_Y2)
    ffn_forward(1, A_Y2)
    out, n, spread = ln_forward(R.y2f[...] + rs_sum(R_FF + 1), gain_row(1, 1), bias_row(1, 1))

    dr, dg, db = ln_backward(n, spread, gain_row(1, 1), R.cot[rows_t, :].astype(F32))
    ag_start(A_DR2 + 1, dr)
    R.dres[1] = dr
    vec_put(5, dg, db)
    ffn_backward(1)
    ag_start(A_BO + 1, out)
    flush("")
    put(R.g_ffd, 0, 0, in_grad(1, A_Y2))
    g0("ffd", (0,))
    put(R.g_ffd, 1, 0, out_grad(1))
    g0("ffd", (1,))
    dy = R.dres[1] + rs_sum(R_DFF + 1)
    dr, dg, db = ln_backward(R.nc[...], get_norm(4), cross_gain, dy)
    ag_start(A_DRC, dr)
    R.dres[1] = dr
    vec_put(8, dg, db, 1)
    g1("ffd")
    ag_wait(A_DRC)

    def compact(u):
        for k in RINGS:
            m = 3 * u + k - 1
            part = R.dkvct.at[pl.ds(u * QW, QW)]
            push(part, R.dkr.at[u, k - 1], R.m_dps.at[m], R.m_kvr.at[m], dev_second[u](k))

    doc = nt(R.wcr[192:384, :], R.ag[A_DRC]).astype(BF)
    heads = list(enumerate(HEADS))
    for h, lo in heads:
        dvt = nt(doc[lo : lo + 64, :], R.ptc[h].astype(BF))
        R.dkvct[QW + lo : QW + lo + 64, :] = dvt.astype(BF)
    compact(1)
    dpts = [tn(R.kvct[QW + lo : QW + lo + 64, :], doc[lo : lo + 64, :]) for h, lo in heads]
    sums = [jnp.sum(dpts[h] * R.ptc[h], axis=0, keepdims=True) for h, lo in heads]
    dsts = [(R.ptc[h] * (dpts[h] - sums[h])).astype(BF) for h, lo in heads]
    for h, lo in heads:
        dkt = nt(R.qct[lo : lo + 64, :], dsts[h]) * SCALE
        R.dkvct[lo : lo + 64, :] = dkt.astype(BF)
    compact(0)
    for h, lo in heads:
        dqt = nn(R.kvct[lo : lo + 64, :], dsts[h]) * SCALE
        R.dqct[lo : lo + 64, :] = dqt.astype(BF)
    rs_start(R_DQ, tn(R.dqct[...], R.wcr[0:192, :]))
    put(R.g_crx, 0, 0, nn(R.dqct[...], R.ag[A_Y1 + 1]))
    put(R.g_crx, 0, 192, nn(R.oct[...], R.ag[A_DRC]))
    g0("crx", (0,))
    dy = R.dres[1] + rs_sum(R_DQ)
    dr, dg, db = ln_backward(R.n1[1], get_norm(1), gain_row(1, 0), dy)
    ag_start(A_DR1 + 1, dr)
    R.dres[1] = dr
    vec_put(4, dg, db)
    g1b("ffd", (0,))

    def self_backward(s):
        ag_wait(A_DR1 + s)
        dot = nt(R.wsa[s, 576:768, :], R.ag[A_DR1 + s]).astype(BF)
        dqts, dkts, dvts = attend_backward(
            [R.pk[s, lo : lo + 64, :] for lo in HEADS],
            [R.pk[s, QW + lo : QW + lo + 64, :] for lo in HEADS],
            [R.pk[s, 2 * QW + lo : 2 * QW + lo + 64, :] for lo in HEADS],
            [R.pt[s, h] for h in range(NH)],
            [dot[lo : lo + 64, :] for lo in HEADS],
        )
        for h, lo in enumerate(HEADS):
            R.dpk[s, lo : lo + 64, :] = dqts[h].astype(BF)
            R.dpk[s, QW + lo : QW + lo + 64, :] = dkts[h].astype(BF)
            R.dpk[s, 2 * QW + lo : 2 * QW + lo + 64, :] = dvts[h].astype(BF)

    def self_grads(s, name):
        ref = getattr(R, "g_" + name)
        put(ref, 0, 0, nn(R.dpk[s, 0:384, :], R.xin[s]))
        g0(name, (0,))
        put(ref, 1, 0, nn(R.dpk[s, 384:576, :], R.xin[s]))
        put(ref, 1, 192, nn(R.ot[s], R.ag[A_DR1 + s]))
        g0(name, (1,))

    def input_part(s):
        rs_start(R_DSA + s, tn(R.dpk[s], R.wsa[s, 0:576, :]))

    for u in (1, 0):
        for j in range(4):
            R.dkf[u, j] = nt(R.dkvct[u * QW : u * QW + QW, :], hot(u, 0, j))
    for u in (1, 0):
        for k in (1, 3):
            landed(R.dkr.at[u, k - 1], R.m_kvr.at[3 * u + k - 1], dev_c)
            for j in range(4):
                R.dkf[u, j] += nt(R.dkr[u, k - 1], hot(u, k, j))
        landed(R.dkr.at[u, 1], R.m_kvr.at[3 * u + 1], dev_c)
        for k in RINGS + (0,):
            to = lax.rem(first[u] + k, 4)
            R.dks[u, to] = (R.dkf[u, to] + nt(R.dkr[u, 1], hot(u, 2, to))).astype(BF)
            if k:
                m = 6 + 3 * (1 - u) + k - 1
                dst = R.dk2.at[u, k - 1]
                push(R.dks.at[u, to], dst, R.m_dps.at[m], R.m_kvr.at[m], dev_first[u](k))
    g1b("ffd", (1,))
    self_backward(1)
    input_part(1)
    self_grads(1, "sad")
    g1("crx", (0,))
    for u in (1, 0):
        for k in (1, 3, 2):
            landed(R.dk2.at[u, k - 1], R.m_kvr.at[6 + 3 * (1 - u) + k - 1], dev_c)
        total = R.dks[u, first[u]].astype(F32)
        for k in range(3):
            total += R.dk2[u, k].astype(F32)
        R.dkv[u * QW : u * QW + QW, :] = total.astype(BF)
    rs_start(R_DST, tn(R.dkv[...], R.wcr[384:768, :]))
    put(R.g_crx, 1, 0, nn(R.dkv[...], R.ag[A_BO]))
    g0("crx", (1,))
    g2("ffd")
    g1("sad")
    g1b("crx", (0,))
    dy = rs_sum(R_DST)
    dr, dg, db = ln_backward(R.n2[0], get_norm(2), gain_row(0, 1), dy)
    ag_start(A_DR2, dr)
    R.dres[0] = dr
    vec_put(1, dg, db)
    flush("")
    ag_wait(A_BO + 1)
    push(R.ag.at[A_BO + o], bo_o.at[c], R.m_hs.at[0], R.m_hr.at[0], dev_c)
    outs = [pltpu.make_async_copy(R.ag.at[A_BO + c], bo_o.at[c], R.m_o.at[0])]
    outs[0].start()
    g3("ffd")
    g1("crx", (1,))
    g1b("sad")
    g2("crx", (0,))
    ffn_backward(0)
    put_halves(R.g_ffo, out_grad(0))
    g0("ffo")
    put_halves(R.g_ffi, in_grad(0, A_Y1))
    g0("ffi")
    g4("ffd")
    g1b("crx", (1,))
    g3("crx", (0,))
    g2("sad")
    g1("ffo")
    dy = R.dres[0] + rs_sum(R_DFF)
    dr, dg, db = ln_backward(R.n1[0], get_norm(0), gain_row(0, 0), dy)
    ag_start(A_DR1, dr)
    R.dres[0] = dr
    vec_put(0, dg, db)
    g1("ffi")
    g4b("ffd")
    g4("crx", (0,))
    g2("crx", (1,))
    g3("sad")
    g1b("ffo")
    self_backward(0)
    g1b("ffi")
    self_grads(0, "sae")
    vec_send(R.vx, t, R.vec[...], 0, dev_x, 4)
    input_part(0)
    ag_start(A_IG + 1, R.dres[1] + rs_sum(R_DSA + 1))
    g1("sae")
    g2("ffo")
    total = vec_sum(R.vx, t, 0, dev_x, 4)
    vec_send(R.vc, c, total, 3, dev_c1, 2)
    g3("crx", (1,))
    g4b("crx", (0,))
    g4("sad")
    g2("ffi")
    total = vec_sum(R.vc, c, 3, dev_c1, 2)
    vec_send(R.vy, y, total, 12, dev_y, 4)
    ag_start(A_IG, R.dres[0] + rs_sum(R_DSA))
    g3("ffo")
    g2("sae")
    g4("crx", (1,))
    g3("ffi")
    total = vec_sum(R.vy, y, 12, dev_y, 4)
    vec_send(R.vz, z, total, 15, dev_z, 4)
    g4("ffo")
    g3("sae")
    g4b("sad")
    g4b("crx", (1,))
    g4("ffi")
    g4("sae")
    g5("crx")
    ag_wait(A_IG)
    ag_wait(A_IG + 1)
    push(R.ag.at[A_IG + o], ig_o.at[c], R.m_hs.at[1], R.m_hr.at[1], dev_c)
    outs.append(pltpu.make_async_copy(R.ag.at[A_IG + c], ig_o.at[c], R.m_o.at[1]))
    outs[1].start()
    g4b("ffo")
    total = vec_sum(R.vz, z, 15, dev_z, 4)
    on_o[...] = jnp.where(c == 0, total[0:4, :], total[4:8, :])
    oe_o[...] = total[8:10, :]
    flush("")
    g4b("ffi")
    landed(bo_o.at[c], R.m_hr.at[0], dev_c)
    landed(ig_o.at[c], R.m_hr.at[1], dev_c)
    for cp in outs:
        cp.wait()
    g5("ffd")
    g5("sad")
    g5("ffo")
    g5("ffi")
    for name in ("ffd", "sad", "crx", "ffo", "ffi", "sae"):
        g6(name)
    for kind in list(sends):
        flush(kind)


JOBS = (
    [("gf", 0, r, "win", r) for r in (0, 192, 384, 576)]
    + [("gf", 1, r, "wfo", r) for r in (0, 192, 384, 576)]
    + [("gc", 0, 0, "q", 0), ("gc", 0, 192, "co", 0), ("gc", 1, 0, "kv", 0), ("gc", 1, 192, "kv", 192)]
    + [("gs", 0, 0, "qkv", 0), ("gs", 0, 192, "qkv", 192), ("gs", 1, 0, "qkv", 384)]
    + [("gs", 1, 192, "out", 0)]
)


def widen(*refs):
    bo, ig, gf, gs, gc, gn, ge = refs[:7]
    bo_o, ig_o, qkv_o, out_o, win_o, wfo_o, ng_o, nb_o, q_o, kv_o, co_o, cg_o, cb_o = refs[7:20]
    wide, ig_wide, m_out, m_x = refs[20:]
    from_ = {"gf": gf, "gs": gs, "gc": gc}
    to = {"qkv": qkv_o, "out": out_o, "win": win_o, "wfo": wfo_o, "q": q_o, "kv": kv_o, "co": co_o}
    stores = [pltpu.make_async_copy(bo, bo_o, m_x.at[0])]
    stores[0].start()
    for i, (src, piece, r0, dst, d0) in enumerate(JOBS):
        wide[i, :, 0:384] = from_[src][piece, 0, r0 : r0 + 192, :].astype(F32)
        wide[i, :, 384:768] = from_[src][piece, 1, r0 : r0 + 192, :].astype(F32)
        cp = pltpu.make_async_copy(wide.at[i], to[dst].at[pl.ds(d0, 192)], m_out.at[i])
        cp.start()
        stores.append(cp)
    ig_wide[...] = ig[...].astype(F32)
    stores.append(pltpu.make_async_copy(ig_wide, ig_o, m_x.at[1]))
    stores[-1].start()
    ng_o[...] = gn[0:2, :]
    nb_o[...] = gn[2:4, :]
    cg_o[...] = ge[0:1, :].reshape(D)
    cb_o[...] = ge[1:2, :].reshape(D)
    for cp in stores:
        cp.wait()


def body(
    layer_inputs,
    cotangent,
    doc_groups,
    retrieved_at,
    sa_qkv,
    sa_out,
    ffn_in,
    ffn_out,
    norm_gain,
    norm_bias,
    cross_q,
    cross_kv,
    cross_out,
    cross_gain,
    cross_bias,
):
    ins = (
        layer_inputs[0],
        cotangent,
        doc_groups,
        retrieved_at,
        norm_gain[0],
        norm_bias[0],
        cross_gain,
        cross_bias,
        jnp.transpose(sa_qkv[0], (1, 2, 0)).reshape(576, D),
        sa_out[0],
        ffn_in[0],
        ffn_out[0],
        jnp.transpose(cross_q, (1, 0)),
        jnp.transpose(cross_kv, (1, 2, 0)).reshape(384, D),
        cross_out,
    )
    hbm = pl.BlockSpec(memory_space=pl.ANY)
    vm = pl.BlockSpec(memory_space=VMEM)
    outs = (
        VMEM((2, TOK, D), BF),
        VMEM((2, TOK, D), BF),
        VMEM((2, 2, 768, 384), BF),
        VMEM((2, 2, 384, 384), BF),
        VMEM((2, 2, 384, 384), BF),
        VMEM((4, D), F32),
        VMEM((2, D), F32),
    )
    names = [n for n, _ in scratch_list()]

    def run(*refs):
        kernel(names, len(ins), len(outs), *refs)

    results = pl.pallas_call(
        run,
        out_shape=outs,
        in_specs=[hbm, hbm, vm, vm, hbm, hbm, vm, vm] + [hbm] * 7,
        out_specs=[vm] * len(outs),
        scratch_shapes=[s for _, s in scratch_list()],
        compiler_params=pltpu.CompilerParams(
            collective_id=0, has_side_effects=True, vmem_limit_bytes=52 << 20
        ),
        name="layers",
    )(*ins)
    wide_outs = (
        jax.ShapeDtypeStruct((2, TOK, D), BF),
        jax.ShapeDtypeStruct((2, TOK, D), F32),
        jax.ShapeDtypeStruct((576, D), F32),
        jax.ShapeDtypeStruct((192, D), F32),
        jax.ShapeDtypeStruct((768, D), F32),
        jax.ShapeDtypeStruct((768, D), F32),
        jax.ShapeDtypeStruct((2, D), F32),
        jax.ShapeDtypeStruct((2, D), F32),
        jax.ShapeDtypeStruct((192, D), F32),
        jax.ShapeDtypeStruct((384, D), F32),
        jax.ShapeDtypeStruct((192, D), F32),
        jax.ShapeDtypeStruct((D,), F32),
        jax.ShapeDtypeStruct((D,), F32),
    )
    bo, ig, d_qkv, d_out, d_in, d_fo, ng, nb, d_q, d_kv, d_co, dcg, dcb = pl.pallas_call(
        widen,
        out_shape=wide_outs,
        in_specs=[vm] * 7,
        out_specs=[hbm] * 6 + [vm] * 2 + [hbm] * 3 + [vm] * 2,
        scratch_shapes=[
            VMEM((len(JOBS), 192, D), F32),
            VMEM((2, TOK, D), F32),
            DMA((len(JOBS),)),
            DMA((2,)),
        ],
        compiler_params=pltpu.CompilerParams(vmem_limit_bytes=32 << 20),
        name="widen",
    )(*[pltpu.with_memory_space_constraint(r, VMEM) for r in results])
    return (
        bo[None],
        ig[None],
        jnp.transpose(d_qkv.reshape(3, 192, D), (2, 0, 1))[None],
        d_out[None],
        d_in[None],
        d_fo[None],
        ng[None],
        nb[None],
        jnp.transpose(d_q, (1, 0)),
        jnp.transpose(d_kv.reshape(2, 192, D), (2, 0, 1)),
        d_co,
        dcg,
        dcb,
    )


def solution(mesh):
    placed = (
        P("section", None, "dp", None),
        P(None, "dp", None),
        P(),
        P(None, "dp", None),
        P("section", None, None, "tensor"),
        P("section", "tensor", None),
        P("section", None, "tensor"),
        P("section", "tensor", None),
        P("section", None, None),
        P("section", None, None),
        P(None, "tensor"),
        P(None, None, "tensor"),
        P("tensor", None),
        P(),
        P(),
    )
    return jax.shard_map(
        body,
        mesh=mesh,
        in_specs=placed,
        out_specs=(
            P("section", None, "dp", None),
            P("section", None, "dp", None),
            P("section", None, None, "tensor"),
            P("section", "tensor", None),
            P("section", None, "tensor"),
            P("section", "tensor", None),
            P("section", None, None),
            P("section", None, None),
            P(None, "tensor"),
            P(None, None, "tensor"),
            P("tensor", None),
            P(),
            P(),
        ),
        check_vma=False,
    )
```
